32 devices in a mesh: outer: 8 (over y, x, core), inner: 4 (over z).
Axes of the slice: x: 2, y: 2, z: 4, core: 2. Of those that a mesh axis runs over, the one named last changes fastest.
Arguments:
- gate: float32 [128, 16384], P(None, ('outer', 'inner')), may hold values from -6 to 6
- keys: float32 [128, 16384], P(None, ('outer', 'inner')), may hold values from -6 to 6
- values: float32 [128, 16384], P(None, ('outer', 'inner')), may hold values from -6 to 6
- taps: float32 [128, 16384], P(None, ('outer', 'inner')), may hold values from -0.046875 to 0.046875
- skip_gain: float32 [128], replicated, may hold values from 0.5 to 2
Outputs:
- mixed: float32 [128, 16384], P(None, ('outer', 'inner'))
The draws below stay inside these ranges and needn't reach their ends.
All inputs are finite; a program needn't handle non-finite values.
Results may differ from the reference program's by a relative error of at most 0.000053.
Values sent between devices are 32-bit elements; how exact they have to be, the bound alone decides.
No kernel may reach another device: no remote copies, remote signals or barrier semaphores. Data moves between devices by JAX's collectives and lax.ppermute only.
A program may use at most 64 MiB of HBM per device.

```python
import math
import jax
import jax.numpy as jnp
from jax import lax

CH = 128
LENGTH = 16384


def levels(rng, shape, cuts, smallest, high):
    loudness = 1.0
    for axis_at, shards_of in cuts:
        draws = jax.random.uniform(jax.random.fold_in(jax.random.fold_in(rng, 6), axis_at), (shards_of,), jnp.float32, smallest / len(cuts), high / len(cuts))
        loudness = loudness * jnp.repeat(jnp.exp(draws), shape[axis_at] // shards_of).reshape((-1,) + (1,) * (len(shape) - 1 - axis_at))
    return loudness


def noise(rng, extent, scale, limit, split=(), kind=jnp.bfloat16):
    drawn = scale * jax.random.normal(rng, extent, jnp.float32)
    if split:
        drawn = drawn * levels(rng, extent, split, -0.22, 0.18)
    return jnp.clip(drawn, -limit, limit).astype(kind)


def setup_inputs(seed: int = 0) -> dict:
    arg_keys = jax.random.split(jax.random.key(seed), 6)
    return {
        "gate": noise(arg_keys[0], (CH, LENGTH), 1.0, 6.0, ((1, 32),), jnp.float32),
        "keys": noise(arg_keys[1], (CH, LENGTH), 1.0, 6.0, ((1, 32),), jnp.float32),
        "values": noise(arg_keys[2], (CH, LENGTH), 1.0, 6.0, ((1, 32),), jnp.float32),
        "taps": noise(arg_keys[3], (CH, LENGTH), LENGTH ** -0.5, 0.046875, ((1, 32),), jnp.float32),
        "skip_gain": jnp.clip(jnp.exp(jax.random.uniform(arg_keys[4], (CH,), jnp.float32, math.log(0.5), math.log(2.0))), 0.5, 2.0),
    }


def reference(gate, keys, values, taps, skip_gain):
    product = keys * values

    def one_channel(args):
        row, filt = args
        padded = jnp.concatenate([row, jnp.zeros_like(row)])
        padded_taps = jnp.concatenate([filt, jnp.zeros_like(filt)])
        spectrum = jnp.fft.rfft(padded)
        taps_spectrum = jnp.fft.rfft(padded_taps)
        return jnp.fft.irfft(spectrum * taps_spectrum, n=2 * LENGTH)[:LENGTH].astype(row.dtype)

    conv = lax.map(one_channel, (product, taps))
    return gate * (conv + skip_gain[:, None] * product)
```

```python
from functools import partial
import math

import jax
import jax.numpy as jnp
import ml_dtypes
import numpy as np
from jax import lax
from jax.experimental import pallas as pl
from jax.experimental.pallas import tpu as pltpu
from jax.sharding import PartitionSpec as P

LANES = 128
AXES = ("outer", "inner")

TWO_PI = 2.0 * math.pi
HIGHEST = lax.Precision.HIGHEST


def table(count_a, count_b, modulus, sign):
    left = lax.broadcasted_iota(jnp.int32, (count_a, count_b), 0)
    right = lax.broadcasted_iota(jnp.int32, (count_a, count_b), 1)
    phase = TWO_PI / modulus * (left * right % modulus).astype(jnp.float32)
    return (jnp.cos(phase), sign * jnp.sin(phase))


def mix(form, cosine, sine, real, imag):
    contract = partial(jnp.einsum, precision=HIGHEST)
    return (
        contract(form, cosine, real) - contract(form, sine, imag),
        contract(form, sine, real) + contract(form, cosine, imag),
    )


def rotate(real, imag, cosine, sine):
    return (real * cosine - imag * sine, real * sine + imag * cosine)


def forward_rows(real, imag):
    split = 16
    lead = real.shape[:-1]
    size = real.shape[-1]
    short = size // split
    real = real.reshape(lead + (split, short))
    imag = imag.reshape(lead + (split, short))
    cosine, sine = table(split, split, split, -1.0)
    real, imag = mix("ka,...as->...ks", cosine, sine, real, imag)
    cosine, sine = table(split, short, size, -1.0)
    real, imag = rotate(real, imag, cosine, sine)
    cosine, sine = table(short, short, short, -1.0)
    real, imag = mix("sb,...ks->...bk", cosine, sine, real, imag)
    return (real.reshape(lead + (size,)), imag.reshape(lead + (size,)))


def inverse_rows(real, imag):
    split = 16
    lead = real.shape[:-1]
    size = real.shape[-1]
    short = size // split
    real = real.reshape(lead + (short, split))
    imag = imag.reshape(lead + (short, split))
    cosine, sine = table(short, short, short, 1.0)
    real, imag = mix("sb,...bk->...sk", cosine, sine, real, imag)
    cosine, sine = table(short, split, size, 1.0)
    real, imag = rotate(real, imag, cosine, sine)
    cosine, sine = table(split, split, split, 1.0)
    real, imag = mix("ak,...sk->...as", cosine, sine, real, imag)
    return (real.reshape(lead + (size,)), imag.reshape(lead + (size,)))


def by_sections(gate, keys, values, taps, skip_gain):
    inner_count = lax.axis_size("inner")
    devices = lax.axis_size("outer") * inner_count
    rank = lax.axis_index("outer") * inner_count + lax.axis_index("inner")
    chans, seg = keys.shape
    both = 2 * chans
    cols = seg // devices
    blocks = 2 * devices
    full = blocks * seg
    contract = partial(jnp.einsum, precision=HIGHEST)
    product = keys * values
    source = jnp.concatenate([product, taps], axis=0)
    sectioned = lax.all_to_all(
        lax.all_to_all(
            source.reshape(both, 1, 1, seg), "outer", split_axis=3, concat_axis=1, tiled=True
        ),
        "inner",
        split_axis=3,
        concat_axis=2,
        tiled=True,
    )
    sectioned = sectioned.reshape(both, devices, cols)
    cosine, sine = table(blocks, devices, blocks, -1.0)
    real = contract("km,cmj->ckj", cosine, sectioned)
    imag = contract("km,cmj->ckj", sine, sectioned)
    offset = rank * cols + lax.broadcasted_iota(jnp.int32, (blocks, cols), 1)
    residue = lax.broadcasted_iota(jnp.int32, (blocks, cols), 0)
    phase = TWO_PI / full * (offset * residue).astype(jnp.float32)
    real, imag = rotate(real, imag, jnp.cos(phase)[None], -jnp.sin(phase)[None])
    outgoing = jnp.stack([real, imag]).reshape(2, both, blocks, 1, 1, cols)
    moved = lax.all_to_all(
        lax.all_to_all(outgoing, "outer", split_axis=2, concat_axis=3, tiled=True),
        "inner",
        split_axis=2,
        concat_axis=4,
        tiled=True,
    )
    moved = moved.reshape(2, both, 2, seg)
    spec_real, spec_imag = forward_rows(moved[0], moved[1])
    sig_real, filt_real = (spec_real[:chans], spec_real[chans:])
    sig_imag, filt_imag = (spec_imag[:chans], spec_imag[chans:])
    real = sig_real * filt_real - sig_imag * filt_imag
    imag = sig_real * filt_imag + sig_imag * filt_real
    real, imag = inverse_rows(real, imag)
    residue = 2 * rank + lax.broadcasted_iota(jnp.int32, (2, seg), 0)
    offset = lax.broadcasted_iota(jnp.int32, (2, seg), 1)
    phase = TWO_PI / full * (offset * residue).astype(jnp.float32)
    real, imag = rotate(real, imag, jnp.cos(phase)[None], jnp.sin(phase)[None])
    returning = jnp.stack([real, imag]).reshape(2, chans, 1, 1, 2, seg)
    gathered = lax.all_to_all(
        lax.all_to_all(returning, "outer", split_axis=5, concat_axis=2, tiled=True),
        "inner",
        split_axis=5,
        concat_axis=3,
        tiled=True,
    )
    gathered = gathered.reshape(2, chans, blocks, cols)
    cosine, sine = table(devices, blocks, blocks, 1.0)
    conv = contract("mk,ckj->cmj", cosine, gathered[0]) - contract("mk,ckj->cmj", sine, gathered[1])
    conv = conv * (1.0 / full)
    conv = lax.all_to_all(
        lax.all_to_all(
            conv.reshape(chans, devices, 1, 1, cols),
            "outer",
            split_axis=1,
            concat_axis=2,
            tiled=True,
        ),
        "inner",
        split_axis=1,
        concat_axis=3,
        tiled=True,
    )
    conv = conv.reshape(chans, seg)
    return gate * (conv + skip_gain[:, None] * product)


def halves(array):
    high = array.astype(ml_dtypes.bfloat16)
    low = (array - high.astype(np.float64)).astype(ml_dtypes.bfloat16)
    return high, low


def transform_tables(devices, seg):
    length = devices * seg
    count = length // LANES
    parts = seg // LANES
    odd = 2 * np.arange(count) + 1
    place = (np.arange(devices)[None, :] * parts + np.arange(parts)[:, None]).reshape(-1)
    angle = 2 * np.pi / (4 * count) * ((odd[:, None] * place[None, :]) % (4 * count))
    first = np.concatenate([np.cos(angle), -np.sin(angle)], axis=0)
    last = np.concatenate([np.cos(angle).T, -np.sin(angle).T], axis=1) / length
    angle = 2 * np.pi / (4 * length) * ((odd[:, None] * np.arange(LANES)[None, :]) % (4 * length))
    twiddle = np.stack([np.cos(angle), np.sin(angle)]).astype(np.float32)
    angle = 2 * np.pi / LANES * ((np.arange(LANES)[:, None] * np.arange(LANES)[None, :]) % LANES)
    cosine, sine = np.cos(angle), np.sin(angle)
    rows = np.block([[cosine, -sine], [sine, cosine]])
    back = np.block([[cosine, sine], [-sine, cosine]])
    first_high, first_low = halves(first)
    rows_high, rows_low = halves(rows)
    back_high, back_low = halves(back)
    last_high, last_low = halves(last)
    return (
        np.concatenate([first_high, first_high, first_low], axis=1),
        np.concatenate([rows_high, rows_high, rows_low], axis=0),
        np.concatenate([back_high, back_high, back_low], axis=0),
        np.concatenate([last_high, last_high, last_low], axis=1),
        twiddle,
    )


def split(array):
    high = array.astype(jnp.bfloat16)
    return high, (array - high.astype(jnp.float32)).astype(jnp.bfloat16)


def dot(left, right):
    return jnp.dot(left, right, preferred_element_type=jnp.float32)


def convolve_kernel(devices, chans, seg, data_ref, first_ref, rows_ref, back_ref, last_ref, twiddle_ref, out_ref):
    parts = seg // LANES
    count = devices * parts
    signals = 2 * chans
    cosine, sine = twiddle_ref[0], twiddle_ref[1]

    def lanes(at):
        return slice(at * LANES, (at + 1) * LANES)

    columns = []
    for signal in range(signals):
        columns.append(
            jnp.concatenate(
                [
                    data_ref[pl.ds(part * signals + signal, devices, stride=parts * signals), :]
                    for part in range(parts)
                ],
                axis=0,
            )
        )
    high, low = split(jnp.concatenate(columns, axis=1))
    begun = dot(first_ref[...], jnp.concatenate([high, low, high], axis=0))
    turned = []
    for signal in range(signals):
        real, imag = begun[:count, lanes(signal)], begun[count:, lanes(signal)]
        turned.append(jnp.concatenate([real * cosine + imag * sine, imag * cosine - real * sine], axis=1))
    high, low = split(jnp.concatenate(turned, axis=0))
    spectrum = dot(jnp.concatenate([high, low, high], axis=1), rows_ref[...])
    mid = chans * count
    sig_real, sig_imag = spectrum[:mid, :LANES], spectrum[:mid, LANES:]
    filt_real, filt_imag = spectrum[mid:, :LANES], spectrum[mid:, LANES:]
    filtered = jnp.concatenate(
        [sig_real * filt_real - sig_imag * filt_imag, sig_real * filt_imag + sig_imag * filt_real], axis=1
    )
    high, low = split(filtered)
    backed = dot(jnp.concatenate([high, low, high], axis=1), back_ref[...])
    turned = []
    for chan in range(chans):
        real = backed[chan * count : (chan + 1) * count, :LANES]
        imag = backed[chan * count : (chan + 1) * count, LANES:]
        turned.append(jnp.concatenate([real * cosine - imag * sine, imag * cosine + real * sine], axis=0))
    high, low = split(jnp.concatenate(turned, axis=1))
    conv = dot(last_ref[...], jnp.concatenate([high, low, high], axis=0))
    for chan in range(chans):
        for part in range(parts):
            out_ref[pl.ds(part * chans + chan, devices, stride=parts * chans), :] = conv[
                part * devices : (part + 1) * devices, lanes(chan)
            ]


def convolve(data, devices, chans, seg):
    tables = transform_tables(devices, seg)
    return pl.pallas_call(
        partial(convolve_kernel, devices, chans, seg),
        out_shape=jax.ShapeDtypeStruct((devices * chans * seg // LANES, LANES), jnp.float32),
        in_specs=[pl.BlockSpec(memory_space=pltpu.VMEM)] * 6,
        out_specs=pl.BlockSpec(memory_space=pltpu.VMEM),
        compiler_params=pltpu.CompilerParams(vmem_limit_bytes=32 * 2**20),
        cost_estimate=pl.CostEstimate(flops=2 * 10**9, bytes_accessed=2 * 10**6, transcendentals=0),
    )(data, *(jnp.asarray(table) for table in tables))


def by_channels(gate, keys, values, taps, skip_gain):
    devices = lax.axis_size("outer") * lax.axis_size("inner")
    chans, seg = keys.shape
    own = chans // devices
    product = keys * values
    outgoing = jnp.concatenate([product.reshape(devices, own, seg), taps.reshape(devices, own, seg)], axis=1)
    outgoing = outgoing.reshape(devices, 2 * own, seg // LANES, LANES).swapaxes(1, 2)
    arrived = lax.all_to_all(outgoing, AXES, split_axis=0, concat_axis=0, tiled=True)
    conv = convolve(arrived.reshape(-1, LANES), devices, own, seg)
    conv = lax.all_to_all(conv, AXES, split_axis=0, concat_axis=0, tiled=True)
    conv = conv.reshape(devices, seg // LANES, own, LANES).swapaxes(1, 2).reshape(chans, seg)
    return gate * (conv + skip_gain[:, None] * product)


def on_device(gate, keys, values, taps, skip_gain):
    devices = lax.axis_size("outer") * lax.axis_size("inner")
    chans, seg = keys.shape
    if chans % devices == 0 and seg % LANES == 0 and devices % 8 == 0:
        return by_channels(gate, keys, values, taps, skip_gain)
    return by_sections(gate, keys, values, taps, skip_gain)


def solution(mesh):
    placed = (
        P(None, ("outer", "inner")),
        P(None, ("outer", "inner")),
        P(None, ("outer", "inner")),
        P(None, ("outer", "inner")),
        P(),
    )
    return jax.shard_map(
        on_device,
        mesh=mesh,
        in_specs=placed,
        out_specs=P(None, ("outer", "inner")),
        check_vma=False,
    )
```

```python
from functools import partial
import math

import jax
import jax.numpy as jnp
import ml_dtypes
import numpy as np
from jax import lax
from jax.experimental import pallas as pl
from jax.experimental.pallas import tpu as pltpu
from jax.sharding import PartitionSpec as P

LANES = 128
AXES = ("outer", "inner")

TWO_PI = 2.0 * math.pi
HIGHEST = lax.Precision.HIGHEST


def table(count_a, count_b, modulus, sign):
    left = lax.broadcasted_iota(jnp.int32, (count_a, count_b), 0)
    right = lax.broadcasted_iota(jnp.int32, (count_a, count_b), 1)
    phase = TWO_PI / modulus * (left * right % modulus).astype(jnp.float32)
    return (jnp.cos(phase), sign * jnp.sin(phase))


def mix(form, cosine, sine, real, imag):
    contract = partial(jnp.einsum, precision=HIGHEST)
    return (
        contract(form, cosine, real) - contract(form, sine, imag),
        contract(form, sine, real) + contract(form, cosine, imag),
    )


def rotate(real, imag, cosine, sine):
    return (real * cosine - imag * sine, real * sine + imag * cosine)


def forward_rows(real, imag):
    split = 16
    lead = real.shape[:-1]
    size = real.shape[-1]
    short = size // split
    real = real.reshape(lead + (split, short))
    imag = imag.reshape(lead + (split, short))
    cosine, sine = table(split, split, split, -1.0)
    real, imag = mix("ka,...as->...ks", cosine, sine, real, imag)
    cosine, sine = table(split, short, size, -1.0)
    real, imag = rotate(real, imag, cosine, sine)
    cosine, sine = table(short, short, short, -1.0)
    real, imag = mix("sb,...ks->...bk", cosine, sine, real, imag)
    return (real.reshape(lead + (size,)), imag.reshape(lead + (size,)))


def inverse_rows(real, imag):
    split = 16
    lead = real.shape[:-1]
    size = real.shape[-1]
    short = size // split
    real = real.reshape(lead + (short, split))
    imag = imag.reshape(lead + (short, split))
    cosine, sine = table(short, short, short, 1.0)
    real, imag = mix("sb,...bk->...sk", cosine, sine, real, imag)
    cosine, sine = table(short, split, size, 1.0)
    real, imag = rotate(real, imag, cosine, sine)
    cosine, sine = table(split, split, split, 1.0)
    real, imag = mix("ak,...sk->...as", cosine, sine, real, imag)
    return (real.reshape(lead + (size,)), imag.reshape(lead + (size,)))


def by_sections(gate, keys, values, taps, skip_gain):
    inner_count = lax.axis_size("inner")
    devices = lax.axis_size("outer") * inner_count
    rank = lax.axis_index("outer") * inner_count + lax.axis_index("inner")
    chans, seg = keys.shape
    both = 2 * chans
    cols = seg // devices
    blocks = 2 * devices
    full = blocks * seg
    contract = partial(jnp.einsum, precision=HIGHEST)
    product = keys * values
    source = jnp.concatenate([product, taps], axis=0)
    sectioned = lax.all_to_all(
        lax.all_to_all(
            source.reshape(both, 1, 1, seg), "outer", split_axis=3, concat_axis=1, tiled=True
        ),
        "inner",
        split_axis=3,
        concat_axis=2,
        tiled=True,
    )
    sectioned = sectioned.reshape(both, devices, cols)
    cosine, sine = table(blocks, devices, blocks, -1.0)
    real = contract("km,cmj->ckj", cosine, sectioned)
    imag = contract("km,cmj->ckj", sine, sectioned)
    offset = rank * cols + lax.broadcasted_iota(jnp.int32, (blocks, cols), 1)
    residue = lax.broadcasted_iota(jnp.int32, (blocks, cols), 0)
    phase = TWO_PI / full * (offset * residue).astype(jnp.float32)
    real, imag = rotate(real, imag, jnp.cos(phase)[None], -jnp.sin(phase)[None])
    outgoing = jnp.stack([real, imag]).reshape(2, both, blocks, 1, 1, cols)
    moved = lax.all_to_all(
        lax.all_to_all(outgoing, "outer", split_axis=2, concat_axis=3, tiled=True),
        "inner",
        split_axis=2,
        concat_axis=4,
        tiled=True,
    )
    moved = moved.reshape(2, both, 2, seg)
    spec_real, spec_imag = forward_rows(moved[0], moved[1])
    sig_real, filt_real = (spec_real[:chans], spec_real[chans:])
    sig_imag, filt_imag = (spec_imag[:chans], spec_imag[chans:])
    real = sig_real * filt_real - sig_imag * filt_imag
    imag = sig_real * filt_imag + sig_imag * filt_real
    real, imag = inverse_rows(real, imag)
    residue = 2 * rank + lax.broadcasted_iota(jnp.int32, (2, seg), 0)
    offset = lax.broadcasted_iota(jnp.int32, (2, seg), 1)
    phase = TWO_PI / full * (offset * residue).astype(jnp.float32)
    real, imag = rotate(real, imag, jnp.cos(phase)[None], jnp.sin(phase)[None])
    returning = jnp.stack([real, imag]).reshape(2, chans, 1, 1, 2, seg)
    gathered = lax.all_to_all(
        lax.all_to_all(returning, "outer", split_axis=5, concat_axis=2, tiled=True),
        "inner",
        split_axis=5,
        concat_axis=3,
        tiled=True,
    )
    gathered = gathered.reshape(2, chans, blocks, cols)
    cosine, sine = table(devices, blocks, blocks, 1.0)
    conv = contract("mk,ckj->cmj", cosine, gathered[0]) - contract("mk,ckj->cmj", sine, gathered[1])
    conv = conv * (1.0 / full)
    conv = lax.all_to_all(
        lax.all_to_all(
            conv.reshape(chans, devices, 1, 1, cols),
            "outer",
            split_axis=1,
            concat_axis=2,
            tiled=True,
        ),
        "inner",
        split_axis=1,
        concat_axis=3,
        tiled=True,
    )
    conv = conv.reshape(chans, seg)
    return gate * (conv + skip_gain[:, None] * product)


def halves(array):
    high = array.astype(ml_dtypes.bfloat16)
    low = (array - high.astype(np.float64)).astype(ml_dtypes.bfloat16)
    return high, low


def transform_tables(devices, seg):
    length = devices * seg
    count = length // LANES
    parts = seg // LANES
    odd = 2 * np.arange(count) + 1
    place = (np.arange(devices)[None, :] * parts + np.arange(parts)[:, None]).reshape(-1)
    angle = 2 * np.pi / (4 * count) * ((odd[:, None] * place[None, :]) % (4 * count))
    first = np.concatenate([np.cos(angle), -np.sin(angle)], axis=0)
    last = np.concatenate([np.cos(angle).T, -np.sin(angle).T], axis=1) / length
    angle = 2 * np.pi / (4 * length) * ((odd[:, None] * np.arange(LANES)[None, :]) % (4 * length))
    twiddle = np.stack([np.cos(angle), np.sin(angle)]).astype(np.float32)
    angle = 2 * np.pi / LANES * ((np.arange(LANES)[:, None] * np.arange(LANES)[None, :]) % LANES)
    cosine, sine = np.cos(angle), np.sin(angle)
    rows = np.block([[cosine, -sine], [sine, cosine]])
    back = np.block([[cosine, sine], [-sine, cosine]])
    first_high, first_low = halves(first)
    rows_high, rows_low = halves(rows)
    back_high, back_low = halves(back)
    last_high, last_low = halves(last)
    return (
        np.concatenate([first_high, first_high, first_low], axis=1),
        np.concatenate([rows_high, rows_high, rows_low], axis=0),
        np.concatenate([back_high, back_high, back_low], axis=0),
        np.concatenate([last_high, last_high, last_low], axis=1),
        twiddle,
    )


def split(array):
    high = array.astype(jnp.bfloat16)
    return high, (array - high.astype(jnp.float32)).astype(jnp.bfloat16)


def dot(left, right):
    return jnp.dot(left, right, preferred_element_type=jnp.float32)


def convolve_kernel(devices, chans, seg, data_ref, first_ref, rows_ref, back_ref, last_ref, twiddle_ref, out_ref):
    parts = seg // LANES
    count = devices * parts
    signals = 2 * chans
    cosine, sine = twiddle_ref[0], twiddle_ref[1]

    def lanes(at):
        return slice(at * LANES, (at + 1) * LANES)

    columns = []
    for signal in range(signals):
        columns.append(
            jnp.concatenate(
                [
                    data_ref[pl.ds(part * signals + signal, devices, stride=parts * signals), :]
                    for part in range(parts)
                ],
                axis=0,
            )
        )
    high, low = split(jnp.concatenate(columns, axis=1))
    begun = dot(first_ref[...], jnp.concatenate([high, low, high], axis=0))
    turned = []
    for signal in range(signals):
        real, imag = begun[:count, lanes(signal)], begun[count:, lanes(signal)]
        turned.append(jnp.concatenate([real * cosine + imag * sine, imag * cosine - real * sine], axis=1))
    high, low = split(jnp.concatenate(turned, axis=0))
    spectrum = dot(jnp.concatenate([high, low, high], axis=1), rows_ref[...])
    mid = chans * count
    sig_real, sig_imag = spectrum[:mid, :LANES], spectrum[:mid, LANES:]
    filt_real, filt_imag = spectrum[mid:, :LANES], spectrum[mid:, LANES:]
    filtered = jnp.concatenate(
        [sig_real * filt_real - sig_imag * filt_imag, sig_real * filt_imag + sig_imag * filt_real], axis=1
    )
    high, low = split(filtered)
    backed = dot(jnp.concatenate([high, low, high], axis=1), back_ref[...])
    turned = []
    for chan in range(chans):
        real = backed[chan * count : (chan + 1) * count, :LANES]
        imag = backed[chan * count : (chan + 1) * count, LANES:]
        turned.append(jnp.concatenate([real * cosine - imag * sine, imag * cosine + real * sine], axis=0))
    high, low = split(jnp.concatenate(turned, axis=1))
    conv = dot(last_ref[...], jnp.concatenate([high, low, high], axis=0))
    for chan in range(chans):
        for part in range(parts):
            out_ref[pl.ds(part * chans + chan, devices, stride=parts * chans), :] = conv[
                part * devices : (part + 1) * devices, lanes(chan)
            ]


def gather_kernel(chunks, devices, keys_ref, values_ref, taps_ref, *out_refs):
    chans, seg = keys_ref.shape
    own = chans // devices
    each = own // chunks
    parts = seg // LANES
    for part in range(parts):
        lanes = slice(part * LANES, (part + 1) * LANES)
        product = keys_ref[:, lanes] * values_ref[:, lanes]
        filt = taps_ref[:, lanes]
        for device in range(devices):
            for chunk in range(chunks):
                row = device * own + chunk * each
                to = (device * parts + part) * 2 * each
                out_refs[chunk][to : to + each, :] = product[row : row + each]
                out_refs[chunk][to + each : to + 2 * each, :] = filt[row : row + each]


def mix_kernel(chunks, devices, gate_ref, keys_ref, values_ref, gain_ref, *refs):
    conv_refs, out_ref = refs[:chunks], refs[chunks]
    chans, seg = keys_ref.shape
    own = chans // devices
    each = own // chunks
    parts = seg // LANES
    for part in range(parts):
        lanes = slice(part * LANES, (part + 1) * LANES)
        for device in range(devices):
            for chunk in range(chunks):
                row = device * own + chunk * each
                came = (device * parts + part) * each
                out_ref[row : row + each, lanes] = conv_refs[chunk][came : came + each, :]
    product = keys_ref[...] * values_ref[...]
    out_ref[...] = gate_ref[...] * (out_ref[...] + gain_ref[...] * product)


def on_core(kernel, shapes, moved, flops=10**6):
    return pl.pallas_call(
        kernel,
        out_shape=[jax.ShapeDtypeStruct(shape, jnp.float32) for shape in shapes],
        compiler_params=pltpu.CompilerParams(vmem_limit_bytes=32 * 2**20),
        cost_estimate=pl.CostEstimate(flops=flops, bytes_accessed=moved, transcendentals=0),
    )


def by_channels(gate, keys, values, taps, skip_gain):
    devices = lax.axis_size("outer") * lax.axis_size("inner")
    chans, seg = keys.shape
    own = chans // devices
    chunks = 2 if own % 2 == 0 else 1
    each = own // chunks
    tiles = devices * seg // LANES
    tables = [jnp.asarray(table) for table in transform_tables(devices, seg)]
    regroup = partial(lax.all_to_all, axis_name=AXES, split_axis=0, concat_axis=0, tiled=True)
    sent = on_core(partial(gather_kernel, chunks, devices), [(2 * each * tiles, LANES)] * chunks, 5 * chans * seg * 4)(
        keys, values, taps
    )
    arrived = [regroup(rows) for rows in sent]
    back = []
    for rows in arrived:
        (conv,) = on_core(partial(convolve_kernel, devices, each, seg), [(each * tiles, LANES)], 2 * 10**6, 10**9)(
            rows, *tables
        )
        back.append(regroup(conv))
    (mixed,) = on_core(partial(mix_kernel, chunks, devices), [(chans, seg)], 5 * chans * seg * 4)(
        gate, keys, values, skip_gain[:, None], *back
    )
    return mixed


def on_device(gate, keys, values, taps, skip_gain):
    devices = lax.axis_size("outer") * lax.axis_size("inner")
    chans, seg = keys.shape
    if chans % devices == 0 and seg % LANES == 0 and devices % 8 == 0:
        return by_channels(gate, keys, values, taps, skip_gain)
    return by_sections(gate, keys, values, taps, skip_gain)


def solution(mesh):
    placed = (
        P(None, ("outer", "inner")),
        P(None, ("outer", "inner")),
        P(None, ("outer", "inner")),
        P(None, ("outer", "inner")),
        P(),
    )
    return jax.shard_map(
        on_device,
        mesh=mesh,
        in_specs=placed,
        out_specs=P(None, ("outer", "inner")),
        check_vma=False,
    )
```

```python
from functools import partial
import math

import jax
import jax.numpy as jnp
import ml_dtypes
import numpy as np
from jax import lax
from jax.experimental import pallas as pl
from jax.experimental.pallas import tpu as pltpu
from jax.sharding import PartitionSpec as P

LANES = 128
AXES = ("outer", "inner")

TWO_PI = 2.0 * math.pi
HIGHEST = lax.Precision.HIGHEST


def table(count_a, count_b, modulus, sign):
    left = lax.broadcasted_iota(jnp.int32, (count_a, count_b), 0)
    right = lax.broadcasted_iota(jnp.int32, (count_a, count_b), 1)
    phase = TWO_PI / modulus * (left * right % modulus).astype(jnp.float32)
    return (jnp.cos(phase), sign * jnp.sin(phase))


def mix(form, cosine, sine, real, imag):
    contract = partial(jnp.einsum, precision=HIGHEST)
    return (
        contract(form, cosine, real) - contract(form, sine, imag),
        contract(form, sine, real) + contract(form, cosine, imag),
    )


def rotate(real, imag, cosine, sine):
    return (real * cosine - imag * sine, real * sine + imag * cosine)


def forward_rows(real, imag):
    split = 16
    lead = real.shape[:-1]
    size = real.shape[-1]
    short = size // split
    real = real.reshape(lead + (split, short))
    imag = imag.reshape(lead + (split, short))
    cosine, sine = table(split, split, split, -1.0)
    real, imag = mix("ka,...as->...ks", cosine, sine, real, imag)
    cosine, sine = table(split, short, size, -1.0)
    real, imag = rotate(real, imag, cosine, sine)
    cosine, sine = table(short, short, short, -1.0)
    real, imag = mix("sb,...ks->...bk", cosine, sine, real, imag)
    return (real.reshape(lead + (size,)), imag.reshape(lead + (size,)))


def inverse_rows(real, imag):
    split = 16
    lead = real.shape[:-1]
    size = real.shape[-1]
    short = size // split
    real = real.reshape(lead + (short, split))
    imag = imag.reshape(lead + (short, split))
    cosine, sine = table(short, short, short, 1.0)
    real, imag = mix("sb,...bk->...sk", cosine, sine, real, imag)
    cosine, sine = table(short, split, size, 1.0)
    real, imag = rotate(real, imag, cosine, sine)
    cosine, sine = table(split, split, split, 1.0)
    real, imag = mix("ak,...sk->...as", cosine, sine, real, imag)
    return (real.reshape(lead + (size,)), imag.reshape(lead + (size,)))


def by_sections(gate, keys, values, taps, skip_gain):
    inner_count = lax.axis_size("inner")
    devices = lax.axis_size("outer") * inner_count
    rank = lax.axis_index("outer") * inner_count + lax.axis_index("inner")
    chans, seg = keys.shape
    both = 2 * chans
    cols = seg // devices
    blocks = 2 * devices
    full = blocks * seg
    contract = partial(jnp.einsum, precision=HIGHEST)
    product = keys * values
    source = jnp.concatenate([product, taps], axis=0)
    sectioned = lax.all_to_all(
        lax.all_to_all(
            source.reshape(both, 1, 1, seg), "outer", split_axis=3, concat_axis=1, tiled=True
        ),
        "inner",
        split_axis=3,
        concat_axis=2,
        tiled=True,
    )
    sectioned = sectioned.reshape(both, devices, cols)
    cosine, sine = table(blocks, devices, blocks, -1.0)
    real = contract("km,cmj->ckj", cosine, sectioned)
    imag = contract("km,cmj->ckj", sine, sectioned)
    offset = rank * cols + lax.broadcasted_iota(jnp.int32, (blocks, cols), 1)
    residue = lax.broadcasted_iota(jnp.int32, (blocks, cols), 0)
    phase = TWO_PI / full * (offset * residue).astype(jnp.float32)
    real, imag = rotate(real, imag, jnp.cos(phase)[None], -jnp.sin(phase)[None])
    outgoing = jnp.stack([real, imag]).reshape(2, both, blocks, 1, 1, cols)
    moved = lax.all_to_all(
        lax.all_to_all(outgoing, "outer", split_axis=2, concat_axis=3, tiled=True),
        "inner",
        split_axis=2,
        concat_axis=4,
        tiled=True,
    )
    moved = moved.reshape(2, both, 2, seg)
    spec_real, spec_imag = forward_rows(moved[0], moved[1])
    sig_real, filt_real = (spec_real[:chans], spec_real[chans:])
    sig_imag, filt_imag = (spec_imag[:chans], spec_imag[chans:])
    real = sig_real * filt_real - sig_imag * filt_imag
    imag = sig_real * filt_imag + sig_imag * filt_real
    real, imag = inverse_rows(real, imag)
    residue = 2 * rank + lax.broadcasted_iota(jnp.int32, (2, seg), 0)
    offset = lax.broadcasted_iota(jnp.int32, (2, seg), 1)
    phase = TWO_PI / full * (offset * residue).astype(jnp.float32)
    real, imag = rotate(real, imag, jnp.cos(phase)[None], jnp.sin(phase)[None])
    returning = jnp.stack([real, imag]).reshape(2, chans, 1, 1, 2, seg)
    gathered = lax.all_to_all(
        lax.all_to_all(returning, "outer", split_axis=5, concat_axis=2, tiled=True),
        "inner",
        split_axis=5,
        concat_axis=3,
        tiled=True,
    )
    gathered = gathered.reshape(2, chans, blocks, cols)
    cosine, sine = table(devices, blocks, blocks, 1.0)
    conv = contract("mk,ckj->cmj", cosine, gathered[0]) - contract("mk,ckj->cmj", sine, gathered[1])
    conv = conv * (1.0 / full)
    conv = lax.all_to_all(
        lax.all_to_all(
            conv.reshape(chans, devices, 1, 1, cols),
            "outer",
            split_axis=1,
            concat_axis=2,
            tiled=True,
        ),
        "inner",
        split_axis=1,
        concat_axis=3,
        tiled=True,
    )
    conv = conv.reshape(chans, seg)
    return gate * (conv + skip_gain[:, None] * product)


def halves(array):
    high = array.astype(ml_dtypes.bfloat16)
    low = (array - high.astype(np.float64)).astype(ml_dtypes.bfloat16)
    return high, low


def transform_tables(devices, seg):
    length = devices * seg
    count = length // LANES
    parts = seg // LANES
    odd = 2 * np.arange(count) + 1
    place = (np.arange(devices)[None, :] * parts + np.arange(parts)[:, None]).reshape(-1)
    angle = 2 * np.pi / (4 * count) * ((odd[:, None] * place[None, :]) % (4 * count))
    first = np.concatenate([np.cos(angle), -np.sin(angle)], axis=0)
    last = np.concatenate([np.cos(angle).T, -np.sin(angle).T], axis=1) / length
    angle = 2 * np.pi / (4 * length) * ((odd[:, None] * np.arange(LANES)[None, :]) % (4 * length))
    twiddle = np.stack([np.cos(angle), np.sin(angle)]).astype(np.float32)
    angle = 2 * np.pi / LANES * ((np.arange(LANES)[:, None] * np.arange(LANES)[None, :]) % LANES)
    cosine, sine = np.cos(angle), np.sin(angle)
    rows = np.block([[cosine, -sine], [sine, cosine]])
    back = np.block([[cosine, sine], [-sine, cosine]])
    first_high, first_low = halves(first)
    rows_high, rows_low = halves(rows)
    back_high, back_low = halves(back)
    last_high, last_low = halves(last)
    return (
        np.concatenate([first_high, first_high, first_low], axis=1),
        np.concatenate([rows_high, rows_high, rows_low], axis=0),
        np.concatenate([back_high, back_high, back_low], axis=0),
        np.concatenate([last_high, last_high, last_low], axis=1),
        twiddle,
    )


def split(array):
    high = array.astype(jnp.bfloat16)
    return high, (array - high.astype(jnp.float32)).astype(jnp.bfloat16)


def dot(left, right):
    return jnp.dot(left, right, preferred_element_type=jnp.float32)


def partner(step):
    return (lax.axis_index("outer") * lax.axis_size("inner") + lax.axis_index("inner")) ^ step


def convolve_kernel(devices, chans, seg, first_ref, rows_ref, back_ref, last_ref, twiddle_ref, *refs):
    in_refs, out_refs, (data_ref, conv_ref) = refs[:devices], refs[devices : 2 * devices], refs[2 * devices :]
    rows = in_refs[0].shape[0]
    for step in range(devices):
        data_ref[pl.ds(pl.multiple_of(partner(step) * rows, rows), rows), :] = in_refs[step][...]
    parts = seg // LANES
    count = devices * parts
    signals = 2 * chans
    cosine, sine = twiddle_ref[0], twiddle_ref[1]

    def lanes(at):
        return slice(at * LANES, (at + 1) * LANES)

    columns = []
    for signal in range(signals):
        columns.append(
            jnp.concatenate(
                [
                    data_ref[pl.ds(part * signals + signal, devices, stride=parts * signals), :]
                    for part in range(parts)
                ],
                axis=0,
            )
        )
    high, low = split(jnp.concatenate(columns, axis=1))
    begun = dot(first_ref[...], jnp.concatenate([high, low, high], axis=0))
    turned = []
    for signal in range(signals):
        real, imag = begun[:count, lanes(signal)], begun[count:, lanes(signal)]
        turned.append(jnp.concatenate([real * cosine + imag * sine, imag * cosine - real * sine], axis=1))
    high, low = split(jnp.concatenate(turned, axis=0))
    spectrum = dot(jnp.concatenate([high, low, high], axis=1), rows_ref[...])
    mid = chans * count
    sig_real, sig_imag = spectrum[:mid, :LANES], spectrum[:mid, LANES:]
    filt_real, filt_imag = spectrum[mid:, :LANES], spectrum[mid:, LANES:]
    filtered = jnp.concatenate(
        [sig_real * filt_real - sig_imag * filt_imag, sig_real * filt_imag + sig_imag * filt_real], axis=1
    )
    high, low = split(filtered)
    backed = dot(jnp.concatenate([high, low, high], axis=1), back_ref[...])
    turned = []
    for chan in range(chans):
        real = backed[chan * count : (chan + 1) * count, :LANES]
        imag = backed[chan * count : (chan + 1) * count, LANES:]
        turned.append(jnp.concatenate([real * cosine - imag * sine, imag * cosine + real * sine], axis=0))
    high, low = split(jnp.concatenate(turned, axis=1))
    conv = dot(last_ref[...], jnp.concatenate([high, low, high], axis=0))
    for chan in range(chans):
        for part in range(parts):
            conv_ref[pl.ds(part * chans + chan, devices, stride=parts * chans), :] = conv[
                part * devices : (part + 1) * devices, lanes(chan)
            ]
    rows = parts * chans
    for step in range(devices):
        out_refs[step][...] = conv_ref[pl.ds(pl.multiple_of(partner(step) * rows, rows), rows), :]


def gather_kernel(devices, keys_ref, values_ref, taps_ref, *refs):
    out_refs, all_ref = refs[:devices], refs[devices]
    chans, seg = keys_ref.shape
    own = chans // devices
    parts = seg // LANES
    rows = parts * 2 * own
    for part in range(parts):
        lanes = slice(part * LANES, (part + 1) * LANES)
        product = keys_ref[:, lanes] * values_ref[:, lanes]
        filt = taps_ref[:, lanes]
        for device in range(devices):
            row = device * own
            to = device * rows + part * 2 * own
            all_ref[to : to + own, :] = product[row : row + own]
            all_ref[to + own : to + 2 * own, :] = filt[row : row + own]
    for step in range(devices):
        out_refs[step][...] = all_ref[pl.ds(pl.multiple_of(partner(step) * rows, rows), rows), :]


def mix_kernel(devices, gate_ref, keys_ref, values_ref, gain_ref, *refs):
    in_refs, out_ref, conv_ref = refs[:devices], refs[devices], refs[devices + 1]
    chans, seg = keys_ref.shape
    own = chans // devices
    parts = seg // LANES
    rows = parts * own
    for step in range(devices):
        conv_ref[pl.ds(pl.multiple_of(partner(step) * rows, rows), rows), :] = in_refs[step][...]
    for part in range(parts):
        lanes = slice(part * LANES, (part + 1) * LANES)
        for device in range(devices):
            row = device * own
            came = device * rows + part * own
            out_ref[row : row + own, lanes] = conv_ref[came : came + own, :]
    product = keys_ref[...] * values_ref[...]
    out_ref[...] = gate_ref[...] * (out_ref[...] + gain_ref[...] * product)


def on_core(kernel, shapes, scratch, moved, flops=10**6):
    return pl.pallas_call(
        kernel,
        out_shape=[jax.ShapeDtypeStruct(shape, jnp.float32) for shape in shapes],
        scratch_shapes=[pltpu.VMEM(shape, jnp.float32) for shape in scratch],
        compiler_params=pltpu.CompilerParams(vmem_limit_bytes=32 * 2**20),
        cost_estimate=pl.CostEstimate(flops=flops, bytes_accessed=moved, transcendentals=0),
    )


def exchange(blocks):
    steps = range(len(blocks))
    return [
        blocks[step] if step == 0 else lax.ppermute(blocks[step], AXES, [(rank, rank ^ step) for rank in steps])
        for step in steps
    ]


def by_channels(gate, keys, values, taps, skip_gain):
    devices = lax.axis_size("outer") * lax.axis_size("inner")
    chans, seg = keys.shape
    own = chans // devices
    tiles = seg // LANES
    tables = [jnp.asarray(table) for table in transform_tables(devices, seg)]
    sent = on_core(
        partial(gather_kernel, devices),
        [(2 * own * tiles, LANES)] * devices,
        [(2 * chans * tiles, LANES)],
        5 * chans * seg * 4,
    )(keys, values, taps)
    conv = on_core(
        partial(convolve_kernel, devices, own, seg),
        [(own * tiles, LANES)] * devices,
        [(2 * chans * tiles, LANES), (chans * tiles, LANES)],
        2 * 10**6,
        10**9,
    )(*tables, *exchange(sent))
    (mixed,) = on_core(
        partial(mix_kernel, devices), [(chans, seg)], [(chans * tiles, LANES)], 5 * chans * seg * 4
    )(gate, keys, values, skip_gain[:, None], *exchange(conv))
    return mixed


def on_device(gate, keys, values, taps, skip_gain):
    devices = lax.axis_size("outer") * lax.axis_size("inner")
    chans, seg = keys.shape
    if chans % devices == 0 and seg % LANES == 0 and devices % 8 == 0 and devices & (devices - 1) == 0:
        return by_channels(gate, keys, values, taps, skip_gain)
    return by_sections(gate, keys, values, taps, skip_gain)


def solution(mesh):
    placed = (
        P(None, ("outer", "inner")),
        P(None, ("outer", "inner")),
        P(None, ("outer", "inner")),
        P(None, ("outer", "inner")),
        P(),
    )
    return jax.shard_map(
        on_device,
        mesh=mesh,
        in_specs=placed,
        out_specs=P(None, ("outer", "inner")),
        check_vma=False,
    )
```

```python
from functools import partial
import math

import jax
import jax.numpy as jnp
import ml_dtypes
import numpy as np
from jax import lax
from jax.experimental import pallas as pl
from jax.experimental.pallas import tpu as pltpu
from jax.sharding import PartitionSpec as P

LANES = 128
AXES = ("outer", "inner")

TWO_PI = 2.0 * math.pi
HIGHEST = lax.Precision.HIGHEST


def table(count_a, count_b, modulus, sign):
    left = lax.broadcasted_iota(jnp.int32, (count_a, count_b), 0)
    right = lax.broadcasted_iota(jnp.int32, (count_a, count_b), 1)
    phase = TWO_PI / modulus * (left * right % modulus).astype(jnp.float32)
    return (jnp.cos(phase), sign * jnp.sin(phase))


def mix(form, cosine, sine, real, imag):
    contract = partial(jnp.einsum, precision=HIGHEST)
    return (
        contract(form, cosine, real) - contract(form, sine, imag),
        contract(form, sine, real) + contract(form, cosine, imag),
    )


def rotate(real, imag, cosine, sine):
    return (real * cosine - imag * sine, real * sine + imag * cosine)


def forward_rows(real, imag):
    split = 16
    lead = real.shape[:-1]
    size = real.shape[-1]
    short = size // split
    real = real.reshape(lead + (split, short))
    imag = imag.reshape(lead + (split, short))
    cosine, sine = table(split, split, split, -1.0)
    real, imag = mix("ka,...as->...ks", cosine, sine, real, imag)
    cosine, sine = table(split, short, size, -1.0)
    real, imag = rotate(real, imag, cosine, sine)
    cosine, sine = table(short, short, short, -1.0)
    real, imag = mix("sb,...ks->...bk", cosine, sine, real, imag)
    return (real.reshape(lead + (size,)), imag.reshape(lead + (size,)))


def inverse_rows(real, imag):
    split = 16
    lead = real.shape[:-1]
    size = real.shape[-1]
    short = size // split
    real = real.reshape(lead + (short, split))
    imag = imag.reshape(lead + (short, split))
    cosine, sine = table(short, short, short, 1.0)
    real, imag = mix("sb,...bk->...sk", cosine, sine, real, imag)
    cosine, sine = table(short, split, size, 1.0)
    real, imag = rotate(real, imag, cosine, sine)
    cosine, sine = table(split, split, split, 1.0)
    real, imag = mix("ak,...sk->...as", cosine, sine, real, imag)
    return (real.reshape(lead + (size,)), imag.reshape(lead + (size,)))


def by_sections(gate, keys, values, taps, skip_gain):
    inner_count = lax.axis_size("inner")
    devices = lax.axis_size("outer") * inner_count
    rank = lax.axis_index("outer") * inner_count + lax.axis_index("inner")
    chans, seg = keys.shape
    both = 2 * chans
    cols = seg // devices
    blocks = 2 * devices
    full = blocks * seg
    contract = partial(jnp.einsum, precision=HIGHEST)
    product = keys * values
    source = jnp.concatenate([product, taps], axis=0)
    sectioned = lax.all_to_all(
        lax.all_to_all(
            source.reshape(both, 1, 1, seg), "outer", split_axis=3, concat_axis=1, tiled=True
        ),
        "inner",
        split_axis=3,
        concat_axis=2,
        tiled=True,
    )
    sectioned = sectioned.reshape(both, devices, cols)
    cosine, sine = table(blocks, devices, blocks, -1.0)
    real = contract("km,cmj->ckj", cosine, sectioned)
    imag = contract("km,cmj->ckj", sine, sectioned)
    offset = rank * cols + lax.broadcasted_iota(jnp.int32, (blocks, cols), 1)
    residue = lax.broadcasted_iota(jnp.int32, (blocks, cols), 0)
    phase = TWO_PI / full * (offset * residue).astype(jnp.float32)
    real, imag = rotate(real, imag, jnp.cos(phase)[None], -jnp.sin(phase)[None])
    outgoing = jnp.stack([real, imag]).reshape(2, both, blocks, 1, 1, cols)
    moved = lax.all_to_all(
        lax.all_to_all(outgoing, "outer", split_axis=2, concat_axis=3, tiled=True),
        "inner",
        split_axis=2,
        concat_axis=4,
        tiled=True,
    )
    moved = moved.reshape(2, both, 2, seg)
    spec_real, spec_imag = forward_rows(moved[0], moved[1])
    sig_real, filt_real = (spec_real[:chans], spec_real[chans:])
    sig_imag, filt_imag = (spec_imag[:chans], spec_imag[chans:])
    real = sig_real * filt_real - sig_imag * filt_imag
    imag = sig_real * filt_imag + sig_imag * filt_real
    real, imag = inverse_rows(real, imag)
    residue = 2 * rank + lax.broadcasted_iota(jnp.int32, (2, seg), 0)
    offset = lax.broadcasted_iota(jnp.int32, (2, seg), 1)
    phase = TWO_PI / full * (offset * residue).astype(jnp.float32)
    real, imag = rotate(real, imag, jnp.cos(phase)[None], jnp.sin(phase)[None])
    returning = jnp.stack([real, imag]).reshape(2, chans, 1, 1, 2, seg)
    gathered = lax.all_to_all(
        lax.all_to_all(returning, "outer", split_axis=5, concat_axis=2, tiled=True),
        "inner",
        split_axis=5,
        concat_axis=3,
        tiled=True,
    )
    gathered = gathered.reshape(2, chans, blocks, cols)
    cosine, sine = table(devices, blocks, blocks, 1.0)
    conv = contract("mk,ckj->cmj", cosine, gathered[0]) - contract("mk,ckj->cmj", sine, gathered[1])
    conv = conv * (1.0 / full)
    conv = lax.all_to_all(
        lax.all_to_all(
            conv.reshape(chans, devices, 1, 1, cols),
            "outer",
            split_axis=1,
            concat_axis=2,
            tiled=True,
        ),
        "inner",
        split_axis=1,
        concat_axis=3,
        tiled=True,
    )
    conv = conv.reshape(chans, seg)
    return gate * (conv + skip_gain[:, None] * product)


def halves(array):
    high = array.astype(ml_dtypes.bfloat16)
    low = (array - high.astype(np.float64)).astype(ml_dtypes.bfloat16)
    return high, low


def transform_tables(devices, seg):
    length = devices * seg
    count = length // LANES
    parts = seg // LANES
    odd = 2 * np.arange(count) + 1
    place = (np.arange(devices)[None, :] * parts + np.arange(parts)[:, None]).reshape(-1)
    angle = 2 * np.pi / (4 * count) * ((odd[:, None] * place[None, :]) % (4 * count))
    first = np.concatenate([np.cos(angle), -np.sin(angle)], axis=0)
    last = np.concatenate([np.cos(angle).T, -np.sin(angle).T], axis=1) / length
    angle = 2 * np.pi / (4 * length) * ((odd[:, None] * np.arange(LANES)[None, :]) % (4 * length))
    twiddle = np.stack([np.cos(angle), np.sin(angle)]).astype(np.float32)
    angle = 2 * np.pi / LANES * ((np.arange(LANES)[:, None] * np.arange(LANES)[None, :]) % LANES)
    cosine, sine = np.cos(angle), np.sin(angle)
    rows = np.block([[cosine, -sine], [sine, cosine]])
    back = np.block([[cosine, sine], [-sine, cosine]])
    first_high, first_low = halves(first)
    rows_high, rows_low = halves(rows)
    back_high, back_low = halves(back)
    last_high, last_low = halves(last)
    return (
        np.concatenate([first_high, first_high, first_low], axis=1),
        np.concatenate([rows_high, rows_high, rows_low], axis=0),
        np.concatenate([back_high, back_high, back_low], axis=0),
        np.concatenate([last_high, last_high, last_low], axis=1),
        twiddle,
    )


def split(array):
    high = array.astype(jnp.bfloat16)
    return high, (array - high.astype(jnp.float32)).astype(jnp.bfloat16)


def dot(left, right):
    return jnp.dot(left, right, preferred_element_type=jnp.float32)


def convolve_kernel(devices, chans, seg, data_ref, first_ref, rows_ref, back_ref, last_ref, twiddle_ref, out_ref):
    parts = seg // LANES
    count = devices * parts
    signals = 2 * chans
    cosine, sine = twiddle_ref[0], twiddle_ref[1]

    def lanes(at):
        return slice(at * LANES, (at + 1) * LANES)

    columns = []
    for signal in range(signals):
        columns.append(
            jnp.concatenate(
                [
                    data_ref[pl.ds(part * signals + signal, devices, stride=parts * signals), :]
                    for part in range(parts)
                ],
                axis=0,
            )
        )
    high, low = split(jnp.concatenate(columns, axis=1))
    begun = dot(first_ref[...], jnp.concatenate([high, low, high], axis=0))
    turned = []
    for signal in range(signals):
        real, imag = begun[:count, lanes(signal)], begun[count:, lanes(signal)]
        turned.append(jnp.concatenate([real * cosine + imag * sine, imag * cosine - real * sine], axis=1))
    high, low = split(jnp.concatenate(turned, axis=0))
    spectrum = dot(jnp.concatenate([high, low, high], axis=1), rows_ref[...])
    mid = chans * count
    sig_real, sig_imag = spectrum[:mid, :LANES], spectrum[:mid, LANES:]
    filt_real, filt_imag = spectrum[mid:, :LANES], spectrum[mid:, LANES:]
    filtered = jnp.concatenate(
        [sig_real * filt_real - sig_imag * filt_imag, sig_real * filt_imag + sig_imag * filt_real], axis=1
    )
    high, low = split(filtered)
    backed = dot(jnp.concatenate([high, low, high], axis=1), back_ref[...])
    turned = []
    for chan in range(chans):
        real = backed[chan * count : (chan + 1) * count, :LANES]
        imag = backed[chan * count : (chan + 1) * count, LANES:]
        turned.append(jnp.concatenate([real * cosine - imag * sine, imag * cosine + real * sine], axis=0))
    high, low = split(jnp.concatenate(turned, axis=1))
    conv = dot(last_ref[...], jnp.concatenate([high, low, high], axis=0))
    for chan in range(chans):
        for part in range(parts):
            out_ref[pl.ds(part * chans + chan, devices, stride=parts * chans), :] = conv[
                part * devices : (part + 1) * devices, lanes(chan)
            ]


def gather_kernel(devices, keys_hbm, values_hbm, taps_hbm, out_ref, keys_ref, values_ref, taps_ref, sems):
    chans, seg = keys_ref.shape
    own = chans // devices
    parts = seg // LANES
    pairs = ((keys_hbm, keys_ref), (values_hbm, values_ref), (taps_hbm, taps_ref))
    copies = [pltpu.make_async_copy(source, target, sems.at[at]) for at, (source, target) in enumerate(pairs)]
    for copy in copies:
        copy.start()
    for copy in copies:
        copy.wait()
    for part in range(parts):
        lanes = slice(part * LANES, (part + 1) * LANES)
        product = keys_ref[:, lanes] * values_ref[:, lanes]
        filt = taps_ref[:, lanes]
        for device in range(devices):
            row = device * own
            to = (device * parts + part) * 2 * own
            out_ref[to : to + own, :] = product[row : row + own]
            out_ref[to + own : to + 2 * own, :] = filt[row : row + own]


def mix_kernel(devices, gate_ref, keys_ref, values_ref, gain_ref, conv_ref, out_ref):
    chans, seg = keys_ref.shape
    own = chans // devices
    parts = seg // LANES
    for part in range(parts):
        lanes = slice(part * LANES, (part + 1) * LANES)
        for device in range(devices):
            row = device * own
            came = (device * parts + part) * own
            out_ref[row : row + own, lanes] = conv_ref[came : came + own, :]
    product = keys_ref[...] * values_ref[...]
    out_ref[...] = gate_ref[...] * (out_ref[...] + gain_ref[...] * product)


def on_core(kernel, shape, moved, flops=10**6, **more):
    return pl.pallas_call(
        kernel,
        out_shape=jax.ShapeDtypeStruct(shape, jnp.float32),
        compiler_params=pltpu.CompilerParams(vmem_limit_bytes=32 * 2**20),
        cost_estimate=pl.CostEstimate(flops=flops, bytes_accessed=moved, transcendentals=0),
        **more,
    )


def by_channels(gate, keys, values, taps, skip_gain):
    devices = lax.axis_size("outer") * lax.axis_size("inner")
    chans, seg = keys.shape
    own = chans // devices
    tiles = seg // LANES
    tables = [jnp.asarray(table) for table in transform_tables(devices, seg)]
    regroup = partial(lax.all_to_all, axis_name=AXES, split_axis=0, concat_axis=0, tiled=True)
    sent = on_core(
        partial(gather_kernel, devices),
        (2 * chans * tiles, LANES),
        5 * chans * seg * 4,
        in_specs=[pl.BlockSpec(memory_space=pltpu.HBM)] * 3,
        scratch_shapes=[pltpu.VMEM((chans, seg), jnp.float32)] * 3 + [pltpu.SemaphoreType.DMA((3,))],
    )(keys, values, taps)
    conv = on_core(partial(convolve_kernel, devices, own, seg), (chans * tiles, LANES), 2 * 10**6, 10**9)(
        regroup(sent), *tables
    )
    return on_core(partial(mix_kernel, devices), (chans, seg), 5 * chans * seg * 4)(
        gate, keys, values, skip_gain[:, None], regroup(conv)
    )


def on_device(gate, keys, values, taps, skip_gain):
    devices = lax.axis_size("outer") * lax.axis_size("inner")
    chans, seg = keys.shape
    if chans % devices == 0 and seg % LANES == 0 and devices % 8 == 0:
        return by_channels(gate, keys, values, taps, skip_gain)
    return by_sections(gate, keys, values, taps, skip_gain)


def solution(mesh):
    placed = (
        P(None, ("outer", "inner")),
        P(None, ("outer", "inner")),
        P(None, ("outer", "inner")),
        P(None, ("outer", "inner")),
        P(),
    )
    return jax.shard_map(
        on_device,
        mesh=mesh,
        in_specs=placed,
        out_specs=P(None, ("outer", "inner")),
        check_vma=False,
    )
```

```python
from functools import partial
import math

import jax
import jax.numpy as jnp
import ml_dtypes
import numpy as np
from jax import lax
from jax.experimental import pallas as pl
from jax.experimental.pallas import tpu as pltpu
from jax.sharding import PartitionSpec as P

LANES = 128
AXES = ("outer", "inner")

TWO_PI = 2.0 * math.pi
HIGHEST = lax.Precision.HIGHEST


def table(count_a, count_b, modulus, sign):
    left = lax.broadcasted_iota(jnp.int32, (count_a, count_b), 0)
    right = lax.broadcasted_iota(jnp.int32, (count_a, count_b), 1)
    phase = TWO_PI / modulus * (left * right % modulus).astype(jnp.float32)
    return (jnp.cos(phase), sign * jnp.sin(phase))


def mix(form, cosine, sine, real, imag):
    contract = partial(jnp.einsum, precision=HIGHEST)
    return (
        contract(form, cosine, real) - contract(form, sine, imag),
        contract(form, sine, real) + contract(form, cosine, imag),
    )


def rotate(real, imag, cosine, sine):
    return (real * cosine - imag * sine, real * sine + imag * cosine)


def forward_rows(real, imag):
    split = 16
    lead = real.shape[:-1]
    size = real.shape[-1]
    short = size // split
    real = real.reshape(lead + (split, short))
    imag = imag.reshape(lead + (split, short))
    cosine, sine = table(split, split, split, -1.0)
    real, imag = mix("ka,...as->...ks", cosine, sine, real, imag)
    cosine, sine = table(split, short, size, -1.0)
    real, imag = rotate(real, imag, cosine, sine)
    cosine, sine = table(short, short, short, -1.0)
    real, imag = mix("sb,...ks->...bk", cosine, sine, real, imag)
    return (real.reshape(lead + (size,)), imag.reshape(lead + (size,)))


def inverse_rows(real, imag):
    split = 16
    lead = real.shape[:-1]
    size = real.shape[-1]
    short = size // split
    real = real.reshape(lead + (short, split))
    imag = imag.reshape(lead + (short, split))
    cosine, sine = table(short, short, short, 1.0)
    real, imag = mix("sb,...bk->...sk", cosine, sine, real, imag)
    cosine, sine = table(short, split, size, 1.0)
    real, imag = rotate(real, imag, cosine, sine)
    cosine, sine = table(split, split, split, 1.0)
    real, imag = mix("ak,...sk->...as", cosine, sine, real, imag)
    return (real.reshape(lead + (size,)), imag.reshape(lead + (size,)))


def by_sections(gate, keys, values, taps, skip_gain):
    inner_count = lax.axis_size("inner")
    devices = lax.axis_size("outer") * inner_count
    rank = lax.axis_index("outer") * inner_count + lax.axis_index("inner")
    chans, seg = keys.shape
    both = 2 * chans
    cols = seg // devices
    blocks = 2 * devices
    full = blocks * seg
    contract = partial(jnp.einsum, precision=HIGHEST)
    product = keys * values
    source = jnp.concatenate([product, taps], axis=0)
    sectioned = lax.all_to_all(
        lax.all_to_all(
            source.reshape(both, 1, 1, seg), "outer", split_axis=3, concat_axis=1, tiled=True
        ),
        "inner",
        split_axis=3,
        concat_axis=2,
        tiled=True,
    )
    sectioned = sectioned.reshape(both, devices, cols)
    cosine, sine = table(blocks, devices, blocks, -1.0)
    real = contract("km,cmj->ckj", cosine, sectioned)
    imag = contract("km,cmj->ckj", sine, sectioned)
    offset = rank * cols + lax.broadcasted_iota(jnp.int32, (blocks, cols), 1)
    residue = lax.broadcasted_iota(jnp.int32, (blocks, cols), 0)
    phase = TWO_PI / full * (offset * residue).astype(jnp.float32)
    real, imag = rotate(real, imag, jnp.cos(phase)[None], -jnp.sin(phase)[None])
    outgoing = jnp.stack([real, imag]).reshape(2, both, blocks, 1, 1, cols)
    moved = lax.all_to_all(
        lax.all_to_all(outgoing, "outer", split_axis=2, concat_axis=3, tiled=True),
        "inner",
        split_axis=2,
        concat_axis=4,
        tiled=True,
    )
    moved = moved.reshape(2, both, 2, seg)
    spec_real, spec_imag = forward_rows(moved[0], moved[1])
    sig_real, filt_real = (spec_real[:chans], spec_real[chans:])
    sig_imag, filt_imag = (spec_imag[:chans], spec_imag[chans:])
    real = sig_real * filt_real - sig_imag * filt_imag
    imag = sig_real * filt_imag + sig_imag * filt_real
    real, imag = inverse_rows(real, imag)
    residue = 2 * rank + lax.broadcasted_iota(jnp.int32, (2, seg), 0)
    offset = lax.broadcasted_iota(jnp.int32, (2, seg), 1)
    phase = TWO_PI / full * (offset * residue).astype(jnp.float32)
    real, imag = rotate(real, imag, jnp.cos(phase)[None], jnp.sin(phase)[None])
    returning = jnp.stack([real, imag]).reshape(2, chans, 1, 1, 2, seg)
    gathered = lax.all_to_all(
        lax.all_to_all(returning, "outer", split_axis=5, concat_axis=2, tiled=True),
        "inner",
        split_axis=5,
        concat_axis=3,
        tiled=True,
    )
    gathered = gathered.reshape(2, chans, blocks, cols)
    cosine, sine = table(devices, blocks, blocks, 1.0)
    conv = contract("mk,ckj->cmj", cosine, gathered[0]) - contract("mk,ckj->cmj", sine, gathered[1])
    conv = conv * (1.0 / full)
    conv = lax.all_to_all(
        lax.all_to_all(
            conv.reshape(chans, devices, 1, 1, cols),
            "outer",
            split_axis=1,
            concat_axis=2,
            tiled=True,
        ),
        "inner",
        split_axis=1,
        concat_axis=3,
        tiled=True,
    )
    conv = conv.reshape(chans, seg)
    return gate * (conv + skip_gain[:, None] * product)


def halves(array):
    high = array.astype(ml_dtypes.bfloat16)
    low = (array - high.astype(np.float64)).astype(ml_dtypes.bfloat16)
    return high, low


def transform_tables(devices, seg):
    length = devices * seg
    count = length // LANES
    parts = seg // LANES
    odd = 2 * np.arange(count) + 1
    place = (np.arange(devices)[None, :] * parts + np.arange(parts)[:, None]).reshape(-1)
    angle = 2 * np.pi / (4 * count) * ((odd[:, None] * place[None, :]) % (4 * count))
    first = np.concatenate([np.cos(angle), -np.sin(angle)], axis=0)
    last = np.concatenate([np.cos(angle).T, -np.sin(angle).T], axis=1) / length
    angle = 2 * np.pi / (4 * length) * ((odd[:, None] * np.arange(LANES)[None, :]) % (4 * length))
    twiddle = np.stack([np.cos(angle), np.sin(angle)]).astype(np.float32)
    angle = 2 * np.pi / LANES * ((np.arange(LANES)[:, None] * np.arange(LANES)[None, :]) % LANES)
    cosine, sine = np.cos(angle), np.sin(angle)
    rows = np.block([[cosine, -sine], [sine, cosine]])
    back = np.block([[cosine, sine], [-sine, cosine]])
    first_high, first_low = halves(first)
    rows_high, rows_low = halves(rows)
    back_high, back_low = halves(back)
    last_high, last_low = halves(last)
    return (
        np.concatenate([first_high, first_high, first_low], axis=1),
        np.concatenate([rows_high, rows_high, rows_low], axis=0),
        np.concatenate([back_high, back_high, back_low], axis=0),
        np.concatenate([last_high, last_high, last_low], axis=1),
        twiddle,
    )


def split(array):
    high = array.astype(jnp.bfloat16)
    return high, (array - high.astype(jnp.float32)).astype(jnp.bfloat16)


def dot(left, right):
    return jnp.dot(left, right, preferred_element_type=jnp.float32)


def convolve_kernel(devices, chans, seg, data_ref, first_ref, rows_ref, back_ref, last_ref, twiddle_ref, out_ref):
    parts = seg // LANES
    count = devices * parts
    signals = 2 * chans
    cosine, sine = twiddle_ref[0], twiddle_ref[1]

    def lanes(at):
        return slice(at * LANES, (at + 1) * LANES)

    columns = []
    for signal in range(signals):
        columns.append(
            jnp.concatenate(
                [
                    data_ref[pl.ds(part * signals + signal, devices, stride=parts * signals), :]
                    for part in range(parts)
                ],
                axis=0,
            )
        )
    high, low = split(jnp.concatenate(columns, axis=1))
    begun = dot(first_ref[...], jnp.concatenate([high, low, high], axis=0))
    turned = []
    for signal in range(signals):
        real, imag = begun[:count, lanes(signal)], begun[count:, lanes(signal)]
        turned.append(jnp.concatenate([real * cosine + imag * sine, imag * cosine - real * sine], axis=1))
    high, low = split(jnp.concatenate(turned, axis=0))
    spectrum = dot(jnp.concatenate([high, low, high], axis=1), rows_ref[...])
    mid = chans * count
    sig_real, sig_imag = spectrum[:mid, :LANES], spectrum[:mid, LANES:]
    filt_real, filt_imag = spectrum[mid:, :LANES], spectrum[mid:, LANES:]
    filtered = jnp.concatenate(
        [sig_real * filt_real - sig_imag * filt_imag, sig_real * filt_imag + sig_imag * filt_real], axis=1
    )
    high, low = split(filtered)
    backed = dot(jnp.concatenate([high, low, high], axis=1), back_ref[...])
    turned = []
    for chan in range(chans):
        real = backed[chan * count : (chan + 1) * count, :LANES]
        imag = backed[chan * count : (chan + 1) * count, LANES:]
        turned.append(jnp.concatenate([real * cosine - imag * sine, imag * cosine + real * sine], axis=0))
    high, low = split(jnp.concatenate(turned, axis=1))
    conv = dot(last_ref[...], jnp.concatenate([high, low, high], axis=0))
    for chan in range(chans):
        for part in range(parts):
            out_ref[pl.ds(part * chans + chan, devices, stride=parts * chans), :] = conv[
                part * devices : (part + 1) * devices, lanes(chan)
            ]


def gather_kernel(devices, product_ref, taps_ref, out_ref):
    chans, seg = product_ref.shape
    own = chans // devices
    parts = seg // LANES
    for part in range(parts):
        lanes = slice(part * LANES, (part + 1) * LANES)
        for device in range(devices):
            rows = slice(device * own, (device + 1) * own)
            to = (device * parts + part) * 2 * own
            out_ref[to : to + own, :] = product_ref[rows, lanes]
            out_ref[to + own : to + 2 * own, :] = taps_ref[rows, lanes]


def mix_kernel(devices, gate_ref, product_ref, gain_ref, conv_ref, out_ref):
    chans, seg = product_ref.shape
    own = chans // devices
    parts = seg // LANES
    for part in range(parts):
        lanes = slice(part * LANES, (part + 1) * LANES)
        for device in range(devices):
            row = device * own
            came = (device * parts + part) * own
            out_ref[row : row + own, lanes] = conv_ref[came : came + own, :]
    diagonal = lax.broadcasted_iota(jnp.int32, (chans, chans), 0) == lax.broadcasted_iota(jnp.int32, (chans, chans), 1)
    gain = jnp.sum(jnp.where(diagonal, gain_ref[...], 0.0), axis=1, keepdims=True)
    out_ref[...] = gate_ref[...] * (out_ref[...] + gain * product_ref[...])


def on_core(kernel, shape, moved, flops=10**6):
    return pl.pallas_call(
        kernel,
        out_shape=jax.ShapeDtypeStruct(shape, jnp.float32),
        compiler_params=pltpu.CompilerParams(vmem_limit_bytes=32 * 2**20),
        cost_estimate=pl.CostEstimate(flops=flops, bytes_accessed=moved, transcendentals=0),
    )


def by_channels(gate, keys, values, taps, skip_gain):
    devices = lax.axis_size("outer") * lax.axis_size("inner")
    chans, seg = keys.shape
    own = chans // devices
    tiles = seg // LANES
    tables = [jnp.asarray(table) for table in transform_tables(devices, seg)]
    regroup = partial(lax.all_to_all, axis_name=AXES, split_axis=0, concat_axis=0, tiled=True)
    product = keys * values
    sent = on_core(partial(gather_kernel, devices), (2 * chans * tiles, LANES), 4 * chans * seg * 4)(product, taps)
    conv = on_core(partial(convolve_kernel, devices, own, seg), (chans * tiles, LANES), 2 * 10**6, 10**9)(
        regroup(sent), *tables
    )
    return on_core(partial(mix_kernel, devices), (chans, seg), 5 * chans * seg * 4)(
        gate, product, skip_gain[None, :], regroup(conv)
    )


def on_device(gate, keys, values, taps, skip_gain):
    devices = lax.axis_size("outer") * lax.axis_size("inner")
    chans, seg = keys.shape
    if chans % devices == 0 and seg % LANES == 0 and devices % 8 == 0:
        return by_channels(gate, keys, values, taps, skip_gain)
    return by_sections(gate, keys, values, taps, skip_gain)


def solution(mesh):
    placed = (
        P(None, ("outer", "inner")),
        P(None, ("outer", "inner")),
        P(None, ("outer", "inner")),
        P(None, ("outer", "inner")),
        P(),
    )
    return jax.shard_map(
        on_device,
        mesh=mesh,
        in_specs=placed,
        out_specs=P(None, ("outer", "inner")),
        check_vma=False,
    )
```

```python
from functools import partial
import math

import jax
import jax.numpy as jnp
import ml_dtypes
import numpy as np
from jax import lax
from jax.experimental import pallas as pl
from jax.experimental.pallas import tpu as pltpu
from jax.sharding import PartitionSpec as P

LANES = 128
AXES = ("outer", "inner")

TWO_PI = 2.0 * math.pi
HIGHEST = lax.Precision.HIGHEST


def table(count_a, count_b, modulus, sign):
    left = lax.broadcasted_iota(jnp.int32, (count_a, count_b), 0)
    right = lax.broadcasted_iota(jnp.int32, (count_a, count_b), 1)
    phase = TWO_PI / modulus * (left * right % modulus).astype(jnp.float32)
    return (jnp.cos(phase), sign * jnp.sin(phase))


def mix(form, cosine, sine, real, imag):
    contract = partial(jnp.einsum, precision=HIGHEST)
    return (
        contract(form, cosine, real) - contract(form, sine, imag),
        contract(form, sine, real) + contract(form, cosine, imag),
    )


def rotate(real, imag, cosine, sine):
    return (real * cosine - imag * sine, real * sine + imag * cosine)


def forward_rows(real, imag):
    split = 16
    lead = real.shape[:-1]
    size = real.shape[-1]
    short = size // split
    real = real.reshape(lead + (split, short))
    imag = imag.reshape(lead + (split, short))
    cosine, sine = table(split, split, split, -1.0)
    real, imag = mix("ka,...as->...ks", cosine, sine, real, imag)
    cosine, sine = table(split, short, size, -1.0)
    real, imag = rotate(real, imag, cosine, sine)
    cosine, sine = table(short, short, short, -1.0)
    real, imag = mix("sb,...ks->...bk", cosine, sine, real, imag)
    return (real.reshape(lead + (size,)), imag.reshape(lead + (size,)))


def inverse_rows(real, imag):
    split = 16
    lead = real.shape[:-1]
    size = real.shape[-1]
    short = size // split
    real = real.reshape(lead + (short, split))
    imag = imag.reshape(lead + (short, split))
    cosine, sine = table(short, short, short, 1.0)
    real, imag = mix("sb,...bk->...sk", cosine, sine, real, imag)
    cosine, sine = table(short, split, size, 1.0)
    real, imag = rotate(real, imag, cosine, sine)
    cosine, sine = table(split, split, split, 1.0)
    real, imag = mix("ak,...sk->...as", cosine, sine, real, imag)
    return (real.reshape(lead + (size,)), imag.reshape(lead + (size,)))


def by_sections(gate, keys, values, taps, skip_gain):
    inner_count = lax.axis_size("inner")
    devices = lax.axis_size("outer") * inner_count
    rank = lax.axis_index("outer") * inner_count + lax.axis_index("inner")
    chans, seg = keys.shape
    both = 2 * chans
    cols = seg // devices
    blocks = 2 * devices
    full = blocks * seg
    contract = partial(jnp.einsum, precision=HIGHEST)
    product = keys * values
    source = jnp.concatenate([product, taps], axis=0)
    sectioned = lax.all_to_all(
        lax.all_to_all(
            source.reshape(both, 1, 1, seg), "outer", split_axis=3, concat_axis=1, tiled=True
        ),
        "inner",
        split_axis=3,
        concat_axis=2,
        tiled=True,
    )
    sectioned = sectioned.reshape(both, devices, cols)
    cosine, sine = table(blocks, devices, blocks, -1.0)
    real = contract("km,cmj->ckj", cosine, sectioned)
    imag = contract("km,cmj->ckj", sine, sectioned)
    offset = rank * cols + lax.broadcasted_iota(jnp.int32, (blocks, cols), 1)
    residue = lax.broadcasted_iota(jnp.int32, (blocks, cols), 0)
    phase = TWO_PI / full * (offset * residue).astype(jnp.float32)
    real, imag = rotate(real, imag, jnp.cos(phase)[None], -jnp.sin(phase)[None])
    outgoing = jnp.stack([real, imag]).reshape(2, both, blocks, 1, 1, cols)
    moved = lax.all_to_all(
        lax.all_to_all(outgoing, "outer", split_axis=2, concat_axis=3, tiled=True),
        "inner",
        split_axis=2,
        concat_axis=4,
        tiled=True,
    )
    moved = moved.reshape(2, both, 2, seg)
    spec_real, spec_imag = forward_rows(moved[0], moved[1])
    sig_real, filt_real = (spec_real[:chans], spec_real[chans:])
    sig_imag, filt_imag = (spec_imag[:chans], spec_imag[chans:])
    real = sig_real * filt_real - sig_imag * filt_imag
    imag = sig_real * filt_imag + sig_imag * filt_real
    real, imag = inverse_rows(real, imag)
    residue = 2 * rank + lax.broadcasted_iota(jnp.int32, (2, seg), 0)
    offset = lax.broadcasted_iota(jnp.int32, (2, seg), 1)
    phase = TWO_PI / full * (offset * residue).astype(jnp.float32)
    real, imag = rotate(real, imag, jnp.cos(phase)[None], jnp.sin(phase)[None])
    returning = jnp.stack([real, imag]).reshape(2, chans, 1, 1, 2, seg)
    gathered = lax.all_to_all(
        lax.all_to_all(returning, "outer", split_axis=5, concat_axis=2, tiled=True),
        "inner",
        split_axis=5,
        concat_axis=3,
        tiled=True,
    )
    gathered = gathered.reshape(2, chans, blocks, cols)
    cosine, sine = table(devices, blocks, blocks, 1.0)
    conv = contract("mk,ckj->cmj", cosine, gathered[0]) - contract("mk,ckj->cmj", sine, gathered[1])
    conv = conv * (1.0 / full)
    conv = lax.all_to_all(
        lax.all_to_all(
            conv.reshape(chans, devices, 1, 1, cols),
            "outer",
            split_axis=1,
            concat_axis=2,
            tiled=True,
        ),
        "inner",
        split_axis=1,
        concat_axis=3,
        tiled=True,
    )
    conv = conv.reshape(chans, seg)
    return gate * (conv + skip_gain[:, None] * product)


def halves(array):
    high = array.astype(ml_dtypes.bfloat16)
    low = (array - high.astype(np.float64)).astype(ml_dtypes.bfloat16)
    return high, low


def transform_tables(devices, seg):
    length = devices * seg
    count = length // LANES
    odd = 2 * np.arange(count) + 1
    angle = 2 * np.pi / (4 * count) * ((odd[:, None] * np.arange(count)[None, :]) % (4 * count))
    first = np.concatenate([np.cos(angle), -np.sin(angle)], axis=0)
    last = np.concatenate([np.cos(angle).T, -np.sin(angle).T], axis=1) / length
    angle = 2 * np.pi / (4 * length) * ((odd[:, None] * np.arange(LANES)[None, :]) % (4 * length))
    twiddle = np.stack([np.cos(angle), np.sin(angle)]).astype(np.float32)
    angle = 2 * np.pi / LANES * ((np.arange(LANES)[:, None] * np.arange(LANES)[None, :]) % LANES)
    cosine, sine = np.cos(angle), np.sin(angle)
    rows = np.block([[cosine, -sine], [sine, cosine]])
    back = np.block([[cosine, sine], [-sine, cosine]])
    first_high, first_low = halves(first)
    rows_high, rows_low = halves(rows)
    back_high, back_low = halves(back)
    last_high, last_low = halves(last)
    return (
        np.concatenate([first_high, first_high, first_low], axis=1),
        np.concatenate([rows_high, rows_high, rows_low], axis=0),
        np.concatenate([back_high, back_high, back_low], axis=0),
        np.concatenate([last_high, last_high, last_low], axis=1),
        twiddle,
    )


def split(array):
    high = array.astype(jnp.bfloat16)
    return high, (array - high.astype(jnp.float32)).astype(jnp.bfloat16)


def dot(left, right):
    return jnp.dot(left, right, preferred_element_type=jnp.float32)


def convolve_kernel(
    devices, chans, seg, data_ref, first_ref, rows_ref, back_ref, last_ref, twiddle_ref, out_ref, signal_ref
):
    parts = seg // LANES
    count = devices * parts
    signals = 2 * chans
    cosine, sine = twiddle_ref[0], twiddle_ref[1]

    def lanes(at):
        return slice(at * LANES, (at + 1) * LANES)

    for device in range(devices):
        for signal in range(signals):
            came = (device * signals + signal) * parts
            signal_ref[device * parts : (device + 1) * parts, lanes(signal)] = data_ref[came : came + parts, :]
    high, low = split(signal_ref[...])
    begun = dot(first_ref[...], jnp.concatenate([high, low, high], axis=0))
    turned = []
    for signal in range(signals):
        real, imag = begun[:count, lanes(signal)], begun[count:, lanes(signal)]
        turned.append(jnp.concatenate([real * cosine + imag * sine, imag * cosine - real * sine], axis=1))
    high, low = split(jnp.concatenate(turned, axis=0))
    spectrum = dot(jnp.concatenate([high, low, high], axis=1), rows_ref[...])
    mid = chans * count
    sig_real, sig_imag = spectrum[:mid, :LANES], spectrum[:mid, LANES:]
    filt_real, filt_imag = spectrum[mid:, :LANES], spectrum[mid:, LANES:]
    filtered = jnp.concatenate(
        [sig_real * filt_real - sig_imag * filt_imag, sig_real * filt_imag + sig_imag * filt_real], axis=1
    )
    high, low = split(filtered)
    backed = dot(jnp.concatenate([high, low, high], axis=1), back_ref[...])
    turned = []
    for chan in range(chans):
        real = backed[chan * count : (chan + 1) * count, :LANES]
        imag = backed[chan * count : (chan + 1) * count, LANES:]
        turned.append(jnp.concatenate([real * cosine - imag * sine, imag * cosine + real * sine], axis=0))
    high, low = split(jnp.concatenate(turned, axis=1))
    conv = dot(last_ref[...], jnp.concatenate([high, low, high], axis=0))
    for device in range(devices):
        for chan in range(chans):
            to = (device * chans + chan) * parts
            out_ref[to : to + parts, :] = conv[device * parts : (device + 1) * parts, lanes(chan)]


def gather_kernel(devices, product_ref, taps_ref, gain_ref, out_ref, skip_ref):
    chans, seg = product_ref.shape
    rows = chans // devices * seg // LANES
    product = product_ref[...].reshape(devices, rows, LANES)
    filt = taps_ref[...].reshape(devices, rows, LANES)
    out_ref[...] = jnp.concatenate([product, filt], axis=1).reshape(2 * devices * rows, LANES)
    diagonal = lax.broadcasted_iota(jnp.int32, (chans, chans), 0) == lax.broadcasted_iota(jnp.int32, (chans, chans), 1)
    gain = jnp.sum(jnp.where(diagonal, gain_ref[...], 0.0), axis=1, keepdims=True)
    skip_ref[...] = gain * product_ref[...]


def mix_kernel(gate_ref, skip_ref, conv_ref, out_ref):
    out_ref[...] = gate_ref[...] * (conv_ref[...].reshape(out_ref.shape) + skip_ref[...])


def on_core(kernel, shapes, moved, flops=10**6, scratch=()):
    return pl.pallas_call(
        kernel,
        out_shape=[jax.ShapeDtypeStruct(shape, jnp.float32) for shape in shapes],
        scratch_shapes=[pltpu.VMEM(shape, jnp.float32) for shape in scratch],
        compiler_params=pltpu.CompilerParams(vmem_limit_bytes=32 * 2**20),
        cost_estimate=pl.CostEstimate(flops=flops, bytes_accessed=moved, transcendentals=0),
    )


def by_channels(gate, keys, values, taps, skip_gain):
    devices = lax.axis_size("outer") * lax.axis_size("inner")
    chans, seg = keys.shape
    own = chans // devices
    tiles = seg // LANES
    tables = [jnp.asarray(table) for table in transform_tables(devices, seg)]
    regroup = partial(lax.all_to_all, axis_name=AXES, split_axis=0, concat_axis=0, tiled=True)
    product = keys * values
    sent, skip = on_core(
        partial(gather_kernel, devices), [(2 * chans * tiles, LANES), (chans, seg)], 5 * chans * seg * 4
    )(product, taps, skip_gain[None, :])
    (conv,) = on_core(
        partial(convolve_kernel, devices, own, seg),
        [(chans * tiles, LANES)],
        2 * 10**6,
        10**9,
        [(devices * tiles, 2 * own * LANES)],
    )(regroup(sent), *tables)
    (mixed,) = on_core(mix_kernel, [(chans, seg)], 4 * chans * seg * 4)(gate, skip, regroup(conv))
    return mixed


def on_device(gate, keys, values, taps, skip_gain):
    devices = lax.axis_size("outer") * lax.axis_size("inner")
    chans, seg = keys.shape
    if chans % devices == 0 and seg % LANES == 0 and devices % 8 == 0:
        return by_channels(gate, keys, values, taps, skip_gain)
    return by_sections(gate, keys, values, taps, skip_gain)


def solution(mesh):
    placed = (
        P(None, ("outer", "inner")),
        P(None, ("outer", "inner")),
        P(None, ("outer", "inner")),
        P(None, ("outer", "inner")),
        P(),
    )
    return jax.shard_map(
        on_device,
        mesh=mesh,
        in_specs=placed,
        out_specs=P(None, ("outer", "inner")),
        check_vma=False,
    )
```

```python
from functools import partial
import math

import jax
import jax.numpy as jnp
import ml_dtypes
import numpy as np
from jax import lax
from jax.experimental import pallas as pl
from jax.experimental.pallas import tpu as pltpu
from jax.sharding import PartitionSpec as P

LANES = 128
AXES = ("outer", "inner")

TWO_PI = 2.0 * math.pi
HIGHEST = lax.Precision.HIGHEST


def table(count_a, count_b, modulus, sign):
    left = lax.broadcasted_iota(jnp.int32, (count_a, count_b), 0)
    right = lax.broadcasted_iota(jnp.int32, (count_a, count_b), 1)
    phase = TWO_PI / modulus * (left * right % modulus).astype(jnp.float32)
    return (jnp.cos(phase), sign * jnp.sin(phase))


def mix(form, cosine, sine, real, imag):
    contract = partial(jnp.einsum, precision=HIGHEST)
    return (
        contract(form, cosine, real) - contract(form, sine, imag),
        contract(form, sine, real) + contract(form, cosine, imag),
    )


def rotate(real, imag, cosine, sine):
    return (real * cosine - imag * sine, real * sine + imag * cosine)


def forward_rows(real, imag):
    split = 16
    lead = real.shape[:-1]
    size = real.shape[-1]
    short = size // split
    real = real.reshape(lead + (split, short))
    imag = imag.reshape(lead + (split, short))
    cosine, sine = table(split, split, split, -1.0)
    real, imag = mix("ka,...as->...ks", cosine, sine, real, imag)
    cosine, sine = table(split, short, size, -1.0)
    real, imag = rotate(real, imag, cosine, sine)
    cosine, sine = table(short, short, short, -1.0)
    real, imag = mix("sb,...ks->...bk", cosine, sine, real, imag)
    return (real.reshape(lead + (size,)), imag.reshape(lead + (size,)))


def inverse_rows(real, imag):
    split = 16
    lead = real.shape[:-1]
    size = real.shape[-1]
    short = size // split
    real = real.reshape(lead + (short, split))
    imag = imag.reshape(lead + (short, split))
    cosine, sine = table(short, short, short, 1.0)
    real, imag = mix("sb,...bk->...sk", cosine, sine, real, imag)
    cosine, sine = table(short, split, size, 1.0)
    real, imag = rotate(real, imag, cosine, sine)
    cosine, sine = table(split, split, split, 1.0)
    real, imag = mix("ak,...sk->...as", cosine, sine, real, imag)
    return (real.reshape(lead + (size,)), imag.reshape(lead + (size,)))


def by_sections(gate, keys, values, taps, skip_gain):
    inner_count = lax.axis_size("inner")
    devices = lax.axis_size("outer") * inner_count
    rank = lax.axis_index("outer") * inner_count + lax.axis_index("inner")
    chans, seg = keys.shape
    both = 2 * chans
    cols = seg // devices
    blocks = 2 * devices
    full = blocks * seg
    contract = partial(jnp.einsum, precision=HIGHEST)
    product = keys * values
    source = jnp.concatenate([product, taps], axis=0)
    sectioned = lax.all_to_all(
        lax.all_to_all(
            source.reshape(both, 1, 1, seg), "outer", split_axis=3, concat_axis=1, tiled=True
        ),
        "inner",
        split_axis=3,
        concat_axis=2,
        tiled=True,
    )
    sectioned = sectioned.reshape(both, devices, cols)
    cosine, sine = table(blocks, devices, blocks, -1.0)
    real = contract("km,cmj->ckj", cosine, sectioned)
    imag = contract("km,cmj->ckj", sine, sectioned)
    offset = rank * cols + lax.broadcasted_iota(jnp.int32, (blocks, cols), 1)
    residue = lax.broadcasted_iota(jnp.int32, (blocks, cols), 0)
    phase = TWO_PI / full * (offset * residue).astype(jnp.float32)
    real, imag = rotate(real, imag, jnp.cos(phase)[None], -jnp.sin(phase)[None])
    outgoing = jnp.stack([real, imag]).reshape(2, both, blocks, 1, 1, cols)
    moved = lax.all_to_all(
        lax.all_to_all(outgoing, "outer", split_axis=2, concat_axis=3, tiled=True),
        "inner",
        split_axis=2,
        concat_axis=4,
        tiled=True,
    )
    moved = moved.reshape(2, both, 2, seg)
    spec_real, spec_imag = forward_rows(moved[0], moved[1])
    sig_real, filt_real = (spec_real[:chans], spec_real[chans:])
    sig_imag, filt_imag = (spec_imag[:chans], spec_imag[chans:])
    real = sig_real * filt_real - sig_imag * filt_imag
    imag = sig_real * filt_imag + sig_imag * filt_real
    real, imag = inverse_rows(real, imag)
    residue = 2 * rank + lax.broadcasted_iota(jnp.int32, (2, seg), 0)
    offset = lax.broadcasted_iota(jnp.int32, (2, seg), 1)
    phase = TWO_PI / full * (offset * residue).astype(jnp.float32)
    real, imag = rotate(real, imag, jnp.cos(phase)[None], jnp.sin(phase)[None])
    returning = jnp.stack([real, imag]).reshape(2, chans, 1, 1, 2, seg)
    gathered = lax.all_to_all(
        lax.all_to_all(returning, "outer", split_axis=5, concat_axis=2, tiled=True),
        "inner",
        split_axis=5,
        concat_axis=3,
        tiled=True,
    )
    gathered = gathered.reshape(2, chans, blocks, cols)
    cosine, sine = table(devices, blocks, blocks, 1.0)
    conv = contract("mk,ckj->cmj", cosine, gathered[0]) - contract("mk,ckj->cmj", sine, gathered[1])
    conv = conv * (1.0 / full)
    conv = lax.all_to_all(
        lax.all_to_all(
            conv.reshape(chans, devices, 1, 1, cols),
            "outer",
            split_axis=1,
            concat_axis=2,
            tiled=True,
        ),
        "inner",
        split_axis=1,
        concat_axis=3,
        tiled=True,
    )
    conv = conv.reshape(chans, seg)
    return gate * (conv + skip_gain[:, None] * product)


def halves(array):
    high = array.astype(ml_dtypes.bfloat16)
    low = (array - high.astype(np.float64)).astype(ml_dtypes.bfloat16)
    return high, low


def transform_tables(devices, seg):
    length = devices * seg
    count = length // LANES
    odd = 2 * np.arange(count) + 1
    angle = 2 * np.pi / (4 * count) * ((odd[:, None] * np.arange(count)[None, :]) % (4 * count))
    first = np.concatenate([np.cos(angle), -np.sin(angle)], axis=0)
    last = np.concatenate([np.cos(angle).T, -np.sin(angle).T], axis=1) / length
    angle = 2 * np.pi / (4 * length) * ((odd[:, None] * np.arange(LANES)[None, :]) % (4 * length))
    twiddle = np.stack([np.cos(angle), np.sin(angle)]).astype(np.float32)
    angle = 2 * np.pi / LANES * ((np.arange(LANES)[:, None] * np.arange(LANES)[None, :]) % LANES)
    cosine, sine = np.cos(angle), np.sin(angle)
    rows = np.block([[cosine, -sine], [sine, cosine]])
    back = np.block([[cosine, sine], [-sine, cosine]])
    first_high, first_low = halves(first)
    rows_high, rows_low = halves(rows)
    back_high, back_low = halves(back)
    last_high, last_low = halves(last)
    return (
        np.concatenate([first_high, first_high, first_low], axis=1),
        np.concatenate([rows_high, rows_high, rows_low], axis=0),
        np.concatenate([back_high, back_high, back_low], axis=0),
        np.concatenate([last_high, last_high, last_low], axis=1),
        twiddle,
    )


def split(array):
    high = array.astype(jnp.bfloat16)
    return high, (array - high.astype(jnp.float32)).astype(jnp.bfloat16)


def dot(left, right):
    return jnp.dot(left, right, preferred_element_type=jnp.float32)


def convolve_kernel(
    devices, chans, seg, data_ref, first_ref, rows_ref, back_ref, last_ref, twiddle_ref, gain_ref, out_ref, signal_ref
):
    parts = seg // LANES
    count = devices * parts
    rank = lax.axis_index("outer") * lax.axis_size("inner") + lax.axis_index("inner")
    cosine, sine = twiddle_ref[0], twiddle_ref[1]
    lane = lax.broadcasted_iota(jnp.int32, gain_ref.shape, 1)

    def lanes(at):
        return slice(at * LANES, (at + 1) * LANES)

    groups = 2 if chans % 2 == 0 else 1
    each = chans // groups
    at = range(groups)
    for group in at:
        for kind in range(2):
            for chan in range(each):
                for device in range(devices):
                    came = ((device * 2 + kind) * chans + group * each + chan) * parts
                    signal_ref[group, device * parts : (device + 1) * parts, lanes(kind * each + chan)] = data_ref[
                        came : came + parts, :
                    ]

    def start(group):
        high, low = split(signal_ref[group])
        return dot(first_ref[...], jnp.concatenate([high, low, high], axis=0))

    def spectra(begun):
        turned = []
        for signal in range(2 * each):
            real, imag = begun[:count, lanes(signal)], begun[count:, lanes(signal)]
            turned.append(jnp.concatenate([real * cosine + imag * sine, imag * cosine - real * sine], axis=1))
        high, low = split(jnp.concatenate(turned, axis=0))
        return dot(jnp.concatenate([high, low, high], axis=1), rows_ref[...])

    def back(spectrum):
        mid = each * count
        sig_real, sig_imag = spectrum[:mid, :LANES], spectrum[:mid, LANES:]
        filt_real, filt_imag = spectrum[mid:, :LANES], spectrum[mid:, LANES:]
        real = sig_real * filt_real - sig_imag * filt_imag
        imag = sig_real * filt_imag + sig_imag * filt_real
        high, low = split(jnp.concatenate([real, imag], axis=1))
        return dot(jnp.concatenate([high, low, high], axis=1), back_ref[...])

    def end(backed):
        turned = []
        for chan in range(each):
            real = backed[chan * count : (chan + 1) * count, :LANES]
            imag = backed[chan * count : (chan + 1) * count, LANES:]
            turned.append(jnp.concatenate([real * cosine - imag * sine, imag * cosine + real * sine], axis=0))
        high, low = split(jnp.concatenate(turned, axis=1))
        return dot(last_ref[...], jnp.concatenate([high, low, high], axis=0))

    begun = [start(group) for group in at]
    spectrum = [spectra(begun[group]) for group in at]
    backed = [back(spectrum[group]) for group in at]
    conv = [end(backed[group]) for group in at]
    for group in at:
        for chan in range(each):
            own = group * each + chan
            gain = jnp.sum(jnp.where(lane == rank * chans + own, gain_ref[...], 0.0), axis=1, keepdims=True)
            mixed = conv[group][:, lanes(chan)] + gain * signal_ref[group, :, lanes(chan)]
            for device in range(devices):
                to = (device * chans + own) * parts
                out_ref[to : to + parts, :] = mixed[device * parts : (device + 1) * parts]


def gather_kernel(devices, product_ref, taps_ref, out_ref):
    chans, seg = product_ref.shape
    rows = chans // devices * seg // LANES
    product = product_ref[...].reshape(devices, rows, LANES)
    filt = taps_ref[...].reshape(devices, rows, LANES)
    out_ref[...] = jnp.concatenate([product, filt], axis=1).reshape(2 * devices * rows, LANES)


def gate_kernel(gate_ref, conv_ref, out_ref):
    out_ref[...] = gate_ref[...] * conv_ref[...].reshape(out_ref.shape)


def on_core(kernel, shape, moved, flops=10**6, scratch=()):
    return pl.pallas_call(
        kernel,
        out_shape=jax.ShapeDtypeStruct(shape, jnp.float32),
        scratch_shapes=[pltpu.VMEM(part, jnp.float32) for part in scratch],
        compiler_params=pltpu.CompilerParams(vmem_limit_bytes=32 * 2**20),
        cost_estimate=pl.CostEstimate(flops=flops, bytes_accessed=moved, transcendentals=0),
    )


def by_channels(gate, keys, values, taps, skip_gain):
    devices = lax.axis_size("outer") * lax.axis_size("inner")
    chans, seg = keys.shape
    own = chans // devices
    tiles = seg // LANES
    tables = [jnp.asarray(table) for table in transform_tables(devices, seg)]
    regroup = partial(lax.all_to_all, axis_name=AXES, split_axis=0, concat_axis=0, tiled=True)
    sent = on_core(partial(gather_kernel, devices), (2 * chans * tiles, LANES), 4 * chans * seg * 4)(
        keys * values, taps
    )
    groups = 2 if own % 2 == 0 else 1
    conv = on_core(
        partial(convolve_kernel, devices, own, seg),
        (chans * tiles, LANES),
        2 * 10**6,
        10**9,
        [(groups, devices * tiles, 2 * own // groups * LANES)],
    )(regroup(sent), *tables, skip_gain[None, :])
    return on_core(gate_kernel, (chans, seg), 3 * chans * seg * 4)(gate, regroup(conv))


def on_device(gate, keys, values, taps, skip_gain):
    devices = lax.axis_size("outer") * lax.axis_size("inner")
    chans, seg = keys.shape
    if chans % devices == 0 and seg % LANES == 0 and devices % 8 == 0:
        return by_channels(gate, keys, values, taps, skip_gain)
    return by_sections(gate, keys, values, taps, skip_gain)


def solution(mesh):
    placed = (
        P(None, ("outer", "inner")),
        P(None, ("outer", "inner")),
        P(None, ("outer", "inner")),
        P(None, ("outer", "inner")),
        P(),
    )
    return jax.shard_map(
        on_device,
        mesh=mesh,
        in_specs=placed,
        out_specs=P(None, ("outer", "inner")),
        check_vma=False,
    )
```

```python
from functools import partial
import math

import jax
import jax.numpy as jnp
import ml_dtypes
import numpy as np
from jax import lax
from jax.experimental import pallas as pl
from jax.experimental.pallas import tpu as pltpu
from jax.sharding import PartitionSpec as P

LANES = 128
AXES = ("outer", "inner")

TWO_PI = 2.0 * math.pi
HIGHEST = lax.Precision.HIGHEST


def table(count_a, count_b, modulus, sign):
    left = lax.broadcasted_iota(jnp.int32, (count_a, count_b), 0)
    right = lax.broadcasted_iota(jnp.int32, (count_a, count_b), 1)
    phase = TWO_PI / modulus * (left * right % modulus).astype(jnp.float32)
    return (jnp.cos(phase), sign * jnp.sin(phase))


def mix(form, cosine, sine, real, imag):
    contract = partial(jnp.einsum, precision=HIGHEST)
    return (
        contract(form, cosine, real) - contract(form, sine, imag),
        contract(form, sine, real) + contract(form, cosine, imag),
    )


def rotate(real, imag, cosine, sine):
    return (real * cosine - imag * sine, real * sine + imag * cosine)


def forward_rows(real, imag):
    split = 16
    lead = real.shape[:-1]
    size = real.shape[-1]
    short = size // split
    real = real.reshape(lead + (split, short))
    imag = imag.reshape(lead + (split, short))
    cosine, sine = table(split, split, split, -1.0)
    real, imag = mix("ka,...as->...ks", cosine, sine, real, imag)
    cosine, sine = table(split, short, size, -1.0)
    real, imag = rotate(real, imag, cosine, sine)
    cosine, sine = table(short, short, short, -1.0)
    real, imag = mix("sb,...ks->...bk", cosine, sine, real, imag)
    return (real.reshape(lead + (size,)), imag.reshape(lead + (size,)))


def inverse_rows(real, imag):
    split = 16
    lead = real.shape[:-1]
    size = real.shape[-1]
    short = size // split
    real = real.reshape(lead + (short, split))
    imag = imag.reshape(lead + (short, split))
    cosine, sine = table(short, short, short, 1.0)
    real, imag = mix("sb,...bk->...sk", cosine, sine, real, imag)
    cosine, sine = table(short, split, size, 1.0)
    real, imag = rotate(real, imag, cosine, sine)
    cosine, sine = table(split, split, split, 1.0)
    real, imag = mix("ak,...sk->...as", cosine, sine, real, imag)
    return (real.reshape(lead + (size,)), imag.reshape(lead + (size,)))


def by_sections(gate, keys, values, taps, skip_gain):
    inner_count = lax.axis_size("inner")
    devices = lax.axis_size("outer") * inner_count
    rank = lax.axis_index("outer") * inner_count + lax.axis_index("inner")
    chans, seg = keys.shape
    both = 2 * chans
    cols = seg // devices
    blocks = 2 * devices
    full = blocks * seg
    contract = partial(jnp.einsum, precision=HIGHEST)
    product = keys * values
    source = jnp.concatenate([product, taps], axis=0)
    sectioned = lax.all_to_all(
        lax.all_to_all(
            source.reshape(both, 1, 1, seg), "outer", split_axis=3, concat_axis=1, tiled=True
        ),
        "inner",
        split_axis=3,
        concat_axis=2,
        tiled=True,
    )
    sectioned = sectioned.reshape(both, devices, cols)
    cosine, sine = table(blocks, devices, blocks, -1.0)
    real = contract("km,cmj->ckj", cosine, sectioned)
    imag = contract("km,cmj->ckj", sine, sectioned)
    offset = rank * cols + lax.broadcasted_iota(jnp.int32, (blocks, cols), 1)
    residue = lax.broadcasted_iota(jnp.int32, (blocks, cols), 0)
    phase = TWO_PI / full * (offset * residue).astype(jnp.float32)
    real, imag = rotate(real, imag, jnp.cos(phase)[None], -jnp.sin(phase)[None])
    outgoing = jnp.stack([real, imag]).reshape(2, both, blocks, 1, 1, cols)
    moved = lax.all_to_all(
        lax.all_to_all(outgoing, "outer", split_axis=2, concat_axis=3, tiled=True),
        "inner",
        split_axis=2,
        concat_axis=4,
        tiled=True,
    )
    moved = moved.reshape(2, both, 2, seg)
    spec_real, spec_imag = forward_rows(moved[0], moved[1])
    sig_real, filt_real = (spec_real[:chans], spec_real[chans:])
    sig_imag, filt_imag = (spec_imag[:chans], spec_imag[chans:])
    real = sig_real * filt_real - sig_imag * filt_imag
    imag = sig_real * filt_imag + sig_imag * filt_real
    real, imag = inverse_rows(real, imag)
    residue = 2 * rank + lax.broadcasted_iota(jnp.int32, (2, seg), 0)
    offset = lax.broadcasted_iota(jnp.int32, (2, seg), 1)
    phase = TWO_PI / full * (offset * residue).astype(jnp.float32)
    real, imag = rotate(real, imag, jnp.cos(phase)[None], jnp.sin(phase)[None])
    returning = jnp.stack([real, imag]).reshape(2, chans, 1, 1, 2, seg)
    gathered = lax.all_to_all(
        lax.all_to_all(returning, "outer", split_axis=5, concat_axis=2, tiled=True),
        "inner",
        split_axis=5,
        concat_axis=3,
        tiled=True,
    )
    gathered = gathered.reshape(2, chans, blocks, cols)
    cosine, sine = table(devices, blocks, blocks, 1.0)
    conv = contract("mk,ckj->cmj", cosine, gathered[0]) - contract("mk,ckj->cmj", sine, gathered[1])
    conv = conv * (1.0 / full)
    conv = lax.all_to_all(
        lax.all_to_all(
            conv.reshape(chans, devices, 1, 1, cols),
            "outer",
            split_axis=1,
            concat_axis=2,
            tiled=True,
        ),
        "inner",
        split_axis=1,
        concat_axis=3,
        tiled=True,
    )
    conv = conv.reshape(chans, seg)
    return gate * (conv + skip_gain[:, None] * product)


def halves(array):
    high = array.astype(ml_dtypes.bfloat16)
    low = (array - high.astype(np.float64)).astype(ml_dtypes.bfloat16)
    return high, low


def transform_tables(devices, seg):
    length = devices * seg
    count = length // LANES
    odd = 2 * np.arange(count) + 1
    angle = 2 * np.pi / (4 * count) * ((odd[:, None] * np.arange(count)[None, :]) % (4 * count))
    first = np.concatenate([np.cos(angle), -np.sin(angle)], axis=0)
    last = np.concatenate([np.cos(angle).T, -np.sin(angle).T], axis=1) / length
    angle = 2 * np.pi / (4 * length) * ((odd[:, None] * np.arange(LANES)[None, :]) % (4 * length))
    twiddle = np.stack([np.cos(angle), np.sin(angle)]).astype(np.float32)
    angle = 2 * np.pi / LANES * ((np.arange(LANES)[:, None] * np.arange(LANES)[None, :]) % LANES)
    cosine, sine = np.cos(angle), np.sin(angle)
    rows = np.block([[cosine, -sine], [sine, cosine]])
    back = np.block([[cosine, sine], [-sine, cosine]])
    first_high, first_low = halves(first)
    rows_high, rows_low = halves(rows)
    back_high, back_low = halves(back)
    last_high, last_low = halves(last)
    return (
        np.concatenate([first_high, first_high, first_low], axis=1),
        np.concatenate([rows_high, rows_high, rows_low], axis=0),
        np.concatenate([back_high, back_high, back_low], axis=0),
        np.concatenate([last_high, last_high, last_low], axis=1),
        twiddle,
    )


def split(array):
    high = array.astype(jnp.bfloat16)
    return high, (array - high.astype(jnp.float32)).astype(jnp.bfloat16)


def dot(left, right):
    return jnp.dot(left, right, preferred_element_type=jnp.float32)


def convolve_kernel(
    devices, chans, seg, data_ref, first_ref, rows_ref, back_ref, last_ref, twiddle_ref, out_ref, signal_ref
):
    parts = seg // LANES
    count = devices * parts
    cosine, sine = twiddle_ref[0], twiddle_ref[1]

    def lanes(at):
        return slice(at * LANES, (at + 1) * LANES)

    groups = chans
    each = chans // groups
    at = range(groups)
    for group in at:
        for kind in range(2):
            for chan in range(each):
                for device in range(devices):
                    came = ((device * 2 + kind) * chans + group * each + chan) * parts
                    signal_ref[group, device * parts : (device + 1) * parts, lanes(kind * each + chan)] = data_ref[
                        came : came + parts, :
                    ]

    def start(group):
        high, low = split(signal_ref[group])
        return dot(first_ref[...], jnp.concatenate([high, low, high], axis=0))

    def spectra(begun):
        turned = []
        for signal in range(2 * each):
            real, imag = begun[:count, lanes(signal)], begun[count:, lanes(signal)]
            turned.append(jnp.concatenate([real * cosine + imag * sine, imag * cosine - real * sine], axis=1))
        high, low = split(jnp.concatenate(turned, axis=0))
        return dot(jnp.concatenate([high, low, high], axis=1), rows_ref[...])

    def back(spectrum):
        mid = each * count
        sig_real, sig_imag = spectrum[:mid, :LANES], spectrum[:mid, LANES:]
        filt_real, filt_imag = spectrum[mid:, :LANES], spectrum[mid:, LANES:]
        real = sig_real * filt_real - sig_imag * filt_imag
        imag = sig_real * filt_imag + sig_imag * filt_real
        high, low = split(jnp.concatenate([real, imag], axis=1))
        return dot(jnp.concatenate([high, low, high], axis=1), back_ref[...])

    def end(backed):
        turned = []
        for chan in range(each):
            real = backed[chan * count : (chan + 1) * count, :LANES]
            imag = backed[chan * count : (chan + 1) * count, LANES:]
            turned.append(jnp.concatenate([real * cosine - imag * sine, imag * cosine + real * sine], axis=0))
        high, low = split(jnp.concatenate(turned, axis=1))
        return dot(last_ref[...], jnp.concatenate([high, low, high], axis=0))

    begun = [start(group) for group in at]
    spectrum = [spectra(begun[group]) for group in at]
    backed = [back(spectrum[group]) for group in at]
    conv = [end(backed[group]) for group in at]
    for group in at:
        for chan in range(each):
            own = group * each + chan
            for device in range(devices):
                to = (device * chans + own) * parts
                out_ref[to : to + parts, :] = conv[group][device * parts : (device + 1) * parts, lanes(chan)]


def gather_kernel(devices, product_ref, taps_ref, out_ref):
    chans, seg = product_ref.shape
    rows = chans // devices * seg // LANES
    product = product_ref[...].reshape(devices, rows, LANES)
    filt = taps_ref[...].reshape(devices, rows, LANES)
    out_ref[...] = jnp.concatenate([product, filt], axis=1).reshape(2 * devices * rows, LANES)


def gate_kernel(gate_ref, skip_ref, conv_ref, out_ref):
    out_ref[...] = gate_ref[...] * (conv_ref[...].reshape(out_ref.shape) + skip_ref[...])


def on_core(kernel, shape, moved, flops=10**6, scratch=()):
    return pl.pallas_call(
        kernel,
        out_shape=jax.ShapeDtypeStruct(shape, jnp.float32),
        scratch_shapes=[pltpu.VMEM(part, jnp.float32) for part in scratch],
        compiler_params=pltpu.CompilerParams(vmem_limit_bytes=32 * 2**20),
        cost_estimate=pl.CostEstimate(flops=flops, bytes_accessed=moved, transcendentals=0),
    )


def by_channels(gate, keys, values, taps, skip_gain):
    devices = lax.axis_size("outer") * lax.axis_size("inner")
    chans, seg = keys.shape
    own = chans // devices
    tiles = seg // LANES
    tables = [jnp.asarray(table) for table in transform_tables(devices, seg)]
    regroup = partial(lax.all_to_all, axis_name=AXES, split_axis=0, concat_axis=0, tiled=True)
    product = keys * values
    product, skip = lax.optimization_barrier((product, skip_gain[:, None] * product))
    sent = on_core(partial(gather_kernel, devices), (2 * chans * tiles, LANES), 4 * chans * seg * 4)(product, taps)
    groups = own
    conv = on_core(
        partial(convolve_kernel, devices, own, seg),
        (chans * tiles, LANES),
        2 * 10**6,
        10**9,
        [(groups, devices * tiles, 2 * own // groups * LANES)],
    )(regroup(sent), *tables)
    return on_core(gate_kernel, (chans, seg), 4 * chans * seg * 4)(gate, skip, regroup(conv))


def on_device(gate, keys, values, taps, skip_gain):
    devices = lax.axis_size("outer") * lax.axis_size("inner")
    chans, seg = keys.shape
    if chans % devices == 0 and seg % LANES == 0 and devices % 8 == 0:
        return by_channels(gate, keys, values, taps, skip_gain)
    return by_sections(gate, keys, values, taps, skip_gain)


def solution(mesh):
    placed = (
        P(None, ("outer", "inner")),
        P(None, ("outer", "inner")),
        P(None, ("outer", "inner")),
        P(None, ("outer", "inner")),
        P(),
    )
    return jax.shard_map(
        on_device,
        mesh=mesh,
        in_specs=placed,
        out_specs=P(None, ("outer", "inner")),
        check_vma=False,
    )
```

```python
from functools import partial
import math

import jax
import jax.numpy as jnp
import ml_dtypes
import numpy as np
from jax import lax
from jax.experimental import pallas as pl
from jax.experimental.pallas import tpu as pltpu
from jax.sharding import PartitionSpec as P

LANES = 128
AXES = ("inner", "outer")

TWO_PI = 2.0 * math.pi
HIGHEST = lax.Precision.HIGHEST


def table(count_a, count_b, modulus, sign):
    left = lax.broadcasted_iota(jnp.int32, (count_a, count_b), 0)
    right = lax.broadcasted_iota(jnp.int32, (count_a, count_b), 1)
    phase = TWO_PI / modulus * (left * right % modulus).astype(jnp.float32)
    return (jnp.cos(phase), sign * jnp.sin(phase))


def mix(form, cosine, sine, real, imag):
    contract = partial(jnp.einsum, precision=HIGHEST)
    return (
        contract(form, cosine, real) - contract(form, sine, imag),
        contract(form, sine, real) + contract(form, cosine, imag),
    )


def rotate(real, imag, cosine, sine):
    return (real * cosine - imag * sine, real * sine + imag * cosine)


def forward_rows(real, imag):
    split = 16
    lead = real.shape[:-1]
    size = real.shape[-1]
    short = size // split
    real = real.reshape(lead + (split, short))
    imag = imag.reshape(lead + (split, short))
    cosine, sine = table(split, split, split, -1.0)
    real, imag = mix("ka,...as->...ks", cosine, sine, real, imag)
    cosine, sine = table(split, short, size, -1.0)
    real, imag = rotate(real, imag, cosine, sine)
    cosine, sine = table(short, short, short, -1.0)
    real, imag = mix("sb,...ks->...bk", cosine, sine, real, imag)
    return (real.reshape(lead + (size,)), imag.reshape(lead + (size,)))


def inverse_rows(real, imag):
    split = 16
    lead = real.shape[:-1]
    size = real.shape[-1]
    short = size // split
    real = real.reshape(lead + (short, split))
    imag = imag.reshape(lead + (short, split))
    cosine, sine = table(short, short, short, 1.0)
    real, imag = mix("sb,...bk->...sk", cosine, sine, real, imag)
    cosine, sine = table(short, split, size, 1.0)
    real, imag = rotate(real, imag, cosine, sine)
    cosine, sine = table(split, split, split, 1.0)
    real, imag = mix("ak,...sk->...as", cosine, sine, real, imag)
    return (real.reshape(lead + (size,)), imag.reshape(lead + (size,)))


def by_sections(gate, keys, values, taps, skip_gain):
    inner_count = lax.axis_size("inner")
    devices = lax.axis_size("outer") * inner_count
    rank = lax.axis_index("outer") * inner_count + lax.axis_index("inner")
    chans, seg = keys.shape
    both = 2 * chans
    cols = seg // devices
    blocks = 2 * devices
    full = blocks * seg
    contract = partial(jnp.einsum, precision=HIGHEST)
    product = keys * values
    source = jnp.concatenate([product, taps], axis=0)
    sectioned = lax.all_to_all(
        lax.all_to_all(
            source.reshape(both, 1, 1, seg), "outer", split_axis=3, concat_axis=1, tiled=True
        ),
        "inner",
        split_axis=3,
        concat_axis=2,
        tiled=True,
    )
    sectioned = sectioned.reshape(both, devices, cols)
    cosine, sine = table(blocks, devices, blocks, -1.0)
    real = contract("km,cmj->ckj", cosine, sectioned)
    imag = contract("km,cmj->ckj", sine, sectioned)
    offset = rank * cols + lax.broadcasted_iota(jnp.int32, (blocks, cols), 1)
    residue = lax.broadcasted_iota(jnp.int32, (blocks, cols), 0)
    phase = TWO_PI / full * (offset * residue).astype(jnp.float32)
    real, imag = rotate(real, imag, jnp.cos(phase)[None], -jnp.sin(phase)[None])
    outgoing = jnp.stack([real, imag]).reshape(2, both, blocks, 1, 1, cols)
    moved = lax.all_to_all(
        lax.all_to_all(outgoing, "outer", split_axis=2, concat_axis=3, tiled=True),
        "inner",
        split_axis=2,
        concat_axis=4,
        tiled=True,
    )
    moved = moved.reshape(2, both, 2, seg)
    spec_real, spec_imag = forward_rows(moved[0], moved[1])
    sig_real, filt_real = (spec_real[:chans], spec_real[chans:])
    sig_imag, filt_imag = (spec_imag[:chans], spec_imag[chans:])
    real = sig_real * filt_real - sig_imag * filt_imag
    imag = sig_real * filt_imag + sig_imag * filt_real
    real, imag = inverse_rows(real, imag)
    residue = 2 * rank + lax.broadcasted_iota(jnp.int32, (2, seg), 0)
    offset = lax.broadcasted_iota(jnp.int32, (2, seg), 1)
    phase = TWO_PI / full * (offset * residue).astype(jnp.float32)
    real, imag = rotate(real, imag, jnp.cos(phase)[None], jnp.sin(phase)[None])
    returning = jnp.stack([real, imag]).reshape(2, chans, 1, 1, 2, seg)
    gathered = lax.all_to_all(
        lax.all_to_all(returning, "outer", split_axis=5, concat_axis=2, tiled=True),
        "inner",
        split_axis=5,
        concat_axis=3,
        tiled=True,
    )
    gathered = gathered.reshape(2, chans, blocks, cols)
    cosine, sine = table(devices, blocks, blocks, 1.0)
    conv = contract("mk,ckj->cmj", cosine, gathered[0]) - contract("mk,ckj->cmj", sine, gathered[1])
    conv = conv * (1.0 / full)
    conv = lax.all_to_all(
        lax.all_to_all(
            conv.reshape(chans, devices, 1, 1, cols),
            "outer",
            split_axis=1,
            concat_axis=2,
            tiled=True,
        ),
        "inner",
        split_axis=1,
        concat_axis=3,
        tiled=True,
    )
    conv = conv.reshape(chans, seg)
    return gate * (conv + skip_gain[:, None] * product)


def halves(array):
    high = array.astype(ml_dtypes.bfloat16)
    low = (array - high.astype(np.float64)).astype(ml_dtypes.bfloat16)
    return high, low


def transform_tables(devices, seg):
    length = devices * seg
    count = length // LANES
    odd = 2 * np.arange(count) + 1
    angle = 2 * np.pi / (4 * count) * ((odd[:, None] * np.arange(count)[None, :]) % (4 * count))
    first = np.concatenate([np.cos(angle), -np.sin(angle)], axis=0)
    last = np.concatenate([np.cos(angle).T, -np.sin(angle).T], axis=1) / length
    angle = 2 * np.pi / (4 * length) * ((odd[:, None] * np.arange(LANES)[None, :]) % (4 * length))
    twiddle = np.stack([np.cos(angle), np.sin(angle)]).astype(np.float32)
    angle = 2 * np.pi / LANES * ((np.arange(LANES)[:, None] * np.arange(LANES)[None, :]) % LANES)
    cosine, sine = np.cos(angle), np.sin(angle)
    rows = np.block([[cosine, -sine], [sine, cosine]])
    back = np.block([[cosine, sine], [-sine, cosine]])
    first_high, first_low = halves(first)
    rows_high, rows_low = halves(rows)
    back_high, back_low = halves(back)
    last_high, last_low = halves(last)
    return (
        np.concatenate([first_high, first_high, first_low], axis=1),
        np.concatenate([rows_high, rows_high, rows_low], axis=0),
        np.concatenate([back_high, back_high, back_low], axis=0),
        np.concatenate([last_high, last_high, last_low], axis=1),
        twiddle,
    )


def split(array):
    high = array.astype(jnp.bfloat16)
    return high, (array - high.astype(jnp.float32)).astype(jnp.bfloat16)


def dot(left, right):
    return jnp.dot(left, right, preferred_element_type=jnp.float32)


def convolve_kernel(
    devices, chans, seg, data_ref, first_ref, rows_ref, back_ref, last_ref, twiddle_ref, out_ref, signal_ref
):
    parts = seg // LANES
    count = devices * parts
    cosine, sine = twiddle_ref[0], twiddle_ref[1]

    def lanes(at):
        return slice(at * LANES, (at + 1) * LANES)

    def place(device):
        outer = lax.axis_size("outer")
        return device % outer * lax.axis_size("inner") + device // outer

    groups = chans
    each = chans // groups
    at = range(groups)
    for group in at:
        for kind in range(2):
            for chan in range(each):
                for device in range(devices):
                    came = ((device * 2 + kind) * chans + group * each + chan) * parts
                    to = place(device) * parts
                    signal_ref[group, to : to + parts, lanes(kind * each + chan)] = data_ref[came : came + parts, :]

    def start(group):
        high, low = split(signal_ref[group])
        return dot(first_ref[...], jnp.concatenate([high, low, high], axis=0))

    def spectra(begun):
        turned = []
        for signal in range(2 * each):
            real, imag = begun[:count, lanes(signal)], begun[count:, lanes(signal)]
            turned.append(jnp.concatenate([real * cosine + imag * sine, imag * cosine - real * sine], axis=1))
        high, low = split(jnp.concatenate(turned, axis=0))
        return dot(jnp.concatenate([high, low, high], axis=1), rows_ref[...])

    def back(spectrum):
        mid = each * count
        sig_real, sig_imag = spectrum[:mid, :LANES], spectrum[:mid, LANES:]
        filt_real, filt_imag = spectrum[mid:, :LANES], spectrum[mid:, LANES:]
        real = sig_real * filt_real - sig_imag * filt_imag
        imag = sig_real * filt_imag + sig_imag * filt_real
        high, low = split(jnp.concatenate([real, imag], axis=1))
        return dot(jnp.concatenate([high, low, high], axis=1), back_ref[...])

    def end(backed):
        turned = []
        for chan in range(each):
            real = backed[chan * count : (chan + 1) * count, :LANES]
            imag = backed[chan * count : (chan + 1) * count, LANES:]
            turned.append(jnp.concatenate([real * cosine - imag * sine, imag * cosine + real * sine], axis=0))
        high, low = split(jnp.concatenate(turned, axis=1))
        return dot(last_ref[...], jnp.concatenate([high, low, high], axis=0))

    begun = [start(group) for group in at]
    spectrum = [spectra(begun[group]) for group in at]
    backed = [back(spectrum[group]) for group in at]
    conv = [end(backed[group]) for group in at]
    for group in at:
        for chan in range(each):
            own = group * each + chan
            for device in range(devices):
                to = (device * chans + own) * parts
                came = place(device) * parts
                out_ref[to : to + parts, :] = conv[group][came : came + parts, lanes(chan)]


def gather_kernel(devices, product_ref, taps_ref, out_ref):
    chans, seg = product_ref.shape
    rows = chans // devices * seg // LANES
    product = product_ref[...].reshape(devices, rows, LANES)
    filt = taps_ref[...].reshape(devices, rows, LANES)
    out_ref[...] = jnp.concatenate([product, filt], axis=1).reshape(2 * devices * rows, LANES)


def gate_kernel(gate_ref, skip_ref, conv_ref, out_ref):
    out_ref[...] = gate_ref[...] * (conv_ref[...].reshape(out_ref.shape) + skip_ref[...])


def on_core(kernel, shape, moved, flops=10**6, scratch=()):
    return pl.pallas_call(
        kernel,
        out_shape=jax.ShapeDtypeStruct(shape, jnp.float32),
        scratch_shapes=[pltpu.VMEM(part, jnp.float32) for part in scratch],
        compiler_params=pltpu.CompilerParams(vmem_limit_bytes=32 * 2**20),
        cost_estimate=pl.CostEstimate(flops=flops, bytes_accessed=moved, transcendentals=0),
    )


def by_channels(gate, keys, values, taps, skip_gain):
    devices = lax.axis_size("outer") * lax.axis_size("inner")
    chans, seg = keys.shape
    own = chans // devices
    tiles = seg // LANES
    tables = [jnp.asarray(table) for table in transform_tables(devices, seg)]
    regroup = partial(lax.all_to_all, axis_name=AXES, split_axis=0, concat_axis=0, tiled=True)
    product = keys * values
    product, skip = lax.optimization_barrier((product, skip_gain[:, None] * product))
    sent = on_core(partial(gather_kernel, devices), (2 * chans * tiles, LANES), 4 * chans * seg * 4)(product, taps)
    groups = own
    conv = on_core(
        partial(convolve_kernel, devices, own, seg),
        (chans * tiles, LANES),
        2 * 10**6,
        10**9,
        [(groups, devices * tiles, 2 * own // groups * LANES)],
    )(regroup(sent), *tables)
    return on_core(gate_kernel, (chans, seg), 4 * chans * seg * 4)(gate, skip, regroup(conv))


def on_device(gate, keys, values, taps, skip_gain):
    devices = lax.axis_size("outer") * lax.axis_size("inner")
    chans, seg = keys.shape
    if chans % devices == 0 and seg % LANES == 0 and devices % 8 == 0:
        return by_channels(gate, keys, values, taps, skip_gain)
    return by_sections(gate, keys, values, taps, skip_gain)


def solution(mesh):
    placed = (
        P(None, ("outer", "inner")),
        P(None, ("outer", "inner")),
        P(None, ("outer", "inner")),
        P(None, ("outer", "inner")),
        P(),
    )
    return jax.shard_map(
        on_device,
        mesh=mesh,
        in_specs=placed,
        out_specs=P(None, ("outer", "inner")),
        check_vma=False,
    )
```

```python
from functools import partial
import math

import jax
import jax.numpy as jnp
import ml_dtypes
import numpy as np
from jax import lax
from jax.experimental import pallas as pl
from jax.experimental.pallas import tpu as pltpu
from jax.sharding import PartitionSpec as P

LANES = 128
AXES = ("outer", "inner")

TWO_PI = 2.0 * math.pi
HIGHEST = lax.Precision.HIGHEST


def table(count_a, count_b, modulus, sign):
    left = lax.broadcasted_iota(jnp.int32, (count_a, count_b), 0)
    right = lax.broadcasted_iota(jnp.int32, (count_a, count_b), 1)
    phase = TWO_PI / modulus * (left * right % modulus).astype(jnp.float32)
    return (jnp.cos(phase), sign * jnp.sin(phase))


def mix(form, cosine, sine, real, imag):
    contract = partial(jnp.einsum, precision=HIGHEST)
    return (
        contract(form, cosine, real) - contract(form, sine, imag),
        contract(form, sine, real) + contract(form, cosine, imag),
    )


def rotate(real, imag, cosine, sine):
    return (real * cosine - imag * sine, real * sine + imag * cosine)


def forward_rows(real, imag):
    split = 16
    lead = real.shape[:-1]
    size = real.shape[-1]
    short = size // split
    real = real.reshape(lead + (split, short))
    imag = imag.reshape(lead + (split, short))
    cosine, sine = table(split, split, split, -1.0)
    real, imag = mix("ka,...as->...ks", cosine, sine, real, imag)
    cosine, sine = table(split, short, size, -1.0)
    real, imag = rotate(real, imag, cosine, sine)
    cosine, sine = table(short, short, short, -1.0)
    real, imag = mix("sb,...ks->...bk", cosine, sine, real, imag)
    return (real.reshape(lead + (size,)), imag.reshape(lead + (size,)))


def inverse_rows(real, imag):
    split = 16
    lead = real.shape[:-1]
    size = real.shape[-1]
    short = size // split
    real = real.reshape(lead + (short, split))
    imag = imag.reshape(lead + (short, split))
    cosine, sine = table(short, short, short, 1.0)
    real, imag = mix("sb,...bk->...sk", cosine, sine, real, imag)
    cosine, sine = table(short, split, size, 1.0)
    real, imag = rotate(real, imag, cosine, sine)
    cosine, sine = table(split, split, split, 1.0)
    real, imag = mix("ak,...sk->...as", cosine, sine, real, imag)
    return (real.reshape(lead + (size,)), imag.reshape(lead + (size,)))


def by_sections(gate, keys, values, taps, skip_gain):
    inner_count = lax.axis_size("inner")
    devices = lax.axis_size("outer") * inner_count
    rank = lax.axis_index("outer") * inner_count + lax.axis_index("inner")
    chans, seg = keys.shape
    both = 2 * chans
    cols = seg // devices
    blocks = 2 * devices
    full = blocks * seg
    contract = partial(jnp.einsum, precision=HIGHEST)
    product = keys * values
    source = jnp.concatenate([product, taps], axis=0)
    sectioned = lax.all_to_all(
        lax.all_to_all(
            source.reshape(both, 1, 1, seg), "outer", split_axis=3, concat_axis=1, tiled=True
        ),
        "inner",
        split_axis=3,
        concat_axis=2,
        tiled=True,
    )
    sectioned = sectioned.reshape(both, devices, cols)
    cosine, sine = table(blocks, devices, blocks, -1.0)
    real = contract("km,cmj->ckj", cosine, sectioned)
    imag = contract("km,cmj->ckj", sine, sectioned)
    offset = rank * cols + lax.broadcasted_iota(jnp.int32, (blocks, cols), 1)
    residue = lax.broadcasted_iota(jnp.int32, (blocks, cols), 0)
    phase = TWO_PI / full * (offset * residue).astype(jnp.float32)
    real, imag = rotate(real, imag, jnp.cos(phase)[None], -jnp.sin(phase)[None])
    outgoing = jnp.stack([real, imag]).reshape(2, both, blocks, 1, 1, cols)
    moved = lax.all_to_all(
        lax.all_to_all(outgoing, "outer", split_axis=2, concat_axis=3, tiled=True),
        "inner",
        split_axis=2,
        concat_axis=4,
        tiled=True,
    )
    moved = moved.reshape(2, both, 2, seg)
    spec_real, spec_imag = forward_rows(moved[0], moved[1])
    sig_real, filt_real = (spec_real[:chans], spec_real[chans:])
    sig_imag, filt_imag = (spec_imag[:chans], spec_imag[chans:])
    real = sig_real * filt_real - sig_imag * filt_imag
    imag = sig_real * filt_imag + sig_imag * filt_real
    real, imag = inverse_rows(real, imag)
    residue = 2 * rank + lax.broadcasted_iota(jnp.int32, (2, seg), 0)
    offset = lax.broadcasted_iota(jnp.int32, (2, seg), 1)
    phase = TWO_PI / full * (offset * residue).astype(jnp.float32)
    real, imag = rotate(real, imag, jnp.cos(phase)[None], jnp.sin(phase)[None])
    returning = jnp.stack([real, imag]).reshape(2, chans, 1, 1, 2, seg)
    gathered = lax.all_to_all(
        lax.all_to_all(returning, "outer", split_axis=5, concat_axis=2, tiled=True),
        "inner",
        split_axis=5,
        concat_axis=3,
        tiled=True,
    )
    gathered = gathered.reshape(2, chans, blocks, cols)
    cosine, sine = table(devices, blocks, blocks, 1.0)
    conv = contract("mk,ckj->cmj", cosine, gathered[0]) - contract("mk,ckj->cmj", sine, gathered[1])
    conv = conv * (1.0 / full)
    conv = lax.all_to_all(
        lax.all_to_all(
            conv.reshape(chans, devices, 1, 1, cols),
            "outer",
            split_axis=1,
            concat_axis=2,
            tiled=True,
        ),
        "inner",
        split_axis=1,
        concat_axis=3,
        tiled=True,
    )
    conv = conv.reshape(chans, seg)
    return gate * (conv + skip_gain[:, None] * product)


def halves(array):
    high = array.astype(ml_dtypes.bfloat16)
    low = (array - high.astype(np.float64)).astype(ml_dtypes.bfloat16)
    return high, low


def transform_tables(devices, seg):
    length = devices * seg
    count = length // LANES
    odd = 2 * np.arange(count) + 1
    angle = 2 * np.pi / (4 * count) * ((odd[:, None] * np.arange(count)[None, :]) % (4 * count))
    first = np.concatenate([np.cos(angle), -np.sin(angle)], axis=0)
    last = np.concatenate([np.cos(angle).T, -np.sin(angle).T], axis=1) / length
    angle = 2 * np.pi / (4 * length) * ((odd[:, None] * np.arange(LANES)[None, :]) % (4 * length))
    twiddle = np.stack([np.cos(angle), np.sin(angle)]).astype(np.float32)
    angle = 2 * np.pi / LANES * ((np.arange(LANES)[:, None] * np.arange(LANES)[None, :]) % LANES)
    cosine, sine = np.cos(angle), np.sin(angle)
    rows = np.block([[cosine, -sine], [sine, cosine]])
    back = np.block([[cosine, sine], [-sine, cosine]])
    first_high, first_low = halves(first)
    rows_high, rows_low = halves(rows)
    back_high, back_low = halves(back)
    last_high, last_low = halves(last)
    return (
        np.concatenate([first_high, first_high, first_low], axis=1),
        np.concatenate([rows_high, rows_high, rows_low], axis=0),
        np.concatenate([back_high, back_high, back_low], axis=0),
        np.concatenate([last_high, last_high, last_low], axis=1),
        twiddle,
    )


def send_order(outer, inner):
    half = inner // 2
    along = [at // 2 + half * (at % 2) for at in range(2 * half)] + list(range(2 * half, inner))
    return [at * inner + step for at in range(outer) for step in along]


def split(array):
    high = array.astype(jnp.bfloat16)
    return high, (array - high.astype(jnp.float32)).astype(jnp.bfloat16)


def dot(left, right):
    return jnp.dot(left, right, preferred_element_type=jnp.float32)


def convolve_kernel(
    devices, chans, seg, data_ref, first_ref, rows_ref, back_ref, last_ref, twiddle_ref, out_ref, signal_ref
):
    parts = seg // LANES
    count = devices * parts
    cosine, sine = twiddle_ref[0], twiddle_ref[1]

    def lanes(at):
        return slice(at * LANES, (at + 1) * LANES)

    order = send_order(lax.axis_size("outer"), lax.axis_size("inner"))

    groups = chans
    each = chans // groups
    at = range(groups)
    for group in at:
        for kind in range(2):
            for chan in range(each):
                for device in range(devices):
                    came = ((device * 2 + kind) * chans + group * each + chan) * parts
                    to = order[device] * parts
                    signal_ref[group, to : to + parts, lanes(kind * each + chan)] = data_ref[came : came + parts, :]

    def start(group):
        high, low = split(signal_ref[group])
        return dot(first_ref[...], jnp.concatenate([high, low, high], axis=0))

    def spectra(begun):
        turned = []
        for signal in range(2 * each):
            real, imag = begun[:count, lanes(signal)], begun[count:, lanes(signal)]
            turned.append(jnp.concatenate([real * cosine + imag * sine, imag * cosine - real * sine], axis=1))
        high, low = split(jnp.concatenate(turned, axis=0))
        return dot(jnp.concatenate([high, low, high], axis=1), rows_ref[...])

    def back(spectrum):
        mid = each * count
        sig_real, sig_imag = spectrum[:mid, :LANES], spectrum[:mid, LANES:]
        filt_real, filt_imag = spectrum[mid:, :LANES], spectrum[mid:, LANES:]
        real = sig_real * filt_real - sig_imag * filt_imag
        imag = sig_real * filt_imag + sig_imag * filt_real
        high, low = split(jnp.concatenate([real, imag], axis=1))
        return dot(jnp.concatenate([high, low, high], axis=1), back_ref[...])

    def end(backed):
        turned = []
        for chan in range(each):
            real = backed[chan * count : (chan + 1) * count, :LANES]
            imag = backed[chan * count : (chan + 1) * count, LANES:]
            turned.append(jnp.concatenate([real * cosine - imag * sine, imag * cosine + real * sine], axis=0))
        high, low = split(jnp.concatenate(turned, axis=1))
        return dot(last_ref[...], jnp.concatenate([high, low, high], axis=0))

    begun = [start(group) for group in at]
    spectrum = [spectra(begun[group]) for group in at]
    backed = [back(spectrum[group]) for group in at]
    conv = [end(backed[group]) for group in at]
    for group in at:
        for chan in range(each):
            own = group * each + chan
            for device in range(devices):
                to = (device * chans + own) * parts
                came = order[device] * parts
                out_ref[to : to + parts, :] = conv[group][came : came + parts, lanes(chan)]


def gather_kernel(devices, product_ref, taps_ref, out_ref):
    chans, seg = product_ref.shape
    rows = chans // devices * seg // LANES
    product = product_ref[...].reshape(devices, rows, LANES)
    filt = taps_ref[...].reshape(devices, rows, LANES)
    out_ref[...] = jnp.concatenate([product, filt], axis=1).reshape(2 * devices * rows, LANES)


def gate_kernel(gate_ref, skip_ref, conv_ref, out_ref):
    out_ref[...] = gate_ref[...] * (conv_ref[...].reshape(out_ref.shape) + skip_ref[...])


def on_core(kernel, shape, moved, flops=10**6, scratch=()):
    return pl.pallas_call(
        kernel,
        out_shape=jax.ShapeDtypeStruct(shape, jnp.float32),
        scratch_shapes=[pltpu.VMEM(part, jnp.float32) for part in scratch],
        compiler_params=pltpu.CompilerParams(vmem_limit_bytes=32 * 2**20),
        cost_estimate=pl.CostEstimate(flops=flops, bytes_accessed=moved, transcendentals=0),
    )


def by_channels(gate, keys, values, taps, skip_gain):
    devices = lax.axis_size("outer") * lax.axis_size("inner")
    chans, seg = keys.shape
    own = chans // devices
    tiles = seg // LANES
    tables = [jnp.asarray(table) for table in transform_tables(devices, seg)]
    groups = [send_order(lax.axis_size("outer"), lax.axis_size("inner"))]
    regroup = partial(
        lax.all_to_all, axis_name=AXES, split_axis=0, concat_axis=0, tiled=True, axis_index_groups=groups
    )
    product = keys * values
    product, skip = lax.optimization_barrier((product, skip_gain[:, None] * product))
    sent = on_core(partial(gather_kernel, devices), (2 * chans * tiles, LANES), 4 * chans * seg * 4)(product, taps)
    groups = own
    conv = on_core(
        partial(convolve_kernel, devices, own, seg),
        (chans * tiles, LANES),
        2 * 10**6,
        10**9,
        [(groups, devices * tiles, 2 * own // groups * LANES)],
    )(regroup(sent), *tables)
    return on_core(gate_kernel, (chans, seg), 4 * chans * seg * 4)(gate, skip, regroup(conv))


def on_device(gate, keys, values, taps, skip_gain):
    devices = lax.axis_size("outer") * lax.axis_size("inner")
    chans, seg = keys.shape
    if chans % devices == 0 and seg % LANES == 0 and devices % 8 == 0:
        return by_channels(gate, keys, values, taps, skip_gain)
    return by_sections(gate, keys, values, taps, skip_gain)


def solution(mesh):
    placed = (
        P(None, ("outer", "inner")),
        P(None, ("outer", "inner")),
        P(None, ("outer", "inner")),
        P(None, ("outer", "inner")),
        P(),
    )
    return jax.shard_map(
        on_device,
        mesh=mesh,
        in_specs=placed,
        out_specs=P(None, ("outer", "inner")),
        check_vma=False,
    )
```

```python
from functools import partial
import math

import jax
import jax.numpy as jnp
import ml_dtypes
import numpy as np
from jax import lax
from jax.experimental import pallas as pl
from jax.experimental.pallas import tpu as pltpu
from jax.sharding import PartitionSpec as P

LANES = 128
AXES = ("outer", "inner")

TWO_PI = 2.0 * math.pi
HIGHEST = lax.Precision.HIGHEST


def table(count_a, count_b, modulus, sign):
    left = lax.broadcasted_iota(jnp.int32, (count_a, count_b), 0)
    right = lax.broadcasted_iota(jnp.int32, (count_a, count_b), 1)
    phase = TWO_PI / modulus * (left * right % modulus).astype(jnp.float32)
    return (jnp.cos(phase), sign * jnp.sin(phase))


def mix(form, cosine, sine, real, imag):
    contract = partial(jnp.einsum, precision=HIGHEST)
    return (
        contract(form, cosine, real) - contract(form, sine, imag),
        contract(form, sine, real) + contract(form, cosine, imag),
    )


def rotate(real, imag, cosine, sine):
    return (real * cosine - imag * sine, real * sine + imag * cosine)


def forward_rows(real, imag):
    split = 16
    lead = real.shape[:-1]
    size = real.shape[-1]
    short = size // split
    real = real.reshape(lead + (split, short))
    imag = imag.reshape(lead + (split, short))
    cosine, sine = table(split, split, split, -1.0)
    real, imag = mix("ka,...as->...ks", cosine, sine, real, imag)
    cosine, sine = table(split, short, size, -1.0)
    real, imag = rotate(real, imag, cosine, sine)
    cosine, sine = table(short, short, short, -1.0)
    real, imag = mix("sb,...ks->...bk", cosine, sine, real, imag)
    return (real.reshape(lead + (size,)), imag.reshape(lead + (size,)))


def inverse_rows(real, imag):
    split = 16
    lead = real.shape[:-1]
    size = real.shape[-1]
    short = size // split
    real = real.reshape(lead + (short, split))
    imag = imag.reshape(lead + (short, split))
    cosine, sine = table(short, short, short, 1.0)
    real, imag = mix("sb,...bk->...sk", cosine, sine, real, imag)
    cosine, sine = table(short, split, size, 1.0)
    real, imag = rotate(real, imag, cosine, sine)
    cosine, sine = table(split, split, split, 1.0)
    real, imag = mix("ak,...sk->...as", cosine, sine, real, imag)
    return (real.reshape(lead + (size,)), imag.reshape(lead + (size,)))


def by_sections(gate, keys, values, taps, skip_gain):
    inner_count = lax.axis_size("inner")
    devices = lax.axis_size("outer") * inner_count
    rank = lax.axis_index("outer") * inner_count + lax.axis_index("inner")
    chans, seg = keys.shape
    both = 2 * chans
    cols = seg // devices
    blocks = 2 * devices
    full = blocks * seg
    contract = partial(jnp.einsum, precision=HIGHEST)
    product = keys * values
    source = jnp.concatenate([product, taps], axis=0)
    sectioned = lax.all_to_all(
        lax.all_to_all(
            source.reshape(both, 1, 1, seg), "outer", split_axis=3, concat_axis=1, tiled=True
        ),
        "inner",
        split_axis=3,
        concat_axis=2,
        tiled=True,
    )
    sectioned = sectioned.reshape(both, devices, cols)
    cosine, sine = table(blocks, devices, blocks, -1.0)
    real = contract("km,cmj->ckj", cosine, sectioned)
    imag = contract("km,cmj->ckj", sine, sectioned)
    offset = rank * cols + lax.broadcasted_iota(jnp.int32, (blocks, cols), 1)
    residue = lax.broadcasted_iota(jnp.int32, (blocks, cols), 0)
    phase = TWO_PI / full * (offset * residue).astype(jnp.float32)
    real, imag = rotate(real, imag, jnp.cos(phase)[None], -jnp.sin(phase)[None])
    outgoing = jnp.stack([real, imag]).reshape(2, both, blocks, 1, 1, cols)
    moved = lax.all_to_all(
        lax.all_to_all(outgoing, "outer", split_axis=2, concat_axis=3, tiled=True),
        "inner",
        split_axis=2,
        concat_axis=4,
        tiled=True,
    )
    moved = moved.reshape(2, both, 2, seg)
    spec_real, spec_imag = forward_rows(moved[0], moved[1])
    sig_real, filt_real = (spec_real[:chans], spec_real[chans:])
    sig_imag, filt_imag = (spec_imag[:chans], spec_imag[chans:])
    real = sig_real * filt_real - sig_imag * filt_imag
    imag = sig_real * filt_imag + sig_imag * filt_real
    real, imag = inverse_rows(real, imag)
    residue = 2 * rank + lax.broadcasted_iota(jnp.int32, (2, seg), 0)
    offset = lax.broadcasted_iota(jnp.int32, (2, seg), 1)
    phase = TWO_PI / full * (offset * residue).astype(jnp.float32)
    real, imag = rotate(real, imag, jnp.cos(phase)[None], jnp.sin(phase)[None])
    returning = jnp.stack([real, imag]).reshape(2, chans, 1, 1, 2, seg)
    gathered = lax.all_to_all(
        lax.all_to_all(returning, "outer", split_axis=5, concat_axis=2, tiled=True),
        "inner",
        split_axis=5,
        concat_axis=3,
        tiled=True,
    )
    gathered = gathered.reshape(2, chans, blocks, cols)
    cosine, sine = table(devices, blocks, blocks, 1.0)
    conv = contract("mk,ckj->cmj", cosine, gathered[0]) - contract("mk,ckj->cmj", sine, gathered[1])
    conv = conv * (1.0 / full)
    conv = lax.all_to_all(
        lax.all_to_all(
            conv.reshape(chans, devices, 1, 1, cols),
            "outer",
            split_axis=1,
            concat_axis=2,
            tiled=True,
        ),
        "inner",
        split_axis=1,
        concat_axis=3,
        tiled=True,
    )
    conv = conv.reshape(chans, seg)
    return gate * (conv + skip_gain[:, None] * product)


def halves(array):
    high = array.astype(ml_dtypes.bfloat16)
    low = (array - high.astype(np.float64)).astype(ml_dtypes.bfloat16)
    return high, low


def transform_tables(devices, seg):
    length = devices * seg
    count = length // LANES
    odd = 2 * np.arange(count) + 1
    angle = 2 * np.pi / (4 * count) * ((odd[:, None] * np.arange(count)[None, :]) % (4 * count))
    first = np.concatenate([np.cos(angle), -np.sin(angle)], axis=0)
    last = np.concatenate([np.cos(angle).T, -np.sin(angle).T], axis=1) / length
    angle = 2 * np.pi / (4 * length) * ((odd[:, None] * np.arange(LANES)[None, :]) % (4 * length))
    twiddle = np.stack([np.cos(angle), np.sin(angle)]).astype(np.float32)
    angle = 2 * np.pi / LANES * ((np.arange(LANES)[:, None] * np.arange(LANES)[None, :]) % LANES)
    cosine, sine = np.cos(angle), np.sin(angle)
    rows = np.block([[cosine, -sine], [sine, cosine]])
    back = np.block([[cosine, sine], [-sine, cosine]])
    first_high, first_low = halves(first)
    rows_high, rows_low = halves(rows)
    back_high, back_low = halves(back)
    last_high, last_low = halves(last)
    return (
        np.concatenate([first_high, first_high, first_low], axis=1),
        np.concatenate([rows_high, rows_high, rows_low], axis=0),
        np.concatenate([back_high, back_high, back_low], axis=0),
        np.concatenate([last_high, last_high, last_low], axis=1),
        twiddle,
    )


def split(array):
    high = array.astype(jnp.bfloat16)
    return high, (array - high.astype(jnp.float32)).astype(jnp.bfloat16)


def dot(left, right):
    return jnp.dot(left, right, preferred_element_type=jnp.float32)


def convolve_kernel(
    devices, chans, seg, data_ref, first_ref, rows_ref, back_ref, last_ref, twiddle_ref, out_ref, signal_ref
):
    parts = seg // LANES
    count = devices * parts
    cosine, sine = twiddle_ref[0], twiddle_ref[1]

    def lanes(at):
        return slice(at * LANES, (at + 1) * LANES)

    groups = chans
    each = chans // groups

    def start(group):
        for kind in range(2):
            for chan in range(each):
                for device in range(devices):
                    came = ((device * 2 + kind) * chans + group * each + chan) * parts
                    signal_ref[group, device * parts : (device + 1) * parts, lanes(kind * each + chan)] = data_ref[
                        came : came + parts, :
                    ]
        high, low = split(signal_ref[group])
        return dot(first_ref[...], jnp.concatenate([high, low, high], axis=0))

    def spectra(begun):
        turned = []
        for signal in range(2 * each):
            real, imag = begun[:count, lanes(signal)], begun[count:, lanes(signal)]
            turned.append(jnp.concatenate([real * cosine + imag * sine, imag * cosine - real * sine], axis=1))
        high, low = split(jnp.concatenate(turned, axis=0))
        return dot(jnp.concatenate([high, low, high], axis=1), rows_ref[...])

    def back(spectrum):
        mid = each * count
        sig_real, sig_imag = spectrum[:mid, :LANES], spectrum[:mid, LANES:]
        filt_real, filt_imag = spectrum[mid:, :LANES], spectrum[mid:, LANES:]
        real = sig_real * filt_real - sig_imag * filt_imag
        imag = sig_real * filt_imag + sig_imag * filt_real
        high, low = split(jnp.concatenate([real, imag], axis=1))
        return dot(jnp.concatenate([high, low, high], axis=1), back_ref[...])

    def end(backed):
        turned = []
        for chan in range(each):
            real = backed[chan * count : (chan + 1) * count, :LANES]
            imag = backed[chan * count : (chan + 1) * count, LANES:]
            turned.append(jnp.concatenate([real * cosine - imag * sine, imag * cosine + real * sine], axis=0))
        high, low = split(jnp.concatenate(turned, axis=1))
        return dot(last_ref[...], jnp.concatenate([high, low, high], axis=0))

    def store(group, conv):
        for chan in range(each):
            for device in range(devices):
                to = (device * chans + group * each + chan) * parts
                out_ref[to : to + parts, :] = conv[device * parts : (device + 1) * parts, lanes(chan)]

    held = {}
    for step in range(groups + 3):
        if step < groups:
            held[step] = start(step)
        if 0 <= step - 1 < groups:
            held[step - 1] = spectra(held[step - 1])
        if 0 <= step - 2 < groups:
            held[step - 2] = back(held[step - 2])
        if 0 <= step - 3 < groups:
            store(step - 3, end(held.pop(step - 3)))


def gather_kernel(devices, product_ref, taps_ref, out_ref):
    chans, seg = product_ref.shape
    rows = chans // devices * seg // LANES
    product = product_ref[...].reshape(devices, rows, LANES)
    filt = taps_ref[...].reshape(devices, rows, LANES)
    out_ref[...] = jnp.concatenate([product, filt], axis=1).reshape(2 * devices * rows, LANES)


def gate_kernel(gate_ref, skip_ref, conv_ref, out_ref):
    out_ref[...] = gate_ref[...] * (conv_ref[...].reshape(out_ref.shape) + skip_ref[...])


def on_core(kernel, shape, moved, flops=10**6, scratch=()):
    return pl.pallas_call(
        kernel,
        out_shape=jax.ShapeDtypeStruct(shape, jnp.float32),
        scratch_shapes=[pltpu.VMEM(part, jnp.float32) for part in scratch],
        compiler_params=pltpu.CompilerParams(vmem_limit_bytes=32 * 2**20),
        cost_estimate=pl.CostEstimate(flops=flops, bytes_accessed=moved, transcendentals=0),
    )


def by_channels(gate, keys, values, taps, skip_gain):
    devices = lax.axis_size("outer") * lax.axis_size("inner")
    chans, seg = keys.shape
    own = chans // devices
    tiles = seg // LANES
    tables = [jnp.asarray(table) for table in transform_tables(devices, seg)]
    regroup = partial(lax.all_to_all, axis_name=AXES, split_axis=0, concat_axis=0, tiled=True)
    product = keys * values
    product, skip = lax.optimization_barrier((product, skip_gain[:, None] * product))
    sent = on_core(partial(gather_kernel, devices), (2 * chans * tiles, LANES), 4 * chans * seg * 4)(product, taps)
    groups = own
    conv = on_core(
        partial(convolve_kernel, devices, own, seg),
        (chans * tiles, LANES),
        2 * 10**6,
        10**9,
        [(groups, devices * tiles, 2 * own // groups * LANES)],
    )(regroup(sent), *tables)
    return on_core(gate_kernel, (chans, seg), 4 * chans * seg * 4)(gate, skip, regroup(conv))


def on_device(gate, keys, values, taps, skip_gain):
    devices = lax.axis_size("outer") * lax.axis_size("inner")
    chans, seg = keys.shape
    if chans % devices == 0 and seg % LANES == 0 and devices % 8 == 0:
        return by_channels(gate, keys, values, taps, skip_gain)
    return by_sections(gate, keys, values, taps, skip_gain)


def solution(mesh):
    placed = (
        P(None, ("outer", "inner")),
        P(None, ("outer", "inner")),
        P(None, ("outer", "inner")),
        P(None, ("outer", "inner")),
        P(),
    )
    return jax.shard_map(
        on_device,
        mesh=mesh,
        in_specs=placed,
        out_specs=P(None, ("outer", "inner")),
        check_vma=False,
    )
```

```python
from functools import partial
import math

import jax
import jax.numpy as jnp
import ml_dtypes
import numpy as np
from jax import lax
from jax.experimental import pallas as pl
from jax.experimental.pallas import tpu as pltpu
from jax.sharding import PartitionSpec as P

LANES = 128
AXES = ("outer", "inner")

TWO_PI = 2.0 * math.pi
HIGHEST = lax.Precision.HIGHEST


def table(count_a, count_b, modulus, sign):
    left = lax.broadcasted_iota(jnp.int32, (count_a, count_b), 0)
    right = lax.broadcasted_iota(jnp.int32, (count_a, count_b), 1)
    phase = TWO_PI / modulus * (left * right % modulus).astype(jnp.float32)
    return (jnp.cos(phase), sign * jnp.sin(phase))


def mix(form, cosine, sine, real, imag):
    contract = partial(jnp.einsum, precision=HIGHEST)
    return (
        contract(form, cosine, real) - contract(form, sine, imag),
        contract(form, sine, real) + contract(form, cosine, imag),
    )


def rotate(real, imag, cosine, sine):
    return (real * cosine - imag * sine, real * sine + imag * cosine)


def forward_rows(real, imag):
    split = 16
    lead = real.shape[:-1]
    size = real.shape[-1]
    short = size // split
    real = real.reshape(lead + (split, short))
    imag = imag.reshape(lead + (split, short))
    cosine, sine = table(split, split, split, -1.0)
    real, imag = mix("ka,...as->...ks", cosine, sine, real, imag)
    cosine, sine = table(split, short, size, -1.0)
    real, imag = rotate(real, imag, cosine, sine)
    cosine, sine = table(short, short, short, -1.0)
    real, imag = mix("sb,...ks->...bk", cosine, sine, real, imag)
    return (real.reshape(lead + (size,)), imag.reshape(lead + (size,)))


def inverse_rows(real, imag):
    split = 16
    lead = real.shape[:-1]
    size = real.shape[-1]
    short = size // split
    real = real.reshape(lead + (short, split))
    imag = imag.reshape(lead + (short, split))
    cosine, sine = table(short, short, short, 1.0)
    real, imag = mix("sb,...bk->...sk", cosine, sine, real, imag)
    cosine, sine = table(short, split, size, 1.0)
    real, imag = rotate(real, imag, cosine, sine)
    cosine, sine = table(split, split, split, 1.0)
    real, imag = mix("ak,...sk->...as", cosine, sine, real, imag)
    return (real.reshape(lead + (size,)), imag.reshape(lead + (size,)))


def by_sections(gate, keys, values, taps, skip_gain):
    inner_count = lax.axis_size("inner")
    devices = lax.axis_size("outer") * inner_count
    rank = lax.axis_index("outer") * inner_count + lax.axis_index("inner")
    chans, seg = keys.shape
    both = 2 * chans
    cols = seg // devices
    blocks = 2 * devices
    full = blocks * seg
    contract = partial(jnp.einsum, precision=HIGHEST)
    product = keys * values
    source = jnp.concatenate([product, taps], axis=0)
    sectioned = lax.all_to_all(
        lax.all_to_all(
            source.reshape(both, 1, 1, seg), "outer", split_axis=3, concat_axis=1, tiled=True
        ),
        "inner",
        split_axis=3,
        concat_axis=2,
        tiled=True,
    )
    sectioned = sectioned.reshape(both, devices, cols)
    cosine, sine = table(blocks, devices, blocks, -1.0)
    real = contract("km,cmj->ckj", cosine, sectioned)
    imag = contract("km,cmj->ckj", sine, sectioned)
    offset = rank * cols + lax.broadcasted_iota(jnp.int32, (blocks, cols), 1)
    residue = lax.broadcasted_iota(jnp.int32, (blocks, cols), 0)
    phase = TWO_PI / full * (offset * residue).astype(jnp.float32)
    real, imag = rotate(real, imag, jnp.cos(phase)[None], -jnp.sin(phase)[None])
    outgoing = jnp.stack([real, imag]).reshape(2, both, blocks, 1, 1, cols)
    moved = lax.all_to_all(
        lax.all_to_all(outgoing, "outer", split_axis=2, concat_axis=3, tiled=True),
        "inner",
        split_axis=2,
        concat_axis=4,
        tiled=True,
    )
    moved = moved.reshape(2, both, 2, seg)
    spec_real, spec_imag = forward_rows(moved[0], moved[1])
    sig_real, filt_real = (spec_real[:chans], spec_real[chans:])
    sig_imag, filt_imag = (spec_imag[:chans], spec_imag[chans:])
    real = sig_real * filt_real - sig_imag * filt_imag
    imag = sig_real * filt_imag + sig_imag * filt_real
    real, imag = inverse_rows(real, imag)
    residue = 2 * rank + lax.broadcasted_iota(jnp.int32, (2, seg), 0)
    offset = lax.broadcasted_iota(jnp.int32, (2, seg), 1)
    phase = TWO_PI / full * (offset * residue).astype(jnp.float32)
    real, imag = rotate(real, imag, jnp.cos(phase)[None], jnp.sin(phase)[None])
    returning = jnp.stack([real, imag]).reshape(2, chans, 1, 1, 2, seg)
    gathered = lax.all_to_all(
        lax.all_to_all(returning, "outer", split_axis=5, concat_axis=2, tiled=True),
        "inner",
        split_axis=5,
        concat_axis=3,
        tiled=True,
    )
    gathered = gathered.reshape(2, chans, blocks, cols)
    cosine, sine = table(devices, blocks, blocks, 1.0)
    conv = contract("mk,ckj->cmj", cosine, gathered[0]) - contract("mk,ckj->cmj", sine, gathered[1])
    conv = conv * (1.0 / full)
    conv = lax.all_to_all(
        lax.all_to_all(
            conv.reshape(chans, devices, 1, 1, cols),
            "outer",
            split_axis=1,
            concat_axis=2,
            tiled=True,
        ),
        "inner",
        split_axis=1,
        concat_axis=3,
        tiled=True,
    )
    conv = conv.reshape(chans, seg)
    return gate * (conv + skip_gain[:, None] * product)


def halves(array):
    high = array.astype(ml_dtypes.bfloat16)
    low = (array - high.astype(np.float64)).astype(ml_dtypes.bfloat16)
    return high, low


def transform_tables(devices, seg):
    length = devices * seg
    count = length // LANES
    odd = 2 * np.arange(count) + 1
    angle = 2 * np.pi / (4 * count) * ((odd[:, None] * np.arange(count)[None, :]) % (4 * count))
    first = np.concatenate([np.cos(angle), -np.sin(angle)], axis=0)
    last = np.concatenate([np.cos(angle).T, -np.sin(angle).T], axis=1) / length
    angle = 2 * np.pi / (4 * length) * ((odd[:, None] * np.arange(LANES)[None, :]) % (4 * length))
    twiddle = np.stack([np.cos(angle), np.sin(angle)]).astype(np.float32)
    angle = 2 * np.pi / LANES * ((np.arange(LANES)[:, None] * np.arange(LANES)[None, :]) % LANES)
    cosine, sine = np.cos(angle), np.sin(angle)
    rows = np.block([[cosine, -sine], [sine, cosine]])
    back = np.block([[cosine, sine], [-sine, cosine]])
    first_high, first_low = halves(first)
    rows_high, rows_low = halves(rows)
    back_high, back_low = halves(back)
    last_high, last_low = halves(last)
    return (
        np.concatenate([first_high, first_high, first_low], axis=1),
        np.concatenate([rows_high, rows_high, rows_low], axis=0),
        np.concatenate([back_high, back_high, back_low], axis=0),
        np.concatenate([last_high, last_high, last_low], axis=1),
        twiddle,
    )


def send_order(outer, inner):
    first = outer * 3 // 4 * inner + inner // 2
    return [(first + at) % (outer * inner) for at in range(outer * inner)]


def split(array):
    high = array.astype(jnp.bfloat16)
    return high, (array - high.astype(jnp.float32)).astype(jnp.bfloat16)


def dot(left, right):
    return jnp.dot(left, right, preferred_element_type=jnp.float32)


def convolve_kernel(
    devices, chans, seg, data_ref, first_ref, rows_ref, back_ref, last_ref, twiddle_ref, out_ref, signal_ref
):
    parts = seg // LANES
    count = devices * parts
    cosine, sine = twiddle_ref[0], twiddle_ref[1]

    def lanes(at):
        return slice(at * LANES, (at + 1) * LANES)

    order = send_order(lax.axis_size("outer"), lax.axis_size("inner"))

    groups = chans
    each = chans // groups
    at = range(groups)
    for group in at:
        for kind in range(2):
            for chan in range(each):
                for device in range(devices):
                    came = ((device * 2 + kind) * chans + group * each + chan) * parts
                    to = order[device] * parts
                    signal_ref[group, to : to + parts, lanes(kind * each + chan)] = data_ref[came : came + parts, :]

    def start(group):
        high, low = split(signal_ref[group])
        return dot(first_ref[...], jnp.concatenate([high, low, high], axis=0))

    def spectra(begun):
        turned = []
        for signal in range(2 * each):
            real, imag = begun[:count, lanes(signal)], begun[count:, lanes(signal)]
            turned.append(jnp.concatenate([real * cosine + imag * sine, imag * cosine - real * sine], axis=1))
        high, low = split(jnp.concatenate(turned, axis=0))
        return dot(jnp.concatenate([high, low, high], axis=1), rows_ref[...])

    def back(spectrum):
        mid = each * count
        sig_real, sig_imag = spectrum[:mid, :LANES], spectrum[:mid, LANES:]
        filt_real, filt_imag = spectrum[mid:, :LANES], spectrum[mid:, LANES:]
        real = sig_real * filt_real - sig_imag * filt_imag
        imag = sig_real * filt_imag + sig_imag * filt_real
        high, low = split(jnp.concatenate([real, imag], axis=1))
        return dot(jnp.concatenate([high, low, high], axis=1), back_ref[...])

    def end(backed):
        turned = []
        for chan in range(each):
            real = backed[chan * count : (chan + 1) * count, :LANES]
            imag = backed[chan * count : (chan + 1) * count, LANES:]
            turned.append(jnp.concatenate([real * cosine - imag * sine, imag * cosine + real * sine], axis=0))
        high, low = split(jnp.concatenate(turned, axis=1))
        return dot(last_ref[...], jnp.concatenate([high, low, high], axis=0))

    begun = [start(group) for group in at]
    spectrum = [spectra(begun[group]) for group in at]
    backed = [back(spectrum[group]) for group in at]
    conv = [end(backed[group]) for group in at]
    for group in at:
        for chan in range(each):
            own = group * each + chan
            for device in range(devices):
                to = (device * chans + own) * parts
                came = order[device] * parts
                out_ref[to : to + parts, :] = conv[group][came : came + parts, lanes(chan)]


def gather_kernel(devices, product_ref, taps_ref, out_ref):
    chans, seg = product_ref.shape
    rows = chans // devices * seg // LANES
    product = product_ref[...].reshape(devices, rows, LANES)
    filt = taps_ref[...].reshape(devices, rows, LANES)
    out_ref[...] = jnp.concatenate([product, filt], axis=1).reshape(2 * devices * rows, LANES)


def gate_kernel(gate_ref, skip_ref, conv_ref, out_ref):
    out_ref[...] = gate_ref[...] * (conv_ref[...].reshape(out_ref.shape) + skip_ref[...])


def on_core(kernel, shape, moved, flops=10**6, scratch=()):
    return pl.pallas_call(
        kernel,
        out_shape=jax.ShapeDtypeStruct(shape, jnp.float32),
        scratch_shapes=[pltpu.VMEM(part, jnp.float32) for part in scratch],
        compiler_params=pltpu.CompilerParams(vmem_limit_bytes=32 * 2**20),
        cost_estimate=pl.CostEstimate(flops=flops, bytes_accessed=moved, transcendentals=0),
    )


def by_channels(gate, keys, values, taps, skip_gain):
    devices = lax.axis_size("outer") * lax.axis_size("inner")
    chans, seg = keys.shape
    own = chans // devices
    tiles = seg // LANES
    tables = [jnp.asarray(table) for table in transform_tables(devices, seg)]
    groups = [send_order(lax.axis_size("outer"), lax.axis_size("inner"))]
    regroup = partial(
        lax.all_to_all, axis_name=AXES, split_axis=0, concat_axis=0, tiled=True, axis_index_groups=groups
    )
    product = keys * values
    product, skip = lax.optimization_barrier((product, skip_gain[:, None] * product))
    sent = on_core(partial(gather_kernel, devices), (2 * chans * tiles, LANES), 4 * chans * seg * 4)(product, taps)
    groups = own
    conv = on_core(
        partial(convolve_kernel, devices, own, seg),
        (chans * tiles, LANES),
        2 * 10**6,
        10**9,
        [(groups, devices * tiles, 2 * own // groups * LANES)],
    )(regroup(sent), *tables)
    return on_core(gate_kernel, (chans, seg), 4 * chans * seg * 4)(gate, skip, regroup(conv))


def on_device(gate, keys, values, taps, skip_gain):
    devices = lax.axis_size("outer") * lax.axis_size("inner")
    chans, seg = keys.shape
    if chans % devices == 0 and seg % LANES == 0 and devices % 8 == 0:
        return by_channels(gate, keys, values, taps, skip_gain)
    return by_sections(gate, keys, values, taps, skip_gain)


def solution(mesh):
    placed = (
        P(None, ("outer", "inner")),
        P(None, ("outer", "inner")),
        P(None, ("outer", "inner")),
        P(None, ("outer", "inner")),
        P(),
    )
    return jax.shard_map(
        on_device,
        mesh=mesh,
        in_specs=placed,
        out_specs=P(None, ("outer", "inner")),
        check_vma=False,
    )
```

```python
from functools import partial
import math

import jax
import jax.numpy as jnp
import ml_dtypes
import numpy as np
from jax import lax
from jax.experimental import pallas as pl
from jax.experimental.pallas import tpu as pltpu
from jax.sharding import PartitionSpec as P

LANES = 128
AXES = ("outer", "inner")

TWO_PI = 2.0 * math.pi
HIGHEST = lax.Precision.HIGHEST


def table(count_a, count_b, modulus, sign):
    left = lax.broadcasted_iota(jnp.int32, (count_a, count_b), 0)
    right = lax.broadcasted_iota(jnp.int32, (count_a, count_b), 1)
    phase = TWO_PI / modulus * (left * right % modulus).astype(jnp.float32)
    return (jnp.cos(phase), sign * jnp.sin(phase))


def mix(form, cosine, sine, real, imag):
    contract = partial(jnp.einsum, precision=HIGHEST)
    return (
        contract(form, cosine, real) - contract(form, sine, imag),
        contract(form, sine, real) + contract(form, cosine, imag),
    )


def rotate(real, imag, cosine, sine):
    return (real * cosine - imag * sine, real * sine + imag * cosine)


def forward_rows(real, imag):
    split = 16
    lead = real.shape[:-1]
    size = real.shape[-1]
    short = size // split
    real = real.reshape(lead + (split, short))
    imag = imag.reshape(lead + (split, short))
    cosine, sine = table(split, split, split, -1.0)
    real, imag = mix("ka,...as->...ks", cosine, sine, real, imag)
    cosine, sine = table(split, short, size, -1.0)
    real, imag = rotate(real, imag, cosine, sine)
    cosine, sine = table(short, short, short, -1.0)
    real, imag = mix("sb,...ks->...bk", cosine, sine, real, imag)
    return (real.reshape(lead + (size,)), imag.reshape(lead + (size,)))


def inverse_rows(real, imag):
    split = 16
    lead = real.shape[:-1]
    size = real.shape[-1]
    short = size // split
    real = real.reshape(lead + (short, split))
    imag = imag.reshape(lead + (short, split))
    cosine, sine = table(short, short, short, 1.0)
    real, imag = mix("sb,...bk->...sk", cosine, sine, real, imag)
    cosine, sine = table(short, split, size, 1.0)
    real, imag = rotate(real, imag, cosine, sine)
    cosine, sine = table(split, split, split, 1.0)
    real, imag = mix("ak,...sk->...as", cosine, sine, real, imag)
    return (real.reshape(lead + (size,)), imag.reshape(lead + (size,)))


def by_sections(gate, keys, values, taps, skip_gain):
    inner_count = lax.axis_size("inner")
    devices = lax.axis_size("outer") * inner_count
    rank = lax.axis_index("outer") * inner_count + lax.axis_index("inner")
    chans, seg = keys.shape
    both = 2 * chans
    cols = seg // devices
    blocks = 2 * devices
    full = blocks * seg
    contract = partial(jnp.einsum, precision=HIGHEST)
    product = keys * values
    source = jnp.concatenate([product, taps], axis=0)
    sectioned = lax.all_to_all(
        lax.all_to_all(
            source.reshape(both, 1, 1, seg), "outer", split_axis=3, concat_axis=1, tiled=True
        ),
        "inner",
        split_axis=3,
        concat_axis=2,
        tiled=True,
    )
    sectioned = sectioned.reshape(both, devices, cols)
    cosine, sine = table(blocks, devices, blocks, -1.0)
    real = contract("km,cmj->ckj", cosine, sectioned)
    imag = contract("km,cmj->ckj", sine, sectioned)
    offset = rank * cols + lax.broadcasted_iota(jnp.int32, (blocks, cols), 1)
    residue = lax.broadcasted_iota(jnp.int32, (blocks, cols), 0)
    phase = TWO_PI / full * (offset * residue).astype(jnp.float32)
    real, imag = rotate(real, imag, jnp.cos(phase)[None], -jnp.sin(phase)[None])
    outgoing = jnp.stack([real, imag]).reshape(2, both, blocks, 1, 1, cols)
    moved = lax.all_to_all(
        lax.all_to_all(outgoing, "outer", split_axis=2, concat_axis=3, tiled=True),
        "inner",
        split_axis=2,
        concat_axis=4,
        tiled=True,
    )
    moved = moved.reshape(2, both, 2, seg)
    spec_real, spec_imag = forward_rows(moved[0], moved[1])
    sig_real, filt_real = (spec_real[:chans], spec_real[chans:])
    sig_imag, filt_imag = (spec_imag[:chans], spec_imag[chans:])
    real = sig_real * filt_real - sig_imag * filt_imag
    imag = sig_real * filt_imag + sig_imag * filt_real
    real, imag = inverse_rows(real, imag)
    residue = 2 * rank + lax.broadcasted_iota(jnp.int32, (2, seg), 0)
    offset = lax.broadcasted_iota(jnp.int32, (2, seg), 1)
    phase = TWO_PI / full * (offset * residue).astype(jnp.float32)
    real, imag = rotate(real, imag, jnp.cos(phase)[None], jnp.sin(phase)[None])
    returning = jnp.stack([real, imag]).reshape(2, chans, 1, 1, 2, seg)
    gathered = lax.all_to_all(
        lax.all_to_all(returning, "outer", split_axis=5, concat_axis=2, tiled=True),
        "inner",
        split_axis=5,
        concat_axis=3,
        tiled=True,
    )
    gathered = gathered.reshape(2, chans, blocks, cols)
    cosine, sine = table(devices, blocks, blocks, 1.0)
    conv = contract("mk,ckj->cmj", cosine, gathered[0]) - contract("mk,ckj->cmj", sine, gathered[1])
    conv = conv * (1.0 / full)
    conv = lax.all_to_all(
        lax.all_to_all(
            conv.reshape(chans, devices, 1, 1, cols),
            "outer",
            split_axis=1,
            concat_axis=2,
            tiled=True,
        ),
        "inner",
        split_axis=1,
        concat_axis=3,
        tiled=True,
    )
    conv = conv.reshape(chans, seg)
    return gate * (conv + skip_gain[:, None] * product)


def halves(array):
    high = array.astype(ml_dtypes.bfloat16)
    low = (array - high.astype(np.float64)).astype(ml_dtypes.bfloat16)
    return high, low


def transform_tables(devices, seg):
    length = devices * seg
    count = length // LANES
    odd = 2 * np.arange(count) + 1
    angle = 2 * np.pi / (4 * count) * ((odd[:, None] * np.arange(count)[None, :]) % (4 * count))
    first = np.concatenate([np.cos(angle), -np.sin(angle)], axis=0)
    last = np.concatenate([np.cos(angle).T, -np.sin(angle).T], axis=1) / length
    angle = 2 * np.pi / (4 * length) * ((odd[:, None] * np.arange(LANES)[None, :]) % (4 * length))
    twiddle = np.stack([np.cos(angle), np.sin(angle)]).astype(np.float32)
    angle = 2 * np.pi / LANES * ((np.arange(LANES)[:, None] * np.arange(LANES)[None, :]) % LANES)
    cosine, sine = np.cos(angle), np.sin(angle)
    rows = np.block([[cosine, -sine], [sine, cosine]])
    back = np.block([[cosine, sine], [-sine, cosine]])
    first_high, first_low = halves(first)
    rows_high, rows_low = halves(rows)
    back_high, back_low = halves(back)
    last_high, last_low = halves(last)
    return (
        np.concatenate([first_high, first_high, first_low], axis=1),
        np.concatenate([rows_high, rows_high, rows_low], axis=0),
        np.concatenate([back_high, back_high, back_low], axis=0),
        np.concatenate([last_high, last_high, last_low], axis=1),
        twiddle,
    )


def split(array):
    high = array.astype(jnp.bfloat16)
    return high, (array - high.astype(jnp.float32)).astype(jnp.bfloat16)


def dot(left, right):
    return jnp.dot(left, right, preferred_element_type=jnp.float32)


def partner(outer_turn, inner_turn):
    outer = lax.axis_index("outer") ^ outer_turn
    return outer * lax.axis_size("inner") + (lax.axis_index("inner") ^ inner_turn)


def block(ref, at, rows):
    return ref.at[pl.ds(pl.multiple_of(at * rows, rows), rows), :]


def convolve_kernel(outers, inners, chans, seg, *refs):
    first_ref, rows_ref, back_ref, last_ref, twiddle_ref = refs[:5]
    by_inner, by_outer = refs[5 : 5 + inners], refs[5 + inners : 5 + inners + outers]
    out_ref, data_ref, signal_ref = refs[5 + inners + outers :]
    parts = seg // LANES
    devices = outers * inners
    count = devices * parts
    cosine, sine = twiddle_ref[0], twiddle_ref[1]

    def lanes(at):
        return slice(at * LANES, (at + 1) * LANES)

    unit = chans * parts
    for outer in range(outers):
        for inner in range(inners):
            source = partner(outer, inner)
            block(data_ref.at[0], source, unit)[...] = by_inner[inner][outer * unit : (outer + 1) * unit, :]
            block(data_ref.at[1], source, unit)[...] = by_outer[outer][inner * unit : (inner + 1) * unit, :]

    groups = chans
    each = chans // groups
    at = range(groups)
    for group in at:
        for kind in range(2):
            for chan in range(each):
                own = group * each + chan
                half, row = own // (chans // 2), own % (chans // 2)
                for device in range(devices):
                    came = ((device * 2 + kind) * (chans // 2) + row) * parts
                    signal_ref[group, device * parts : (device + 1) * parts, lanes(kind * each + chan)] = data_ref[
                        half, came : came + parts, :
                    ]

    def start(group):
        high, low = split(signal_ref[group])
        return dot(first_ref[...], jnp.concatenate([high, low, high], axis=0))

    def spectra(begun):
        turned = []
        for signal in range(2 * each):
            real, imag = begun[:count, lanes(signal)], begun[count:, lanes(signal)]
            turned.append(jnp.concatenate([real * cosine + imag * sine, imag * cosine - real * sine], axis=1))
        high, low = split(jnp.concatenate(turned, axis=0))
        return dot(jnp.concatenate([high, low, high], axis=1), rows_ref[...])

    def back(spectrum):
        mid = each * count
        sig_real, sig_imag = spectrum[:mid, :LANES], spectrum[:mid, LANES:]
        filt_real, filt_imag = spectrum[mid:, :LANES], spectrum[mid:, LANES:]
        real = sig_real * filt_real - sig_imag * filt_imag
        imag = sig_real * filt_imag + sig_imag * filt_real
        high, low = split(jnp.concatenate([real, imag], axis=1))
        return dot(jnp.concatenate([high, low, high], axis=1), back_ref[...])

    def end(backed):
        turned = []
        for chan in range(each):
            real = backed[chan * count : (chan + 1) * count, :LANES]
            imag = backed[chan * count : (chan + 1) * count, LANES:]
            turned.append(jnp.concatenate([real * cosine - imag * sine, imag * cosine + real * sine], axis=0))
        high, low = split(jnp.concatenate(turned, axis=1))
        return dot(last_ref[...], jnp.concatenate([high, low, high], axis=0))

    begun = [start(group) for group in at]
    spectrum = [spectra(begun[group]) for group in at]
    backed = [back(spectrum[group]) for group in at]
    conv = [end(backed[group]) for group in at]
    for group in at:
        for chan in range(each):
            own = group * each + chan
            for device in range(devices):
                to = (device * chans + own) * parts
                out_ref[to : to + parts, :] = conv[group][device * parts : (device + 1) * parts, lanes(chan)]


def gather_kernel(outers, inners, product_ref, taps_ref, *refs):
    by_inner, by_outer = refs[:inners], refs[inners : inners + outers]
    rows_refs = refs[inners + outers :]
    chans, seg = product_ref.shape
    for kind, ref in enumerate((product_ref, taps_ref)):
        rows_refs[kind][...] = ref[...].reshape(rows_refs[kind].shape)
    half = chans // (outers * inners) * seg // LANES // 2
    for outer in range(outers):
        for inner in range(inners):
            owner = partner(outer, inner)
            for kind in range(2):
                to = (inner * 2 + kind) * half
                by_outer[outer][to : to + half, :] = block(rows_refs[kind], 2 * owner, half)[...]
                to = (outer * 2 + kind) * half
                by_inner[inner][to : to + half, :] = block(rows_refs[kind], 2 * owner + 1, half)[...]


def turn_kernel(count, *refs):
    ins, outs = refs[:count], refs[count:]
    unit = ins[0].shape[0] // len(outs)
    for a, in_ref in enumerate(ins):
        for b, out_ref in enumerate(outs):
            out_ref[a * unit : (a + 1) * unit, :] = in_ref[b * unit : (b + 1) * unit, :]


def gate_kernel(gate_ref, skip_ref, conv_ref, out_ref):
    out_ref[...] = gate_ref[...] * (conv_ref[...].reshape(out_ref.shape) + skip_ref[...])


def on_core(kernel, shapes, moved, flops=10**6, scratch=()):
    return pl.pallas_call(
        kernel,
        out_shape=[jax.ShapeDtypeStruct(shape, jnp.float32) for shape in shapes],
        scratch_shapes=[pltpu.VMEM(shape, jnp.float32) for shape in scratch],
        compiler_params=pltpu.CompilerParams(vmem_limit_bytes=32 * 2**20),
        cost_estimate=pl.CostEstimate(flops=flops, bytes_accessed=moved, transcendentals=0),
    )


def exchange(blocks, axis):
    ranks = range(len(blocks))
    return [
        blocks[turn] if turn == 0 else lax.ppermute(blocks[turn], axis, [(rank, rank ^ turn) for rank in ranks])
        for turn in ranks
    ]


def turn(blocks, count):
    size = sum(block.size for block in blocks)
    rows = size // LANES // count
    return on_core(partial(turn_kernel, len(blocks)), [(rows, LANES)] * count, 8 * size)(*blocks)


def by_channels(gate, keys, values, taps, skip_gain):
    outers, inners = lax.axis_size("outer"), lax.axis_size("inner")
    devices = outers * inners
    chans, seg = keys.shape
    own = chans // devices
    tiles = seg // LANES
    tables = [jnp.asarray(table) for table in transform_tables(devices, seg)]
    product = keys * values
    product, skip = lax.optimization_barrier((product, skip_gain[:, None] * product))
    total = chans * tiles
    sent = on_core(
        partial(gather_kernel, outers, inners),
        [(total // inners, LANES)] * inners + [(total // outers, LANES)] * outers,
        4 * chans * seg * 4,
        10**6,
        [(total, LANES)] * 2,
    )(product, taps)
    second = exchange(sent[:inners], "inner")
    first = exchange(sent[inners:], "outer")
    first = exchange(turn(first, inners), "inner")
    second = exchange(turn(second, outers), "outer")
    (conv,) = on_core(
        partial(convolve_kernel, outers, inners, own, seg),
        [(total, LANES)],
        2 * 10**6,
        10**9,
        [(2, total, LANES), (own, devices * tiles, 2 * LANES)],
    )(*tables, *first, *second)
    conv = lax.all_to_all(conv, AXES, split_axis=0, concat_axis=0, tiled=True)
    (mixed,) = on_core(gate_kernel, [(chans, seg)], 4 * chans * seg * 4)(gate, skip, conv)
    return mixed


def halving(size):
    return size & (size - 1) == 0


def on_device(gate, keys, values, taps, skip_gain):
    devices = lax.axis_size("outer") * lax.axis_size("inner")
    chans, seg = keys.shape
    whole = chans % devices == 0 and seg % LANES == 0 and chans * seg % (devices * 16 * LANES) == 0
    if whole and chans // devices % 2 == 0 and halving(devices):
        return by_channels(gate, keys, values, taps, skip_gain)
    return by_sections(gate, keys, values, taps, skip_gain)


def solution(mesh):
    placed = (
        P(None, ("outer", "inner")),
        P(None, ("outer", "inner")),
        P(None, ("outer", "inner")),
        P(None, ("outer", "inner")),
        P(),
    )
    return jax.shard_map(
        on_device,
        mesh=mesh,
        in_specs=placed,
        out_specs=P(None, ("outer", "inner")),
        check_vma=False,
    )
```

```python
from functools import partial
import math

import jax
import jax.numpy as jnp
import ml_dtypes
import numpy as np
from jax import lax
from jax.experimental import pallas as pl
from jax.experimental.pallas import tpu as pltpu
from jax.sharding import PartitionSpec as P

LANES = 128
AXES = ("outer", "inner")

TWO_PI = 2.0 * math.pi
HIGHEST = lax.Precision.HIGHEST


def table(count_a, count_b, modulus, sign):
    left = lax.broadcasted_iota(jnp.int32, (count_a, count_b), 0)
    right = lax.broadcasted_iota(jnp.int32, (count_a, count_b), 1)
    phase = TWO_PI / modulus * (left * right % modulus).astype(jnp.float32)
    return (jnp.cos(phase), sign * jnp.sin(phase))


def mix(form, cosine, sine, real, imag):
    contract = partial(jnp.einsum, precision=HIGHEST)
    return (
        contract(form, cosine, real) - contract(form, sine, imag),
        contract(form, sine, real) + contract(form, cosine, imag),
    )


def rotate(real, imag, cosine, sine):
    return (real * cosine - imag * sine, real * sine + imag * cosine)


def forward_rows(real, imag):
    split = 16
    lead = real.shape[:-1]
    size = real.shape[-1]
    short = size // split
    real = real.reshape(lead + (split, short))
    imag = imag.reshape(lead + (split, short))
    cosine, sine = table(split, split, split, -1.0)
    real, imag = mix("ka,...as->...ks", cosine, sine, real, imag)
    cosine, sine = table(split, short, size, -1.0)
    real, imag = rotate(real, imag, cosine, sine)
    cosine, sine = table(short, short, short, -1.0)
    real, imag = mix("sb,...ks->...bk", cosine, sine, real, imag)
    return (real.reshape(lead + (size,)), imag.reshape(lead + (size,)))


def inverse_rows(real, imag):
    split = 16
    lead = real.shape[:-1]
    size = real.shape[-1]
    short = size // split
    real = real.reshape(lead + (short, split))
    imag = imag.reshape(lead + (short, split))
    cosine, sine = table(short, short, short, 1.0)
    real, imag = mix("sb,...bk->...sk", cosine, sine, real, imag)
    cosine, sine = table(short, split, size, 1.0)
    real, imag = rotate(real, imag, cosine, sine)
    cosine, sine = table(split, split, split, 1.0)
    real, imag = mix("ak,...sk->...as", cosine, sine, real, imag)
    return (real.reshape(lead + (size,)), imag.reshape(lead + (size,)))


def by_sections(gate, keys, values, taps, skip_gain):
    inner_count = lax.axis_size("inner")
    devices = lax.axis_size("outer") * inner_count
    rank = lax.axis_index("outer") * inner_count + lax.axis_index("inner")
    chans, seg = keys.shape
    both = 2 * chans
    cols = seg // devices
    blocks = 2 * devices
    full = blocks * seg
    contract = partial(jnp.einsum, precision=HIGHEST)
    product = keys * values
    source = jnp.concatenate([product, taps], axis=0)
    sectioned = lax.all_to_all(
        lax.all_to_all(
            source.reshape(both, 1, 1, seg), "outer", split_axis=3, concat_axis=1, tiled=True
        ),
        "inner",
        split_axis=3,
        concat_axis=2,
        tiled=True,
    )
    sectioned = sectioned.reshape(both, devices, cols)
    cosine, sine = table(blocks, devices, blocks, -1.0)
    real = contract("km,cmj->ckj", cosine, sectioned)
    imag = contract("km,cmj->ckj", sine, sectioned)
    offset = rank * cols + lax.broadcasted_iota(jnp.int32, (blocks, cols), 1)
    residue = lax.broadcasted_iota(jnp.int32, (blocks, cols), 0)
    phase = TWO_PI / full * (offset * residue).astype(jnp.float32)
    real, imag = rotate(real, imag, jnp.cos(phase)[None], -jnp.sin(phase)[None])
    outgoing = jnp.stack([real, imag]).reshape(2, both, blocks, 1, 1, cols)
    moved = lax.all_to_all(
        lax.all_to_all(outgoing, "outer", split_axis=2, concat_axis=3, tiled=True),
        "inner",
        split_axis=2,
        concat_axis=4,
        tiled=True,
    )
    moved = moved.reshape(2, both, 2, seg)
    spec_real, spec_imag = forward_rows(moved[0], moved[1])
    sig_real, filt_real = (spec_real[:chans], spec_real[chans:])
    sig_imag, filt_imag = (spec_imag[:chans], spec_imag[chans:])
    real = sig_real * filt_real - sig_imag * filt_imag
    imag = sig_real * filt_imag + sig_imag * filt_real
    real, imag = inverse_rows(real, imag)
    residue = 2 * rank + lax.broadcasted_iota(jnp.int32, (2, seg), 0)
    offset = lax.broadcasted_iota(jnp.int32, (2, seg), 1)
    phase = TWO_PI / full * (offset * residue).astype(jnp.float32)
    real, imag = rotate(real, imag, jnp.cos(phase)[None], jnp.sin(phase)[None])
    returning = jnp.stack([real, imag]).reshape(2, chans, 1, 1, 2, seg)
    gathered = lax.all_to_all(
        lax.all_to_all(returning, "outer", split_axis=5, concat_axis=2, tiled=True),
        "inner",
        split_axis=5,
        concat_axis=3,
        tiled=True,
    )
    gathered = gathered.reshape(2, chans, blocks, cols)
    cosine, sine = table(devices, blocks, blocks, 1.0)
    conv = contract("mk,ckj->cmj", cosine, gathered[0]) - contract("mk,ckj->cmj", sine, gathered[1])
    conv = conv * (1.0 / full)
    conv = lax.all_to_all(
        lax.all_to_all(
            conv.reshape(chans, devices, 1, 1, cols),
            "outer",
            split_axis=1,
            concat_axis=2,
            tiled=True,
        ),
        "inner",
        split_axis=1,
        concat_axis=3,
        tiled=True,
    )
    conv = conv.reshape(chans, seg)
    return gate * (conv + skip_gain[:, None] * product)


def halves(array):
    high = array.astype(ml_dtypes.bfloat16)
    low = (array - high.astype(np.float64)).astype(ml_dtypes.bfloat16)
    return high, low


def transform_tables(devices, seg):
    length = devices * seg
    count = length // LANES
    odd = 2 * np.arange(count) + 1
    angle = 2 * np.pi / (4 * count) * ((odd[:, None] * np.arange(count)[None, :]) % (4 * count))
    first = np.concatenate([np.cos(angle), -np.sin(angle)], axis=0)
    last = np.concatenate([np.cos(angle).T, -np.sin(angle).T], axis=1) / length
    angle = 2 * np.pi / (4 * length) * ((odd[:, None] * np.arange(LANES)[None, :]) % (4 * length))
    twiddle = np.stack([np.cos(angle), np.sin(angle)]).astype(np.float32)
    angle = 2 * np.pi / LANES * ((np.arange(LANES)[:, None] * np.arange(LANES)[None, :]) % LANES)
    cosine, sine = np.cos(angle), np.sin(angle)
    rows = np.block([[cosine, -sine], [sine, cosine]])
    back = np.block([[cosine, sine], [-sine, cosine]])
    first_high, first_low = halves(first)
    rows_high, rows_low = halves(rows)
    back_high, back_low = halves(back)
    last_high, last_low = halves(last)
    return (
        np.concatenate([first_high, first_high, first_low], axis=1),
        np.concatenate([rows_high, rows_high, rows_low], axis=0),
        np.concatenate([back_high, back_high, back_low], axis=0),
        np.concatenate([last_high, last_high, last_low], axis=1),
        twiddle,
    )


def split(array):
    high = array.astype(jnp.bfloat16)
    return high, (array - high.astype(jnp.float32)).astype(jnp.bfloat16)


def dot(left, right):
    return jnp.dot(left, right, preferred_element_type=jnp.float32)


def convolve_kernel(
    devices, chans, seg, data_ref, first_ref, rows_ref, back_ref, last_ref, twiddle_ref, out_ref, signal_ref
):
    parts = seg // LANES
    count = devices * parts
    cosine, sine = twiddle_ref[0], twiddle_ref[1]

    def lanes(at):
        return slice(at * LANES, (at + 1) * LANES)

    groups = chans
    each = chans // groups
    at = range(groups)
    for group in at:
        for kind in range(2):
            for chan in range(each):
                for device in range(devices):
                    came = ((device * 2 + kind) * chans + group * each + chan) * parts
                    signal_ref[group, device * parts : (device + 1) * parts, lanes(kind * each + chan)] = data_ref[
                        came : came + parts, :
                    ]

    def start(group):
        high, low = split(signal_ref[group])
        return dot(first_ref[...], jnp.concatenate([high, low, high], axis=0))

    def spectra(begun):
        turned = []
        for signal in range(2 * each):
            real, imag = begun[:count, lanes(signal)], begun[count:, lanes(signal)]
            turned.append(jnp.concatenate([real * cosine + imag * sine, imag * cosine - real * sine], axis=1))
        high, low = split(jnp.concatenate(turned, axis=0))
        return dot(jnp.concatenate([high, low, high], axis=1), rows_ref[...])

    def product(spectrum):
        mid = each * count
        sig_real, sig_imag = spectrum[:mid, :LANES], spectrum[:mid, LANES:]
        filt_real, filt_imag = spectrum[mid:, :LANES], spectrum[mid:, LANES:]
        real = sig_real * filt_real - sig_imag * filt_imag
        imag = sig_real * filt_imag + sig_imag * filt_real
        return jnp.concatenate([real, imag], axis=1)

    def back(filtered):
        high, low = split(filtered)
        return dot(jnp.concatenate([high, low, high], axis=1), back_ref[...])

    def end(backed):
        turned = []
        for chan in range(backed.shape[0] // count):
            real = backed[chan * count : (chan + 1) * count, :LANES]
            imag = backed[chan * count : (chan + 1) * count, LANES:]
            turned.append(jnp.concatenate([real * cosine - imag * sine, imag * cosine + real * sine], axis=0))
        high, low = split(jnp.concatenate(turned, axis=1))
        return dot(last_ref[...], jnp.concatenate([high, low, high], axis=0))

    begun = [start(group) for group in at]
    spectrum = [spectra(begun[group]) for group in at]
    backed = back(jnp.concatenate([product(spectrum[group]) for group in at], axis=0))
    pair = 2 if chans % 2 == 0 else 1
    for own in range(0, chans, pair):
        conv = end(backed[own * count : (own + pair) * count])
        for chan in range(pair):
            for device in range(devices):
                to = (device * chans + own + chan) * parts
                out_ref[to : to + parts, :] = conv[device * parts : (device + 1) * parts, lanes(chan)]


def gather_kernel(devices, product_ref, taps_ref, out_ref):
    chans, seg = product_ref.shape
    rows = chans // devices * seg // LANES
    product = product_ref[...].reshape(devices, rows, LANES)
    filt = taps_ref[...].reshape(devices, rows, LANES)
    out_ref[...] = jnp.concatenate([product, filt], axis=1).reshape(2 * devices * rows, LANES)


def gate_kernel(gate_ref, skip_ref, conv_ref, out_hbm, out_ref, sems):
    chans, seg = gate_ref.shape
    pieces = sems.shape[0]
    step = chans // pieces
    rows = conv_ref.shape[0] // pieces
    copies = []
    for piece in range(pieces):
        at = slice(piece * step, (piece + 1) * step)
        conv = conv_ref[piece * rows : (piece + 1) * rows, :].reshape(step, seg)
        out_ref[at, :] = gate_ref[at, :] * (conv + skip_ref[at, :])
        copies.append(pltpu.make_async_copy(out_ref.at[at, :], out_hbm.at[at, :], sems.at[piece]))
        copies[piece].start()
    for copy in copies:
        copy.wait()


def on_core(kernel, shape, moved, flops=10**6, scratch=(), **more):
    return pl.pallas_call(
        kernel,
        out_shape=jax.ShapeDtypeStruct(shape, jnp.float32),
        scratch_shapes=scratch,
        compiler_params=pltpu.CompilerParams(vmem_limit_bytes=32 * 2**20),
        cost_estimate=pl.CostEstimate(flops=flops, bytes_accessed=moved, transcendentals=0),
        **more,
    )


def by_channels(gate, keys, values, taps, skip_gain):
    devices = lax.axis_size("outer") * lax.axis_size("inner")
    chans, seg = keys.shape
    own = chans // devices
    tiles = seg // LANES
    tables = [jnp.asarray(table) for table in transform_tables(devices, seg)]
    regroup = partial(lax.all_to_all, axis_name=AXES, split_axis=0, concat_axis=0, tiled=True)
    product = keys * values
    product, skip = lax.optimization_barrier((product, skip_gain[:, None] * product))
    sent = on_core(partial(gather_kernel, devices), (2 * chans * tiles, LANES), 4 * chans * seg * 4)(product, taps)
    groups = own
    conv = on_core(
        partial(convolve_kernel, devices, own, seg),
        (chans * tiles, LANES),
        2 * 10**6,
        10**9,
        [pltpu.VMEM((groups, devices * tiles, 2 * own // groups * LANES), jnp.float32)],
    )(regroup(sent), *tables)
    pieces = math.gcd(chans // 8, 4) if chans % 8 == 0 else 1
    return on_core(
        gate_kernel,
        (chans, seg),
        4 * chans * seg * 4,
        scratch=[pltpu.VMEM((chans, seg), jnp.float32), pltpu.SemaphoreType.DMA((pieces,))],
        out_specs=pl.BlockSpec(memory_space=pl.ANY),
    )(gate, skip, regroup(conv))


def on_device(gate, keys, values, taps, skip_gain):
    devices = lax.axis_size("outer") * lax.axis_size("inner")
    chans, seg = keys.shape
    if chans % devices == 0 and seg % LANES == 0 and devices % 8 == 0:
        return by_channels(gate, keys, values, taps, skip_gain)
    return by_sections(gate, keys, values, taps, skip_gain)


def solution(mesh):
    placed = (
        P(None, ("outer", "inner")),
        P(None, ("outer", "inner")),
        P(None, ("outer", "inner")),
        P(None, ("outer", "inner")),
        P(),
    )
    return jax.shard_map(
        on_device,
        mesh=mesh,
        in_specs=placed,
        out_specs=P(None, ("outer", "inner")),
        check_vma=False,
    )
```

```python
from functools import partial
import math

import jax
import jax.numpy as jnp
import ml_dtypes
import numpy as np
from jax import lax
from jax.experimental import pallas as pl
from jax.experimental.pallas import tpu as pltpu
from jax.sharding import PartitionSpec as P

LANES = 128
AXES = ("outer", "inner")

TWO_PI = 2.0 * math.pi
HIGHEST = lax.Precision.HIGHEST


def table(count_a, count_b, modulus, sign):
    left = lax.broadcasted_iota(jnp.int32, (count_a, count_b), 0)
    right = lax.broadcasted_iota(jnp.int32, (count_a, count_b), 1)
    phase = TWO_PI / modulus * (left * right % modulus).astype(jnp.float32)
    return (jnp.cos(phase), sign * jnp.sin(phase))


def mix(form, cosine, sine, real, imag):
    contract = partial(jnp.einsum, precision=HIGHEST)
    return (
        contract(form, cosine, real) - contract(form, sine, imag),
        contract(form, sine, real) + contract(form, cosine, imag),
    )


def rotate(real, imag, cosine, sine):
    return (real * cosine - imag * sine, real * sine + imag * cosine)


def forward_rows(real, imag):
    split = 16
    lead = real.shape[:-1]
    size = real.shape[-1]
    short = size // split
    real = real.reshape(lead + (split, short))
    imag = imag.reshape(lead + (split, short))
    cosine, sine = table(split, split, split, -1.0)
    real, imag = mix("ka,...as->...ks", cosine, sine, real, imag)
    cosine, sine = table(split, short, size, -1.0)
    real, imag = rotate(real, imag, cosine, sine)
    cosine, sine = table(short, short, short, -1.0)
    real, imag = mix("sb,...ks->...bk", cosine, sine, real, imag)
    return (real.reshape(lead + (size,)), imag.reshape(lead + (size,)))


def inverse_rows(real, imag):
    split = 16
    lead = real.shape[:-1]
    size = real.shape[-1]
    short = size // split
    real = real.reshape(lead + (short, split))
    imag = imag.reshape(lead + (short, split))
    cosine, sine = table(short, short, short, 1.0)
    real, imag = mix("sb,...bk->...sk", cosine, sine, real, imag)
    cosine, sine = table(short, split, size, 1.0)
    real, imag = rotate(real, imag, cosine, sine)
    cosine, sine = table(split, split, split, 1.0)
    real, imag = mix("ak,...sk->...as", cosine, sine, real, imag)
    return (real.reshape(lead + (size,)), imag.reshape(lead + (size,)))


def by_sections(gate, keys, values, taps, skip_gain):
    inner_count = lax.axis_size("inner")
    devices = lax.axis_size("outer") * inner_count
    rank = lax.axis_index("outer") * inner_count + lax.axis_index("inner")
    chans, seg = keys.shape
    both = 2 * chans
    cols = seg // devices
    blocks = 2 * devices
    full = blocks * seg
    contract = partial(jnp.einsum, precision=HIGHEST)
    product = keys * values
    source = jnp.concatenate([product, taps], axis=0)
    sectioned = lax.all_to_all(
        lax.all_to_all(
            source.reshape(both, 1, 1, seg), "outer", split_axis=3, concat_axis=1, tiled=True
        ),
        "inner",
        split_axis=3,
        concat_axis=2,
        tiled=True,
    )
    sectioned = sectioned.reshape(both, devices, cols)
    cosine, sine = table(blocks, devices, blocks, -1.0)
    real = contract("km,cmj->ckj", cosine, sectioned)
    imag = contract("km,cmj->ckj", sine, sectioned)
    offset = rank * cols + lax.broadcasted_iota(jnp.int32, (blocks, cols), 1)
    residue = lax.broadcasted_iota(jnp.int32, (blocks, cols), 0)
    phase = TWO_PI / full * (offset * residue).astype(jnp.float32)
    real, imag = rotate(real, imag, jnp.cos(phase)[None], -jnp.sin(phase)[None])
    outgoing = jnp.stack([real, imag]).reshape(2, both, blocks, 1, 1, cols)
    moved = lax.all_to_all(
        lax.all_to_all(outgoing, "outer", split_axis=2, concat_axis=3, tiled=True),
        "inner",
        split_axis=2,
        concat_axis=4,
        tiled=True,
    )
    moved = moved.reshape(2, both, 2, seg)
    spec_real, spec_imag = forward_rows(moved[0], moved[1])
    sig_real, filt_real = (spec_real[:chans], spec_real[chans:])
    sig_imag, filt_imag = (spec_imag[:chans], spec_imag[chans:])
    real = sig_real * filt_real - sig_imag * filt_imag
    imag = sig_real * filt_imag + sig_imag * filt_real
    real, imag = inverse_rows(real, imag)
    residue = 2 * rank + lax.broadcasted_iota(jnp.int32, (2, seg), 0)
    offset = lax.broadcasted_iota(jnp.int32, (2, seg), 1)
    phase = TWO_PI / full * (offset * residue).astype(jnp.float32)
    real, imag = rotate(real, imag, jnp.cos(phase)[None], jnp.sin(phase)[None])
    returning = jnp.stack([real, imag]).reshape(2, chans, 1, 1, 2, seg)
    gathered = lax.all_to_all(
        lax.all_to_all(returning, "outer", split_axis=5, concat_axis=2, tiled=True),
        "inner",
        split_axis=5,
        concat_axis=3,
        tiled=True,
    )
    gathered = gathered.reshape(2, chans, blocks, cols)
    cosine, sine = table(devices, blocks, blocks, 1.0)
    conv = contract("mk,ckj->cmj", cosine, gathered[0]) - contract("mk,ckj->cmj", sine, gathered[1])
    conv = conv * (1.0 / full)
    conv = lax.all_to_all(
        lax.all_to_all(
            conv.reshape(chans, devices, 1, 1, cols),
            "outer",
            split_axis=1,
            concat_axis=2,
            tiled=True,
        ),
        "inner",
        split_axis=1,
        concat_axis=3,
        tiled=True,
    )
    conv = conv.reshape(chans, seg)
    return gate * (conv + skip_gain[:, None] * product)


def halves(array):
    high = array.astype(ml_dtypes.bfloat16)
    low = (array - high.astype(np.float64)).astype(ml_dtypes.bfloat16)
    return high, low


def transform_tables(devices, seg):
    length = devices * seg
    count = length // LANES
    odd = 2 * np.arange(count) + 1
    angle = 2 * np.pi / (4 * count) * ((odd[:, None] * np.arange(count)[None, :]) % (4 * count))
    first = np.concatenate([np.cos(angle), -np.sin(angle)], axis=0)
    last = np.concatenate([np.cos(angle).T, -np.sin(angle).T], axis=1) / length
    angle = 2 * np.pi / (4 * length) * ((odd[:, None] * np.arange(LANES)[None, :]) % (4 * length))
    twiddle = np.stack([np.cos(angle), np.sin(angle)]).astype(np.float32)
    angle = 2 * np.pi / LANES * ((np.arange(LANES)[:, None] * np.arange(LANES)[None, :]) % LANES)
    cosine, sine = np.cos(angle), np.sin(angle)
    rows = np.block([[cosine, -sine], [sine, cosine]])
    back = np.block([[cosine, sine], [-sine, cosine]])
    first_high, first_low = halves(first)
    rows_high, rows_low = halves(rows)
    back_high, back_low = halves(back)
    last_high, last_low = halves(last)
    return (
        np.concatenate([first_high, first_high, first_low], axis=1),
        np.concatenate([rows_high, rows_high, rows_low], axis=0),
        np.concatenate([back_high, back_high, back_low], axis=0),
        np.concatenate([last_high, last_high, last_low], axis=1),
        twiddle,
    )


def split(array):
    high = array.astype(jnp.bfloat16)
    return high, (array - high.astype(jnp.float32)).astype(jnp.bfloat16)


def dot(left, right):
    return jnp.dot(left, right, preferred_element_type=jnp.float32)


def convolve_kernel(
    devices, chans, seg, data_ref, first_ref, rows_ref, back_ref, last_ref, twiddle_ref, out_ref, signal_ref
):
    parts = seg // LANES
    count = devices * parts
    turn_chans = signal_ref.shape[0]
    unit = turn_chans * parts
    turns = chans // turn_chans

    def lanes(at):
        return slice(at * LANES, (at + 1) * LANES)

    def tile(ref, at):
        return ref[pl.ds(pl.multiple_of(at * unit, unit), unit), :]

    def start(chan):
        high, low = split(signal_ref[chan])
        return dot(first_ref[...], jnp.concatenate([high, low, high], axis=0))

    def spectra(begun):
        cosine, sine = twiddle_ref[0], twiddle_ref[1]
        turned = []
        for kind in range(2):
            real, imag = begun[:count, lanes(kind)], begun[count:, lanes(kind)]
            turned.append(jnp.concatenate([real * cosine + imag * sine, imag * cosine - real * sine], axis=1))
        high, low = split(jnp.concatenate(turned, axis=0))
        return dot(jnp.concatenate([high, low, high], axis=1), rows_ref[...])

    def back(spectrum):
        sig_real, sig_imag = spectrum[:count, :LANES], spectrum[:count, LANES:]
        filt_real, filt_imag = spectrum[count:, :LANES], spectrum[count:, LANES:]
        real = sig_real * filt_real - sig_imag * filt_imag
        imag = sig_real * filt_imag + sig_imag * filt_real
        high, low = split(jnp.concatenate([real, imag], axis=1))
        return dot(jnp.concatenate([high, low, high], axis=1), back_ref[...])

    def end(backed):
        cosine, sine = twiddle_ref[0], twiddle_ref[1]
        real, imag = backed[:, :LANES], backed[:, LANES:]
        high, low = split(jnp.concatenate([real * cosine - imag * sine, imag * cosine + real * sine], axis=0))
        return dot(last_ref[...], jnp.concatenate([high, low, high], axis=0))

    def some_channels(turn):
        at = range(turn_chans)
        for device in range(devices):
            for kind in range(2):
                rows = tile(data_ref, (device * 2 + kind) * turns + turn)
                for chan in at:
                    signal_ref[chan, device * parts : (device + 1) * parts, lanes(kind)] = rows[
                        chan * parts : (chan + 1) * parts
                    ]
        begun = [start(chan) for chan in at]
        spectrum = [spectra(begun[chan]) for chan in at]
        backed = [back(spectrum[chan]) for chan in at]
        conv = [end(backed[chan]) for chan in at]
        for device in range(devices):
            rows = [conv[chan][device * parts : (device + 1) * parts] for chan in at]
            to = (device * turns + turn) * unit
            out_ref[pl.ds(pl.multiple_of(to, unit), unit), :] = jnp.concatenate(rows, axis=0)

    pl.loop(0, turns)(some_channels)


def gather_kernel(devices, product_ref, taps_ref, out_ref):
    chans, seg = product_ref.shape
    rows = chans // devices * seg // LANES
    product = product_ref[...].reshape(devices, rows, LANES)
    filt = taps_ref[...].reshape(devices, rows, LANES)
    out_ref[...] = jnp.concatenate([product, filt], axis=1).reshape(2 * devices * rows, LANES)


def gate_kernel(gate_ref, skip_ref, conv_ref, out_hbm, out_ref, sems):
    chans, seg = gate_ref.shape
    pieces = sems.shape[0]
    step = chans // pieces
    rows = conv_ref.shape[0] // pieces
    copies = []
    for piece in range(pieces):
        at = slice(piece * step, (piece + 1) * step)
        conv = conv_ref[piece * rows : (piece + 1) * rows, :].reshape(step, seg)
        out_ref[at, :] = gate_ref[at, :] * (conv + skip_ref[at, :])
        copies.append(pltpu.make_async_copy(out_ref.at[at, :], out_hbm.at[at, :], sems.at[piece]))
        copies[piece].start()
    for copy in copies:
        copy.wait()


def on_core(kernel, shape, moved, flops=10**6, scratch=(), **more):
    return pl.pallas_call(
        kernel,
        out_shape=jax.ShapeDtypeStruct(shape, jnp.float32),
        scratch_shapes=scratch,
        compiler_params=pltpu.CompilerParams(vmem_limit_bytes=32 * 2**20),
        cost_estimate=pl.CostEstimate(flops=flops, bytes_accessed=moved, transcendentals=0),
        **more,
    )


def by_channels(gate, keys, values, taps, skip_gain):
    devices = lax.axis_size("outer") * lax.axis_size("inner")
    chans, seg = keys.shape
    own = chans // devices
    tiles = seg // LANES
    tables = [jnp.asarray(table) for table in transform_tables(devices, seg)]
    regroup = partial(lax.all_to_all, axis_name=AXES, split_axis=0, concat_axis=0, tiled=True)
    product = keys * values
    product, skip = lax.optimization_barrier((product, skip_gain[:, None] * product))
    sent = on_core(partial(gather_kernel, devices), (2 * chans * tiles, LANES), 4 * chans * seg * 4)(product, taps)
    turn_chans = 2
    conv = on_core(
        partial(convolve_kernel, devices, own, seg),
        (chans * tiles, LANES),
        2 * 10**6,
        10**9,
        [pltpu.VMEM((turn_chans, devices * tiles, 2 * LANES), jnp.float32)],
    )(regroup(sent), *tables)
    pieces = math.gcd(chans // 8, 4) if chans % 8 == 0 else 1
    return on_core(
        gate_kernel,
        (chans, seg),
        4 * chans * seg * 4,
        scratch=[pltpu.VMEM((chans, seg), jnp.float32), pltpu.SemaphoreType.DMA((pieces,))],
        out_specs=pl.BlockSpec(memory_space=pl.ANY),
    )(gate, skip, regroup(conv))


def on_device(gate, keys, values, taps, skip_gain):
    devices = lax.axis_size("outer") * lax.axis_size("inner")
    chans, seg = keys.shape
    if chans % (2 * devices) == 0 and seg % (4 * LANES) == 0 and devices % 8 == 0:
        return by_channels(gate, keys, values, taps, skip_gain)
    return by_sections(gate, keys, values, taps, skip_gain)


def solution(mesh):
    placed = (
        P(None, ("outer", "inner")),
        P(None, ("outer", "inner")),
        P(None, ("outer", "inner")),
        P(None, ("outer", "inner")),
        P(),
    )
    return jax.shard_map(
        on_device,
        mesh=mesh,
        in_specs=placed,
        out_specs=P(None, ("outer", "inner")),
        check_vma=False,
    )
```

```python
from functools import partial
import math

import jax
import jax.numpy as jnp
import ml_dtypes
import numpy as np
from jax import lax
from jax.experimental import pallas as pl
from jax.experimental.pallas import tpu as pltpu
from jax.sharding import PartitionSpec as P

LANES = 128
AXES = ("outer", "inner")

TWO_PI = 2.0 * math.pi
HIGHEST = lax.Precision.HIGHEST


def table(count_a, count_b, modulus, sign):
    left = lax.broadcasted_iota(jnp.int32, (count_a, count_b), 0)
    right = lax.broadcasted_iota(jnp.int32, (count_a, count_b), 1)
    phase = TWO_PI / modulus * (left * right % modulus).astype(jnp.float32)
    return (jnp.cos(phase), sign * jnp.sin(phase))


def mix(form, cosine, sine, real, imag):
    contract = partial(jnp.einsum, precision=HIGHEST)
    return (
        contract(form, cosine, real) - contract(form, sine, imag),
        contract(form, sine, real) + contract(form, cosine, imag),
    )


def rotate(real, imag, cosine, sine):
    return (real * cosine - imag * sine, real * sine + imag * cosine)


def forward_rows(real, imag):
    split = 16
    lead = real.shape[:-1]
    size = real.shape[-1]
    short = size // split
    real = real.reshape(lead + (split, short))
    imag = imag.reshape(lead + (split, short))
    cosine, sine = table(split, split, split, -1.0)
    real, imag = mix("ka,...as->...ks", cosine, sine, real, imag)
    cosine, sine = table(split, short, size, -1.0)
    real, imag = rotate(real, imag, cosine, sine)
    cosine, sine = table(short, short, short, -1.0)
    real, imag = mix("sb,...ks->...bk", cosine, sine, real, imag)
    return (real.reshape(lead + (size,)), imag.reshape(lead + (size,)))


def inverse_rows(real, imag):
    split = 16
    lead = real.shape[:-1]
    size = real.shape[-1]
    short = size // split
    real = real.reshape(lead + (short, split))
    imag = imag.reshape(lead + (short, split))
    cosine, sine = table(short, short, short, 1.0)
    real, imag = mix("sb,...bk->...sk", cosine, sine, real, imag)
    cosine, sine = table(short, split, size, 1.0)
    real, imag = rotate(real, imag, cosine, sine)
    cosine, sine = table(split, split, split, 1.0)
    real, imag = mix("ak,...sk->...as", cosine, sine, real, imag)
    return (real.reshape(lead + (size,)), imag.reshape(lead + (size,)))


def by_sections(gate, keys, values, taps, skip_gain):
    inner_count = lax.axis_size("inner")
    devices = lax.axis_size("outer") * inner_count
    rank = lax.axis_index("outer") * inner_count + lax.axis_index("inner")
    chans, seg = keys.shape
    both = 2 * chans
    cols = seg // devices
    blocks = 2 * devices
    full = blocks * seg
    contract = partial(jnp.einsum, precision=HIGHEST)
    product = keys * values
    source = jnp.concatenate([product, taps], axis=0)
    sectioned = lax.all_to_all(
        lax.all_to_all(
            source.reshape(both, 1, 1, seg), "outer", split_axis=3, concat_axis=1, tiled=True
        ),
        "inner",
        split_axis=3,
        concat_axis=2,
        tiled=True,
    )
    sectioned = sectioned.reshape(both, devices, cols)
    cosine, sine = table(blocks, devices, blocks, -1.0)
    real = contract("km,cmj->ckj", cosine, sectioned)
    imag = contract("km,cmj->ckj", sine, sectioned)
    offset = rank * cols + lax.broadcasted_iota(jnp.int32, (blocks, cols), 1)
    residue = lax.broadcasted_iota(jnp.int32, (blocks, cols), 0)
    phase = TWO_PI / full * (offset * residue).astype(jnp.float32)
    real, imag = rotate(real, imag, jnp.cos(phase)[None], -jnp.sin(phase)[None])
    outgoing = jnp.stack([real, imag]).reshape(2, both, blocks, 1, 1, cols)
    moved = lax.all_to_all(
        lax.all_to_all(outgoing, "outer", split_axis=2, concat_axis=3, tiled=True),
        "inner",
        split_axis=2,
        concat_axis=4,
        tiled=True,
    )
    moved = moved.reshape(2, both, 2, seg)
    spec_real, spec_imag = forward_rows(moved[0], moved[1])
    sig_real, filt_real = (spec_real[:chans], spec_real[chans:])
    sig_imag, filt_imag = (spec_imag[:chans], spec_imag[chans:])
    real = sig_real * filt_real - sig_imag * filt_imag
    imag = sig_real * filt_imag + sig_imag * filt_real
    real, imag = inverse_rows(real, imag)
    residue = 2 * rank + lax.broadcasted_iota(jnp.int32, (2, seg), 0)
    offset = lax.broadcasted_iota(jnp.int32, (2, seg), 1)
    phase = TWO_PI / full * (offset * residue).astype(jnp.float32)
    real, imag = rotate(real, imag, jnp.cos(phase)[None], jnp.sin(phase)[None])
    returning = jnp.stack([real, imag]).reshape(2, chans, 1, 1, 2, seg)
    gathered = lax.all_to_all(
        lax.all_to_all(returning, "outer", split_axis=5, concat_axis=2, tiled=True),
        "inner",
        split_axis=5,
        concat_axis=3,
        tiled=True,
    )
    gathered = gathered.reshape(2, chans, blocks, cols)
    cosine, sine = table(devices, blocks, blocks, 1.0)
    conv = contract("mk,ckj->cmj", cosine, gathered[0]) - contract("mk,ckj->cmj", sine, gathered[1])
    conv = conv * (1.0 / full)
    conv = lax.all_to_all(
        lax.all_to_all(
            conv.reshape(chans, devices, 1, 1, cols),
            "outer",
            split_axis=1,
            concat_axis=2,
            tiled=True,
        ),
        "inner",
        split_axis=1,
        concat_axis=3,
        tiled=True,
    )
    conv = conv.reshape(chans, seg)
    return gate * (conv + skip_gain[:, None] * product)


def halves(array):
    high = array.astype(ml_dtypes.bfloat16)
    low = (array - high.astype(np.float64)).astype(ml_dtypes.bfloat16)
    return high, low


def transform_tables(devices, seg):
    length = devices * seg
    count = length // LANES
    odd = 2 * np.arange(count) + 1
    angle = 2 * np.pi / (4 * count) * ((odd[:, None] * np.arange(count)[None, :]) % (4 * count))
    first = np.concatenate([np.cos(angle), -np.sin(angle)], axis=0)
    last = np.concatenate([np.cos(angle).T, -np.sin(angle).T], axis=1) / length
    angle = 2 * np.pi / (4 * length) * ((odd[:, None] * np.arange(LANES)[None, :]) % (4 * length))
    twiddle = np.stack([np.cos(angle), np.sin(angle)]).astype(np.float32)
    angle = 2 * np.pi / LANES * ((np.arange(LANES)[:, None] * np.arange(LANES)[None, :]) % LANES)
    cosine, sine = np.cos(angle), np.sin(angle)
    rows = np.block([[cosine, -sine], [sine, cosine]])
    back = np.block([[cosine, sine], [-sine, cosine]])
    first_high, first_low = halves(first)
    rows_high, rows_low = halves(rows)
    back_high, back_low = halves(back)
    last_high, last_low = halves(last)
    return (
        np.concatenate([first_high, first_high, first_low], axis=1),
        np.concatenate([rows_high, rows_high, rows_low], axis=0),
        np.concatenate([back_high, back_high, back_low], axis=0),
        np.concatenate([last_high, last_high, last_low], axis=1),
        twiddle,
    )


def send_order(outer, inner):
    return [at * inner + step for step in reversed(range(inner)) for at in reversed(range(outer))]


def split(array):
    high = array.astype(jnp.bfloat16)
    return high, (array - high.astype(jnp.float32)).astype(jnp.bfloat16)


def dot(left, right):
    return jnp.dot(left, right, preferred_element_type=jnp.float32)


def convolve_kernel(
    devices, chans, seg, data_ref, first_ref, rows_ref, back_ref, last_ref, twiddle_ref, out_ref, signal_ref
):
    parts = seg // LANES
    count = devices * parts
    cosine, sine = twiddle_ref[0], twiddle_ref[1]

    def lanes(at):
        return slice(at * LANES, (at + 1) * LANES)

    order = send_order(lax.axis_size("outer"), lax.axis_size("inner"))

    groups = chans
    each = chans // groups
    at = range(groups)
    for group in at:
        for kind in range(2):
            for chan in range(each):
                for device in range(devices):
                    came = ((device * 2 + kind) * chans + group * each + chan) * parts
                    to = order[device] * parts
                    signal_ref[group, to : to + parts, lanes(kind * each + chan)] = data_ref[came : came + parts, :]

    def start(group):
        high, low = split(signal_ref[group])
        return dot(first_ref[...], jnp.concatenate([high, low, high], axis=0))

    def spectra(begun):
        turned = []
        for signal in range(2 * each):
            real, imag = begun[:count, lanes(signal)], begun[count:, lanes(signal)]
            turned.append(jnp.concatenate([real * cosine + imag * sine, imag * cosine - real * sine], axis=1))
        high, low = split(jnp.concatenate(turned, axis=0))
        return dot(jnp.concatenate([high, low, high], axis=1), rows_ref[...])

    def back(spectrum):
        mid = each * count
        sig_real, sig_imag = spectrum[:mid, :LANES], spectrum[:mid, LANES:]
        filt_real, filt_imag = spectrum[mid:, :LANES], spectrum[mid:, LANES:]
        real = sig_real * filt_real - sig_imag * filt_imag
        imag = sig_real * filt_imag + sig_imag * filt_real
        high, low = split(jnp.concatenate([real, imag], axis=1))
        return dot(jnp.concatenate([high, low, high], axis=1), back_ref[...])

    def end(backed):
        turned = []
        for chan in range(each):
            real = backed[chan * count : (chan + 1) * count, :LANES]
            imag = backed[chan * count : (chan + 1) * count, LANES:]
            turned.append(jnp.concatenate([real * cosine - imag * sine, imag * cosine + real * sine], axis=0))
        high, low = split(jnp.concatenate(turned, axis=1))
        return dot(last_ref[...], jnp.concatenate([high, low, high], axis=0))

    begun = [start(group) for group in at]
    spectrum = [spectra(begun[group]) for group in at]
    backed = [back(spectrum[group]) for group in at]
    conv = [end(backed[group]) for group in at]
    for group in at:
        for chan in range(each):
            own = group * each + chan
            for device in range(devices):
                to = (device * chans + own) * parts
                came = order[device] * parts
                out_ref[to : to + parts, :] = conv[group][came : came + parts, lanes(chan)]


def gather_kernel(devices, product_ref, taps_ref, out_ref):
    chans, seg = product_ref.shape
    rows = chans // devices * seg // LANES
    product = product_ref[...].reshape(devices, rows, LANES)
    filt = taps_ref[...].reshape(devices, rows, LANES)
    out_ref[...] = jnp.concatenate([product, filt], axis=1).reshape(2 * devices * rows, LANES)


def gate_kernel(gate_ref, skip_ref, conv_ref, out_hbm, out_ref, sems):
    chans, seg = gate_ref.shape
    pieces = sems.shape[0]
    step = chans // pieces
    rows = conv_ref.shape[0] // pieces
    copies = []
    for piece in range(pieces):
        at = slice(piece * step, (piece + 1) * step)
        conv = conv_ref[piece * rows : (piece + 1) * rows, :].reshape(step, seg)
        out_ref[at, :] = gate_ref[at, :] * (conv + skip_ref[at, :])
        copies.append(pltpu.make_async_copy(out_ref.at[at, :], out_hbm.at[at, :], sems.at[piece]))
        copies[piece].start()
    for copy in copies:
        copy.wait()


def on_core(kernel, shape, moved, flops=10**6, scratch=(), **more):
    return pl.pallas_call(
        kernel,
        out_shape=jax.ShapeDtypeStruct(shape, jnp.float32),
        scratch_shapes=scratch,
        compiler_params=pltpu.CompilerParams(vmem_limit_bytes=32 * 2**20),
        cost_estimate=pl.CostEstimate(flops=flops, bytes_accessed=moved, transcendentals=0),
        **more,
    )


def by_channels(gate, keys, values, taps, skip_gain):
    devices = lax.axis_size("outer") * lax.axis_size("inner")
    chans, seg = keys.shape
    own = chans // devices
    tiles = seg // LANES
    tables = [jnp.asarray(table) for table in transform_tables(devices, seg)]
    order = [send_order(lax.axis_size("outer"), lax.axis_size("inner"))]
    regroup = partial(lax.all_to_all, axis_name=AXES, split_axis=0, concat_axis=0, tiled=True, axis_index_groups=order)
    product = keys * values
    product, skip = lax.optimization_barrier((product, skip_gain[:, None] * product))
    sent = on_core(partial(gather_kernel, devices), (2 * chans * tiles, LANES), 4 * chans * seg * 4)(product, taps)
    groups = own
    conv = on_core(
        partial(convolve_kernel, devices, own, seg),
        (chans * tiles, LANES),
        2 * 10**6,
        10**9,
        [pltpu.VMEM((groups, devices * tiles, 2 * own // groups * LANES), jnp.float32)],
    )(regroup(sent), *tables)
    pieces = math.gcd(chans // 8, 4) if chans % 8 == 0 else 1
    return on_core(
        gate_kernel,
        (chans, seg),
        4 * chans * seg * 4,
        scratch=[pltpu.VMEM((chans, seg), jnp.float32), pltpu.SemaphoreType.DMA((pieces,))],
        out_specs=pl.BlockSpec(memory_space=pl.ANY),
    )(gate, skip, regroup(conv))


def on_device(gate, keys, values, taps, skip_gain):
    devices = lax.axis_size("outer") * lax.axis_size("inner")
    chans, seg = keys.shape
    if chans % devices == 0 and seg % LANES == 0 and devices % 8 == 0:
        return by_channels(gate, keys, values, taps, skip_gain)
    return by_sections(gate, keys, values, taps, skip_gain)


def solution(mesh):
    placed = (
        P(None, ("outer", "inner")),
        P(None, ("outer", "inner")),
        P(None, ("outer", "inner")),
        P(None, ("outer", "inner")),
        P(),
    )
    return jax.shard_map(
        on_device,
        mesh=mesh,
        in_specs=placed,
        out_specs=P(None, ("outer", "inner")),
        check_vma=False,
    )
```

```python
from functools import partial
import math

import jax
import jax.numpy as jnp
import ml_dtypes
import numpy as np
from jax import lax
from jax.experimental import pallas as pl
from jax.experimental.pallas import tpu as pltpu
from jax.sharding import PartitionSpec as P

LANES = 128
AXES = ("outer", "inner")

TWO_PI = 2.0 * math.pi
HIGHEST = lax.Precision.HIGHEST


def table(count_a, count_b, modulus, sign):
    left = lax.broadcasted_iota(jnp.int32, (count_a, count_b), 0)
    right = lax.broadcasted_iota(jnp.int32, (count_a, count_b), 1)
    phase = TWO_PI / modulus * (left * right % modulus).astype(jnp.float32)
    return (jnp.cos(phase), sign * jnp.sin(phase))


def mix(form, cosine, sine, real, imag):
    contract = partial(jnp.einsum, precision=HIGHEST)
    return (
        contract(form, cosine, real) - contract(form, sine, imag),
        contract(form, sine, real) + contract(form, cosine, imag),
    )


def rotate(real, imag, cosine, sine):
    return (real * cosine - imag * sine, real * sine + imag * cosine)


def forward_rows(real, imag):
    split = 16
    lead = real.shape[:-1]
    size = real.shape[-1]
    short = size // split
    real = real.reshape(lead + (split, short))
    imag = imag.reshape(lead + (split, short))
    cosine, sine = table(split, split, split, -1.0)
    real, imag = mix("ka,...as->...ks", cosine, sine, real, imag)
    cosine, sine = table(split, short, size, -1.0)
    real, imag = rotate(real, imag, cosine, sine)
    cosine, sine = table(short, short, short, -1.0)
    real, imag = mix("sb,...ks->...bk", cosine, sine, real, imag)
    return (real.reshape(lead + (size,)), imag.reshape(lead + (size,)))


def inverse_rows(real, imag):
    split = 16
    lead = real.shape[:-1]
    size = real.shape[-1]
    short = size // split
    real = real.reshape(lead + (short, split))
    imag = imag.reshape(lead + (short, split))
    cosine, sine = table(short, short, short, 1.0)
    real, imag = mix("sb,...bk->...sk", cosine, sine, real, imag)
    cosine, sine = table(short, split, size, 1.0)
    real, imag = rotate(real, imag, cosine, sine)
    cosine, sine = table(split, split, split, 1.0)
    real, imag = mix("ak,...sk->...as", cosine, sine, real, imag)
    return (real.reshape(lead + (size,)), imag.reshape(lead + (size,)))


def by_sections(gate, keys, values, taps, skip_gain):
    inner_count = lax.axis_size("inner")
    devices = lax.axis_size("outer") * inner_count
    rank = lax.axis_index("outer") * inner_count + lax.axis_index("inner")
    chans, seg = keys.shape
    both = 2 * chans
    cols = seg // devices
    blocks = 2 * devices
    full = blocks * seg
    contract = partial(jnp.einsum, precision=HIGHEST)
    product = keys * values
    source = jnp.concatenate([product, taps], axis=0)
    sectioned = lax.all_to_all(
        lax.all_to_all(
            source.reshape(both, 1, 1, seg), "outer", split_axis=3, concat_axis=1, tiled=True
        ),
        "inner",
        split_axis=3,
        concat_axis=2,
        tiled=True,
    )
    sectioned = sectioned.reshape(both, devices, cols)
    cosine, sine = table(blocks, devices, blocks, -1.0)
    real = contract("km,cmj->ckj", cosine, sectioned)
    imag = contract("km,cmj->ckj", sine, sectioned)
    offset = rank * cols + lax.broadcasted_iota(jnp.int32, (blocks, cols), 1)
    residue = lax.broadcasted_iota(jnp.int32, (blocks, cols), 0)
    phase = TWO_PI / full * (offset * residue).astype(jnp.float32)
    real, imag = rotate(real, imag, jnp.cos(phase)[None], -jnp.sin(phase)[None])
    outgoing = jnp.stack([real, imag]).reshape(2, both, blocks, 1, 1, cols)
    moved = lax.all_to_all(
        lax.all_to_all(outgoing, "outer", split_axis=2, concat_axis=3, tiled=True),
        "inner",
        split_axis=2,
        concat_axis=4,
        tiled=True,
    )
    moved = moved.reshape(2, both, 2, seg)
    spec_real, spec_imag = forward_rows(moved[0], moved[1])
    sig_real, filt_real = (spec_real[:chans], spec_real[chans:])
    sig_imag, filt_imag = (spec_imag[:chans], spec_imag[chans:])
    real = sig_real * filt_real - sig_imag * filt_imag
    imag = sig_real * filt_imag + sig_imag * filt_real
    real, imag = inverse_rows(real, imag)
    residue = 2 * rank + lax.broadcasted_iota(jnp.int32, (2, seg), 0)
    offset = lax.broadcasted_iota(jnp.int32, (2, seg), 1)
    phase = TWO_PI / full * (offset * residue).astype(jnp.float32)
    real, imag = rotate(real, imag, jnp.cos(phase)[None], jnp.sin(phase)[None])
    returning = jnp.stack([real, imag]).reshape(2, chans, 1, 1, 2, seg)
    gathered = lax.all_to_all(
        lax.all_to_all(returning, "outer", split_axis=5, concat_axis=2, tiled=True),
        "inner",
        split_axis=5,
        concat_axis=3,
        tiled=True,
    )
    gathered = gathered.reshape(2, chans, blocks, cols)
    cosine, sine = table(devices, blocks, blocks, 1.0)
    conv = contract("mk,ckj->cmj", cosine, gathered[0]) - contract("mk,ckj->cmj", sine, gathered[1])
    conv = conv * (1.0 / full)
    conv = lax.all_to_all(
        lax.all_to_all(
            conv.reshape(chans, devices, 1, 1, cols),
            "outer",
            split_axis=1,
            concat_axis=2,
            tiled=True,
        ),
        "inner",
        split_axis=1,
        concat_axis=3,
        tiled=True,
    )
    conv = conv.reshape(chans, seg)
    return gate * (conv + skip_gain[:, None] * product)


def halves(array):
    high = array.astype(ml_dtypes.bfloat16)
    low = (array - high.astype(np.float64)).astype(ml_dtypes.bfloat16)
    return high, low


def transform_tables(devices, seg):
    length = devices * seg
    count = length // LANES
    odd = 2 * np.arange(count) + 1
    angle = 2 * np.pi / (4 * count) * ((odd[:, None] * np.arange(count)[None, :]) % (4 * count))
    first = np.concatenate([np.cos(angle), -np.sin(angle)], axis=0)
    last = np.concatenate([np.cos(angle).T, -np.sin(angle).T], axis=1) / length
    angle = 2 * np.pi / (4 * length) * ((odd[:, None] * np.arange(LANES)[None, :]) % (4 * length))
    twiddle = np.stack([np.cos(angle), np.sin(angle)]).astype(np.float32)
    angle = 2 * np.pi / LANES * ((np.arange(LANES)[:, None] * np.arange(LANES)[None, :]) % LANES)
    cosine, sine = np.cos(angle), np.sin(angle)
    rows = np.block([[cosine, -sine], [sine, cosine]])
    back = np.block([[cosine, sine], [-sine, cosine]])
    first_high, first_low = halves(first)
    rows_high, rows_low = halves(rows)
    back_high, back_low = halves(back)
    last_high, last_low = halves(last)
    return (
        np.concatenate([first_high, first_high, first_low], axis=1),
        np.concatenate([rows_high, rows_high, rows_low], axis=0),
        np.concatenate([back_high, back_high, back_low], axis=0),
        np.concatenate([last_high, last_high, last_low], axis=1),
        twiddle,
    )


def send_orders(outer, inner):
    half = inner // 2
    turns = [at // 2 + half * (at % 2) for at in range(2 * half)] + list(range(2 * half, inner))
    ring = [at ^ (at >> 1) for at in range(outer)] if outer & (outer - 1) == 0 else list(range(outer))
    first = [at * inner + step for at in ring for step in range(inner)]
    second = [at * inner + step for at in ring for step in turns]
    return first, second


def split(array):
    high = array.astype(jnp.bfloat16)
    return high, (array - high.astype(jnp.float32)).astype(jnp.bfloat16)


def dot(left, right):
    return jnp.dot(left, right, preferred_element_type=jnp.float32)


def convolve_kernel(
    devices, chans, seg, data_ref, first_ref, rows_ref, back_ref, last_ref, twiddle_ref, out_ref, signal_ref
):
    parts = seg // LANES
    count = devices * parts
    cosine, sine = twiddle_ref[0], twiddle_ref[1]

    def lanes(at):
        return slice(at * LANES, (at + 1) * LANES)

    first, second = send_orders(lax.axis_size("outer"), lax.axis_size("inner"))

    groups = chans
    each = chans // groups
    at = range(groups)
    for group in at:
        for kind in range(2):
            for chan in range(each):
                for device in range(devices):
                    came = ((device * 2 + kind) * chans + group * each + chan) * parts
                    to = first[device] * parts
                    signal_ref[group, to : to + parts, lanes(kind * each + chan)] = data_ref[came : came + parts, :]

    def start(group):
        high, low = split(signal_ref[group])
        return dot(first_ref[...], jnp.concatenate([high, low, high], axis=0))

    def spectra(begun):
        turned = []
        for signal in range(2 * each):
            real, imag = begun[:count, lanes(signal)], begun[count:, lanes(signal)]
            turned.append(jnp.concatenate([real * cosine + imag * sine, imag * cosine - real * sine], axis=1))
        high, low = split(jnp.concatenate(turned, axis=0))
        return dot(jnp.concatenate([high, low, high], axis=1), rows_ref[...])

    def back(spectrum):
        mid = each * count
        sig_real, sig_imag = spectrum[:mid, :LANES], spectrum[:mid, LANES:]
        filt_real, filt_imag = spectrum[mid:, :LANES], spectrum[mid:, LANES:]
        real = sig_real * filt_real - sig_imag * filt_imag
        imag = sig_real * filt_imag + sig_imag * filt_real
        high, low = split(jnp.concatenate([real, imag], axis=1))
        return dot(jnp.concatenate([high, low, high], axis=1), back_ref[...])

    def end(backed):
        turned = []
        for chan in range(each):
            real = backed[chan * count : (chan + 1) * count, :LANES]
            imag = backed[chan * count : (chan + 1) * count, LANES:]
            turned.append(jnp.concatenate([real * cosine - imag * sine, imag * cosine + real * sine], axis=0))
        high, low = split(jnp.concatenate(turned, axis=1))
        return dot(last_ref[...], jnp.concatenate([high, low, high], axis=0))

    begun = [start(group) for group in at]
    spectrum = [spectra(begun[group]) for group in at]
    backed = [back(spectrum[group]) for group in at]
    conv = [end(backed[group]) for group in at]
    for group in at:
        for chan in range(each):
            own = group * each + chan
            for device in range(devices):
                to = (device * chans + own) * parts
                came = second[device] * parts
                out_ref[to : to + parts, :] = conv[group][came : came + parts, lanes(chan)]


def gather_kernel(order, product_ref, taps_ref, out_ref):
    rows = product_ref.shape[0] * product_ref.shape[1] // LANES // len(order)
    for kind, ref in enumerate((product_ref, taps_ref)):
        source = ref[...].reshape(len(order) * rows, LANES)
        for at, rank in enumerate(order):
            to = (2 * at + kind) * rows
            out_ref[to : to + rows, :] = source[rank * rows : (rank + 1) * rows]


def gate_kernel(order, gate_ref, skip_ref, conv_ref, out_hbm, out_ref, sems):
    chans, seg = gate_ref.shape
    pieces = sems.shape[0]
    step = chans // pieces
    rows = conv_ref.shape[0] // len(order)
    each = len(order) // pieces
    place = {rank: at * rows for at, rank in enumerate(order)}
    copies = []
    for piece in range(pieces):
        at = slice(piece * step, (piece + 1) * step)
        came = [conv_ref[place[rank] : place[rank] + rows, :] for rank in range(piece * each, (piece + 1) * each)]
        conv = jnp.concatenate(came, axis=0).reshape(step, seg)
        out_ref[at, :] = gate_ref[at, :] * (conv + skip_ref[at, :])
        copies.append(pltpu.make_async_copy(out_ref.at[at, :], out_hbm.at[at, :], sems.at[piece]))
        copies[piece].start()
    for copy in copies:
        copy.wait()


def on_core(kernel, shape, moved, flops=10**6, scratch=(), **more):
    return pl.pallas_call(
        kernel,
        out_shape=jax.ShapeDtypeStruct(shape, jnp.float32),
        scratch_shapes=scratch,
        compiler_params=pltpu.CompilerParams(vmem_limit_bytes=32 * 2**20),
        cost_estimate=pl.CostEstimate(flops=flops, bytes_accessed=moved, transcendentals=0),
        **more,
    )


def by_channels(gate, keys, values, taps, skip_gain):
    devices = lax.axis_size("outer") * lax.axis_size("inner")
    chans, seg = keys.shape
    own = chans // devices
    tiles = seg // LANES
    tables = [jnp.asarray(table) for table in transform_tables(devices, seg)]
    orders = send_orders(lax.axis_size("outer"), lax.axis_size("inner"))

    def regroup(rows, order):
        return lax.all_to_all(rows, AXES, split_axis=0, concat_axis=0, tiled=True, axis_index_groups=[order])

    product = keys * values
    product, skip = lax.optimization_barrier((product, skip_gain[:, None] * product))
    sent = on_core(partial(gather_kernel, orders[0]), (2 * chans * tiles, LANES), 4 * chans * seg * 4)(product, taps)
    groups = own
    conv = on_core(
        partial(convolve_kernel, devices, own, seg),
        (chans * tiles, LANES),
        2 * 10**6,
        10**9,
        [pltpu.VMEM((groups, devices * tiles, 2 * own // groups * LANES), jnp.float32)],
    )(regroup(sent, orders[0]), *tables)
    pieces = 4
    return on_core(
        partial(gate_kernel, orders[1]),
        (chans, seg),
        4 * chans * seg * 4,
        scratch=[pltpu.VMEM((chans, seg), jnp.float32), pltpu.SemaphoreType.DMA((pieces,))],
        out_specs=pl.BlockSpec(memory_space=pl.ANY),
    )(gate, skip, regroup(conv, orders[1]))


def on_device(gate, keys, values, taps, skip_gain):
    devices = lax.axis_size("outer") * lax.axis_size("inner")
    chans, seg = keys.shape
    if chans % devices == 0 and seg % LANES == 0 and devices % 8 == 0:
        return by_channels(gate, keys, values, taps, skip_gain)
    return by_sections(gate, keys, values, taps, skip_gain)


def solution(mesh):
    placed = (
        P(None, ("outer", "inner")),
        P(None, ("outer", "inner")),
        P(None, ("outer", "inner")),
        P(None, ("outer", "inner")),
        P(),
    )
    return jax.shard_map(
        on_device,
        mesh=mesh,
        in_specs=placed,
        out_specs=P(None, ("outer", "inner")),
        check_vma=False,
    )
```

```python
from functools import partial
import math

import jax
import jax.numpy as jnp
import ml_dtypes
import numpy as np
from jax import lax
from jax.experimental import pallas as pl
from jax.experimental.pallas import tpu as pltpu
from jax.sharding import PartitionSpec as P

LANES = 128
AXES = ("outer", "inner")

TWO_PI = 2.0 * math.pi
HIGHEST = lax.Precision.HIGHEST


def table(count_a, count_b, modulus, sign):
    left = lax.broadcasted_iota(jnp.int32, (count_a, count_b), 0)
    right = lax.broadcasted_iota(jnp.int32, (count_a, count_b), 1)
    phase = TWO_PI / modulus * (left * right % modulus).astype(jnp.float32)
    return (jnp.cos(phase), sign * jnp.sin(phase))


def mix(form, cosine, sine, real, imag):
    contract = partial(jnp.einsum, precision=HIGHEST)
    return (
        contract(form, cosine, real) - contract(form, sine, imag),
        contract(form, sine, real) + contract(form, cosine, imag),
    )


def rotate(real, imag, cosine, sine):
    return (real * cosine - imag * sine, real * sine + imag * cosine)


def forward_rows(real, imag):
    split = 16
    lead = real.shape[:-1]
    size = real.shape[-1]
    short = size // split
    real = real.reshape(lead + (split, short))
    imag = imag.reshape(lead + (split, short))
    cosine, sine = table(split, split, split, -1.0)
    real, imag = mix("ka,...as->...ks", cosine, sine, real, imag)
    cosine, sine = table(split, short, size, -1.0)
    real, imag = rotate(real, imag, cosine, sine)
    cosine, sine = table(short, short, short, -1.0)
    real, imag = mix("sb,...ks->...bk", cosine, sine, real, imag)
    return (real.reshape(lead + (size,)), imag.reshape(lead + (size,)))


def inverse_rows(real, imag):
    split = 16
    lead = real.shape[:-1]
    size = real.shape[-1]
    short = size // split
    real = real.reshape(lead + (short, split))
    imag = imag.reshape(lead + (short, split))
    cosine, sine = table(short, short, short, 1.0)
    real, imag = mix("sb,...bk->...sk", cosine, sine, real, imag)
    cosine, sine = table(short, split, size, 1.0)
    real, imag = rotate(real, imag, cosine, sine)
    cosine, sine = table(split, split, split, 1.0)
    real, imag = mix("ak,...sk->...as", cosine, sine, real, imag)
    return (real.reshape(lead + (size,)), imag.reshape(lead + (size,)))


def by_sections(gate, keys, values, taps, skip_gain):
    inner_count = lax.axis_size("inner")
    devices = lax.axis_size("outer") * inner_count
    rank = lax.axis_index("outer") * inner_count + lax.axis_index("inner")
    chans, seg = keys.shape
    both = 2 * chans
    cols = seg // devices
    blocks = 2 * devices
    full = blocks * seg
    contract = partial(jnp.einsum, precision=HIGHEST)
    product = keys * values
    source = jnp.concatenate([product, taps], axis=0)
    sectioned = lax.all_to_all(
        lax.all_to_all(
            source.reshape(both, 1, 1, seg), "outer", split_axis=3, concat_axis=1, tiled=True
        ),
        "inner",
        split_axis=3,
        concat_axis=2,
        tiled=True,
    )
    sectioned = sectioned.reshape(both, devices, cols)
    cosine, sine = table(blocks, devices, blocks, -1.0)
    real = contract("km,cmj->ckj", cosine, sectioned)
    imag = contract("km,cmj->ckj", sine, sectioned)
    offset = rank * cols + lax.broadcasted_iota(jnp.int32, (blocks, cols), 1)
    residue = lax.broadcasted_iota(jnp.int32, (blocks, cols), 0)
    phase = TWO_PI / full * (offset * residue).astype(jnp.float32)
    real, imag = rotate(real, imag, jnp.cos(phase)[None], -jnp.sin(phase)[None])
    outgoing = jnp.stack([real, imag]).reshape(2, both, blocks, 1, 1, cols)
    moved = lax.all_to_all(
        lax.all_to_all(outgoing, "outer", split_axis=2, concat_axis=3, tiled=True),
        "inner",
        split_axis=2,
        concat_axis=4,
        tiled=True,
    )
    moved = moved.reshape(2, both, 2, seg)
    spec_real, spec_imag = forward_rows(moved[0], moved[1])
    sig_real, filt_real = (spec_real[:chans], spec_real[chans:])
    sig_imag, filt_imag = (spec_imag[:chans], spec_imag[chans:])
    real = sig_real * filt_real - sig_imag * filt_imag
    imag = sig_real * filt_imag + sig_imag * filt_real
    real, imag = inverse_rows(real, imag)
    residue = 2 * rank + lax.broadcasted_iota(jnp.int32, (2, seg), 0)
    offset = lax.broadcasted_iota(jnp.int32, (2, seg), 1)
    phase = TWO_PI / full * (offset * residue).astype(jnp.float32)
    real, imag = rotate(real, imag, jnp.cos(phase)[None], jnp.sin(phase)[None])
    returning = jnp.stack([real, imag]).reshape(2, chans, 1, 1, 2, seg)
    gathered = lax.all_to_all(
        lax.all_to_all(returning, "outer", split_axis=5, concat_axis=2, tiled=True),
        "inner",
        split_axis=5,
        concat_axis=3,
        tiled=True,
    )
    gathered = gathered.reshape(2, chans, blocks, cols)
    cosine, sine = table(devices, blocks, blocks, 1.0)
    conv = contract("mk,ckj->cmj", cosine, gathered[0]) - contract("mk,ckj->cmj", sine, gathered[1])
    conv = conv * (1.0 / full)
    conv = lax.all_to_all(
        lax.all_to_all(
            conv.reshape(chans, devices, 1, 1, cols),
            "outer",
            split_axis=1,
            concat_axis=2,
            tiled=True,
        ),
        "inner",
        split_axis=1,
        concat_axis=3,
        tiled=True,
    )
    conv = conv.reshape(chans, seg)
    return gate * (conv + skip_gain[:, None] * product)


def halves(array):
    high = array.astype(ml_dtypes.bfloat16)
    low = (array - high.astype(np.float64)).astype(ml_dtypes.bfloat16)
    return high, low


def transform_tables(devices, seg):
    length = devices * seg
    count = length // LANES
    odd = 2 * np.arange(count) + 1
    angle = 2 * np.pi / (4 * count) * ((odd[:, None] * np.arange(count)[None, :]) % (4 * count))
    first = np.concatenate([np.cos(angle), -np.sin(angle)], axis=0)
    last = np.concatenate([np.cos(angle).T, -np.sin(angle).T], axis=1) / length
    angle = 2 * np.pi / (4 * length) * ((odd[:, None] * np.arange(LANES)[None, :]) % (4 * length))
    twiddle = np.stack([np.cos(angle), np.sin(angle)]).astype(np.float32)
    angle = 2 * np.pi / LANES * ((np.arange(LANES)[:, None] * np.arange(LANES)[None, :]) % LANES)
    cosine, sine = np.cos(angle), np.sin(angle)
    rows = np.block([[cosine, -sine], [sine, cosine]])
    back = np.block([[cosine, sine], [-sine, cosine]])
    first_high, first_low = halves(first)
    rows_high, rows_low = halves(rows)
    back_high, back_low = halves(back)
    last_high, last_low = halves(last)
    return (
        np.concatenate([first_high, first_high, first_low], axis=1),
        np.concatenate([rows_high, rows_high, rows_low], axis=0),
        np.concatenate([back_high, back_high, back_low], axis=0),
        np.concatenate([last_high, last_high, last_low], axis=1),
        twiddle,
    )


def send_orders(outer, inner):
    ring = [at ^ (at >> 1) for at in range(outer)] if outer & (outer - 1) == 0 else list(range(outer))
    first = [at * inner + step for at in ring for step in range(inner)]
    second = [at * inner + step for at in ring for step in range(inner)]
    return first, second


def split(array):
    high = array.astype(jnp.bfloat16)
    return high, (array - high.astype(jnp.float32)).astype(jnp.bfloat16)


def dot(left, right):
    return jnp.dot(left, right, preferred_element_type=jnp.float32)


def convolve_kernel(
    devices, chans, seg, data_ref, first_ref, rows_ref, back_ref, last_ref, twiddle_ref, out_ref, signal_ref
):
    parts = seg // LANES
    count = devices * parts
    cosine, sine = twiddle_ref[0], twiddle_ref[1]

    def lanes(at):
        return slice(at * LANES, (at + 1) * LANES)

    first, second = send_orders(lax.axis_size("outer"), lax.axis_size("inner"))

    groups = chans
    each = chans // groups
    at = range(groups)
    for group in at:
        for kind in range(2):
            for chan in range(each):
                for device in range(devices):
                    came = ((device * 2 + kind) * chans + group * each + chan) * parts
                    to = first[device] * parts
                    signal_ref[group, to : to + parts, lanes(kind * each + chan)] = data_ref[came : came + parts, :]

    def start(group):
        high, low = split(signal_ref[group])
        return dot(first_ref[...], jnp.concatenate([high, low, high], axis=0))

    def spectra(begun):
        turned = []
        for signal in range(2 * each):
            real, imag = begun[:count, lanes(signal)], begun[count:, lanes(signal)]
            turned.append(jnp.concatenate([real * cosine + imag * sine, imag * cosine - real * sine], axis=1))
        high, low = split(jnp.concatenate(turned, axis=0))
        return dot(jnp.concatenate([high, low, high], axis=1), rows_ref[...])

    def back(spectrum):
        mid = each * count
        sig_real, sig_imag = spectrum[:mid, :LANES], spectrum[:mid, LANES:]
        filt_real, filt_imag = spectrum[mid:, :LANES], spectrum[mid:, LANES:]
        real = sig_real * filt_real - sig_imag * filt_imag
        imag = sig_real * filt_imag + sig_imag * filt_real
        high, low = split(jnp.concatenate([real, imag], axis=1))
        return dot(jnp.concatenate([high, low, high], axis=1), back_ref[...])

    def end(backed):
        turned = []
        for chan in range(each):
            real = backed[chan * count : (chan + 1) * count, :LANES]
            imag = backed[chan * count : (chan + 1) * count, LANES:]
            turned.append(jnp.concatenate([real * cosine - imag * sine, imag * cosine + real * sine], axis=0))
        high, low = split(jnp.concatenate(turned, axis=1))
        return dot(last_ref[...], jnp.concatenate([high, low, high], axis=0))

    begun = [start(group) for group in at]
    spectrum = [spectra(begun[group]) for group in at]
    backed = [back(spectrum[group]) for group in at]
    conv = [end(backed[group]) for group in at]
    for group in at:
        for chan in range(each):
            own = group * each + chan
            for device in range(devices):
                to = (device * chans + own) * parts
                came = second[device] * parts
                out_ref[to : to + parts, :] = conv[group][came : came + parts, lanes(chan)]


def gather_kernel(order, product_ref, taps_ref, out_ref):
    rows = product_ref.shape[0] * product_ref.shape[1] // LANES // len(order)
    for kind, ref in enumerate((product_ref, taps_ref)):
        source = ref[...].reshape(len(order) * rows, LANES)
        for at, rank in enumerate(order):
            to = (2 * at + kind) * rows
            out_ref[to : to + rows, :] = source[rank * rows : (rank + 1) * rows]


def gate_kernel(order, gate_ref, skip_ref, conv_ref, out_hbm, out_ref, sems):
    chans, seg = gate_ref.shape
    pieces = sems.shape[0]
    step = chans // pieces
    rows = conv_ref.shape[0] // len(order)
    each = len(order) // pieces
    place = {rank: at * rows for at, rank in enumerate(order)}
    copies = []
    for piece in range(pieces):
        at = slice(piece * step, (piece + 1) * step)
        came = [conv_ref[place[rank] : place[rank] + rows, :] for rank in range(piece * each, (piece + 1) * each)]
        conv = jnp.concatenate(came, axis=0).reshape(step, seg)
        out_ref[at, :] = gate_ref[at, :] * (conv + skip_ref[at, :])
        copies.append(pltpu.make_async_copy(out_ref.at[at, :], out_hbm.at[at, :], sems.at[piece]))
        copies[piece].start()
    for copy in copies:
        copy.wait()


def on_core(kernel, shape, moved, flops=10**6, scratch=(), **more):
    return pl.pallas_call(
        kernel,
        out_shape=jax.ShapeDtypeStruct(shape, jnp.float32),
        scratch_shapes=scratch,
        compiler_params=pltpu.CompilerParams(vmem_limit_bytes=32 * 2**20),
        cost_estimate=pl.CostEstimate(flops=flops, bytes_accessed=moved, transcendentals=0),
        **more,
    )


def by_channels(gate, keys, values, taps, skip_gain):
    devices = lax.axis_size("outer") * lax.axis_size("inner")
    chans, seg = keys.shape
    own = chans // devices
    tiles = seg // LANES
    tables = [jnp.asarray(table) for table in transform_tables(devices, seg)]
    orders = send_orders(lax.axis_size("outer"), lax.axis_size("inner"))

    def regroup(rows, order):
        return lax.all_to_all(rows, AXES, split_axis=0, concat_axis=0, tiled=True, axis_index_groups=[order])

    product = keys * values
    product, skip = lax.optimization_barrier((product, skip_gain[:, None] * product))
    sent = on_core(partial(gather_kernel, orders[0]), (2 * chans * tiles, LANES), 4 * chans * seg * 4)(product, taps)
    groups = own
    conv = on_core(
        partial(convolve_kernel, devices, own, seg),
        (chans * tiles, LANES),
        2 * 10**6,
        10**9,
        [pltpu.VMEM((groups, devices * tiles, 2 * own // groups * LANES), jnp.float32)],
    )(regroup(sent, orders[0]), *tables)
    pieces = 4
    return on_core(
        partial(gate_kernel, orders[1]),
        (chans, seg),
        4 * chans * seg * 4,
        scratch=[pltpu.VMEM((chans, seg), jnp.float32), pltpu.SemaphoreType.DMA((pieces,))],
        out_specs=pl.BlockSpec(memory_space=pl.ANY),
    )(gate, skip, regroup(conv, orders[1]))


def on_device(gate, keys, values, taps, skip_gain):
    devices = lax.axis_size("outer") * lax.axis_size("inner")
    chans, seg = keys.shape
    if chans % devices == 0 and seg % LANES == 0 and devices % 8 == 0:
        return by_channels(gate, keys, values, taps, skip_gain)
    return by_sections(gate, keys, values, taps, skip_gain)


def solution(mesh):
    placed = (
        P(None, ("outer", "inner")),
        P(None, ("outer", "inner")),
        P(None, ("outer", "inner")),
        P(None, ("outer", "inner")),
        P(),
    )
    return jax.shard_map(
        on_device,
        mesh=mesh,
        in_specs=placed,
        out_specs=P(None, ("outer", "inner")),
        check_vma=False,
    )
```

```python
from functools import partial
import math

import jax
import jax.numpy as jnp
import ml_dtypes
import numpy as np
from jax import lax
from jax.experimental import pallas as pl
from jax.experimental.pallas import tpu as pltpu
from jax.sharding import PartitionSpec as P

LANES = 128
AXES = ("outer", "inner")

TWO_PI = 2.0 * math.pi
HIGHEST = lax.Precision.HIGHEST


def table(count_a, count_b, modulus, sign):
    left = lax.broadcasted_iota(jnp.int32, (count_a, count_b), 0)
    right = lax.broadcasted_iota(jnp.int32, (count_a, count_b), 1)
    phase = TWO_PI / modulus * (left * right % modulus).astype(jnp.float32)
    return (jnp.cos(phase), sign * jnp.sin(phase))


def mix(form, cosine, sine, real, imag):
    contract = partial(jnp.einsum, precision=HIGHEST)
    return (
        contract(form, cosine, real) - contract(form, sine, imag),
        contract(form, sine, real) + contract(form, cosine, imag),
    )


def rotate(real, imag, cosine, sine):
    return (real * cosine - imag * sine, real * sine + imag * cosine)


def forward_rows(real, imag):
    split = 16
    lead = real.shape[:-1]
    size = real.shape[-1]
    short = size // split
    real = real.reshape(lead + (split, short))
    imag = imag.reshape(lead + (split, short))
    cosine, sine = table(split, split, split, -1.0)
    real, imag = mix("ka,...as->...ks", cosine, sine, real, imag)
    cosine, sine = table(split, short, size, -1.0)
    real, imag = rotate(real, imag, cosine, sine)
    cosine, sine = table(short, short, short, -1.0)
    real, imag = mix("sb,...ks->...bk", cosine, sine, real, imag)
    return (real.reshape(lead + (size,)), imag.reshape(lead + (size,)))


def inverse_rows(real, imag):
    split = 16
    lead = real.shape[:-1]
    size = real.shape[-1]
    short = size // split
    real = real.reshape(lead + (short, split))
    imag = imag.reshape(lead + (short, split))
    cosine, sine = table(short, short, short, 1.0)
    real, imag = mix("sb,...bk->...sk", cosine, sine, real, imag)
    cosine, sine = table(short, split, size, 1.0)
    real, imag = rotate(real, imag, cosine, sine)
    cosine, sine = table(split, split, split, 1.0)
    real, imag = mix("ak,...sk->...as", cosine, sine, real, imag)
    return (real.reshape(lead + (size,)), imag.reshape(lead + (size,)))


def by_sections(gate, keys, values, taps, skip_gain):
    inner_count = lax.axis_size("inner")
    devices = lax.axis_size("outer") * inner_count
    rank = lax.axis_index("outer") * inner_count + lax.axis_index("inner")
    chans, seg = keys.shape
    both = 2 * chans
    cols = seg // devices
    blocks = 2 * devices
    full = blocks * seg
    contract = partial(jnp.einsum, precision=HIGHEST)
    product = keys * values
    source = jnp.concatenate([product, taps], axis=0)
    sectioned = lax.all_to_all(
        lax.all_to_all(
            source.reshape(both, 1, 1, seg), "outer", split_axis=3, concat_axis=1, tiled=True
        ),
        "inner",
        split_axis=3,
        concat_axis=2,
        tiled=True,
    )
    sectioned = sectioned.reshape(both, devices, cols)
    cosine, sine = table(blocks, devices, blocks, -1.0)
    real = contract("km,cmj->ckj", cosine, sectioned)
    imag = contract("km,cmj->ckj", sine, sectioned)
    offset = rank * cols + lax.broadcasted_iota(jnp.int32, (blocks, cols), 1)
    residue = lax.broadcasted_iota(jnp.int32, (blocks, cols), 0)
    phase = TWO_PI / full * (offset * residue).astype(jnp.float32)
    real, imag = rotate(real, imag, jnp.cos(phase)[None], -jnp.sin(phase)[None])
    outgoing = jnp.stack([real, imag]).reshape(2, both, blocks, 1, 1, cols)
    moved = lax.all_to_all(
        lax.all_to_all(outgoing, "outer", split_axis=2, concat_axis=3, tiled=True),
        "inner",
        split_axis=2,
        concat_axis=4,
        tiled=True,
    )
    moved = moved.reshape(2, both, 2, seg)
    spec_real, spec_imag = forward_rows(moved[0], moved[1])
    sig_real, filt_real = (spec_real[:chans], spec_real[chans:])
    sig_imag, filt_imag = (spec_imag[:chans], spec_imag[chans:])
    real = sig_real * filt_real - sig_imag * filt_imag
    imag = sig_real * filt_imag + sig_imag * filt_real
    real, imag = inverse_rows(real, imag)
    residue = 2 * rank + lax.broadcasted_iota(jnp.int32, (2, seg), 0)
    offset = lax.broadcasted_iota(jnp.int32, (2, seg), 1)
    phase = TWO_PI / full * (offset * residue).astype(jnp.float32)
    real, imag = rotate(real, imag, jnp.cos(phase)[None], jnp.sin(phase)[None])
    returning = jnp.stack([real, imag]).reshape(2, chans, 1, 1, 2, seg)
    gathered = lax.all_to_all(
        lax.all_to_all(returning, "outer", split_axis=5, concat_axis=2, tiled=True),
        "inner",
        split_axis=5,
        concat_axis=3,
        tiled=True,
    )
    gathered = gathered.reshape(2, chans, blocks, cols)
    cosine, sine = table(devices, blocks, blocks, 1.0)
    conv = contract("mk,ckj->cmj", cosine, gathered[0]) - contract("mk,ckj->cmj", sine, gathered[1])
    conv = conv * (1.0 / full)
    conv = lax.all_to_all(
        lax.all_to_all(
            conv.reshape(chans, devices, 1, 1, cols),
            "outer",
            split_axis=1,
            concat_axis=2,
            tiled=True,
        ),
        "inner",
        split_axis=1,
        concat_axis=3,
        tiled=True,
    )
    conv = conv.reshape(chans, seg)
    return gate * (conv + skip_gain[:, None] * product)


def halves(array):
    high = array.astype(ml_dtypes.bfloat16)
    low = (array - high.astype(np.float64)).astype(ml_dtypes.bfloat16)
    return high, low


def transform_tables(devices, seg):
    length = devices * seg
    count = length // LANES
    odd = 2 * np.arange(count) + 1
    angle = 2 * np.pi / (4 * count) * ((odd[:, None] * np.arange(count)[None, :]) % (4 * count))
    first = np.concatenate([np.cos(angle), -np.sin(angle)], axis=0)
    last = np.concatenate([np.cos(angle).T, -np.sin(angle).T], axis=1) / length
    angle = 2 * np.pi / (4 * length) * ((odd[:, None] * np.arange(LANES)[None, :]) % (4 * length))
    twiddle = np.stack([np.cos(angle), np.sin(angle)]).astype(np.float32)
    angle = 2 * np.pi / LANES * ((np.arange(LANES)[:, None] * np.arange(LANES)[None, :]) % LANES)
    cosine, sine = np.cos(angle), np.sin(angle)
    rows = np.block([[cosine, -sine], [sine, cosine]])
    back = np.block([[cosine, sine], [-sine, cosine]])
    first_high, first_low = halves(first)
    rows_high, rows_low = halves(rows)
    back_high, back_low = halves(back)
    last_high, last_low = halves(last)
    return (
        np.concatenate([first_high, first_high, first_low], axis=1),
        np.concatenate([rows_high, rows_high, rows_low], axis=0),
        np.concatenate([back_high, back_high, back_low], axis=0),
        np.concatenate([last_high, last_high, last_low], axis=1),
        twiddle,
    )


def send_orders(outer, inner):
    ring = [at ^ (at >> 1) for at in range(outer)] if outer & (outer - 1) == 0 else list(range(outer))
    first = [at * inner + step for at in ring for step in range(inner)]
    second = list(range(outer * inner))
    return first, second


def split(array):
    high = array.astype(jnp.bfloat16)
    return high, (array - high.astype(jnp.float32)).astype(jnp.bfloat16)


def dot(left, right):
    return jnp.dot(left, right, preferred_element_type=jnp.float32)


def convolve_kernel(
    devices, chans, seg, data_ref, first_ref, rows_ref, back_ref, last_ref, twiddle_ref, out_ref, signal_ref
):
    parts = seg // LANES
    count = devices * parts
    cosine, sine = twiddle_ref[0], twiddle_ref[1]

    def lanes(at):
        return slice(at * LANES, (at + 1) * LANES)

    first, second = send_orders(lax.axis_size("outer"), lax.axis_size("inner"))

    groups = chans
    each = chans // groups
    at = range(groups)
    for group in at:
        for kind in range(2):
            for chan in range(each):
                for device in range(devices):
                    came = ((device * 2 + kind) * chans + group * each + chan) * parts
                    to = first[device] * parts
                    signal_ref[group, to : to + parts, lanes(kind * each + chan)] = data_ref[came : came + parts, :]

    def start(group):
        high, low = split(signal_ref[group])
        return dot(first_ref[...], jnp.concatenate([high, low, high], axis=0))

    def spectra(begun):
        turned = []
        for signal in range(2 * each):
            real, imag = begun[:count, lanes(signal)], begun[count:, lanes(signal)]
            turned.append(jnp.concatenate([real * cosine + imag * sine, imag * cosine - real * sine], axis=1))
        high, low = split(jnp.concatenate(turned, axis=0))
        return dot(jnp.concatenate([high, low, high], axis=1), rows_ref[...])

    def back(spectrum):
        mid = each * count
        sig_real, sig_imag = spectrum[:mid, :LANES], spectrum[:mid, LANES:]
        filt_real, filt_imag = spectrum[mid:, :LANES], spectrum[mid:, LANES:]
        real = sig_real * filt_real - sig_imag * filt_imag
        imag = sig_real * filt_imag + sig_imag * filt_real
        high, low = split(jnp.concatenate([real, imag], axis=1))
        return dot(jnp.concatenate([high, low, high], axis=1), back_ref[...])

    def end(backed):
        turned = []
        for chan in range(each):
            real = backed[chan * count : (chan + 1) * count, :LANES]
            imag = backed[chan * count : (chan + 1) * count, LANES:]
            turned.append(jnp.concatenate([real * cosine - imag * sine, imag * cosine + real * sine], axis=0))
        high, low = split(jnp.concatenate(turned, axis=1))
        return dot(last_ref[...], jnp.concatenate([high, low, high], axis=0))

    begun = [start(group) for group in at]
    spectrum = [spectra(begun[group]) for group in at]
    backed = [back(spectrum[group]) for group in at]
    conv = [end(backed[group]) for group in at]
    for group in at:
        for chan in range(each):
            own = group * each + chan
            for device in range(devices):
                to = (device * chans + own) * parts
                came = second[device] * parts
                out_ref[to : to + parts, :] = conv[group][came : came + parts, lanes(chan)]


def gather_kernel(order, product_ref, taps_ref, out_ref):
    rows = product_ref.shape[0] * product_ref.shape[1] // LANES // len(order)
    for kind, ref in enumerate((product_ref, taps_ref)):
        source = ref[...].reshape(len(order) * rows, LANES)
        for at, rank in enumerate(order):
            to = (2 * at + kind) * rows
            out_ref[to : to + rows, :] = source[rank * rows : (rank + 1) * rows]


def gate_kernel(order, gate_ref, skip_ref, conv_ref, out_hbm, out_ref, sems):
    chans, seg = gate_ref.shape
    pieces = sems.shape[0]
    step = chans // pieces
    rows = conv_ref.shape[0] // len(order)
    each = len(order) // pieces
    place = {rank: at * rows for at, rank in enumerate(order)}
    copies = []
    for piece in range(pieces):
        at = slice(piece * step, (piece + 1) * step)
        came = [conv_ref[place[rank] : place[rank] + rows, :] for rank in range(piece * each, (piece + 1) * each)]
        conv = jnp.concatenate(came, axis=0).reshape(step, seg)
        out_ref[at, :] = gate_ref[at, :] * (conv + skip_ref[at, :])
        copies.append(pltpu.make_async_copy(out_ref.at[at, :], out_hbm.at[at, :], sems.at[piece]))
        copies[piece].start()
    for copy in copies:
        copy.wait()


def on_core(kernel, shape, moved, flops=10**6, scratch=(), **more):
    return pl.pallas_call(
        kernel,
        out_shape=jax.ShapeDtypeStruct(shape, jnp.float32),
        scratch_shapes=scratch,
        compiler_params=pltpu.CompilerParams(vmem_limit_bytes=32 * 2**20),
        cost_estimate=pl.CostEstimate(flops=flops, bytes_accessed=moved, transcendentals=0),
        **more,
    )


def by_channels(gate, keys, values, taps, skip_gain):
    devices = lax.axis_size("outer") * lax.axis_size("inner")
    chans, seg = keys.shape
    own = chans // devices
    tiles = seg // LANES
    tables = [jnp.asarray(table) for table in transform_tables(devices, seg)]
    orders = send_orders(lax.axis_size("outer"), lax.axis_size("inner"))

    def regroup(rows, order):
        return lax.all_to_all(rows, AXES, split_axis=0, concat_axis=0, tiled=True, axis_index_groups=[order])

    product = keys * values
    product, skip = lax.optimization_barrier((product, skip_gain[:, None] * product))
    sent = on_core(partial(gather_kernel, orders[0]), (2 * chans * tiles, LANES), 4 * chans * seg * 4)(product, taps)
    groups = own
    conv = on_core(
        partial(convolve_kernel, devices, own, seg),
        (chans * tiles, LANES),
        2 * 10**6,
        10**9,
        [pltpu.VMEM((groups, devices * tiles, 2 * own // groups * LANES), jnp.float32)],
    )(regroup(sent, orders[0]), *tables)
    pieces = 4
    return on_core(
        partial(gate_kernel, orders[1]),
        (chans, seg),
        4 * chans * seg * 4,
        scratch=[pltpu.VMEM((chans, seg), jnp.float32), pltpu.SemaphoreType.DMA((pieces,))],
        out_specs=pl.BlockSpec(memory_space=pl.ANY),
    )(gate, skip, regroup(conv, orders[1]))


def on_device(gate, keys, values, taps, skip_gain):
    devices = lax.axis_size("outer") * lax.axis_size("inner")
    chans, seg = keys.shape
    if chans % devices == 0 and seg % LANES == 0 and devices % 8 == 0:
        return by_channels(gate, keys, values, taps, skip_gain)
    return by_sections(gate, keys, values, taps, skip_gain)


def solution(mesh):
    placed = (
        P(None, ("outer", "inner")),
        P(None, ("outer", "inner")),
        P(None, ("outer", "inner")),
        P(None, ("outer", "inner")),
        P(),
    )
    return jax.shard_map(
        on_device,
        mesh=mesh,
        in_specs=placed,
        out_specs=P(None, ("outer", "inner")),
        check_vma=False,
    )
```

```python
from functools import partial
import math

import jax
import jax.numpy as jnp
import ml_dtypes
import numpy as np
from jax import lax
from jax.experimental import pallas as pl
from jax.experimental.pallas import tpu as pltpu
from jax.sharding import PartitionSpec as P

LANES = 128
AXES = ("outer", "inner")

TWO_PI = 2.0 * math.pi
HIGHEST = lax.Precision.HIGHEST


def table(count_a, count_b, modulus, sign):
    left = lax.broadcasted_iota(jnp.int32, (count_a, count_b), 0)
    right = lax.broadcasted_iota(jnp.int32, (count_a, count_b), 1)
    phase = TWO_PI / modulus * (left * right % modulus).astype(jnp.float32)
    return (jnp.cos(phase), sign * jnp.sin(phase))


def mix(form, cosine, sine, real, imag):
    contract = partial(jnp.einsum, precision=HIGHEST)
    return (
        contract(form, cosine, real) - contract(form, sine, imag),
        contract(form, sine, real) + contract(form, cosine, imag),
    )


def rotate(real, imag, cosine, sine):
    return (real * cosine - imag * sine, real * sine + imag * cosine)


def forward_rows(real, imag):
    split = 16
    lead = real.shape[:-1]
    size = real.shape[-1]
    short = size // split
    real = real.reshape(lead + (split, short))
    imag = imag.reshape(lead + (split, short))
    cosine, sine = table(split, split, split, -1.0)
    real, imag = mix("ka,...as->...ks", cosine, sine, real, imag)
    cosine, sine = table(split, short, size, -1.0)
    real, imag = rotate(real, imag, cosine, sine)
    cosine, sine = table(short, short, short, -1.0)
    real, imag = mix("sb,...ks->...bk", cosine, sine, real, imag)
    return (real.reshape(lead + (size,)), imag.reshape(lead + (size,)))


def inverse_rows(real, imag):
    split = 16
    lead = real.shape[:-1]
    size = real.shape[-1]
    short = size // split
    real = real.reshape(lead + (short, split))
    imag = imag.reshape(lead + (short, split))
    cosine, sine = table(short, short, short, 1.0)
    real, imag = mix("sb,...bk->...sk", cosine, sine, real, imag)
    cosine, sine = table(short, split, size, 1.0)
    real, imag = rotate(real, imag, cosine, sine)
    cosine, sine = table(split, split, split, 1.0)
    real, imag = mix("ak,...sk->...as", cosine, sine, real, imag)
    return (real.reshape(lead + (size,)), imag.reshape(lead + (size,)))


def by_sections(gate, keys, values, taps, skip_gain):
    inner_count = lax.axis_size("inner")
    devices = lax.axis_size("outer") * inner_count
    rank = lax.axis_index("outer") * inner_count + lax.axis_index("inner")
    chans, seg = keys.shape
    both = 2 * chans
    cols = seg // devices
    blocks = 2 * devices
    full = blocks * seg
    contract = partial(jnp.einsum, precision=HIGHEST)
    product = keys * values
    source = jnp.concatenate([product, taps], axis=0)
    sectioned = lax.all_to_all(
        lax.all_to_all(
            source.reshape(both, 1, 1, seg), "outer", split_axis=3, concat_axis=1, tiled=True
        ),
        "inner",
        split_axis=3,
        concat_axis=2,
        tiled=True,
    )
    sectioned = sectioned.reshape(both, devices, cols)
    cosine, sine = table(blocks, devices, blocks, -1.0)
    real = contract("km,cmj->ckj", cosine, sectioned)
    imag = contract("km,cmj->ckj", sine, sectioned)
    offset = rank * cols + lax.broadcasted_iota(jnp.int32, (blocks, cols), 1)
    residue = lax.broadcasted_iota(jnp.int32, (blocks, cols), 0)
    phase = TWO_PI / full * (offset * residue).astype(jnp.float32)
    real, imag = rotate(real, imag, jnp.cos(phase)[None], -jnp.sin(phase)[None])
    outgoing = jnp.stack([real, imag]).reshape(2, both, blocks, 1, 1, cols)
    moved = lax.all_to_all(
        lax.all_to_all(outgoing, "outer", split_axis=2, concat_axis=3, tiled=True),
        "inner",
        split_axis=2,
        concat_axis=4,
        tiled=True,
    )
    moved = moved.reshape(2, both, 2, seg)
    spec_real, spec_imag = forward_rows(moved[0], moved[1])
    sig_real, filt_real = (spec_real[:chans], spec_real[chans:])
    sig_imag, filt_imag = (spec_imag[:chans], spec_imag[chans:])
    real = sig_real * filt_real - sig_imag * filt_imag
    imag = sig_real * filt_imag + sig_imag * filt_real
    real, imag = inverse_rows(real, imag)
    residue = 2 * rank + lax.broadcasted_iota(jnp.int32, (2, seg), 0)
    offset = lax.broadcasted_iota(jnp.int32, (2, seg), 1)
    phase = TWO_PI / full * (offset * residue).astype(jnp.float32)
    real, imag = rotate(real, imag, jnp.cos(phase)[None], jnp.sin(phase)[None])
    returning = jnp.stack([real, imag]).reshape(2, chans, 1, 1, 2, seg)
    gathered = lax.all_to_all(
        lax.all_to_all(returning, "outer", split_axis=5, concat_axis=2, tiled=True),
        "inner",
        split_axis=5,
        concat_axis=3,
        tiled=True,
    )
    gathered = gathered.reshape(2, chans, blocks, cols)
    cosine, sine = table(devices, blocks, blocks, 1.0)
    conv = contract("mk,ckj->cmj", cosine, gathered[0]) - contract("mk,ckj->cmj", sine, gathered[1])
    conv = conv * (1.0 / full)
    conv = lax.all_to_all(
        lax.all_to_all(
            conv.reshape(chans, devices, 1, 1, cols),
            "outer",
            split_axis=1,
            concat_axis=2,
            tiled=True,
        ),
        "inner",
        split_axis=1,
        concat_axis=3,
        tiled=True,
    )
    conv = conv.reshape(chans, seg)
    return gate * (conv + skip_gain[:, None] * product)


def halves(array):
    high = array.astype(ml_dtypes.bfloat16)
    low = (array - high.astype(np.float64)).astype(ml_dtypes.bfloat16)
    return high, low


def transform_tables(devices, seg):
    length = devices * seg
    count = length // LANES
    odd = 2 * np.arange(count) + 1
    angle = 2 * np.pi / (4 * count) * ((odd[:, None] * np.arange(count)[None, :]) % (4 * count))
    first = np.concatenate([np.cos(angle), -np.sin(angle)], axis=0)
    last = np.concatenate([np.cos(angle).T, -np.sin(angle).T], axis=1) / length
    angle = 2 * np.pi / (4 * length) * ((odd[:, None] * np.arange(LANES)[None, :]) % (4 * length))
    twiddle = np.stack([np.cos(angle), np.sin(angle)]).astype(np.float32)
    angle = 2 * np.pi / LANES * ((np.arange(LANES)[:, None] * np.arange(LANES)[None, :]) % LANES)
    cosine, sine = np.cos(angle), np.sin(angle)
    rows = np.block([[cosine, -sine], [sine, cosine]])
    back = np.block([[cosine, sine], [-sine, cosine]])
    first_high, first_low = halves(first)
    rows_high, rows_low = halves(rows)
    back_high, back_low = halves(back)
    last_high, last_low = halves(last)
    return (
        np.concatenate([first_high, first_high, first_low, first_low], axis=1),
        np.concatenate([rows_high, rows_high, rows_high, rows_low], axis=0),
        np.concatenate([back_high, back_high, back_low], axis=0),
        np.concatenate([last_high, last_high, last_low], axis=1),
        twiddle,
    )


def send_order(outer, inner):
    ring = [at ^ (at >> 1) for at in range(outer)] if outer & (outer - 1) == 0 else list(range(outer))
    return [at * inner + step for at in ring for step in range(inner)]


def split(array, count=2):
    parts = []
    for _ in range(count):
        parts.append(array.astype(jnp.bfloat16))
        array = array - parts[-1].astype(jnp.float32)
    return parts


def dot(left, right):
    return jnp.dot(left, right, preferred_element_type=jnp.float32)


def convolve_kernel(
    devices, chans, seg, data_ref, first_ref, rows_ref, back_ref, last_ref, twiddle_ref, out_ref, signal_ref
):
    parts = seg // LANES
    count = devices * parts
    cosine, sine = twiddle_ref[0], twiddle_ref[1]

    def lanes(at):
        return slice(at * LANES, (at + 1) * LANES)

    order = send_order(lax.axis_size("outer"), lax.axis_size("inner"))

    groups = chans
    each = chans // groups
    at = range(groups)
    for group in at:
        for kind in range(2):
            for chan in range(each):
                for device in range(devices):
                    came = ((device * 2 + kind) * chans + group * each + chan) * parts
                    to = order[device] * parts
                    signal_ref[group, to : to + parts, lanes(kind * each + chan)] = data_ref[came : came + parts, :]

    def start(group):
        high, low = split(signal_ref[group])
        return dot(first_ref[...], jnp.concatenate([high, low, high, low], axis=0))

    def spectra(begun):
        turned = []
        for signal in range(2 * each):
            real, imag = begun[:count, lanes(signal)], begun[count:, lanes(signal)]
            turned.append(jnp.concatenate([real * cosine + imag * sine, imag * cosine - real * sine], axis=1))
        high, low, rest = split(jnp.concatenate(turned, axis=0), 3)
        return dot(jnp.concatenate([high, low, rest, high], axis=1), rows_ref[...])

    def back(spectrum):
        mid = each * count
        sig_real, sig_imag = spectrum[:mid, :LANES], spectrum[:mid, LANES:]
        filt_real, filt_imag = spectrum[mid:, :LANES], spectrum[mid:, LANES:]
        real = sig_real * filt_real - sig_imag * filt_imag
        imag = sig_real * filt_imag + sig_imag * filt_real
        high, low = split(jnp.concatenate([real, imag], axis=1))
        return dot(jnp.concatenate([high, low, high], axis=1), back_ref[...])

    def end(backed):
        turned = []
        for chan in range(each):
            real = backed[chan * count : (chan + 1) * count, :LANES]
            imag = backed[chan * count : (chan + 1) * count, LANES:]
            turned.append(jnp.concatenate([real * cosine - imag * sine, imag * cosine + real * sine], axis=0))
        high, low = split(jnp.concatenate(turned, axis=1))
        return dot(last_ref[...], jnp.concatenate([high, low, high], axis=0))

    begun = [start(group) for group in at]
    spectrum = [spectra(begun[group]) for group in at]
    backed = [back(spectrum[group]) for group in at]
    conv = [end(backed[group]) for group in at]
    for group in at:
        for chan in range(each):
            own = group * each + chan
            for device in range(devices):
                to = (device * chans + own) * parts
                came = order[device] * parts
                out_ref[to : to + parts, :] = conv[group][came : came + parts, lanes(chan)]


def gather_kernel(order, product_ref, taps_ref, out_ref):
    rows = product_ref.shape[0] * product_ref.shape[1] // LANES // len(order)
    for kind, ref in enumerate((product_ref, taps_ref)):
        source = ref[...].reshape(len(order) * rows, LANES)
        for at, rank in enumerate(order):
            to = (2 * at + kind) * rows
            out_ref[to : to + rows, :] = source[rank * rows : (rank + 1) * rows]


def gate_kernel(order, gate_ref, skip_ref, conv_ref, out_hbm, out_ref, sems):
    chans, seg = gate_ref.shape
    pieces = sems.shape[0]
    step = chans // pieces
    rows = conv_ref.shape[0] // len(order)
    each = len(order) // pieces
    place = {rank: at * rows for at, rank in enumerate(order)}
    copies = []
    for piece in range(pieces):
        at = slice(piece * step, (piece + 1) * step)
        came = [conv_ref[place[rank] : place[rank] + rows, :] for rank in range(piece * each, (piece + 1) * each)]
        conv = jnp.concatenate(came, axis=0).reshape(step, seg)
        out_ref[at, :] = gate_ref[at, :] * (conv + skip_ref[at, :])
        copies.append(pltpu.make_async_copy(out_ref.at[at, :], out_hbm.at[at, :], sems.at[piece]))
        copies[piece].start()
    for copy in copies:
        copy.wait()


def on_core(kernel, shape, moved, flops=10**6, scratch=(), **more):
    return pl.pallas_call(
        kernel,
        out_shape=jax.ShapeDtypeStruct(shape, jnp.float32),
        scratch_shapes=scratch,
        compiler_params=pltpu.CompilerParams(vmem_limit_bytes=32 * 2**20),
        cost_estimate=pl.CostEstimate(flops=flops, bytes_accessed=moved, transcendentals=0),
        **more,
    )


def by_channels(gate, keys, values, taps, skip_gain):
    devices = lax.axis_size("outer") * lax.axis_size("inner")
    chans, seg = keys.shape
    own = chans // devices
    tiles = seg // LANES
    tables = [jnp.asarray(table) for table in transform_tables(devices, seg)]
    order = send_order(lax.axis_size("outer"), lax.axis_size("inner"))

    def regroup(rows):
        return lax.all_to_all(rows, AXES, split_axis=0, concat_axis=0, tiled=True, axis_index_groups=[order])

    product = keys * values
    product, skip = lax.optimization_barrier((product, skip_gain[:, None] * product))
    sent = on_core(partial(gather_kernel, order), (2 * chans * tiles, LANES), 4 * chans * seg * 4)(product, taps)
    groups = own
    conv = on_core(
        partial(convolve_kernel, devices, own, seg),
        (chans * tiles, LANES),
        2 * 10**6,
        10**9,
        [pltpu.VMEM((groups, devices * tiles, 2 * own // groups * LANES), jnp.float32)],
    )(regroup(sent), *tables)
    pieces = 4
    return on_core(
        partial(gate_kernel, order),
        (chans, seg),
        4 * chans * seg * 4,
        scratch=[pltpu.VMEM((chans, seg), jnp.float32), pltpu.SemaphoreType.DMA((pieces,))],
        out_specs=pl.BlockSpec(memory_space=pl.ANY),
    )(gate, skip, regroup(conv))


def on_device(gate, keys, values, taps, skip_gain):
    devices = lax.axis_size("outer") * lax.axis_size("inner")
    chans, seg = keys.shape
    if chans % devices == 0 and seg % LANES == 0 and devices % 8 == 0:
        return by_channels(gate, keys, values, taps, skip_gain)
    return by_sections(gate, keys, values, taps, skip_gain)


def solution(mesh):
    placed = (
        P(None, ("outer", "inner")),
        P(None, ("outer", "inner")),
        P(None, ("outer", "inner")),
        P(None, ("outer", "inner")),
        P(),
    )
    return jax.shard_map(
        on_device,
        mesh=mesh,
        in_specs=placed,
        out_specs=P(None, ("outer", "inner")),
        check_vma=False,
    )
```

```python
from functools import partial
import math

import jax
import jax.numpy as jnp
import ml_dtypes
import numpy as np
from jax import lax
from jax.experimental import pallas as pl
from jax.experimental.pallas import tpu as pltpu
from jax.sharding import PartitionSpec as P

LANES = 128
AXES = ("outer", "inner")

TWO_PI = 2.0 * math.pi
HIGHEST = lax.Precision.HIGHEST


def table(count_a, count_b, modulus, sign):
    left = lax.broadcasted_iota(jnp.int32, (count_a, count_b), 0)
    right = lax.broadcasted_iota(jnp.int32, (count_a, count_b), 1)
    phase = TWO_PI / modulus * (left * right % modulus).astype(jnp.float32)
    return (jnp.cos(phase), sign * jnp.sin(phase))


def mix(form, cosine, sine, real, imag):
    contract = partial(jnp.einsum, precision=HIGHEST)
    return (
        contract(form, cosine, real) - contract(form, sine, imag),
        contract(form, sine, real) + contract(form, cosine, imag),
    )


def rotate(real, imag, cosine, sine):
    return (real * cosine - imag * sine, real * sine + imag * cosine)


def forward_rows(real, imag):
    split = 16
    lead = real.shape[:-1]
    size = real.shape[-1]
    short = size // split
    real = real.reshape(lead + (split, short))
    imag = imag.reshape(lead + (split, short))
    cosine, sine = table(split, split, split, -1.0)
    real, imag = mix("ka,...as->...ks", cosine, sine, real, imag)
    cosine, sine = table(split, short, size, -1.0)
    real, imag = rotate(real, imag, cosine, sine)
    cosine, sine = table(short, short, short, -1.0)
    real, imag = mix("sb,...ks->...bk", cosine, sine, real, imag)
    return (real.reshape(lead + (size,)), imag.reshape(lead + (size,)))


def inverse_rows(real, imag):
    split = 16
    lead = real.shape[:-1]
    size = real.shape[-1]
    short = size // split
    real = real.reshape(lead + (short, split))
    imag = imag.reshape(lead + (short, split))
    cosine, sine = table(short, short, short, 1.0)
    real, imag = mix("sb,...bk->...sk", cosine, sine, real, imag)
    cosine, sine = table(short, split, size, 1.0)
    real, imag = rotate(real, imag, cosine, sine)
    cosine, sine = table(split, split, split, 1.0)
    real, imag = mix("ak,...sk->...as", cosine, sine, real, imag)
    return (real.reshape(lead + (size,)), imag.reshape(lead + (size,)))


def by_sections(gate, keys, values, taps, skip_gain):
    inner_count = lax.axis_size("inner")
    devices = lax.axis_size("outer") * inner_count
    rank = lax.axis_index("outer") * inner_count + lax.axis_index("inner")
    chans, seg = keys.shape
    both = 2 * chans
    cols = seg // devices
    blocks = 2 * devices
    full = blocks * seg
    contract = partial(jnp.einsum, precision=HIGHEST)
    product = keys * values
    source = jnp.concatenate([product, taps], axis=0)
    sectioned = lax.all_to_all(
        lax.all_to_all(
            source.reshape(both, 1, 1, seg), "outer", split_axis=3, concat_axis=1, tiled=True
        ),
        "inner",
        split_axis=3,
        concat_axis=2,
        tiled=True,
    )
    sectioned = sectioned.reshape(both, devices, cols)
    cosine, sine = table(blocks, devices, blocks, -1.0)
    real = contract("km,cmj->ckj", cosine, sectioned)
    imag = contract("km,cmj->ckj", sine, sectioned)
    offset = rank * cols + lax.broadcasted_iota(jnp.int32, (blocks, cols), 1)
    residue = lax.broadcasted_iota(jnp.int32, (blocks, cols), 0)
    phase = TWO_PI / full * (offset * residue).astype(jnp.float32)
    real, imag = rotate(real, imag, jnp.cos(phase)[None], -jnp.sin(phase)[None])
    outgoing = jnp.stack([real, imag]).reshape(2, both, blocks, 1, 1, cols)
    moved = lax.all_to_all(
        lax.all_to_all(outgoing, "outer", split_axis=2, concat_axis=3, tiled=True),
        "inner",
        split_axis=2,
        concat_axis=4,
        tiled=True,
    )
    moved = moved.reshape(2, both, 2, seg)
    spec_real, spec_imag = forward_rows(moved[0], moved[1])
    sig_real, filt_real = (spec_real[:chans], spec_real[chans:])
    sig_imag, filt_imag = (spec_imag[:chans], spec_imag[chans:])
    real = sig_real * filt_real - sig_imag * filt_imag
    imag = sig_real * filt_imag + sig_imag * filt_real
    real, imag = inverse_rows(real, imag)
    residue = 2 * rank + lax.broadcasted_iota(jnp.int32, (2, seg), 0)
    offset = lax.broadcasted_iota(jnp.int32, (2, seg), 1)
    phase = TWO_PI / full * (offset * residue).astype(jnp.float32)
    real, imag = rotate(real, imag, jnp.cos(phase)[None], jnp.sin(phase)[None])
    returning = jnp.stack([real, imag]).reshape(2, chans, 1, 1, 2, seg)
    gathered = lax.all_to_all(
        lax.all_to_all(returning, "outer", split_axis=5, concat_axis=2, tiled=True),
        "inner",
        split_axis=5,
        concat_axis=3,
        tiled=True,
    )
    gathered = gathered.reshape(2, chans, blocks, cols)
    cosine, sine = table(devices, blocks, blocks, 1.0)
    conv = contract("mk,ckj->cmj", cosine, gathered[0]) - contract("mk,ckj->cmj", sine, gathered[1])
    conv = conv * (1.0 / full)
    conv = lax.all_to_all(
        lax.all_to_all(
            conv.reshape(chans, devices, 1, 1, cols),
            "outer",
            split_axis=1,
            concat_axis=2,
            tiled=True,
        ),
        "inner",
        split_axis=1,
        concat_axis=3,
        tiled=True,
    )
    conv = conv.reshape(chans, seg)
    return gate * (conv + skip_gain[:, None] * product)


def halves(array):
    high = array.astype(ml_dtypes.bfloat16)
    low = (array - high.astype(np.float64)).astype(ml_dtypes.bfloat16)
    return high, low


def transform_tables(devices, seg):
    length = devices * seg
    count = length // LANES
    odd = 2 * np.arange(count) + 1
    angle = 2 * np.pi / (4 * count) * ((odd[:, None] * np.arange(count)[None, :]) % (4 * count))
    first = np.concatenate([np.cos(angle), -np.sin(angle)], axis=0)
    last = np.concatenate([np.cos(angle).T, -np.sin(angle).T], axis=1) / length
    angle = 2 * np.pi / (4 * length) * ((odd[:, None] * np.arange(LANES)[None, :]) % (4 * length))
    twiddle = np.stack([np.cos(angle), np.sin(angle)]).astype(np.float32)
    angle = 2 * np.pi / LANES * ((np.arange(LANES)[:, None] * np.arange(LANES)[None, :]) % LANES)
    cosine, sine = np.cos(angle), np.sin(angle)
    rows = np.block([[cosine, -sine], [sine, cosine]])
    back = np.block([[cosine, sine], [-sine, cosine]])
    first_high, first_low = halves(first)
    rows_high, rows_low = halves(rows)
    back_high, back_low = halves(back)
    last_high, last_low = halves(last)
    return (
        np.concatenate([first_high, first_high, first_low, first_low], axis=1),
        np.concatenate([rows_high, rows_high, rows_high, rows_low], axis=0),
        np.concatenate([back_high, back_high, back_low], axis=0),
        np.concatenate([last_high, last_high, last_low], axis=1),
        twiddle,
    )


def send_orders(outer, inner):
    half = inner // 2
    turns = [at // 2 + half * (at % 2) for at in range(2 * half)] + list(range(2 * half, inner))
    ring = [2 * (at ^ (at >> 1)) + core for core in range(2) for at in range(outer // 2)] if outer == 8 else list(range(outer))
    first = [at * inner + step for at in ring for step in range(inner)]
    second = [at * inner + step for at in ring for step in turns]
    return first, second


def split(array, count=2):
    parts = []
    for _ in range(count):
        parts.append(array.astype(jnp.bfloat16))
        array = array - parts[-1].astype(jnp.float32)
    return parts


def dot(left, right):
    return jnp.dot(left, right, preferred_element_type=jnp.float32)


def convolve_kernel(
    devices, chans, seg, data_ref, first_ref, rows_ref, back_ref, last_ref, twiddle_ref, out_ref, signal_ref
):
    parts = seg // LANES
    count = devices * parts
    cosine, sine = twiddle_ref[0], twiddle_ref[1]

    def lanes(at):
        return slice(at * LANES, (at + 1) * LANES)

    first, second = send_orders(lax.axis_size("outer"), lax.axis_size("inner"))

    groups = chans
    each = chans // groups
    at = range(groups)
    for group in at:
        for kind in range(2):
            for chan in range(each):
                for device in range(devices):
                    came = ((device * 2 + kind) * chans + group * each + chan) * parts
                    to = first[device] * parts
                    signal_ref[group, to : to + parts, lanes(kind * each + chan)] = data_ref[came : came + parts, :]

    def start(group):
        high, low = split(signal_ref[group])
        return dot(first_ref[...], jnp.concatenate([high, low, high, low], axis=0))

    def spectra(begun):
        turned = []
        for signal in range(2 * each):
            real, imag = begun[:count, lanes(signal)], begun[count:, lanes(signal)]
            turned.append(jnp.concatenate([real * cosine + imag * sine, imag * cosine - real * sine], axis=1))
        high, low, rest = split(jnp.concatenate(turned, axis=0), 3)
        return dot(jnp.concatenate([high, low, rest, high], axis=1), rows_ref[...])

    def back(spectrum):
        mid = each * count
        sig_real, sig_imag = spectrum[:mid, :LANES], spectrum[:mid, LANES:]
        filt_real, filt_imag = spectrum[mid:, :LANES], spectrum[mid:, LANES:]
        real = sig_real * filt_real - sig_imag * filt_imag
        imag = sig_real * filt_imag + sig_imag * filt_real
        high, low = split(jnp.concatenate([real, imag], axis=1))
        return dot(jnp.concatenate([high, low, high], axis=1), back_ref[...])

    def end(backed):
        turned = []
        for chan in range(each):
            real = backed[chan * count : (chan + 1) * count, :LANES]
            imag = backed[chan * count : (chan + 1) * count, LANES:]
            turned.append(jnp.concatenate([real * cosine - imag * sine, imag * cosine + real * sine], axis=0))
        high, low = split(jnp.concatenate(turned, axis=1))
        return dot(last_ref[...], jnp.concatenate([high, low, high], axis=0))

    begun = [start(group) for group in at]
    spectrum = [spectra(begun[group]) for group in at]
    backed = [back(spectrum[group]) for group in at]
    conv = [end(backed[group]) for group in at]
    for group in at:
        for chan in range(each):
            own = group * each + chan
            for device in range(devices):
                to = (device * chans + own) * parts
                came = second[device] * parts
                out_ref[to : to + parts, :] = conv[group][came : came + parts, lanes(chan)]


def gather_kernel(order, product_ref, taps_ref, out_ref):
    rows = product_ref.shape[0] * product_ref.shape[1] // LANES // len(order)
    for kind, ref in enumerate((product_ref, taps_ref)):
        source = ref[...].reshape(len(order) * rows, LANES)
        for at, rank in enumerate(order):
            to = (2 * at + kind) * rows
            out_ref[to : to + rows, :] = source[rank * rows : (rank + 1) * rows]


def gate_kernel(order, gate_ref, skip_ref, conv_ref, out_hbm, out_ref, sems):
    chans, seg = gate_ref.shape
    pieces = sems.shape[0]
    step = chans // pieces
    rows = conv_ref.shape[0] // len(order)
    each = len(order) // pieces
    place = {rank: at * rows for at, rank in enumerate(order)}
    copies = []
    for piece in range(pieces):
        at = slice(piece * step, (piece + 1) * step)
        came = [conv_ref[place[rank] : place[rank] + rows, :] for rank in range(piece * each, (piece + 1) * each)]
        conv = jnp.concatenate(came, axis=0).reshape(step, seg)
        out_ref[at, :] = gate_ref[at, :] * (conv + skip_ref[at, :])
        copies.append(pltpu.make_async_copy(out_ref.at[at, :], out_hbm.at[at, :], sems.at[piece]))
        copies[piece].start()
    for copy in copies:
        copy.wait()


def on_core(kernel, shape, moved, flops=10**6, scratch=(), **more):
    return pl.pallas_call(
        kernel,
        out_shape=jax.ShapeDtypeStruct(shape, jnp.float32),
        scratch_shapes=scratch,
        compiler_params=pltpu.CompilerParams(vmem_limit_bytes=32 * 2**20),
        cost_estimate=pl.CostEstimate(flops=flops, bytes_accessed=moved, transcendentals=0),
        **more,
    )


def by_channels(gate, keys, values, taps, skip_gain):
    devices = lax.axis_size("outer") * lax.axis_size("inner")
    chans, seg = keys.shape
    own = chans // devices
    tiles = seg // LANES
    tables = [jnp.asarray(table) for table in transform_tables(devices, seg)]
    orders = send_orders(lax.axis_size("outer"), lax.axis_size("inner"))

    def regroup(rows, order):
        return lax.all_to_all(rows, AXES, split_axis=0, concat_axis=0, tiled=True, axis_index_groups=[order])

    product = keys * values
    product, skip = lax.optimization_barrier((product, skip_gain[:, None] * product))
    sent = on_core(partial(gather_kernel, orders[0]), (2 * chans * tiles, LANES), 4 * chans * seg * 4)(product, taps)
    groups = own
    conv = on_core(
        partial(convolve_kernel, devices, own, seg),
        (chans * tiles, LANES),
        2 * 10**6,
        10**9,
        [pltpu.VMEM((groups, devices * tiles, 2 * own // groups * LANES), jnp.float32)],
    )(regroup(sent, orders[0]), *tables)
    pieces = 4
    return on_core(
        partial(gate_kernel, orders[1]),
        (chans, seg),
        4 * chans * seg * 4,
        scratch=[pltpu.VMEM((chans, seg), jnp.float32), pltpu.SemaphoreType.DMA((pieces,))],
        out_specs=pl.BlockSpec(memory_space=pl.ANY),
    )(gate, skip, regroup(conv, orders[1]))


def on_device(gate, keys, values, taps, skip_gain):
    devices = lax.axis_size("outer") * lax.axis_size("inner")
    chans, seg = keys.shape
    if chans % devices == 0 and seg % LANES == 0 and devices % 8 == 0:
        return by_channels(gate, keys, values, taps, skip_gain)
    return by_sections(gate, keys, values, taps, skip_gain)


def solution(mesh):
    placed = (
        P(None, ("outer", "inner")),
        P(None, ("outer", "inner")),
        P(None, ("outer", "inner")),
        P(None, ("outer", "inner")),
        P(),
    )
    return jax.shard_map(
        on_device,
        mesh=mesh,
        in_specs=placed,
        out_specs=P(None, ("outer", "inner")),
        check_vma=False,
    )
```

```python
from functools import partial
import math

import jax
import jax.numpy as jnp
import ml_dtypes
import numpy as np
from jax import lax
from jax.experimental import pallas as pl
from jax.experimental.pallas import tpu as pltpu
from jax.sharding import PartitionSpec as P

LANES = 128
AXES = ("outer", "inner")

TWO_PI = 2.0 * math.pi
HIGHEST = lax.Precision.HIGHEST


def table(count_a, count_b, modulus, sign):
    left = lax.broadcasted_iota(jnp.int32, (count_a, count_b), 0)
    right = lax.broadcasted_iota(jnp.int32, (count_a, count_b), 1)
    phase = TWO_PI / modulus * (left * right % modulus).astype(jnp.float32)
    return (jnp.cos(phase), sign * jnp.sin(phase))


def mix(form, cosine, sine, real, imag):
    contract = partial(jnp.einsum, precision=HIGHEST)
    return (
        contract(form, cosine, real) - contract(form, sine, imag),
        contract(form, sine, real) + contract(form, cosine, imag),
    )


def rotate(real, imag, cosine, sine):
    return (real * cosine - imag * sine, real * sine + imag * cosine)


def forward_rows(real, imag):
    split = 16
    lead = real.shape[:-1]
    size = real.shape[-1]
    short = size // split
    real = real.reshape(lead + (split, short))
    imag = imag.reshape(lead + (split, short))
    cosine, sine = table(split, split, split, -1.0)
    real, imag = mix("ka,...as->...ks", cosine, sine, real, imag)
    cosine, sine = table(split, short, size, -1.0)
    real, imag = rotate(real, imag, cosine, sine)
    cosine, sine = table(short, short, short, -1.0)
    real, imag = mix("sb,...ks->...bk", cosine, sine, real, imag)
    return (real.reshape(lead + (size,)), imag.reshape(lead + (size,)))


def inverse_rows(real, imag):
    split = 16
    lead = real.shape[:-1]
    size = real.shape[-1]
    short = size // split
    real = real.reshape(lead + (short, split))
    imag = imag.reshape(lead + (short, split))
    cosine, sine = table(short, short, short, 1.0)
    real, imag = mix("sb,...bk->...sk", cosine, sine, real, imag)
    cosine, sine = table(short, split, size, 1.0)
    real, imag = rotate(real, imag, cosine, sine)
    cosine, sine = table(split, split, split, 1.0)
    real, imag = mix("ak,...sk->...as", cosine, sine, real, imag)
    return (real.reshape(lead + (size,)), imag.reshape(lead + (size,)))


def by_sections(gate, keys, values, taps, skip_gain):
    inner_count = lax.axis_size("inner")
    devices = lax.axis_size("outer") * inner_count
    rank = lax.axis_index("outer") * inner_count + lax.axis_index("inner")
    chans, seg = keys.shape
    both = 2 * chans
    cols = seg // devices
    blocks = 2 * devices
    full = blocks * seg
    contract = partial(jnp.einsum, precision=HIGHEST)
    product = keys * values
    source = jnp.concatenate([product, taps], axis=0)
    sectioned = lax.all_to_all(
        lax.all_to_all(
            source.reshape(both, 1, 1, seg), "outer", split_axis=3, concat_axis=1, tiled=True
        ),
        "inner",
        split_axis=3,
        concat_axis=2,
        tiled=True,
    )
    sectioned = sectioned.reshape(both, devices, cols)
    cosine, sine = table(blocks, devices, blocks, -1.0)
    real = contract("km,cmj->ckj", cosine, sectioned)
    imag = contract("km,cmj->ckj", sine, sectioned)
    offset = rank * cols + lax.broadcasted_iota(jnp.int32, (blocks, cols), 1)
    residue = lax.broadcasted_iota(jnp.int32, (blocks, cols), 0)
    phase = TWO_PI / full * (offset * residue).astype(jnp.float32)
    real, imag = rotate(real, imag, jnp.cos(phase)[None], -jnp.sin(phase)[None])
    outgoing = jnp.stack([real, imag]).reshape(2, both, blocks, 1, 1, cols)
    moved = lax.all_to_all(
        lax.all_to_all(outgoing, "outer", split_axis=2, concat_axis=3, tiled=True),
        "inner",
        split_axis=2,
        concat_axis=4,
        tiled=True,
    )
    moved = moved.reshape(2, both, 2, seg)
    spec_real, spec_imag = forward_rows(moved[0], moved[1])
    sig_real, filt_real = (spec_real[:chans], spec_real[chans:])
    sig_imag, filt_imag = (spec_imag[:chans], spec_imag[chans:])
    real = sig_real * filt_real - sig_imag * filt_imag
    imag = sig_real * filt_imag + sig_imag * filt_real
    real, imag = inverse_rows(real, imag)
    residue = 2 * rank + lax.broadcasted_iota(jnp.int32, (2, seg), 0)
    offset = lax.broadcasted_iota(jnp.int32, (2, seg), 1)
    phase = TWO_PI / full * (offset * residue).astype(jnp.float32)
    real, imag = rotate(real, imag, jnp.cos(phase)[None], jnp.sin(phase)[None])
    returning = jnp.stack([real, imag]).reshape(2, chans, 1, 1, 2, seg)
    gathered = lax.all_to_all(
        lax.all_to_all(returning, "outer", split_axis=5, concat_axis=2, tiled=True),
        "inner",
        split_axis=5,
        concat_axis=3,
        tiled=True,
    )
    gathered = gathered.reshape(2, chans, blocks, cols)
    cosine, sine = table(devices, blocks, blocks, 1.0)
    conv = contract("mk,ckj->cmj", cosine, gathered[0]) - contract("mk,ckj->cmj", sine, gathered[1])
    conv = conv * (1.0 / full)
    conv = lax.all_to_all(
        lax.all_to_all(
            conv.reshape(chans, devices, 1, 1, cols),
            "outer",
            split_axis=1,
            concat_axis=2,
            tiled=True,
        ),
        "inner",
        split_axis=1,
        concat_axis=3,
        tiled=True,
    )
    conv = conv.reshape(chans, seg)
    return gate * (conv + skip_gain[:, None] * product)


def halves(array):
    high = array.astype(ml_dtypes.bfloat16)
    low = (array - high.astype(np.float64)).astype(ml_dtypes.bfloat16)
    return high, low


def transform_tables(devices, seg):
    length = devices * seg
    count = length // LANES
    odd = 2 * np.arange(count) + 1
    angle = 2 * np.pi / (4 * count) * ((odd[:, None] * np.arange(count)[None, :]) % (4 * count))
    first = np.concatenate([np.cos(angle), -np.sin(angle)], axis=0)
    last = np.concatenate([np.cos(angle).T, -np.sin(angle).T], axis=1) / length
    angle = 2 * np.pi / (4 * length) * ((odd[:, None] * np.arange(LANES)[None, :]) % (4 * length))
    twiddle = np.stack([np.cos(angle), np.sin(angle)]).astype(np.float32)
    angle = 2 * np.pi / LANES * ((np.arange(LANES)[:, None] * np.arange(LANES)[None, :]) % LANES)
    cosine, sine = np.cos(angle), np.sin(angle)
    rows = np.block([[cosine, -sine], [sine, cosine]])
    back = np.block([[cosine, sine], [-sine, cosine]])
    first_high, first_low = halves(first)
    rows_high, rows_low = halves(rows)
    back_high, back_low = halves(back)
    last_high, last_low = halves(last)
    return (
        np.concatenate([first_high, first_high, first_low, first_low], axis=1),
        np.concatenate([rows_high, rows_high, rows_high, rows_low], axis=0),
        np.concatenate([back_high, back_high, back_low], axis=0),
        np.concatenate([last_high, last_high, last_low], axis=1),
        twiddle,
    )


def send_orders(outer, inner):
    half = inner // 2
    turns = [at // 2 + half * (at % 2) for at in range(2 * half)] + list(range(2 * half, inner))
    ring = [at ^ (at >> 1) for at in range(outer)] if outer & (outer - 1) == 0 else list(range(outer))
    first = [at * inner + step for at in ring for step in range(inner)]
    second = [at * inner + step for at in ring for step in turns[1:] + turns[:1]]
    return first, second


def split(array, count=2):
    parts = []
    for _ in range(count):
        parts.append(array.astype(jnp.bfloat16))
        array = array - parts[-1].astype(jnp.float32)
    return parts


def dot(left, right):
    return jnp.dot(left, right, preferred_element_type=jnp.float32)


def convolve_kernel(
    devices, chans, seg, data_ref, first_ref, rows_ref, back_ref, last_ref, twiddle_ref, out_ref, signal_ref
):
    parts = seg // LANES
    count = devices * parts
    cosine, sine = twiddle_ref[0], twiddle_ref[1]

    def lanes(at):
        return slice(at * LANES, (at + 1) * LANES)

    first, second = send_orders(lax.axis_size("outer"), lax.axis_size("inner"))

    groups = chans
    each = chans // groups
    at = range(groups)
    for group in at:
        for kind in range(2):
            for chan in range(each):
                for device in range(devices):
                    came = ((device * 2 + kind) * chans + group * each + chan) * parts
                    to = first[device] * parts
                    signal_ref[group, to : to + parts, lanes(kind * each + chan)] = data_ref[came : came + parts, :]

    def start(group):
        high, low = split(signal_ref[group])
        return dot(first_ref[...], jnp.concatenate([high, low, high, low], axis=0))

    def spectra(begun):
        turned = []
        for signal in range(2 * each):
            real, imag = begun[:count, lanes(signal)], begun[count:, lanes(signal)]
            turned.append(jnp.concatenate([real * cosine + imag * sine, imag * cosine - real * sine], axis=1))
        high, low, rest = split(jnp.concatenate(turned, axis=0), 3)
        return dot(jnp.concatenate([high, low, rest, high], axis=1), rows_ref[...])

    def back(spectrum):
        mid = each * count
        sig_real, sig_imag = spectrum[:mid, :LANES], spectrum[:mid, LANES:]
        filt_real, filt_imag = spectrum[mid:, :LANES], spectrum[mid:, LANES:]
        real = sig_real * filt_real - sig_imag * filt_imag
        imag = sig_real * filt_imag + sig_imag * filt_real
        high, low = split(jnp.concatenate([real, imag], axis=1))
        return dot(jnp.concatenate([high, low, high], axis=1), back_ref[...])

    def end(backed):
        turned = []
        for chan in range(each):
            real = backed[chan * count : (chan + 1) * count, :LANES]
            imag = backed[chan * count : (chan + 1) * count, LANES:]
            turned.append(jnp.concatenate([real * cosine - imag * sine, imag * cosine + real * sine], axis=0))
        high, low = split(jnp.concatenate(turned, axis=1))
        return dot(last_ref[...], jnp.concatenate([high, low, high], axis=0))

    begun = [start(group) for group in at]
    spectrum = [spectra(begun[group]) for group in at]
    backed = [back(spectrum[group]) for group in at]
    conv = [end(backed[group]) for group in at]
    for group in at:
        for chan in range(each):
            own = group * each + chan
            for device in range(devices):
                to = (device * chans + own) * parts
                came = second[device] * parts
                out_ref[to : to + parts, :] = conv[group][came : came + parts, lanes(chan)]


def gather_kernel(order, product_ref, taps_ref, out_ref):
    rows = product_ref.shape[0] * product_ref.shape[1] // LANES // len(order)
    for kind, ref in enumerate((product_ref, taps_ref)):
        source = ref[...].reshape(len(order) * rows, LANES)
        for at, rank in enumerate(order):
            to = (2 * at + kind) * rows
            out_ref[to : to + rows, :] = source[rank * rows : (rank + 1) * rows]


def gate_kernel(order, gate_ref, skip_ref, conv_ref, out_hbm, out_ref, sems):
    chans, seg = gate_ref.shape
    pieces = sems.shape[0]
    step = chans // pieces
    rows = conv_ref.shape[0] // len(order)
    each = len(order) // pieces
    place = {rank: at * rows for at, rank in enumerate(order)}
    copies = []
    for piece in range(pieces):
        at = slice(piece * step, (piece + 1) * step)
        came = [conv_ref[place[rank] : place[rank] + rows, :] for rank in range(piece * each, (piece + 1) * each)]
        conv = jnp.concatenate(came, axis=0).reshape(step, seg)
        out_ref[at, :] = gate_ref[at, :] * (conv + skip_ref[at, :])
        copies.append(pltpu.make_async_copy(out_ref.at[at, :], out_hbm.at[at, :], sems.at[piece]))
        copies[piece].start()
    for copy in copies:
        copy.wait()


def on_core(kernel, shape, moved, flops=10**6, scratch=(), **more):
    return pl.pallas_call(
        kernel,
        out_shape=jax.ShapeDtypeStruct(shape, jnp.float32),
        scratch_shapes=scratch,
        compiler_params=pltpu.CompilerParams(vmem_limit_bytes=32 * 2**20),
        cost_estimate=pl.CostEstimate(flops=flops, bytes_accessed=moved, transcendentals=0),
        **more,
    )


def by_channels(gate, keys, values, taps, skip_gain):
    devices = lax.axis_size("outer") * lax.axis_size("inner")
    chans, seg = keys.shape
    own = chans // devices
    tiles = seg // LANES
    tables = [jnp.asarray(table) for table in transform_tables(devices, seg)]
    orders = send_orders(lax.axis_size("outer"), lax.axis_size("inner"))

    def regroup(rows, order):
        return lax.all_to_all(rows, AXES, split_axis=0, concat_axis=0, tiled=True, axis_index_groups=[order])

    product = keys * values
    product, skip = lax.optimization_barrier((product, skip_gain[:, None] * product))
    sent = on_core(partial(gather_kernel, orders[0]), (2 * chans * tiles, LANES), 4 * chans * seg * 4)(product, taps)
    groups = own
    conv = on_core(
        partial(convolve_kernel, devices, own, seg),
        (chans * tiles, LANES),
        2 * 10**6,
        10**9,
        [pltpu.VMEM((groups, devices * tiles, 2 * own // groups * LANES), jnp.float32)],
    )(regroup(sent, orders[0]), *tables)
    pieces = 4
    return on_core(
        partial(gate_kernel, orders[1]),
        (chans, seg),
        4 * chans * seg * 4,
        scratch=[pltpu.VMEM((chans, seg), jnp.float32), pltpu.SemaphoreType.DMA((pieces,))],
        out_specs=pl.BlockSpec(memory_space=pl.ANY),
    )(gate, skip, regroup(conv, orders[1]))


def on_device(gate, keys, values, taps, skip_gain):
    devices = lax.axis_size("outer") * lax.axis_size("inner")
    chans, seg = keys.shape
    if chans % devices == 0 and seg % LANES == 0 and devices % 8 == 0:
        return by_channels(gate, keys, values, taps, skip_gain)
    return by_sections(gate, keys, values, taps, skip_gain)


def solution(mesh):
    placed = (
        P(None, ("outer", "inner")),
        P(None, ("outer", "inner")),
        P(None, ("outer", "inner")),
        P(None, ("outer", "inner")),
        P(),
    )
    return jax.shard_map(
        on_device,
        mesh=mesh,
        in_specs=placed,
        out_specs=P(None, ("outer", "inner")),
        check_vma=False,
    )
```

```python
from functools import partial
import math

import jax
import jax.numpy as jnp
import ml_dtypes
import numpy as np
from jax import lax
from jax.experimental import pallas as pl
from jax.experimental.pallas import tpu as pltpu
from jax.sharding import PartitionSpec as P

LANES = 128
AXES = ("outer", "inner")

TWO_PI = 2.0 * math.pi
HIGHEST = lax.Precision.HIGHEST


def table(count_a, count_b, modulus, sign):
    left = lax.broadcasted_iota(jnp.int32, (count_a, count_b), 0)
    right = lax.broadcasted_iota(jnp.int32, (count_a, count_b), 1)
    phase = TWO_PI / modulus * (left * right % modulus).astype(jnp.float32)
    return (jnp.cos(phase), sign * jnp.sin(phase))


def mix(form, cosine, sine, real, imag):
    contract = partial(jnp.einsum, precision=HIGHEST)
    return (
        contract(form, cosine, real) - contract(form, sine, imag),
        contract(form, sine, real) + contract(form, cosine, imag),
    )


def rotate(real, imag, cosine, sine):
    return (real * cosine - imag * sine, real * sine + imag * cosine)


def forward_rows(real, imag):
    split = 16
    lead = real.shape[:-1]
    size = real.shape[-1]
    short = size // split
    real = real.reshape(lead + (split, short))
    imag = imag.reshape(lead + (split, short))
    cosine, sine = table(split, split, split, -1.0)
    real, imag = mix("ka,...as->...ks", cosine, sine, real, imag)
    cosine, sine = table(split, short, size, -1.0)
    real, imag = rotate(real, imag, cosine, sine)
    cosine, sine = table(short, short, short, -1.0)
    real, imag = mix("sb,...ks->...bk", cosine, sine, real, imag)
    return (real.reshape(lead + (size,)), imag.reshape(lead + (size,)))


def inverse_rows(real, imag):
    split = 16
    lead = real.shape[:-1]
    size = real.shape[-1]
    short = size // split
    real = real.reshape(lead + (short, split))
    imag = imag.reshape(lead + (short, split))
    cosine, sine = table(short, short, short, 1.0)
    real, imag = mix("sb,...bk->...sk", cosine, sine, real, imag)
    cosine, sine = table(short, split, size, 1.0)
    real, imag = rotate(real, imag, cosine, sine)
    cosine, sine = table(split, split, split, 1.0)
    real, imag = mix("ak,...sk->...as", cosine, sine, real, imag)
    return (real.reshape(lead + (size,)), imag.reshape(lead + (size,)))


def by_sections(gate, keys, values, taps, skip_gain):
    inner_count = lax.axis_size("inner")
    devices = lax.axis_size("outer") * inner_count
    rank = lax.axis_index("outer") * inner_count + lax.axis_index("inner")
    chans, seg = keys.shape
    both = 2 * chans
    cols = seg // devices
    blocks = 2 * devices
    full = blocks * seg
    contract = partial(jnp.einsum, precision=HIGHEST)
    product = keys * values
    source = jnp.concatenate([product, taps], axis=0)
    sectioned = lax.all_to_all(
        lax.all_to_all(
            source.reshape(both, 1, 1, seg), "outer", split_axis=3, concat_axis=1, tiled=True
        ),
        "inner",
        split_axis=3,
        concat_axis=2,
        tiled=True,
    )
    sectioned = sectioned.reshape(both, devices, cols)
    cosine, sine = table(blocks, devices, blocks, -1.0)
    real = contract("km,cmj->ckj", cosine, sectioned)
    imag = contract("km,cmj->ckj", sine, sectioned)
    offset = rank * cols + lax.broadcasted_iota(jnp.int32, (blocks, cols), 1)
    residue = lax.broadcasted_iota(jnp.int32, (blocks, cols), 0)
    phase = TWO_PI / full * (offset * residue).astype(jnp.float32)
    real, imag = rotate(real, imag, jnp.cos(phase)[None], -jnp.sin(phase)[None])
    outgoing = jnp.stack([real, imag]).reshape(2, both, blocks, 1, 1, cols)
    moved = lax.all_to_all(
        lax.all_to_all(outgoing, "outer", split_axis=2, concat_axis=3, tiled=True),
        "inner",
        split_axis=2,
        concat_axis=4,
        tiled=True,
    )
    moved = moved.reshape(2, both, 2, seg)
    spec_real, spec_imag = forward_rows(moved[0], moved[1])
    sig_real, filt_real = (spec_real[:chans], spec_real[chans:])
    sig_imag, filt_imag = (spec_imag[:chans], spec_imag[chans:])
    real = sig_real * filt_real - sig_imag * filt_imag
    imag = sig_real * filt_imag + sig_imag * filt_real
    real, imag = inverse_rows(real, imag)
    residue = 2 * rank + lax.broadcasted_iota(jnp.int32, (2, seg), 0)
    offset = lax.broadcasted_iota(jnp.int32, (2, seg), 1)
    phase = TWO_PI / full * (offset * residue).astype(jnp.float32)
    real, imag = rotate(real, imag, jnp.cos(phase)[None], jnp.sin(phase)[None])
    returning = jnp.stack([real, imag]).reshape(2, chans, 1, 1, 2, seg)
    gathered = lax.all_to_all(
        lax.all_to_all(returning, "outer", split_axis=5, concat_axis=2, tiled=True),
        "inner",
        split_axis=5,
        concat_axis=3,
        tiled=True,
    )
    gathered = gathered.reshape(2, chans, blocks, cols)
    cosine, sine = table(devices, blocks, blocks, 1.0)
    conv = contract("mk,ckj->cmj", cosine, gathered[0]) - contract("mk,ckj->cmj", sine, gathered[1])
    conv = conv * (1.0 / full)
    conv = lax.all_to_all(
        lax.all_to_all(
            conv.reshape(chans, devices, 1, 1, cols),
            "outer",
            split_axis=1,
            concat_axis=2,
            tiled=True,
        ),
        "inner",
        split_axis=1,
        concat_axis=3,
        tiled=True,
    )
    conv = conv.reshape(chans, seg)
    return gate * (conv + skip_gain[:, None] * product)


def halves(array):
    high = array.astype(ml_dtypes.bfloat16)
    low = (array - high.astype(np.float64)).astype(ml_dtypes.bfloat16)
    return high, low


def transform_tables(devices, seg):
    length = devices * seg
    count = length // LANES
    odd = 2 * np.arange(count) + 1
    angle = 2 * np.pi / (4 * count) * ((odd[:, None] * np.arange(count)[None, :]) % (4 * count))
    first = np.concatenate([np.cos(angle), -np.sin(angle)], axis=0)
    last = np.concatenate([np.cos(angle).T, -np.sin(angle).T], axis=1) / length
    angle = 2 * np.pi / (4 * length) * ((odd[:, None] * np.arange(LANES)[None, :]) % (4 * length))
    twiddle = np.stack([np.cos(angle), np.sin(angle)]).astype(np.float32)
    angle = 2 * np.pi / LANES * ((np.arange(LANES)[:, None] * np.arange(LANES)[None, :]) % LANES)
    cosine, sine = np.cos(angle), np.sin(angle)
    rows = np.block([[cosine, -sine], [sine, cosine]])
    back = np.block([[cosine, sine], [-sine, cosine]])
    first_high, first_low = halves(first)
    rows_high, rows_low = halves(rows)
    back_high, back_low = halves(back)
    last_high, last_low = halves(last)
    return (
        np.concatenate([first_high, first_high, first_low, first_low], axis=1),
        np.concatenate([rows_high, rows_high, rows_high, rows_low], axis=0),
        np.concatenate([back_high, back_high, back_low], axis=0),
        np.concatenate([last_high, last_high, last_low], axis=1),
        twiddle,
    )


def send_orders(outer, inner):
    half = inner // 2
    turns = [at // 2 + half * (at % 2) for at in range(2 * half)] + list(range(2 * half, inner))
    ring = [at ^ (at >> 1) for at in range(outer)] if outer & (outer - 1) == 0 else list(range(outer))
    first = [at * inner + step for at in ring for step in turns[1:] + turns[:1]]
    second = [at * inner + step for at in ring for step in reversed(range(inner))]
    return first, second


def split(array, count=2):
    parts = []
    for _ in range(count):
        parts.append(array.astype(jnp.bfloat16))
        array = array - parts[-1].astype(jnp.float32)
    return parts


def dot(left, right):
    return jnp.dot(left, right, preferred_element_type=jnp.float32)


def convolve_kernel(
    devices, chans, seg, data_ref, first_ref, rows_ref, back_ref, last_ref, twiddle_ref, out_ref, signal_ref
):
    parts = seg // LANES
    count = devices * parts
    cosine, sine = twiddle_ref[0], twiddle_ref[1]

    def lanes(at):
        return slice(at * LANES, (at + 1) * LANES)

    first, second = send_orders(lax.axis_size("outer"), lax.axis_size("inner"))

    groups = chans
    each = chans // groups
    at = range(groups)
    for group in at:
        for kind in range(2):
            for chan in range(each):
                for device in range(devices):
                    came = ((device * 2 + kind) * chans + group * each + chan) * parts
                    to = first[device] * parts
                    signal_ref[group, to : to + parts, lanes(kind * each + chan)] = data_ref[came : came + parts, :]

    def start(group):
        high, low = split(signal_ref[group])
        return dot(first_ref[...], jnp.concatenate([high, low, high, low], axis=0))

    def spectra(begun):
        turned = []
        for signal in range(2 * each):
            real, imag = begun[:count, lanes(signal)], begun[count:, lanes(signal)]
            turned.append(jnp.concatenate([real * cosine + imag * sine, imag * cosine - real * sine], axis=1))
        high, low, rest = split(jnp.concatenate(turned, axis=0), 3)
        return dot(jnp.concatenate([high, low, rest, high], axis=1), rows_ref[...])

    def back(spectrum):
        mid = each * count
        sig_real, sig_imag = spectrum[:mid, :LANES], spectrum[:mid, LANES:]
        filt_real, filt_imag = spectrum[mid:, :LANES], spectrum[mid:, LANES:]
        real = sig_real * filt_real - sig_imag * filt_imag
        imag = sig_real * filt_imag + sig_imag * filt_real
        high, low = split(jnp.concatenate([real, imag], axis=1))
        return dot(jnp.concatenate([high, low, high], axis=1), back_ref[...])

    def end(backed):
        turned = []
        for chan in range(each):
            real = backed[chan * count : (chan + 1) * count, :LANES]
            imag = backed[chan * count : (chan + 1) * count, LANES:]
            turned.append(jnp.concatenate([real * cosine - imag * sine, imag * cosine + real * sine], axis=0))
        high, low = split(jnp.concatenate(turned, axis=1))
        return dot(last_ref[...], jnp.concatenate([high, low, high], axis=0))

    begun = [start(group) for group in at]
    spectrum = [spectra(begun[group]) for group in at]
    backed = [back(spectrum[group]) for group in at]
    conv = [end(backed[group]) for group in at]
    for group in at:
        for chan in range(each):
            own = group * each + chan
            for device in range(devices):
                to = (device * chans + own) * parts
                came = second[device] * parts
                out_ref[to : to + parts, :] = conv[group][came : came + parts, lanes(chan)]


def gather_kernel(order, product_ref, taps_ref, out_ref):
    rows = product_ref.shape[0] * product_ref.shape[1] // LANES // len(order)
    for kind, ref in enumerate((product_ref, taps_ref)):
        source = ref[...].reshape(len(order) * rows, LANES)
        for at, rank in enumerate(order):
            to = (2 * at + kind) * rows
            out_ref[to : to + rows, :] = source[rank * rows : (rank + 1) * rows]


def gate_kernel(order, gate_ref, skip_ref, conv_ref, out_hbm, out_ref, sems):
    chans, seg = gate_ref.shape
    pieces = sems.shape[0]
    step = chans // pieces
    rows = conv_ref.shape[0] // len(order)
    each = len(order) // pieces
    place = {rank: at * rows for at, rank in enumerate(order)}
    copies = []
    for piece in range(pieces):
        at = slice(piece * step, (piece + 1) * step)
        came = [conv_ref[place[rank] : place[rank] + rows, :] for rank in range(piece * each, (piece + 1) * each)]
        conv = jnp.concatenate(came, axis=0).reshape(step, seg)
        out_ref[at, :] = gate_ref[at, :] * (conv + skip_ref[at, :])
        copies.append(pltpu.make_async_copy(out_ref.at[at, :], out_hbm.at[at, :], sems.at[piece]))
        copies[piece].start()
    for copy in copies:
        copy.wait()


def on_core(kernel, shape, moved, flops=10**6, scratch=(), **more):
    return pl.pallas_call(
        kernel,
        out_shape=jax.ShapeDtypeStruct(shape, jnp.float32),
        scratch_shapes=scratch,
        compiler_params=pltpu.CompilerParams(vmem_limit_bytes=32 * 2**20),
        cost_estimate=pl.CostEstimate(flops=flops, bytes_accessed=moved, transcendentals=0),
        **more,
    )


def by_channels(gate, keys, values, taps, skip_gain):
    devices = lax.axis_size("outer") * lax.axis_size("inner")
    chans, seg = keys.shape
    own = chans // devices
    tiles = seg // LANES
    tables = [jnp.asarray(table) for table in transform_tables(devices, seg)]
    orders = send_orders(lax.axis_size("outer"), lax.axis_size("inner"))

    def regroup(rows, order):
        return lax.all_to_all(rows, AXES, split_axis=0, concat_axis=0, tiled=True, axis_index_groups=[order])

    product = keys * values
    product, skip = lax.optimization_barrier((product, skip_gain[:, None] * product))
    sent = on_core(partial(gather_kernel, orders[0]), (2 * chans * tiles, LANES), 4 * chans * seg * 4)(product, taps)
    groups = own
    conv = on_core(
        partial(convolve_kernel, devices, own, seg),
        (chans * tiles, LANES),
        2 * 10**6,
        10**9,
        [pltpu.VMEM((groups, devices * tiles, 2 * own // groups * LANES), jnp.float32)],
    )(regroup(sent, orders[0]), *tables)
    pieces = 4
    return on_core(
        partial(gate_kernel, orders[1]),
        (chans, seg),
        4 * chans * seg * 4,
        scratch=[pltpu.VMEM((chans, seg), jnp.float32), pltpu.SemaphoreType.DMA((pieces,))],
        out_specs=pl.BlockSpec(memory_space=pl.ANY),
    )(gate, skip, regroup(conv, orders[1]))


def on_device(gate, keys, values, taps, skip_gain):
    devices = lax.axis_size("outer") * lax.axis_size("inner")
    chans, seg = keys.shape
    if chans % devices == 0 and seg % LANES == 0 and devices % 8 == 0:
        return by_channels(gate, keys, values, taps, skip_gain)
    return by_sections(gate, keys, values, taps, skip_gain)


def solution(mesh):
    placed = (
        P(None, ("outer", "inner")),
        P(None, ("outer", "inner")),
        P(None, ("outer", "inner")),
        P(None, ("outer", "inner")),
        P(),
    )
    return jax.shard_map(
        on_device,
        mesh=mesh,
        in_specs=placed,
        out_specs=P(None, ("outer", "inner")),
        check_vma=False,
    )
```

```python
from functools import partial
import math

import jax
import jax.numpy as jnp
import ml_dtypes
import numpy as np
from jax import lax
from jax.experimental import pallas as pl
from jax.experimental.pallas import tpu as pltpu
from jax.sharding import PartitionSpec as P

LANES = 128
AXES = ("outer", "inner")

TWO_PI = 2.0 * math.pi
HIGHEST = lax.Precision.HIGHEST


def table(count_a, count_b, modulus, sign):
    left = lax.broadcasted_iota(jnp.int32, (count_a, count_b), 0)
    right = lax.broadcasted_iota(jnp.int32, (count_a, count_b), 1)
    phase = TWO_PI / modulus * (left * right % modulus).astype(jnp.float32)
    return (jnp.cos(phase), sign * jnp.sin(phase))


def mix(form, cosine, sine, real, imag):
    contract = partial(jnp.einsum, precision=HIGHEST)
    return (
        contract(form, cosine, real) - contract(form, sine, imag),
        contract(form, sine, real) + contract(form, cosine, imag),
    )


def rotate(real, imag, cosine, sine):
    return (real * cosine - imag * sine, real * sine + imag * cosine)


def forward_rows(real, imag):
    split = 16
    lead = real.shape[:-1]
    size = real.shape[-1]
    short = size // split
    real = real.reshape(lead + (split, short))
    imag = imag.reshape(lead + (split, short))
    cosine, sine = table(split, split, split, -1.0)
    real, imag = mix("ka,...as->...ks", cosine, sine, real, imag)
    cosine, sine = table(split, short, size, -1.0)
    real, imag = rotate(real, imag, cosine, sine)
    cosine, sine = table(short, short, short, -1.0)
    real, imag = mix("sb,...ks->...bk", cosine, sine, real, imag)
    return (real.reshape(lead + (size,)), imag.reshape(lead + (size,)))


def inverse_rows(real, imag):
    split = 16
    lead = real.shape[:-1]
    size = real.shape[-1]
    short = size // split
    real = real.reshape(lead + (short, split))
    imag = imag.reshape(lead + (short, split))
    cosine, sine = table(short, short, short, 1.0)
    real, imag = mix("sb,...bk->...sk", cosine, sine, real, imag)
    cosine, sine = table(short, split, size, 1.0)
    real, imag = rotate(real, imag, cosine, sine)
    cosine, sine = table(split, split, split, 1.0)
    real, imag = mix("ak,...sk->...as", cosine, sine, real, imag)
    return (real.reshape(lead + (size,)), imag.reshape(lead + (size,)))


def by_sections(gate, keys, values, taps, skip_gain):
    inner_count = lax.axis_size("inner")
    devices = lax.axis_size("outer") * inner_count
    rank = lax.axis_index("outer") * inner_count + lax.axis_index("inner")
    chans, seg = keys.shape
    both = 2 * chans
    cols = seg // devices
    blocks = 2 * devices
    full = blocks * seg
    contract = partial(jnp.einsum, precision=HIGHEST)
    product = keys * values
    source = jnp.concatenate([product, taps], axis=0)
    sectioned = lax.all_to_all(
        lax.all_to_all(
            source.reshape(both, 1, 1, seg), "outer", split_axis=3, concat_axis=1, tiled=True
        ),
        "inner",
        split_axis=3,
        concat_axis=2,
        tiled=True,
    )
    sectioned = sectioned.reshape(both, devices, cols)
    cosine, sine = table(blocks, devices, blocks, -1.0)
    real = contract("km,cmj->ckj", cosine, sectioned)
    imag = contract("km,cmj->ckj", sine, sectioned)
    offset = rank * cols + lax.broadcasted_iota(jnp.int32, (blocks, cols), 1)
    residue = lax.broadcasted_iota(jnp.int32, (blocks, cols), 0)
    phase = TWO_PI / full * (offset * residue).astype(jnp.float32)
    real, imag = rotate(real, imag, jnp.cos(phase)[None], -jnp.sin(phase)[None])
    outgoing = jnp.stack([real, imag]).reshape(2, both, blocks, 1, 1, cols)
    moved = lax.all_to_all(
        lax.all_to_all(outgoing, "outer", split_axis=2, concat_axis=3, tiled=True),
        "inner",
        split_axis=2,
        concat_axis=4,
        tiled=True,
    )
    moved = moved.reshape(2, both, 2, seg)
    spec_real, spec_imag = forward_rows(moved[0], moved[1])
    sig_real, filt_real = (spec_real[:chans], spec_real[chans:])
    sig_imag, filt_imag = (spec_imag[:chans], spec_imag[chans:])
    real = sig_real * filt_real - sig_imag * filt_imag
    imag = sig_real * filt_imag + sig_imag * filt_real
    real, imag = inverse_rows(real, imag)
    residue = 2 * rank + lax.broadcasted_iota(jnp.int32, (2, seg), 0)
    offset = lax.broadcasted_iota(jnp.int32, (2, seg), 1)
    phase = TWO_PI / full * (offset * residue).astype(jnp.float32)
    real, imag = rotate(real, imag, jnp.cos(phase)[None], jnp.sin(phase)[None])
    returning = jnp.stack([real, imag]).reshape(2, chans, 1, 1, 2, seg)
    gathered = lax.all_to_all(
        lax.all_to_all(returning, "outer", split_axis=5, concat_axis=2, tiled=True),
        "inner",
        split_axis=5,
        concat_axis=3,
        tiled=True,
    )
    gathered = gathered.reshape(2, chans, blocks, cols)
    cosine, sine = table(devices, blocks, blocks, 1.0)
    conv = contract("mk,ckj->cmj", cosine, gathered[0]) - contract("mk,ckj->cmj", sine, gathered[1])
    conv = conv * (1.0 / full)
    conv = lax.all_to_all(
        lax.all_to_all(
            conv.reshape(chans, devices, 1, 1, cols),
            "outer",
            split_axis=1,
            concat_axis=2,
            tiled=True,
        ),
        "inner",
        split_axis=1,
        concat_axis=3,
        tiled=True,
    )
    conv = conv.reshape(chans, seg)
    return gate * (conv + skip_gain[:, None] * product)


def halves(array):
    high = array.astype(ml_dtypes.bfloat16)
    low = (array - high.astype(np.float64)).astype(ml_dtypes.bfloat16)
    return high, low


def transform_tables(devices, seg):
    length = devices * seg
    count = length // LANES
    odd = 2 * np.arange(count) + 1
    angle = 2 * np.pi / (4 * count) * ((odd[:, None] * np.arange(count)[None, :]) % (4 * count))
    first = np.concatenate([np.cos(angle), -np.sin(angle)], axis=0)
    last = np.concatenate([np.cos(angle).T, -np.sin(angle).T], axis=1) / length
    angle = 2 * np.pi / (4 * length) * ((odd[:, None] * np.arange(LANES)[None, :]) % (4 * length))
    twiddle = np.stack([np.cos(angle), np.sin(angle)]).astype(np.float32)
    angle = 2 * np.pi / LANES * ((np.arange(LANES)[:, None] * np.arange(LANES)[None, :]) % LANES)
    cosine, sine = np.cos(angle), np.sin(angle)
    rows = np.block([[cosine, -sine], [sine, cosine]])
    back = np.block([[cosine, sine], [-sine, cosine]])
    first_high, first_low = halves(first)
    rows_high, rows_low = halves(rows)
    back_high, back_low = halves(back)
    last_high, last_low = halves(last)
    return (
        np.concatenate([first_high, first_high, first_low, first_low], axis=1),
        np.concatenate([rows_high, rows_high, rows_high, rows_low], axis=0),
        np.concatenate([back_high, back_high, back_low], axis=0),
        np.concatenate([last_high, last_high, last_low], axis=1),
        twiddle,
    )


def send_orders(outer, inner):
    half = inner // 2
    turns = [at // 2 + half * (at % 2) for at in range(2 * half)] + list(range(2 * half, inner))
    ring = [at ^ (at >> 1) for at in range(outer)] if outer & (outer - 1) == 0 else list(range(outer))
    first = [at * inner + step for at in ring for step in [0, inner - 1, *range(1, inner - 1)]]
    second = [at * inner + step for at in ring for step in turns[1:] + turns[:1]]
    return first, second


def split(array, count=2):
    parts = []
    for _ in range(count):
        parts.append(array.astype(jnp.bfloat16))
        array = array - parts[-1].astype(jnp.float32)
    return parts


def dot(left, right):
    return jnp.dot(left, right, preferred_element_type=jnp.float32)


def convolve_kernel(
    devices, chans, seg, data_ref, first_ref, rows_ref, back_ref, last_ref, twiddle_ref, out_ref, signal_ref
):
    parts = seg // LANES
    count = devices * parts
    cosine, sine = twiddle_ref[0], twiddle_ref[1]

    def lanes(at):
        return slice(at * LANES, (at + 1) * LANES)

    first, second = send_orders(lax.axis_size("outer"), lax.axis_size("inner"))

    groups = chans
    each = chans // groups
    at = range(groups)
    for group in at:
        for kind in range(2):
            for chan in range(each):
                for device in range(devices):
                    came = ((device * 2 + kind) * chans + group * each + chan) * parts
                    to = first[device] * parts
                    signal_ref[group, to : to + parts, lanes(kind * each + chan)] = data_ref[came : came + parts, :]

    def start(group):
        high, low = split(signal_ref[group])
        return dot(first_ref[...], jnp.concatenate([high, low, high, low], axis=0))

    def spectra(begun):
        turned = []
        for signal in range(2 * each):
            real, imag = begun[:count, lanes(signal)], begun[count:, lanes(signal)]
            turned.append(jnp.concatenate([real * cosine + imag * sine, imag * cosine - real * sine], axis=1))
        high, low, rest = split(jnp.concatenate(turned, axis=0), 3)
        return dot(jnp.concatenate([high, low, rest, high], axis=1), rows_ref[...])

    def back(spectrum):
        mid = each * count
        sig_real, sig_imag = spectrum[:mid, :LANES], spectrum[:mid, LANES:]
        filt_real, filt_imag = spectrum[mid:, :LANES], spectrum[mid:, LANES:]
        real = sig_real * filt_real - sig_imag * filt_imag
        imag = sig_real * filt_imag + sig_imag * filt_real
        high, low = split(jnp.concatenate([real, imag], axis=1))
        return dot(jnp.concatenate([high, low, high], axis=1), back_ref[...])

    def end(backed):
        turned = []
        for chan in range(each):
            real = backed[chan * count : (chan + 1) * count, :LANES]
            imag = backed[chan * count : (chan + 1) * count, LANES:]
            turned.append(jnp.concatenate([real * cosine - imag * sine, imag * cosine + real * sine], axis=0))
        high, low = split(jnp.concatenate(turned, axis=1))
        return dot(last_ref[...], jnp.concatenate([high, low, high], axis=0))

    begun = [start(group) for group in at]
    spectrum = [spectra(begun[group]) for group in at]
    backed = [back(spectrum[group]) for group in at]
    conv = [end(backed[group]) for group in at]
    for group in at:
        for chan in range(each):
            own = group * each + chan
            for device in range(devices):
                to = (device * chans + own) * parts
                came = second[device] * parts
                out_ref[to : to + parts, :] = conv[group][came : came + parts, lanes(chan)]


def gather_kernel(order, product_ref, taps_ref, out_ref):
    rows = product_ref.shape[0] * product_ref.shape[1] // LANES // len(order)
    for kind, ref in enumerate((product_ref, taps_ref)):
        source = ref[...].reshape(len(order) * rows, LANES)
        for at, rank in enumerate(order):
            to = (2 * at + kind) * rows
            out_ref[to : to + rows, :] = source[rank * rows : (rank + 1) * rows]


def gate_kernel(order, gate_ref, skip_ref, conv_ref, out_hbm, out_ref, sems):
    chans, seg = gate_ref.shape
    pieces = sems.shape[0]
    step = chans // pieces
    rows = conv_ref.shape[0] // len(order)
    each = len(order) // pieces
    place = {rank: at * rows for at, rank in enumerate(order)}
    copies = []
    for piece in range(pieces):
        at = slice(piece * step, (piece + 1) * step)
        came = [conv_ref[place[rank] : place[rank] + rows, :] for rank in range(piece * each, (piece + 1) * each)]
        conv = jnp.concatenate(came, axis=0).reshape(step, seg)
        out_ref[at, :] = gate_ref[at, :] * (conv + skip_ref[at, :])
        copies.append(pltpu.make_async_copy(out_ref.at[at, :], out_hbm.at[at, :], sems.at[piece]))
        copies[piece].start()
    for copy in copies:
        copy.wait()


def on_core(kernel, shape, moved, flops=10**6, scratch=(), **more):
    return pl.pallas_call(
        kernel,
        out_shape=jax.ShapeDtypeStruct(shape, jnp.float32),
        scratch_shapes=scratch,
        compiler_params=pltpu.CompilerParams(vmem_limit_bytes=32 * 2**20),
        cost_estimate=pl.CostEstimate(flops=flops, bytes_accessed=moved, transcendentals=0),
        **more,
    )


def by_channels(gate, keys, values, taps, skip_gain):
    devices = lax.axis_size("outer") * lax.axis_size("inner")
    chans, seg = keys.shape
    own = chans // devices
    tiles = seg // LANES
    tables = [jnp.asarray(table) for table in transform_tables(devices, seg)]
    orders = send_orders(lax.axis_size("outer"), lax.axis_size("inner"))

    def regroup(rows, order):
        return lax.all_to_all(rows, AXES, split_axis=0, concat_axis=0, tiled=True, axis_index_groups=[order])

    product = keys * values
    product, skip = lax.optimization_barrier((product, skip_gain[:, None] * product))
    sent = on_core(partial(gather_kernel, orders[0]), (2 * chans * tiles, LANES), 4 * chans * seg * 4)(product, taps)
    groups = own
    conv = on_core(
        partial(convolve_kernel, devices, own, seg),
        (chans * tiles, LANES),
        2 * 10**6,
        10**9,
        [pltpu.VMEM((groups, devices * tiles, 2 * own // groups * LANES), jnp.float32)],
    )(regroup(sent, orders[0]), *tables)
    pieces = 4
    return on_core(
        partial(gate_kernel, orders[1]),
        (chans, seg),
        4 * chans * seg * 4,
        scratch=[pltpu.VMEM((chans, seg), jnp.float32), pltpu.SemaphoreType.DMA((pieces,))],
        out_specs=pl.BlockSpec(memory_space=pl.ANY),
    )(gate, skip, regroup(conv, orders[1]))


def on_device(gate, keys, values, taps, skip_gain):
    devices = lax.axis_size("outer") * lax.axis_size("inner")
    chans, seg = keys.shape
    if chans % devices == 0 and seg % LANES == 0 and devices % 8 == 0:
        return by_channels(gate, keys, values, taps, skip_gain)
    return by_sections(gate, keys, values, taps, skip_gain)


def solution(mesh):
    placed = (
        P(None, ("outer", "inner")),
        P(None, ("outer", "inner")),
        P(None, ("outer", "inner")),
        P(None, ("outer", "inner")),
        P(),
    )
    return jax.shard_map(
        on_device,
        mesh=mesh,
        in_specs=placed,
        out_specs=P(None, ("outer", "inner")),
        check_vma=False,
    )
```

```python
from functools import partial
import math

import jax
import jax.numpy as jnp
import ml_dtypes
import numpy as np
from jax import lax
from jax.experimental import pallas as pl
from jax.experimental.pallas import tpu as pltpu
from jax.sharding import PartitionSpec as P

LANES = 128
AXES = ("outer", "inner")

TWO_PI = 2.0 * math.pi
HIGHEST = lax.Precision.HIGHEST


def table(count_a, count_b, modulus, sign):
    left = lax.broadcasted_iota(jnp.int32, (count_a, count_b), 0)
    right = lax.broadcasted_iota(jnp.int32, (count_a, count_b), 1)
    phase = TWO_PI / modulus * (left * right % modulus).astype(jnp.float32)
    return (jnp.cos(phase), sign * jnp.sin(phase))


def mix(form, cosine, sine, real, imag):
    contract = partial(jnp.einsum, precision=HIGHEST)
    return (
        contract(form, cosine, real) - contract(form, sine, imag),
        contract(form, sine, real) + contract(form, cosine, imag),
    )


def rotate(real, imag, cosine, sine):
    return (real * cosine - imag * sine, real * sine + imag * cosine)


def forward_rows(real, imag):
    split = 16
    lead = real.shape[:-1]
    size = real.shape[-1]
    short = size // split
    real = real.reshape(lead + (split, short))
    imag = imag.reshape(lead + (split, short))
    cosine, sine = table(split, split, split, -1.0)
    real, imag = mix("ka,...as->...ks", cosine, sine, real, imag)
    cosine, sine = table(split, short, size, -1.0)
    real, imag = rotate(real, imag, cosine, sine)
    cosine, sine = table(short, short, short, -1.0)
    real, imag = mix("sb,...ks->...bk", cosine, sine, real, imag)
    return (real.reshape(lead + (size,)), imag.reshape(lead + (size,)))


def inverse_rows(real, imag):
    split = 16
    lead = real.shape[:-1]
    size = real.shape[-1]
    short = size // split
    real = real.reshape(lead + (short, split))
    imag = imag.reshape(lead + (short, split))
    cosine, sine = table(short, short, short, 1.0)
    real, imag = mix("sb,...bk->...sk", cosine, sine, real, imag)
    cosine, sine = table(short, split, size, 1.0)
    real, imag = rotate(real, imag, cosine, sine)
    cosine, sine = table(split, split, split, 1.0)
    real, imag = mix("ak,...sk->...as", cosine, sine, real, imag)
    return (real.reshape(lead + (size,)), imag.reshape(lead + (size,)))


def by_sections(gate, keys, values, taps, skip_gain):
    inner_count = lax.axis_size("inner")
    devices = lax.axis_size("outer") * inner_count
    rank = lax.axis_index("outer") * inner_count + lax.axis_index("inner")
    chans, seg = keys.shape
    both = 2 * chans
    cols = seg // devices
    blocks = 2 * devices
    full = blocks * seg
    contract = partial(jnp.einsum, precision=HIGHEST)
    product = keys * values
    source = jnp.concatenate([product, taps], axis=0)
    sectioned = lax.all_to_all(
        lax.all_to_all(
            source.reshape(both, 1, 1, seg), "outer", split_axis=3, concat_axis=1, tiled=True
        ),
        "inner",
        split_axis=3,
        concat_axis=2,
        tiled=True,
    )
    sectioned = sectioned.reshape(both, devices, cols)
    cosine, sine = table(blocks, devices, blocks, -1.0)
    real = contract("km,cmj->ckj", cosine, sectioned)
    imag = contract("km,cmj->ckj", sine, sectioned)
    offset = rank * cols + lax.broadcasted_iota(jnp.int32, (blocks, cols), 1)
    residue = lax.broadcasted_iota(jnp.int32, (blocks, cols), 0)
    phase = TWO_PI / full * (offset * residue).astype(jnp.float32)
    real, imag = rotate(real, imag, jnp.cos(phase)[None], -jnp.sin(phase)[None])
    outgoing = jnp.stack([real, imag]).reshape(2, both, blocks, 1, 1, cols)
    moved = lax.all_to_all(
        lax.all_to_all(outgoing, "outer", split_axis=2, concat_axis=3, tiled=True),
        "inner",
        split_axis=2,
        concat_axis=4,
        tiled=True,
    )
    moved = moved.reshape(2, both, 2, seg)
    spec_real, spec_imag = forward_rows(moved[0], moved[1])
    sig_real, filt_real = (spec_real[:chans], spec_real[chans:])
    sig_imag, filt_imag = (spec_imag[:chans], spec_imag[chans:])
    real = sig_real * filt_real - sig_imag * filt_imag
    imag = sig_real * filt_imag + sig_imag * filt_real
    real, imag = inverse_rows(real, imag)
    residue = 2 * rank + lax.broadcasted_iota(jnp.int32, (2, seg), 0)
    offset = lax.broadcasted_iota(jnp.int32, (2, seg), 1)
    phase = TWO_PI / full * (offset * residue).astype(jnp.float32)
    real, imag = rotate(real, imag, jnp.cos(phase)[None], jnp.sin(phase)[None])
    returning = jnp.stack([real, imag]).reshape(2, chans, 1, 1, 2, seg)
    gathered = lax.all_to_all(
        lax.all_to_all(returning, "outer", split_axis=5, concat_axis=2, tiled=True),
        "inner",
        split_axis=5,
        concat_axis=3,
        tiled=True,
    )
    gathered = gathered.reshape(2, chans, blocks, cols)
    cosine, sine = table(devices, blocks, blocks, 1.0)
    conv = contract("mk,ckj->cmj", cosine, gathered[0]) - contract("mk,ckj->cmj", sine, gathered[1])
    conv = conv * (1.0 / full)
    conv = lax.all_to_all(
        lax.all_to_all(
            conv.reshape(chans, devices, 1, 1, cols),
            "outer",
            split_axis=1,
            concat_axis=2,
            tiled=True,
        ),
        "inner",
        split_axis=1,
        concat_axis=3,
        tiled=True,
    )
    conv = conv.reshape(chans, seg)
    return gate * (conv + skip_gain[:, None] * product)


def halves(array):
    high = array.astype(ml_dtypes.bfloat16)
    low = (array - high.astype(np.float64)).astype(ml_dtypes.bfloat16)
    return high, low


def transform_tables(devices, seg):
    length = devices * seg
    count = length // LANES
    odd = 2 * np.arange(count) + 1
    angle = 2 * np.pi / (4 * count) * ((odd[:, None] * np.arange(count)[None, :]) % (4 * count))
    first = np.concatenate([np.cos(angle), -np.sin(angle)], axis=0)
    last = np.concatenate([np.cos(angle).T, -np.sin(angle).T], axis=1) / length
    angle = 2 * np.pi / (4 * length) * ((odd[:, None] * np.arange(LANES)[None, :]) % (4 * length))
    twiddle = np.stack([np.cos(angle), np.sin(angle)]).astype(np.float32)
    angle = 2 * np.pi / LANES * ((np.arange(LANES)[:, None] * np.arange(LANES)[None, :]) % LANES)
    cosine, sine = np.cos(angle), np.sin(angle)
    rows = np.block([[cosine, -sine], [sine, cosine]])
    back = np.block([[cosine, sine], [-sine, cosine]])
    first_high, first_low = halves(first)
    rows_high, rows_low = halves(rows)
    back_high, back_low = halves(back)
    last_high, last_low = halves(last)
    return (
        np.concatenate([first_high, first_high, first_low, first_low], axis=1),
        np.concatenate([rows_high, rows_high, rows_high, rows_low], axis=0),
        np.concatenate([back_high, back_high, back_low], axis=0),
        np.concatenate([last_high, last_high, last_low], axis=1),
        twiddle,
    )


def send_orders(outer, inner):
    half = inner // 2
    turns = [at // 2 + half * (at % 2) for at in range(2 * half)] + list(range(2 * half, inner))
    ring = [at ^ (at >> 1) for at in range(outer)] if outer & (outer - 1) == 0 else list(range(outer))
    first = [at * inner + step for at in ring for step in range(inner)]
    second = [at * inner + step for at in ring for step in turns[1:] + turns[:1]]
    return first, second


def split(array, count=2):
    parts = []
    for _ in range(count):
        parts.append(array.astype(jnp.bfloat16))
        array = array - parts[-1].astype(jnp.float32)
    return parts


def dot(left, right):
    return jnp.dot(left, right, preferred_element_type=jnp.float32)


def convolve_kernel(
    devices, chans, seg, data_ref, first_ref, rows_ref, back_ref, last_ref, twiddle_ref, out_ref, signal_ref
):
    parts = seg // LANES
    count = devices * parts
    cosine, sine = twiddle_ref[0], twiddle_ref[1]

    def lanes(at):
        return slice(at * LANES, (at + 1) * LANES)

    first, second = send_orders(lax.axis_size("outer"), lax.axis_size("inner"))

    groups = chans
    each = chans // groups
    at = range(groups)

    def start(group):
        for kind in range(2):
            for chan in range(each):
                for device in range(devices):
                    came = ((device * 2 + kind) * chans + group * each + chan) * parts
                    to = first[device] * parts
                    signal_ref[group, to : to + parts, lanes(kind * each + chan)] = data_ref[came : came + parts, :]
        high, low = split(signal_ref[group])
        return dot(first_ref[...], jnp.concatenate([high, low, high, low], axis=0))

    def spectra(begun):
        turned = []
        for signal in range(2 * each):
            real, imag = begun[:count, lanes(signal)], begun[count:, lanes(signal)]
            turned.append(jnp.concatenate([real * cosine + imag * sine, imag * cosine - real * sine], axis=1))
        high, low, rest = split(jnp.concatenate(turned, axis=0), 3)
        return dot(jnp.concatenate([high, low, rest, high], axis=1), rows_ref[...])

    def back(spectrum):
        mid = each * count
        sig_real, sig_imag = spectrum[:mid, :LANES], spectrum[:mid, LANES:]
        filt_real, filt_imag = spectrum[mid:, :LANES], spectrum[mid:, LANES:]
        real = sig_real * filt_real - sig_imag * filt_imag
        imag = sig_real * filt_imag + sig_imag * filt_real
        high, low = split(jnp.concatenate([real, imag], axis=1))
        return dot(jnp.concatenate([high, low, high], axis=1), back_ref[...])

    def end(backed):
        turned = []
        for chan in range(each):
            real = backed[chan * count : (chan + 1) * count, :LANES]
            imag = backed[chan * count : (chan + 1) * count, LANES:]
            turned.append(jnp.concatenate([real * cosine - imag * sine, imag * cosine + real * sine], axis=0))
        high, low = split(jnp.concatenate(turned, axis=1))
        return dot(last_ref[...], jnp.concatenate([high, low, high], axis=0))

    begun = [start(group) for group in at]
    spectrum = [spectra(begun[group]) for group in at]
    backed = [back(spectrum[group]) for group in at]
    for group in at:
        conv = end(backed[group])
        for chan in range(each):
            for device in range(devices):
                to = (device * chans + group * each + chan) * parts
                came = second[device] * parts
                out_ref[to : to + parts, :] = conv[came : came + parts, lanes(chan)]


def gather_kernel(order, product_ref, taps_ref, out_ref):
    rows = product_ref.shape[0] * product_ref.shape[1] // LANES // len(order)
    for kind, ref in enumerate((product_ref, taps_ref)):
        source = ref[...].reshape(len(order) * rows, LANES)
        for at, rank in enumerate(order):
            to = (2 * at + kind) * rows
            out_ref[to : to + rows, :] = source[rank * rows : (rank + 1) * rows]


def gate_kernel(order, gate_ref, skip_ref, conv_ref, out_hbm, out_ref, sems):
    chans, seg = gate_ref.shape
    pieces = sems.shape[0]
    step = chans // pieces
    rows = conv_ref.shape[0] // len(order)
    each = len(order) // pieces
    place = {rank: at * rows for at, rank in enumerate(order)}
    copies = []
    for piece in range(pieces):
        at = slice(piece * step, (piece + 1) * step)
        came = [conv_ref[place[rank] : place[rank] + rows, :] for rank in range(piece * each, (piece + 1) * each)]
        conv = jnp.concatenate(came, axis=0).reshape(step, seg)
        out_ref[at, :] = gate_ref[at, :] * (conv + skip_ref[at, :])
        copies.append(pltpu.make_async_copy(out_ref.at[at, :], out_hbm.at[at, :], sems.at[piece]))
        copies[piece].start()
    for copy in copies:
        copy.wait()


def on_core(kernel, shape, moved, flops=10**6, scratch=(), **more):
    return pl.pallas_call(
        kernel,
        out_shape=jax.ShapeDtypeStruct(shape, jnp.float32),
        scratch_shapes=scratch,
        compiler_params=pltpu.CompilerParams(vmem_limit_bytes=32 * 2**20),
        cost_estimate=pl.CostEstimate(flops=flops, bytes_accessed=moved, transcendentals=0),
        **more,
    )


def by_channels(gate, keys, values, taps, skip_gain):
    devices = lax.axis_size("outer") * lax.axis_size("inner")
    chans, seg = keys.shape
    own = chans // devices
    tiles = seg // LANES
    tables = [jnp.asarray(table) for table in transform_tables(devices, seg)]
    orders = send_orders(lax.axis_size("outer"), lax.axis_size("inner"))

    def regroup(rows, order):
        return lax.all_to_all(rows, AXES, split_axis=0, concat_axis=0, tiled=True, axis_index_groups=[order])

    product = keys * values
    product, skip = lax.optimization_barrier((product, skip_gain[:, None] * product))
    sent = on_core(partial(gather_kernel, orders[0]), (2 * chans * tiles, LANES), 4 * chans * seg * 4)(product, taps)
    groups = own
    conv = on_core(
        partial(convolve_kernel, devices, own, seg),
        (chans * tiles, LANES),
        2 * 10**6,
        10**9,
        [pltpu.VMEM((groups, devices * tiles, 2 * own // groups * LANES), jnp.float32)],
    )(regroup(sent, orders[0]), *tables)
    pieces = 4
    return on_core(
        partial(gate_kernel, orders[1]),
        (chans, seg),
        4 * chans * seg * 4,
        scratch=[pltpu.VMEM((chans, seg), jnp.float32), pltpu.SemaphoreType.DMA((pieces,))],
        out_specs=pl.BlockSpec(memory_space=pl.ANY),
    )(gate, skip, regroup(conv, orders[1]))


def on_device(gate, keys, values, taps, skip_gain):
    devices = lax.axis_size("outer") * lax.axis_size("inner")
    chans, seg = keys.shape
    if chans % devices == 0 and seg % LANES == 0 and devices % 8 == 0:
        return by_channels(gate, keys, values, taps, skip_gain)
    return by_sections(gate, keys, values, taps, skip_gain)


def solution(mesh):
    placed = (
        P(None, ("outer", "inner")),
        P(None, ("outer", "inner")),
        P(None, ("outer", "inner")),
        P(None, ("outer", "inner")),
        P(),
    )
    return jax.shard_map(
        on_device,
        mesh=mesh,
        in_specs=placed,
        out_specs=P(None, ("outer", "inner")),
        check_vma=False,
    )
```

```python
from functools import partial
import math

import jax
import jax.numpy as jnp
import ml_dtypes
import numpy as np
from jax import lax
from jax.experimental import pallas as pl
from jax.experimental.pallas import tpu as pltpu
from jax.sharding import PartitionSpec as P

LANES = 128
AXES = ("outer", "inner")

TWO_PI = 2.0 * math.pi
HIGHEST = lax.Precision.HIGHEST


def table(count_a, count_b, modulus, sign):
    left = lax.broadcasted_iota(jnp.int32, (count_a, count_b), 0)
    right = lax.broadcasted_iota(jnp.int32, (count_a, count_b), 1)
    phase = TWO_PI / modulus * (left * right % modulus).astype(jnp.float32)
    return (jnp.cos(phase), sign * jnp.sin(phase))


def mix(form, cosine, sine, real, imag):
    contract = partial(jnp.einsum, precision=HIGHEST)
    return (
        contract(form, cosine, real) - contract(form, sine, imag),
        contract(form, sine, real) + contract(form, cosine, imag),
    )


def rotate(real, imag, cosine, sine):
    return (real * cosine - imag * sine, real * sine + imag * cosine)


def forward_rows(real, imag):
    split = 16
    lead = real.shape[:-1]
    size = real.shape[-1]
    short = size // split
    real = real.reshape(lead + (split, short))
    imag = imag.reshape(lead + (split, short))
    cosine, sine = table(split, split, split, -1.0)
    real, imag = mix("ka,...as->...ks", cosine, sine, real, imag)
    cosine, sine = table(split, short, size, -1.0)
    real, imag = rotate(real, imag, cosine, sine)
    cosine, sine = table(short, short, short, -1.0)
    real, imag = mix("sb,...ks->...bk", cosine, sine, real, imag)
    return (real.reshape(lead + (size,)), imag.reshape(lead + (size,)))


def inverse_rows(real, imag):
    split = 16
    lead = real.shape[:-1]
    size = real.shape[-1]
    short = size // split
    real = real.reshape(lead + (short, split))
    imag = imag.reshape(lead + (short, split))
    cosine, sine = table(short, short, short, 1.0)
    real, imag = mix("sb,...bk->...sk", cosine, sine, real, imag)
    cosine, sine = table(short, split, size, 1.0)
    real, imag = rotate(real, imag, cosine, sine)
    cosine, sine = table(split, split, split, 1.0)
    real, imag = mix("ak,...sk->...as", cosine, sine, real, imag)
    return (real.reshape(lead + (size,)), imag.reshape(lead + (size,)))


def by_sections(gate, keys, values, taps, skip_gain):
    inner_count = lax.axis_size("inner")
    devices = lax.axis_size("outer") * inner_count
    rank = lax.axis_index("outer") * inner_count + lax.axis_index("inner")
    chans, seg = keys.shape
    both = 2 * chans
    cols = seg // devices
    blocks = 2 * devices
    full = blocks * seg
    contract = partial(jnp.einsum, precision=HIGHEST)
    product = keys * values
    source = jnp.concatenate([product, taps], axis=0)
    sectioned = lax.all_to_all(
        lax.all_to_all(
            source.reshape(both, 1, 1, seg), "outer", split_axis=3, concat_axis=1, tiled=True
        ),
        "inner",
        split_axis=3,
        concat_axis=2,
        tiled=True,
    )
    sectioned = sectioned.reshape(both, devices, cols)
    cosine, sine = table(blocks, devices, blocks, -1.0)
    real = contract("km,cmj->ckj", cosine, sectioned)
    imag = contract("km,cmj->ckj", sine, sectioned)
    offset = rank * cols + lax.broadcasted_iota(jnp.int32, (blocks, cols), 1)
    residue = lax.broadcasted_iota(jnp.int32, (blocks, cols), 0)
    phase = TWO_PI / full * (offset * residue).astype(jnp.float32)
    real, imag = rotate(real, imag, jnp.cos(phase)[None], -jnp.sin(phase)[None])
    outgoing = jnp.stack([real, imag]).reshape(2, both, blocks, 1, 1, cols)
    moved = lax.all_to_all(
        lax.all_to_all(outgoing, "outer", split_axis=2, concat_axis=3, tiled=True),
        "inner",
        split_axis=2,
        concat_axis=4,
        tiled=True,
    )
    moved = moved.reshape(2, both, 2, seg)
    spec_real, spec_imag = forward_rows(moved[0], moved[1])
    sig_real, filt_real = (spec_real[:chans], spec_real[chans:])
    sig_imag, filt_imag = (spec_imag[:chans], spec_imag[chans:])
    real = sig_real * filt_real - sig_imag * filt_imag
    imag = sig_real * filt_imag + sig_imag * filt_real
    real, imag = inverse_rows(real, imag)
    residue = 2 * rank + lax.broadcasted_iota(jnp.int32, (2, seg), 0)
    offset = lax.broadcasted_iota(jnp.int32, (2, seg), 1)
    phase = TWO_PI / full * (offset * residue).astype(jnp.float32)
    real, imag = rotate(real, imag, jnp.cos(phase)[None], jnp.sin(phase)[None])
    returning = jnp.stack([real, imag]).reshape(2, chans, 1, 1, 2, seg)
    gathered = lax.all_to_all(
        lax.all_to_all(returning, "outer", split_axis=5, concat_axis=2, tiled=True),
        "inner",
        split_axis=5,
        concat_axis=3,
        tiled=True,
    )
    gathered = gathered.reshape(2, chans, blocks, cols)
    cosine, sine = table(devices, blocks, blocks, 1.0)
    conv = contract("mk,ckj->cmj", cosine, gathered[0]) - contract("mk,ckj->cmj", sine, gathered[1])
    conv = conv * (1.0 / full)
    conv = lax.all_to_all(
        lax.all_to_all(
            conv.reshape(chans, devices, 1, 1, cols),
            "outer",
            split_axis=1,
            concat_axis=2,
            tiled=True,
        ),
        "inner",
        split_axis=1,
        concat_axis=3,
        tiled=True,
    )
    conv = conv.reshape(chans, seg)
    return gate * (conv + skip_gain[:, None] * product)


def halves(array):
    high = array.astype(ml_dtypes.bfloat16)
    low = (array - high.astype(np.float64)).astype(ml_dtypes.bfloat16)
    return high, low


def transform_tables(devices, seg):
    length = devices * seg
    count = length // LANES
    odd = 2 * np.arange(count) + 1
    angle = 2 * np.pi / (4 * count) * ((odd[:, None] * np.arange(count)[None, :]) % (4 * count))
    first = np.concatenate([np.cos(angle), -np.sin(angle)], axis=0)
    last = np.concatenate([np.cos(angle).T, -np.sin(angle).T], axis=1) / length
    angle = 2 * np.pi / (4 * length) * ((odd[:, None] * np.arange(LANES)[None, :]) % (4 * length))
    twiddle = np.stack([np.cos(angle), np.sin(angle)]).astype(np.float32)
    angle = 2 * np.pi / LANES * ((np.arange(LANES)[:, None] * np.arange(LANES)[None, :]) % LANES)
    cosine, sine = np.cos(angle), np.sin(angle)
    rows = np.block([[cosine, -sine], [sine, cosine]])
    back = np.block([[cosine, sine], [-sine, cosine]])
    first_high, first_low = halves(first)
    rows_high, rows_low = halves(rows)
    back_high, back_low = halves(back)
    last_high, last_low = halves(last)
    return (
        np.concatenate([first_high, first_high, first_low, first_low], axis=1),
        np.concatenate([rows_high, rows_high, rows_high, rows_low], axis=0),
        np.concatenate([back_high, back_high, back_low], axis=0),
        np.concatenate([last_high, last_high, last_low], axis=1),
        twiddle,
    )


def send_orders(outer, inner):
    half = inner // 2
    turns = [at // 2 + half * (at % 2) for at in range(2 * half)] + list(range(2 * half, inner))
    ring = [at ^ (at >> 1) for at in range(outer)] if outer & (outer - 1) == 0 else list(range(outer))
    first = [at * inner + step for at in ring[:1] + ring[:0:-1] for step in range(inner)]
    second = [at * inner + step for at in range(outer) for step in turns[1:] + turns[:1]]
    return first, second


def split(array, count=2):
    parts = []
    for _ in range(count):
        parts.append(array.astype(jnp.bfloat16))
        array = array - parts[-1].astype(jnp.float32)
    return parts


def dot(left, right):
    return jnp.dot(left, right, preferred_element_type=jnp.float32)


def convolve_kernel(
    devices, chans, seg, data_ref, first_ref, rows_ref, back_ref, last_ref, twiddle_ref, out_ref, signal_ref
):
    parts = seg // LANES
    count = devices * parts
    cosine, sine = twiddle_ref[0], twiddle_ref[1]

    def lanes(at):
        return slice(at * LANES, (at + 1) * LANES)

    first, second = send_orders(lax.axis_size("outer"), lax.axis_size("inner"))

    groups = chans
    each = chans // groups
    at = range(groups)
    for group in at:
        for kind in range(2):
            for chan in range(each):
                for device in range(devices):
                    came = ((device * 2 + kind) * chans + group * each + chan) * parts
                    to = first[device] * parts
                    signal_ref[group, to : to + parts, lanes(kind * each + chan)] = data_ref[came : came + parts, :]

    def start(group):
        high, low = split(signal_ref[group])
        return dot(first_ref[...], jnp.concatenate([high, low, high, low], axis=0))

    def spectra(begun):
        turned = []
        for signal in range(2 * each):
            real, imag = begun[:count, lanes(signal)], begun[count:, lanes(signal)]
            turned.append(jnp.concatenate([real * cosine + imag * sine, imag * cosine - real * sine], axis=1))
        high, low, rest = split(jnp.concatenate(turned, axis=0), 3)
        return dot(jnp.concatenate([high, low, rest, high], axis=1), rows_ref[...])

    def back(spectrum):
        mid = each * count
        sig_real, sig_imag = spectrum[:mid, :LANES], spectrum[:mid, LANES:]
        filt_real, filt_imag = spectrum[mid:, :LANES], spectrum[mid:, LANES:]
        real = sig_real * filt_real - sig_imag * filt_imag
        imag = sig_real * filt_imag + sig_imag * filt_real
        high, low = split(jnp.concatenate([real, imag], axis=1))
        return dot(jnp.concatenate([high, low, high], axis=1), back_ref[...])

    def end(backed):
        turned = []
        for chan in range(each):
            real = backed[chan * count : (chan + 1) * count, :LANES]
            imag = backed[chan * count : (chan + 1) * count, LANES:]
            turned.append(jnp.concatenate([real * cosine - imag * sine, imag * cosine + real * sine], axis=0))
        high, low = split(jnp.concatenate(turned, axis=1))
        return dot(last_ref[...], jnp.concatenate([high, low, high], axis=0))

    begun = [start(group) for group in at]
    spectrum = [spectra(begun[group]) for group in at]
    backed = [back(spectrum[group]) for group in at]
    conv = [end(backed[group]) for group in at]
    for group in at:
        for chan in range(each):
            own = group * each + chan
            for device in range(devices):
                to = (device * chans + own) * parts
                came = second[device] * parts
                out_ref[to : to + parts, :] = conv[group][came : came + parts, lanes(chan)]


def gather_kernel(order, product_ref, taps_ref, out_ref):
    rows = product_ref.shape[0] * product_ref.shape[1] // LANES // len(order)
    for kind, ref in enumerate((product_ref, taps_ref)):
        source = ref[...].reshape(len(order) * rows, LANES)
        for at, rank in enumerate(order):
            to = (2 * at + kind) * rows
            out_ref[to : to + rows, :] = source[rank * rows : (rank + 1) * rows]


def gate_kernel(order, gate_ref, skip_ref, conv_ref, out_hbm, out_ref, sems):
    chans, seg = gate_ref.shape
    pieces = sems.shape[0]
    step = chans // pieces
    rows = conv_ref.shape[0] // len(order)
    each = len(order) // pieces
    place = {rank: at * rows for at, rank in enumerate(order)}
    copies = []
    for piece in range(pieces):
        at = slice(piece * step, (piece + 1) * step)
        came = [conv_ref[place[rank] : place[rank] + rows, :] for rank in range(piece * each, (piece + 1) * each)]
        conv = jnp.concatenate(came, axis=0).reshape(step, seg)
        out_ref[at, :] = gate_ref[at, :] * (conv + skip_ref[at, :])
        copies.append(pltpu.make_async_copy(out_ref.at[at, :], out_hbm.at[at, :], sems.at[piece]))
        copies[piece].start()
    for copy in copies:
        copy.wait()


def on_core(kernel, shape, moved, flops=10**6, scratch=(), **more):
    return pl.pallas_call(
        kernel,
        out_shape=jax.ShapeDtypeStruct(shape, jnp.float32),
        scratch_shapes=scratch,
        compiler_params=pltpu.CompilerParams(vmem_limit_bytes=32 * 2**20),
        cost_estimate=pl.CostEstimate(flops=flops, bytes_accessed=moved, transcendentals=0),
        **more,
    )


def by_channels(gate, keys, values, taps, skip_gain):
    devices = lax.axis_size("outer") * lax.axis_size("inner")
    chans, seg = keys.shape
    own = chans // devices
    tiles = seg // LANES
    tables = [jnp.asarray(table) for table in transform_tables(devices, seg)]
    orders = send_orders(lax.axis_size("outer"), lax.axis_size("inner"))

    def regroup(rows, order):
        return lax.all_to_all(rows, AXES, split_axis=0, concat_axis=0, tiled=True, axis_index_groups=[order])

    product = keys * values
    product, skip = lax.optimization_barrier((product, skip_gain[:, None] * product))
    sent = on_core(partial(gather_kernel, orders[0]), (2 * chans * tiles, LANES), 4 * chans * seg * 4)(product, taps)
    groups = own
    conv = on_core(
        partial(convolve_kernel, devices, own, seg),
        (chans * tiles, LANES),
        2 * 10**6,
        10**9,
        [pltpu.VMEM((groups, devices * tiles, 2 * own // groups * LANES), jnp.float32)],
    )(regroup(sent, orders[0]), *tables)
    pieces = 4
    return on_core(
        partial(gate_kernel, orders[1]),
        (chans, seg),
        4 * chans * seg * 4,
        scratch=[pltpu.VMEM((chans, seg), jnp.float32), pltpu.SemaphoreType.DMA((pieces,))],
        out_specs=pl.BlockSpec(memory_space=pl.ANY),
    )(gate, skip, regroup(conv, orders[1]))


def on_device(gate, keys, values, taps, skip_gain):
    devices = lax.axis_size("outer") * lax.axis_size("inner")
    chans, seg = keys.shape
    if chans % devices == 0 and seg % LANES == 0 and devices % 8 == 0:
        return by_channels(gate, keys, values, taps, skip_gain)
    return by_sections(gate, keys, values, taps, skip_gain)


def solution(mesh):
    placed = (
        P(None, ("outer", "inner")),
        P(None, ("outer", "inner")),
        P(None, ("outer", "inner")),
        P(None, ("outer", "inner")),
        P(),
    )
    return jax.shard_map(
        on_device,
        mesh=mesh,
        in_specs=placed,
        out_specs=P(None, ("outer", "inner")),
        check_vma=False,
    )
```

```python
from functools import partial
import math

import jax
import jax.numpy as jnp
import ml_dtypes
import numpy as np
from jax import lax
from jax.experimental import pallas as pl
from jax.experimental.pallas import tpu as pltpu
from jax.sharding import PartitionSpec as P

LANES = 128
AXES = ("outer", "inner")

TWO_PI = 2.0 * math.pi
HIGHEST = lax.Precision.HIGHEST


def table(count_a, count_b, modulus, sign):
    left = lax.broadcasted_iota(jnp.int32, (count_a, count_b), 0)
    right = lax.broadcasted_iota(jnp.int32, (count_a, count_b), 1)
    phase = TWO_PI / modulus * (left * right % modulus).astype(jnp.float32)
    return (jnp.cos(phase), sign * jnp.sin(phase))


def mix(form, cosine, sine, real, imag):
    contract = partial(jnp.einsum, precision=HIGHEST)
    return (
        contract(form, cosine, real) - contract(form, sine, imag),
        contract(form, sine, real) + contract(form, cosine, imag),
    )


def rotate(real, imag, cosine, sine):
    return (real * cosine - imag * sine, real * sine + imag * cosine)


def forward_rows(real, imag):
    split = 16
    lead = real.shape[:-1]
    size = real.shape[-1]
    short = size // split
    real = real.reshape(lead + (split, short))
    imag = imag.reshape(lead + (split, short))
    cosine, sine = table(split, split, split, -1.0)
    real, imag = mix("ka,...as->...ks", cosine, sine, real, imag)
    cosine, sine = table(split, short, size, -1.0)
    real, imag = rotate(real, imag, cosine, sine)
    cosine, sine = table(short, short, short, -1.0)
    real, imag = mix("sb,...ks->...bk", cosine, sine, real, imag)
    return (real.reshape(lead + (size,)), imag.reshape(lead + (size,)))


def inverse_rows(real, imag):
    split = 16
    lead = real.shape[:-1]
    size = real.shape[-1]
    short = size // split
    real = real.reshape(lead + (short, split))
    imag = imag.reshape(lead + (short, split))
    cosine, sine = table(short, short, short, 1.0)
    real, imag = mix("sb,...bk->...sk", cosine, sine, real, imag)
    cosine, sine = table(short, split, size, 1.0)
    real, imag = rotate(real, imag, cosine, sine)
    cosine, sine = table(split, split, split, 1.0)
    real, imag = mix("ak,...sk->...as", cosine, sine, real, imag)
    return (real.reshape(lead + (size,)), imag.reshape(lead + (size,)))


def by_sections(gate, keys, values, taps, skip_gain):
    inner_count = lax.axis_size("inner")
    devices = lax.axis_size("outer") * inner_count
    rank = lax.axis_index("outer") * inner_count + lax.axis_index("inner")
    chans, seg = keys.shape
    both = 2 * chans
    cols = seg // devices
    blocks = 2 * devices
    full = blocks * seg
    contract = partial(jnp.einsum, precision=HIGHEST)
    product = keys * values
    source = jnp.concatenate([product, taps], axis=0)
    sectioned = lax.all_to_all(
        lax.all_to_all(
            source.reshape(both, 1, 1, seg), "outer", split_axis=3, concat_axis=1, tiled=True
        ),
        "inner",
        split_axis=3,
        concat_axis=2,
        tiled=True,
    )
    sectioned = sectioned.reshape(both, devices, cols)
    cosine, sine = table(blocks, devices, blocks, -1.0)
    real = contract("km,cmj->ckj", cosine, sectioned)
    imag = contract("km,cmj->ckj", sine, sectioned)
    offset = rank * cols + lax.broadcasted_iota(jnp.int32, (blocks, cols), 1)
    residue = lax.broadcasted_iota(jnp.int32, (blocks, cols), 0)
    phase = TWO_PI / full * (offset * residue).astype(jnp.float32)
    real, imag = rotate(real, imag, jnp.cos(phase)[None], -jnp.sin(phase)[None])
    outgoing = jnp.stack([real, imag]).reshape(2, both, blocks, 1, 1, cols)
    moved = lax.all_to_all(
        lax.all_to_all(outgoing, "outer", split_axis=2, concat_axis=3, tiled=True),
        "inner",
        split_axis=2,
        concat_axis=4,
        tiled=True,
    )
    moved = moved.reshape(2, both, 2, seg)
    spec_real, spec_imag = forward_rows(moved[0], moved[1])
    sig_real, filt_real = (spec_real[:chans], spec_real[chans:])
    sig_imag, filt_imag = (spec_imag[:chans], spec_imag[chans:])
    real = sig_real * filt_real - sig_imag * filt_imag
    imag = sig_real * filt_imag + sig_imag * filt_real
    real, imag = inverse_rows(real, imag)
    residue = 2 * rank + lax.broadcasted_iota(jnp.int32, (2, seg), 0)
    offset = lax.broadcasted_iota(jnp.int32, (2, seg), 1)
    phase = TWO_PI / full * (offset * residue).astype(jnp.float32)
    real, imag = rotate(real, imag, jnp.cos(phase)[None], jnp.sin(phase)[None])
    returning = jnp.stack([real, imag]).reshape(2, chans, 1, 1, 2, seg)
    gathered = lax.all_to_all(
        lax.all_to_all(returning, "outer", split_axis=5, concat_axis=2, tiled=True),
        "inner",
        split_axis=5,
        concat_axis=3,
        tiled=True,
    )
    gathered = gathered.reshape(2, chans, blocks, cols)
    cosine, sine = table(devices, blocks, blocks, 1.0)
    conv = contract("mk,ckj->cmj", cosine, gathered[0]) - contract("mk,ckj->cmj", sine, gathered[1])
    conv = conv * (1.0 / full)
    conv = lax.all_to_all(
        lax.all_to_all(
            conv.reshape(chans, devices, 1, 1, cols),
            "outer",
            split_axis=1,
            concat_axis=2,
            tiled=True,
        ),
        "inner",
        split_axis=1,
        concat_axis=3,
        tiled=True,
    )
    conv = conv.reshape(chans, seg)
    return gate * (conv + skip_gain[:, None] * product)


def halves(array):
    high = array.astype(ml_dtypes.bfloat16)
    low = (array - high.astype(np.float64)).astype(ml_dtypes.bfloat16)
    return high, low


def transform_tables(devices, seg):
    length = devices * seg
    count = length // LANES
    odd = 2 * np.arange(count) + 1
    angle = 2 * np.pi / (4 * count) * ((odd[:, None] * np.arange(count)[None, :]) % (4 * count))
    first = np.concatenate([np.cos(angle), -np.sin(angle)], axis=0)
    last = np.concatenate([np.cos(angle).T, -np.sin(angle).T], axis=1) / length
    angle = 2 * np.pi / (4 * length) * ((odd[:, None] * np.arange(LANES)[None, :]) % (4 * length))
    twiddle = np.stack([np.cos(angle), np.sin(angle)]).astype(np.float32)
    angle = 2 * np.pi / LANES * ((np.arange(LANES)[:, None] * np.arange(LANES)[None, :]) % LANES)
    cosine, sine = np.cos(angle), np.sin(angle)
    rows = np.block([[cosine, -sine], [sine, cosine]])
    back = np.block([[cosine, sine], [-sine, cosine]])
    first_high, first_low = halves(first)
    rows_high, rows_low = halves(rows)
    back_high, back_low = halves(back)
    last_high, last_low = halves(last)
    return (
        np.concatenate([first_high, first_high, first_low, first_low], axis=1),
        np.concatenate([rows_high, rows_high, rows_high, rows_low], axis=0),
        np.concatenate([back_high, back_high, back_low], axis=0),
        np.concatenate([last_high, last_high, last_low], axis=1),
        twiddle,
    )


def send_orders(outer, inner):
    half = inner // 2
    turns = [at // 2 + half * (at % 2) for at in range(2 * half)] + list(range(2 * half, inner))
    ring = list(range(outer))
    first = [at * inner + step for at in ring for step in [*range(1, inner), 0]]
    second = [at * inner + step for at in reversed(ring) for step in turns[1:] + turns[:1]]
    return first, second


def split(array, count=2):
    parts = []
    for _ in range(count):
        parts.append(array.astype(jnp.bfloat16))
        array = array - parts[-1].astype(jnp.float32)
    return parts


def dot(left, right):
    return jnp.dot(left, right, preferred_element_type=jnp.float32)


def convolve_kernel(
    devices, chans, seg, data_ref, first_ref, rows_ref, back_ref, last_ref, twiddle_ref, out_ref, signal_ref
):
    parts = seg // LANES
    count = devices * parts
    cosine, sine = twiddle_ref[0], twiddle_ref[1]

    def lanes(at):
        return slice(at * LANES, (at + 1) * LANES)

    first, second = send_orders(lax.axis_size("outer"), lax.axis_size("inner"))

    groups = chans
    each = chans // groups
    at = range(groups)
    for group in at:
        for kind in range(2):
            for chan in range(each):
                for device in range(devices):
                    came = ((device * 2 + kind) * chans + group * each + chan) * parts
                    to = first[device] * parts
                    signal_ref[group, to : to + parts, lanes(kind * each + chan)] = data_ref[came : came + parts, :]

    def start(group):
        high, low = split(signal_ref[group])
        return dot(first_ref[...], jnp.concatenate([high, low, high, low], axis=0))

    def spectra(begun):
        turned = []
        for signal in range(2 * each):
            real, imag = begun[:count, lanes(signal)], begun[count:, lanes(signal)]
            turned.append(jnp.concatenate([real * cosine + imag * sine, imag * cosine - real * sine], axis=1))
        high, low, rest = split(jnp.concatenate(turned, axis=0), 3)
        return dot(jnp.concatenate([high, low, rest, high], axis=1), rows_ref[...])

    def back(spectrum):
        mid = each * count
        sig_real, sig_imag = spectrum[:mid, :LANES], spectrum[:mid, LANES:]
        filt_real, filt_imag = spectrum[mid:, :LANES], spectrum[mid:, LANES:]
        real = sig_real * filt_real - sig_imag * filt_imag
        imag = sig_real * filt_imag + sig_imag * filt_real
        high, low = split(jnp.concatenate([real, imag], axis=1))
        return dot(jnp.concatenate([high, low, high], axis=1), back_ref[...])

    def end(backed):
        turned = []
        for chan in range(each):
            real = backed[chan * count : (chan + 1) * count, :LANES]
            imag = backed[chan * count : (chan + 1) * count, LANES:]
            turned.append(jnp.concatenate([real * cosine - imag * sine, imag * cosine + real * sine], axis=0))
        high, low = split(jnp.concatenate(turned, axis=1))
        return dot(last_ref[...], jnp.concatenate([high, low, high], axis=0))

    begun = [start(group) for group in at]
    spectrum = [spectra(begun[group]) for group in at]
    backed = [back(spectrum[group]) for group in at]
    conv = [end(backed[group]) for group in at]
    for group in at:
        for chan in range(each):
            own = group * each + chan
            for device in range(devices):
                to = (device * chans + own) * parts
                came = second[device] * parts
                out_ref[to : to + parts, :] = conv[group][came : came + parts, lanes(chan)]


def gather_kernel(order, product_ref, taps_ref, out_ref):
    rows = product_ref.shape[0] * product_ref.shape[1] // LANES // len(order)
    for kind, ref in enumerate((product_ref, taps_ref)):
        source = ref[...].reshape(len(order) * rows, LANES)
        for at, rank in enumerate(order):
            to = (2 * at + kind) * rows
            out_ref[to : to + rows, :] = source[rank * rows : (rank + 1) * rows]


def gate_kernel(order, gate_ref, skip_ref, conv_ref, out_hbm, out_ref, sems):
    chans, seg = gate_ref.shape
    pieces = sems.shape[0]
    step = chans // pieces
    rows = conv_ref.shape[0] // len(order)
    each = len(order) // pieces
    place = {rank: at * rows for at, rank in enumerate(order)}
    copies = []
    for piece in range(pieces):
        at = slice(piece * step, (piece + 1) * step)
        came = [conv_ref[place[rank] : place[rank] + rows, :] for rank in range(piece * each, (piece + 1) * each)]
        conv = jnp.concatenate(came, axis=0).reshape(step, seg)
        out_ref[at, :] = gate_ref[at, :] * (conv + skip_ref[at, :])
        copies.append(pltpu.make_async_copy(out_ref.at[at, :], out_hbm.at[at, :], sems.at[piece]))
        copies[piece].start()
    for copy in copies:
        copy.wait()


def on_core(kernel, shape, moved, flops=10**6, scratch=(), **more):
    return pl.pallas_call(
        kernel,
        out_shape=jax.ShapeDtypeStruct(shape, jnp.float32),
        scratch_shapes=scratch,
        compiler_params=pltpu.CompilerParams(vmem_limit_bytes=32 * 2**20),
        cost_estimate=pl.CostEstimate(flops=flops, bytes_accessed=moved, transcendentals=0),
        **more,
    )


def by_channels(gate, keys, values, taps, skip_gain):
    devices = lax.axis_size("outer") * lax.axis_size("inner")
    chans, seg = keys.shape
    own = chans // devices
    tiles = seg // LANES
    tables = [jnp.asarray(table) for table in transform_tables(devices, seg)]
    orders = send_orders(lax.axis_size("outer"), lax.axis_size("inner"))

    def regroup(rows, order):
        return lax.all_to_all(rows, AXES, split_axis=0, concat_axis=0, tiled=True, axis_index_groups=[order])

    product = keys * values
    product, skip = lax.optimization_barrier((product, skip_gain[:, None] * product))
    sent = on_core(partial(gather_kernel, orders[0]), (2 * chans * tiles, LANES), 4 * chans * seg * 4)(product, taps)
    groups = own
    conv = on_core(
        partial(convolve_kernel, devices, own, seg),
        (chans * tiles, LANES),
        2 * 10**6,
        10**9,
        [pltpu.VMEM((groups, devices * tiles, 2 * own // groups * LANES), jnp.float32)],
    )(regroup(sent, orders[0]), *tables)
    pieces = 4
    return on_core(
        partial(gate_kernel, orders[1]),
        (chans, seg),
        4 * chans * seg * 4,
        scratch=[pltpu.VMEM((chans, seg), jnp.float32), pltpu.SemaphoreType.DMA((pieces,))],
        out_specs=pl.BlockSpec(memory_space=pl.ANY),
    )(gate, skip, regroup(conv, orders[1]))


def on_device(gate, keys, values, taps, skip_gain):
    devices = lax.axis_size("outer") * lax.axis_size("inner")
    chans, seg = keys.shape
    if chans % devices == 0 and seg % LANES == 0 and devices % 8 == 0:
        return by_channels(gate, keys, values, taps, skip_gain)
    return by_sections(gate, keys, values, taps, skip_gain)


def solution(mesh):
    placed = (
        P(None, ("outer", "inner")),
        P(None, ("outer", "inner")),
        P(None, ("outer", "inner")),
        P(None, ("outer", "inner")),
        P(),
    )
    return jax.shard_map(
        on_device,
        mesh=mesh,
        in_specs=placed,
        out_specs=P(None, ("outer", "inner")),
        check_vma=False,
    )
```

```python
from functools import partial
import math

import jax
import jax.numpy as jnp
import ml_dtypes
import numpy as np
from jax import lax
from jax.experimental import pallas as pl
from jax.experimental.pallas import tpu as pltpu
from jax.sharding import PartitionSpec as P

LANES = 128
AXES = ("outer", "inner")

TWO_PI = 2.0 * math.pi
HIGHEST = lax.Precision.HIGHEST


def table(count_a, count_b, modulus, sign):
    left = lax.broadcasted_iota(jnp.int32, (count_a, count_b), 0)
    right = lax.broadcasted_iota(jnp.int32, (count_a, count_b), 1)
    phase = TWO_PI / modulus * (left * right % modulus).astype(jnp.float32)
    return (jnp.cos(phase), sign * jnp.sin(phase))


def mix(form, cosine, sine, real, imag):
    contract = partial(jnp.einsum, precision=HIGHEST)
    return (
        contract(form, cosine, real) - contract(form, sine, imag),
        contract(form, sine, real) + contract(form, cosine, imag),
    )


def rotate(real, imag, cosine, sine):
    return (real * cosine - imag * sine, real * sine + imag * cosine)


def forward_rows(real, imag):
    split = 16
    lead = real.shape[:-1]
    size = real.shape[-1]
    short = size // split
    real = real.reshape(lead + (split, short))
    imag = imag.reshape(lead + (split, short))
    cosine, sine = table(split, split, split, -1.0)
    real, imag = mix("ka,...as->...ks", cosine, sine, real, imag)
    cosine, sine = table(split, short, size, -1.0)
    real, imag = rotate(real, imag, cosine, sine)
    cosine, sine = table(short, short, short, -1.0)
    real, imag = mix("sb,...ks->...bk", cosine, sine, real, imag)
    return (real.reshape(lead + (size,)), imag.reshape(lead + (size,)))


def inverse_rows(real, imag):
    split = 16
    lead = real.shape[:-1]
    size = real.shape[-1]
    short = size // split
    real = real.reshape(lead + (short, split))
    imag = imag.reshape(lead + (short, split))
    cosine, sine = table(short, short, short, 1.0)
    real, imag = mix("sb,...bk->...sk", cosine, sine, real, imag)
    cosine, sine = table(short, split, size, 1.0)
    real, imag = rotate(real, imag, cosine, sine)
    cosine, sine = table(split, split, split, 1.0)
    real, imag = mix("ak,...sk->...as", cosine, sine, real, imag)
    return (real.reshape(lead + (size,)), imag.reshape(lead + (size,)))


def by_sections(gate, keys, values, taps, skip_gain):
    inner_count = lax.axis_size("inner")
    devices = lax.axis_size("outer") * inner_count
    rank = lax.axis_index("outer") * inner_count + lax.axis_index("inner")
    chans, seg = keys.shape
    both = 2 * chans
    cols = seg // devices
    blocks = 2 * devices
    full = blocks * seg
    contract = partial(jnp.einsum, precision=HIGHEST)
    product = keys * values
    source = jnp.concatenate([product, taps], axis=0)
    sectioned = lax.all_to_all(
        lax.all_to_all(
            source.reshape(both, 1, 1, seg), "outer", split_axis=3, concat_axis=1, tiled=True
        ),
        "inner",
        split_axis=3,
        concat_axis=2,
        tiled=True,
    )
    sectioned = sectioned.reshape(both, devices, cols)
    cosine, sine = table(blocks, devices, blocks, -1.0)
    real = contract("km,cmj->ckj", cosine, sectioned)
    imag = contract("km,cmj->ckj", sine, sectioned)
    offset = rank * cols + lax.broadcasted_iota(jnp.int32, (blocks, cols), 1)
    residue = lax.broadcasted_iota(jnp.int32, (blocks, cols), 0)
    phase = TWO_PI / full * (offset * residue).astype(jnp.float32)
    real, imag = rotate(real, imag, jnp.cos(phase)[None], -jnp.sin(phase)[None])
    outgoing = jnp.stack([real, imag]).reshape(2, both, blocks, 1, 1, cols)
    moved = lax.all_to_all(
        lax.all_to_all(outgoing, "outer", split_axis=2, concat_axis=3, tiled=True),
        "inner",
        split_axis=2,
        concat_axis=4,
        tiled=True,
    )
    moved = moved.reshape(2, both, 2, seg)
    spec_real, spec_imag = forward_rows(moved[0], moved[1])
    sig_real, filt_real = (spec_real[:chans], spec_real[chans:])
    sig_imag, filt_imag = (spec_imag[:chans], spec_imag[chans:])
    real = sig_real * filt_real - sig_imag * filt_imag
    imag = sig_real * filt_imag + sig_imag * filt_real
    real, imag = inverse_rows(real, imag)
    residue = 2 * rank + lax.broadcasted_iota(jnp.int32, (2, seg), 0)
    offset = lax.broadcasted_iota(jnp.int32, (2, seg), 1)
    phase = TWO_PI / full * (offset * residue).astype(jnp.float32)
    real, imag = rotate(real, imag, jnp.cos(phase)[None], jnp.sin(phase)[None])
    returning = jnp.stack([real, imag]).reshape(2, chans, 1, 1, 2, seg)
    gathered = lax.all_to_all(
        lax.all_to_all(returning, "outer", split_axis=5, concat_axis=2, tiled=True),
        "inner",
        split_axis=5,
        concat_axis=3,
        tiled=True,
    )
    gathered = gathered.reshape(2, chans, blocks, cols)
    cosine, sine = table(devices, blocks, blocks, 1.0)
    conv = contract("mk,ckj->cmj", cosine, gathered[0]) - contract("mk,ckj->cmj", sine, gathered[1])
    conv = conv * (1.0 / full)
    conv = lax.all_to_all(
        lax.all_to_all(
            conv.reshape(chans, devices, 1, 1, cols),
            "outer",
            split_axis=1,
            concat_axis=2,
            tiled=True,
        ),
        "inner",
        split_axis=1,
        concat_axis=3,
        tiled=True,
    )
    conv = conv.reshape(chans, seg)
    return gate * (conv + skip_gain[:, None] * product)


def halves(array):
    high = array.astype(ml_dtypes.bfloat16)
    low = (array - high.astype(np.float64)).astype(ml_dtypes.bfloat16)
    return high, low


def transform_tables(devices, seg):
    length = devices * seg
    count = length // LANES
    odd = 2 * np.arange(count) + 1
    angle = 2 * np.pi / (4 * count) * ((odd[:, None] * np.arange(count)[None, :]) % (4 * count))
    first = np.concatenate([np.cos(angle), -np.sin(angle)], axis=0)
    last = np.concatenate([np.cos(angle).T, -np.sin(angle).T], axis=1) / length
    angle = 2 * np.pi / (4 * length) * ((odd[:, None] * np.arange(LANES)[None, :]) % (4 * length))
    twiddle = np.stack([np.cos(angle), np.sin(angle)]).astype(np.float32)
    angle = 2 * np.pi / LANES * ((np.arange(LANES)[:, None] * np.arange(LANES)[None, :]) % LANES)
    cosine, sine = np.cos(angle), np.sin(angle)
    rows = np.block([[cosine, -sine], [sine, cosine]])
    back = np.block([[cosine, sine], [-sine, cosine]])
    first_high, first_low = halves(first)
    rows_high, rows_low = halves(rows)
    back_high, back_low = halves(back)
    last_high, last_low = halves(last)
    return (
        np.concatenate([first_high, first_high, first_low, first_low], axis=1),
        np.concatenate([rows_high, rows_high, rows_high, rows_low], axis=0),
        np.concatenate([back_high, back_high, back_low], axis=0),
        np.concatenate([last_high, last_high, last_low], axis=1),
        twiddle,
    )


def send_orders(outer, inner):
    quarter = outer // 4
    ring = [part * 2 + at // 2 * 4 + core for part in range(2) for at in range(0, quarter * 2, 2) for core in range(2)] if outer == 8 else list(range(outer))
    first = [at * inner + step for at in ring for step in range(inner)]
    second = [at * inner + step for at in range(outer) for step in [*range(1, inner), 0]]
    return first, second


def split(array, count=2):
    parts = []
    for _ in range(count):
        parts.append(array.astype(jnp.bfloat16))
        array = array - parts[-1].astype(jnp.float32)
    return parts


def dot(left, right):
    return jnp.dot(left, right, preferred_element_type=jnp.float32)


def convolve_kernel(
    devices, chans, seg, data_ref, first_ref, rows_ref, back_ref, last_ref, twiddle_ref, out_ref, signal_ref
):
    parts = seg // LANES
    count = devices * parts
    cosine, sine = twiddle_ref[0], twiddle_ref[1]

    def lanes(at):
        return slice(at * LANES, (at + 1) * LANES)

    first, second = send_orders(lax.axis_size("outer"), lax.axis_size("inner"))

    groups = chans
    each = chans // groups
    at = range(groups)
    for group in at:
        for kind in range(2):
            for chan in range(each):
                for device in range(devices):
                    came = ((device * 2 + kind) * chans + group * each + chan) * parts
                    to = first[device] * parts
                    signal_ref[group, to : to + parts, lanes(kind * each + chan)] = data_ref[came : came + parts, :]

    def start(group):
        high, low = split(signal_ref[group])
        return dot(first_ref[...], jnp.concatenate([high, low, high, low], axis=0))

    def spectra(begun):
        turned = []
        for signal in range(2 * each):
            real, imag = begun[:count, lanes(signal)], begun[count:, lanes(signal)]
            turned.append(jnp.concatenate([real * cosine + imag * sine, imag * cosine - real * sine], axis=1))
        high, low, rest = split(jnp.concatenate(turned, axis=0), 3)
        return dot(jnp.concatenate([high, low, rest, high], axis=1), rows_ref[...])

    def back(spectrum):
        mid = each * count
        sig_real, sig_imag = spectrum[:mid, :LANES], spectrum[:mid, LANES:]
        filt_real, filt_imag = spectrum[mid:, :LANES], spectrum[mid:, LANES:]
        real = sig_real * filt_real - sig_imag * filt_imag
        imag = sig_real * filt_imag + sig_imag * filt_real
        high, low = split(jnp.concatenate([real, imag], axis=1))
        return dot(jnp.concatenate([high, low, high], axis=1), back_ref[...])

    def end(backed):
        turned = []
        for chan in range(each):
            real = backed[chan * count : (chan + 1) * count, :LANES]
            imag = backed[chan * count : (chan + 1) * count, LANES:]
            turned.append(jnp.concatenate([real * cosine - imag * sine, imag * cosine + real * sine], axis=0))
        high, low = split(jnp.concatenate(turned, axis=1))
        return dot(last_ref[...], jnp.concatenate([high, low, high], axis=0))

    begun = [start(group) for group in at]
    spectrum = [spectra(begun[group]) for group in at]
    backed = [back(spectrum[group]) for group in at]
    conv = [end(backed[group]) for group in at]
    for group in at:
        for chan in range(each):
            own = group * each + chan
            for device in range(devices):
                to = (device * chans + own) * parts
                came = second[device] * parts
                out_ref[to : to + parts, :] = conv[group][came : came + parts, lanes(chan)]


def gather_kernel(order, product_ref, taps_ref, out_ref):
    rows = product_ref.shape[0] * product_ref.shape[1] // LANES // len(order)
    for kind, ref in enumerate((product_ref, taps_ref)):
        source = ref[...].reshape(len(order) * rows, LANES)
        for at, rank in enumerate(order):
            to = (2 * at + kind) * rows
            out_ref[to : to + rows, :] = source[rank * rows : (rank + 1) * rows]


def gate_kernel(order, gate_ref, skip_ref, conv_ref, out_hbm, out_ref, sems):
    chans, seg = gate_ref.shape
    pieces = sems.shape[0]
    step = chans // pieces
    rows = conv_ref.shape[0] // len(order)
    each = len(order) // pieces
    place = {rank: at * rows for at, rank in enumerate(order)}
    copies = []
    for piece in range(pieces):
        at = slice(piece * step, (piece + 1) * step)
        came = [conv_ref[place[rank] : place[rank] + rows, :] for rank in range(piece * each, (piece + 1) * each)]
        conv = jnp.concatenate(came, axis=0).reshape(step, seg)
        out_ref[at, :] = gate_ref[at, :] * (conv + skip_ref[at, :])
        copies.append(pltpu.make_async_copy(out_ref.at[at, :], out_hbm.at[at, :], sems.at[piece]))
        copies[piece].start()
    for copy in copies:
        copy.wait()


def on_core(kernel, shape, moved, flops=10**6, scratch=(), **more):
    return pl.pallas_call(
        kernel,
        out_shape=jax.ShapeDtypeStruct(shape, jnp.float32),
        scratch_shapes=scratch,
        compiler_params=pltpu.CompilerParams(vmem_limit_bytes=32 * 2**20),
        cost_estimate=pl.CostEstimate(flops=flops, bytes_accessed=moved, transcendentals=0),
        **more,
    )


def by_channels(gate, keys, values, taps, skip_gain):
    devices = lax.axis_size("outer") * lax.axis_size("inner")
    chans, seg = keys.shape
    own = chans // devices
    tiles = seg // LANES
    tables = [jnp.asarray(table) for table in transform_tables(devices, seg)]
    orders = send_orders(lax.axis_size("outer"), lax.axis_size("inner"))

    def regroup(rows, order):
        return lax.all_to_all(rows, AXES, split_axis=0, concat_axis=0, tiled=True, axis_index_groups=[order])

    product = keys * values
    product, skip = lax.optimization_barrier((product, skip_gain[:, None] * product))
    sent = on_core(partial(gather_kernel, orders[0]), (2 * chans * tiles, LANES), 4 * chans * seg * 4)(product, taps)
    groups = own
    conv = on_core(
        partial(convolve_kernel, devices, own, seg),
        (chans * tiles, LANES),
        2 * 10**6,
        10**9,
        [pltpu.VMEM((groups, devices * tiles, 2 * own // groups * LANES), jnp.float32)],
    )(regroup(sent, orders[0]), *tables)
    pieces = 4
    return on_core(
        partial(gate_kernel, orders[1]),
        (chans, seg),
        4 * chans * seg * 4,
        scratch=[pltpu.VMEM((chans, seg), jnp.float32), pltpu.SemaphoreType.DMA((pieces,))],
        out_specs=pl.BlockSpec(memory_space=pl.ANY),
    )(gate, skip, regroup(conv, orders[1]))


def on_device(gate, keys, values, taps, skip_gain):
    devices = lax.axis_size("outer") * lax.axis_size("inner")
    chans, seg = keys.shape
    if chans % devices == 0 and seg % LANES == 0 and devices % 8 == 0:
        return by_channels(gate, keys, values, taps, skip_gain)
    return by_sections(gate, keys, values, taps, skip_gain)


def solution(mesh):
    placed = (
        P(None, ("outer", "inner")),
        P(None, ("outer", "inner")),
        P(None, ("outer", "inner")),
        P(None, ("outer", "inner")),
        P(),
    )
    return jax.shard_map(
        on_device,
        mesh=mesh,
        in_specs=placed,
        out_specs=P(None, ("outer", "inner")),
        check_vma=False,
    )
```

```python
from functools import partial
import math

import jax
import jax.numpy as jnp
import ml_dtypes
import numpy as np
from jax import lax
from jax.experimental import pallas as pl
from jax.experimental.pallas import tpu as pltpu
from jax.sharding import PartitionSpec as P

LANES = 128
AXES = ("outer", "inner")

TWO_PI = 2.0 * math.pi
HIGHEST = lax.Precision.HIGHEST


def table(count_a, count_b, modulus, sign):
    left = lax.broadcasted_iota(jnp.int32, (count_a, count_b), 0)
    right = lax.broadcasted_iota(jnp.int32, (count_a, count_b), 1)
    phase = TWO_PI / modulus * (left * right % modulus).astype(jnp.float32)
    return (jnp.cos(phase), sign * jnp.sin(phase))


def mix(form, cosine, sine, real, imag):
    contract = partial(jnp.einsum, precision=HIGHEST)
    return (
        contract(form, cosine, real) - contract(form, sine, imag),
        contract(form, sine, real) + contract(form, cosine, imag),
    )


def rotate(real, imag, cosine, sine):
    return (real * cosine - imag * sine, real * sine + imag * cosine)


def forward_rows(real, imag):
    split = 16
    lead = real.shape[:-1]
    size = real.shape[-1]
    short = size // split
    real = real.reshape(lead + (split, short))
    imag = imag.reshape(lead + (split, short))
    cosine, sine = table(split, split, split, -1.0)
    real, imag = mix("ka,...as->...ks", cosine, sine, real, imag)
    cosine, sine = table(split, short, size, -1.0)
    real, imag = rotate(real, imag, cosine, sine)
    cosine, sine = table(short, short, short, -1.0)
    real, imag = mix("sb,...ks->...bk", cosine, sine, real, imag)
    return (real.reshape(lead + (size,)), imag.reshape(lead + (size,)))


def inverse_rows(real, imag):
    split = 16
    lead = real.shape[:-1]
    size = real.shape[-1]
    short = size // split
    real = real.reshape(lead + (short, split))
    imag = imag.reshape(lead + (short, split))
    cosine, sine = table(short, short, short, 1.0)
    real, imag = mix("sb,...bk->...sk", cosine, sine, real, imag)
    cosine, sine = table(short, split, size, 1.0)
    real, imag = rotate(real, imag, cosine, sine)
    cosine, sine = table(split, split, split, 1.0)
    real, imag = mix("ak,...sk->...as", cosine, sine, real, imag)
    return (real.reshape(lead + (size,)), imag.reshape(lead + (size,)))


def by_sections(gate, keys, values, taps, skip_gain):
    inner_count = lax.axis_size("inner")
    devices = lax.axis_size("outer") * inner_count
    rank = lax.axis_index("outer") * inner_count + lax.axis_index("inner")
    chans, seg = keys.shape
    both = 2 * chans
    cols = seg // devices
    blocks = 2 * devices
    full = blocks * seg
    contract = partial(jnp.einsum, precision=HIGHEST)
    product = keys * values
    source = jnp.concatenate([product, taps], axis=0)
    sectioned = lax.all_to_all(
        lax.all_to_all(
            source.reshape(both, 1, 1, seg), "outer", split_axis=3, concat_axis=1, tiled=True
        ),
        "inner",
        split_axis=3,
        concat_axis=2,
        tiled=True,
    )
    sectioned = sectioned.reshape(both, devices, cols)
    cosine, sine = table(blocks, devices, blocks, -1.0)
    real = contract("km,cmj->ckj", cosine, sectioned)
    imag = contract("km,cmj->ckj", sine, sectioned)
    offset = rank * cols + lax.broadcasted_iota(jnp.int32, (blocks, cols), 1)
    residue = lax.broadcasted_iota(jnp.int32, (blocks, cols), 0)
    phase = TWO_PI / full * (offset * residue).astype(jnp.float32)
    real, imag = rotate(real, imag, jnp.cos(phase)[None], -jnp.sin(phase)[None])
    outgoing = jnp.stack([real, imag]).reshape(2, both, blocks, 1, 1, cols)
    moved = lax.all_to_all(
        lax.all_to_all(outgoing, "outer", split_axis=2, concat_axis=3, tiled=True),
        "inner",
        split_axis=2,
        concat_axis=4,
        tiled=True,
    )
    moved = moved.reshape(2, both, 2, seg)
    spec_real, spec_imag = forward_rows(moved[0], moved[1])
    sig_real, filt_real = (spec_real[:chans], spec_real[chans:])
    sig_imag, filt_imag = (spec_imag[:chans], spec_imag[chans:])
    real = sig_real * filt_real - sig_imag * filt_imag
    imag = sig_real * filt_imag + sig_imag * filt_real
    real, imag = inverse_rows(real, imag)
    residue = 2 * rank + lax.broadcasted_iota(jnp.int32, (2, seg), 0)
    offset = lax.broadcasted_iota(jnp.int32, (2, seg), 1)
    phase = TWO_PI / full * (offset * residue).astype(jnp.float32)
    real, imag = rotate(real, imag, jnp.cos(phase)[None], jnp.sin(phase)[None])
    returning = jnp.stack([real, imag]).reshape(2, chans, 1, 1, 2, seg)
    gathered = lax.all_to_all(
        lax.all_to_all(returning, "outer", split_axis=5, concat_axis=2, tiled=True),
        "inner",
        split_axis=5,
        concat_axis=3,
        tiled=True,
    )
    gathered = gathered.reshape(2, chans, blocks, cols)
    cosine, sine = table(devices, blocks, blocks, 1.0)
    conv = contract("mk,ckj->cmj", cosine, gathered[0]) - contract("mk,ckj->cmj", sine, gathered[1])
    conv = conv * (1.0 / full)
    conv = lax.all_to_all(
        lax.all_to_all(
            conv.reshape(chans, devices, 1, 1, cols),
            "outer",
            split_axis=1,
            concat_axis=2,
            tiled=True,
        ),
        "inner",
        split_axis=1,
        concat_axis=3,
        tiled=True,
    )
    conv = conv.reshape(chans, seg)
    return gate * (conv + skip_gain[:, None] * product)


def halves(array):
    high = array.astype(ml_dtypes.bfloat16)
    low = (array - high.astype(np.float64)).astype(ml_dtypes.bfloat16)
    return high, low


def transform_tables(devices, seg):
    length = devices * seg
    count = length // LANES
    odd = 2 * np.arange(count) + 1
    angle = 2 * np.pi / (4 * count) * ((odd[:, None] * np.arange(count)[None, :]) % (4 * count))
    first = np.concatenate([np.cos(angle), -np.sin(angle)], axis=0)
    last = np.concatenate([np.cos(angle).T, -np.sin(angle).T], axis=1) / length
    angle = 2 * np.pi / (4 * length) * ((odd[:, None] * np.arange(LANES)[None, :]) % (4 * length))
    twiddle = np.stack([np.cos(angle), np.sin(angle)]).astype(np.float32)
    angle = 2 * np.pi / LANES * ((np.arange(LANES)[:, None] * np.arange(LANES)[None, :]) % LANES)
    cosine, sine = np.cos(angle), np.sin(angle)
    rows = np.block([[cosine, -sine], [sine, cosine]])
    back = np.block([[cosine, sine], [-sine, cosine]])
    first_high, first_low = halves(first)
    rows_high, rows_low = halves(rows)
    back_high, back_low = halves(back)
    last_high, last_low = halves(last)
    return (
        np.concatenate([first_high, first_high, first_low, first_low], axis=1),
        np.concatenate([rows_high, rows_high, rows_high, rows_low], axis=0),
        np.concatenate([back_high, back_high, back_low], axis=0),
        np.concatenate([last_high, last_high, last_low], axis=1),
        twiddle,
    )


def send_orders(outer, inner):
    half = inner // 2
    turns = [at // 2 + half * (at % 2) for at in range(2 * half)] + list(range(2 * half, inner))
    ring, apart = list(range(outer)), list(range(outer))
    if outer == 8:
        ring, apart = [0, 1, 5, 4, 6, 7, 3, 2], [0, 2, 5, 6, 1, 3, 4, 7]
    first = [at * inner + step for at in ring for step in range(inner)]
    second = [at * inner + step for at in apart for step in turns[1:] + turns[:1]]
    return first, second


def split(array, count=2):
    parts = []
    for _ in range(count):
        parts.append(array.astype(jnp.bfloat16))
        array = array - parts[-1].astype(jnp.float32)
    return parts


def dot(left, right):
    return jnp.dot(left, right, preferred_element_type=jnp.float32)


def convolve_kernel(
    devices, chans, seg, data_ref, first_ref, rows_ref, back_ref, last_ref, twiddle_ref, out_ref, signal_ref
):
    parts = seg // LANES
    count = devices * parts
    cosine, sine = twiddle_ref[0], twiddle_ref[1]

    def lanes(at):
        return slice(at * LANES, (at + 1) * LANES)

    first, second = send_orders(lax.axis_size("outer"), lax.axis_size("inner"))

    groups = chans
    each = chans // groups
    at = range(groups)
    for group in at:
        for kind in range(2):
            for chan in range(each):
                for device in range(devices):
                    came = ((device * 2 + kind) * chans + group * each + chan) * parts
                    to = first[device] * parts
                    signal_ref[group, to : to + parts, lanes(kind * each + chan)] = data_ref[came : came + parts, :]

    def start(group):
        high, low = split(signal_ref[group])
        return dot(first_ref[...], jnp.concatenate([high, low, high, low], axis=0))

    def spectra(begun):
        turned = []
        for signal in range(2 * each):
            real, imag = begun[:count, lanes(signal)], begun[count:, lanes(signal)]
            turned.append(jnp.concatenate([real * cosine + imag * sine, imag * cosine - real * sine], axis=1))
        high, low, rest = split(jnp.concatenate(turned, axis=0), 3)
        return dot(jnp.concatenate([high, low, rest, high], axis=1), rows_ref[...])

    def back(spectrum):
        mid = each * count
        sig_real, sig_imag = spectrum[:mid, :LANES], spectrum[:mid, LANES:]
        filt_real, filt_imag = spectrum[mid:, :LANES], spectrum[mid:, LANES:]
        real = sig_real * filt_real - sig_imag * filt_imag
        imag = sig_real * filt_imag + sig_imag * filt_real
        high, low = split(jnp.concatenate([real, imag], axis=1))
        return dot(jnp.concatenate([high, low, high], axis=1), back_ref[...])

    def end(backed):
        turned = []
        for chan in range(each):
            real = backed[chan * count : (chan + 1) * count, :LANES]
            imag = backed[chan * count : (chan + 1) * count, LANES:]
            turned.append(jnp.concatenate([real * cosine - imag * sine, imag * cosine + real * sine], axis=0))
        high, low = split(jnp.concatenate(turned, axis=1))
        return dot(last_ref[...], jnp.concatenate([high, low, high], axis=0))

    begun = [start(group) for group in at]
    spectrum = [spectra(begun[group]) for group in at]
    backed = [back(spectrum[group]) for group in at]
    conv = [end(backed[group]) for group in at]
    for group in at:
        for chan in range(each):
            own = group * each + chan
            for device in range(devices):
                to = (device * chans + own) * parts
                came = second[device] * parts
                out_ref[to : to + parts, :] = conv[group][came : came + parts, lanes(chan)]


def gather_kernel(order, product_ref, taps_ref, out_ref):
    rows = product_ref.shape[0] * product_ref.shape[1] // LANES // len(order)
    for kind, ref in enumerate((product_ref, taps_ref)):
        source = ref[...].reshape(len(order) * rows, LANES)
        for at, rank in enumerate(order):
            to = (2 * at + kind) * rows
            out_ref[to : to + rows, :] = source[rank * rows : (rank + 1) * rows]


def gate_kernel(order, gate_ref, skip_ref, conv_ref, out_hbm, out_ref, sems):
    chans, seg = gate_ref.shape
    pieces = sems.shape[0]
    step = chans // pieces
    rows = conv_ref.shape[0] // len(order)
    each = len(order) // pieces
    place = {rank: at * rows for at, rank in enumerate(order)}
    copies = []
    for piece in range(pieces):
        at = slice(piece * step, (piece + 1) * step)
        came = [conv_ref[place[rank] : place[rank] + rows, :] for rank in range(piece * each, (piece + 1) * each)]
        conv = jnp.concatenate(came, axis=0).reshape(step, seg)
        out_ref[at, :] = gate_ref[at, :] * (conv + skip_ref[at, :])
        copies.append(pltpu.make_async_copy(out_ref.at[at, :], out_hbm.at[at, :], sems.at[piece]))
        copies[piece].start()
    for copy in copies:
        copy.wait()


def on_core(kernel, shape, moved, flops=10**6, scratch=(), **more):
    return pl.pallas_call(
        kernel,
        out_shape=jax.ShapeDtypeStruct(shape, jnp.float32),
        scratch_shapes=scratch,
        compiler_params=pltpu.CompilerParams(vmem_limit_bytes=32 * 2**20),
        cost_estimate=pl.CostEstimate(flops=flops, bytes_accessed=moved, transcendentals=0),
        **more,
    )


def by_channels(gate, keys, values, taps, skip_gain):
    devices = lax.axis_size("outer") * lax.axis_size("inner")
    chans, seg = keys.shape
    own = chans // devices
    tiles = seg // LANES
    tables = [jnp.asarray(table) for table in transform_tables(devices, seg)]
    orders = send_orders(lax.axis_size("outer"), lax.axis_size("inner"))

    def regroup(rows, order):
        return lax.all_to_all(rows, AXES, split_axis=0, concat_axis=0, tiled=True, axis_index_groups=[order])

    product = keys * values
    product, skip = lax.optimization_barrier((product, skip_gain[:, None] * product))
    sent = on_core(partial(gather_kernel, orders[0]), (2 * chans * tiles, LANES), 4 * chans * seg * 4)(product, taps)
    groups = own
    conv = on_core(
        partial(convolve_kernel, devices, own, seg),
        (chans * tiles, LANES),
        2 * 10**6,
        10**9,
        [pltpu.VMEM((groups, devices * tiles, 2 * own // groups * LANES), jnp.float32)],
    )(regroup(sent, orders[0]), *tables)
    pieces = 4
    return on_core(
        partial(gate_kernel, orders[1]),
        (chans, seg),
        4 * chans * seg * 4,
        scratch=[pltpu.VMEM((chans, seg), jnp.float32), pltpu.SemaphoreType.DMA((pieces,))],
        out_specs=pl.BlockSpec(memory_space=pl.ANY),
    )(gate, skip, regroup(conv, orders[1]))


def on_device(gate, keys, values, taps, skip_gain):
    devices = lax.axis_size("outer") * lax.axis_size("inner")
    chans, seg = keys.shape
    if chans % devices == 0 and seg % LANES == 0 and devices % 8 == 0:
        return by_channels(gate, keys, values, taps, skip_gain)
    return by_sections(gate, keys, values, taps, skip_gain)


def solution(mesh):
    placed = (
        P(None, ("outer", "inner")),
        P(None, ("outer", "inner")),
        P(None, ("outer", "inner")),
        P(None, ("outer", "inner")),
        P(),
    )
    return jax.shard_map(
        on_device,
        mesh=mesh,
        in_specs=placed,
        out_specs=P(None, ("outer", "inner")),
        check_vma=False,
    )
```

```python
from functools import partial
import math

import jax
import jax.numpy as jnp
import ml_dtypes
import numpy as np
from jax import lax
from jax.experimental import pallas as pl
from jax.experimental.pallas import tpu as pltpu
from jax.sharding import PartitionSpec as P

LANES = 128
AXES = ("outer", "inner")

TWO_PI = 2.0 * math.pi
HIGHEST = lax.Precision.HIGHEST


def table(count_a, count_b, modulus, sign):
    left = lax.broadcasted_iota(jnp.int32, (count_a, count_b), 0)
    right = lax.broadcasted_iota(jnp.int32, (count_a, count_b), 1)
    phase = TWO_PI / modulus * (left * right % modulus).astype(jnp.float32)
    return (jnp.cos(phase), sign * jnp.sin(phase))


def mix(form, cosine, sine, real, imag):
    contract = partial(jnp.einsum, precision=HIGHEST)
    return (
        contract(form, cosine, real) - contract(form, sine, imag),
        contract(form, sine, real) + contract(form, cosine, imag),
    )


def rotate(real, imag, cosine, sine):
    return (real * cosine - imag * sine, real * sine + imag * cosine)


def forward_rows(real, imag):
    split = 16
    lead = real.shape[:-1]
    size = real.shape[-1]
    short = size // split
    real = real.reshape(lead + (split, short))
    imag = imag.reshape(lead + (split, short))
    cosine, sine = table(split, split, split, -1.0)
    real, imag = mix("ka,...as->...ks", cosine, sine, real, imag)
    cosine, sine = table(split, short, size, -1.0)
    real, imag = rotate(real, imag, cosine, sine)
    cosine, sine = table(short, short, short, -1.0)
    real, imag = mix("sb,...ks->...bk", cosine, sine, real, imag)
    return (real.reshape(lead + (size,)), imag.reshape(lead + (size,)))


def inverse_rows(real, imag):
    split = 16
    lead = real.shape[:-1]
    size = real.shape[-1]
    short = size // split
    real = real.reshape(lead + (short, split))
    imag = imag.reshape(lead + (short, split))
    cosine, sine = table(short, short, short, 1.0)
    real, imag = mix("sb,...bk->...sk", cosine, sine, real, imag)
    cosine, sine = table(short, split, size, 1.0)
    real, imag = rotate(real, imag, cosine, sine)
    cosine, sine = table(split, split, split, 1.0)
    real, imag = mix("ak,...sk->...as", cosine, sine, real, imag)
    return (real.reshape(lead + (size,)), imag.reshape(lead + (size,)))


def by_sections(gate, keys, values, taps, skip_gain):
    inner_count = lax.axis_size("inner")
    devices = lax.axis_size("outer") * inner_count
    rank = lax.axis_index("outer") * inner_count + lax.axis_index("inner")
    chans, seg = keys.shape
    both = 2 * chans
    cols = seg // devices
    blocks = 2 * devices
    full = blocks * seg
    contract = partial(jnp.einsum, precision=HIGHEST)
    product = keys * values
    source = jnp.concatenate([product, taps], axis=0)
    sectioned = lax.all_to_all(
        lax.all_to_all(
            source.reshape(both, 1, 1, seg), "outer", split_axis=3, concat_axis=1, tiled=True
        ),
        "inner",
        split_axis=3,
        concat_axis=2,
        tiled=True,
    )
    sectioned = sectioned.reshape(both, devices, cols)
    cosine, sine = table(blocks, devices, blocks, -1.0)
    real = contract("km,cmj->ckj", cosine, sectioned)
    imag = contract("km,cmj->ckj", sine, sectioned)
    offset = rank * cols + lax.broadcasted_iota(jnp.int32, (blocks, cols), 1)
    residue = lax.broadcasted_iota(jnp.int32, (blocks, cols), 0)
    phase = TWO_PI / full * (offset * residue).astype(jnp.float32)
    real, imag = rotate(real, imag, jnp.cos(phase)[None], -jnp.sin(phase)[None])
    outgoing = jnp.stack([real, imag]).reshape(2, both, blocks, 1, 1, cols)
    moved = lax.all_to_all(
        lax.all_to_all(outgoing, "outer", split_axis=2, concat_axis=3, tiled=True),
        "inner",
        split_axis=2,
        concat_axis=4,
        tiled=True,
    )
    moved = moved.reshape(2, both, 2, seg)
    spec_real, spec_imag = forward_rows(moved[0], moved[1])
    sig_real, filt_real = (spec_real[:chans], spec_real[chans:])
    sig_imag, filt_imag = (spec_imag[:chans], spec_imag[chans:])
    real = sig_real * filt_real - sig_imag * filt_imag
    imag = sig_real * filt_imag + sig_imag * filt_real
    real, imag = inverse_rows(real, imag)
    residue = 2 * rank + lax.broadcasted_iota(jnp.int32, (2, seg), 0)
    offset = lax.broadcasted_iota(jnp.int32, (2, seg), 1)
    phase = TWO_PI / full * (offset * residue).astype(jnp.float32)
    real, imag = rotate(real, imag, jnp.cos(phase)[None], jnp.sin(phase)[None])
    returning = jnp.stack([real, imag]).reshape(2, chans, 1, 1, 2, seg)
    gathered = lax.all_to_all(
        lax.all_to_all(returning, "outer", split_axis=5, concat_axis=2, tiled=True),
        "inner",
        split_axis=5,
        concat_axis=3,
        tiled=True,
    )
    gathered = gathered.reshape(2, chans, blocks, cols)
    cosine, sine = table(devices, blocks, blocks, 1.0)
    conv = contract("mk,ckj->cmj", cosine, gathered[0]) - contract("mk,ckj->cmj", sine, gathered[1])
    conv = conv * (1.0 / full)
    conv = lax.all_to_all(
        lax.all_to_all(
            conv.reshape(chans, devices, 1, 1, cols),
            "outer",
            split_axis=1,
            concat_axis=2,
            tiled=True,
        ),
        "inner",
        split_axis=1,
        concat_axis=3,
        tiled=True,
    )
    conv = conv.reshape(chans, seg)
    return gate * (conv + skip_gain[:, None] * product)


def halves(array):
    high = array.astype(ml_dtypes.bfloat16)
    low = (array - high.astype(np.float64)).astype(ml_dtypes.bfloat16)
    return high, low


def transform_tables(devices, seg):
    length = devices * seg
    count = length // LANES
    odd = 2 * np.arange(count) + 1
    angle = 2 * np.pi / (4 * count) * ((odd[:, None] * np.arange(count)[None, :]) % (4 * count))
    first = np.concatenate([np.cos(angle), -np.sin(angle)], axis=0)
    last = np.concatenate([np.cos(angle).T, -np.sin(angle).T], axis=1) / length
    angle = 2 * np.pi / (4 * length) * ((odd[:, None] * np.arange(LANES)[None, :]) % (4 * length))
    twiddle = np.stack([np.cos(angle), np.sin(angle)]).astype(np.float32)
    angle = 2 * np.pi / LANES * ((np.arange(LANES)[:, None] * np.arange(LANES)[None, :]) % LANES)
    cosine, sine = np.cos(angle), np.sin(angle)
    rows = np.block([[cosine, -sine], [sine, cosine]])
    back = np.block([[cosine, sine], [-sine, cosine]])
    first_high, first_low = halves(first)
    rows_high, rows_low = halves(rows)
    back_high, back_low = halves(back)
    last_high, last_low = halves(last)
    return (
        np.concatenate([first_high, first_high, first_low, first_low], axis=1),
        np.concatenate([rows_high, rows_low], axis=0),
        np.concatenate([back_high, back_low], axis=0),
        np.concatenate([last_high, last_high, last_low], axis=1),
        twiddle,
    )


def send_orders(outer, inner):
    half = inner // 2
    turns = [at // 2 + half * (at % 2) for at in range(2 * half)] + list(range(2 * half, inner))
    ring = [at ^ (at >> 1) for at in range(outer)] if outer & (outer - 1) == 0 else list(range(outer))
    first = [at * inner + step for at in ring[:1] + ring[:0:-1] for step in range(inner)]
    second = [at * inner + step for at in range(outer) for step in turns[1:] + turns[:1]]
    return first, second


def split(array, count=2):
    parts = []
    for _ in range(count):
        parts.append(array.astype(jnp.bfloat16))
        array = array - parts[-1].astype(jnp.float32)
    return parts


def dot(left, right):
    return jnp.dot(left, right, preferred_element_type=jnp.float32)


def convolve_kernel(
    devices, chans, seg, data_ref, first_ref, rows_ref, back_ref, last_ref, twiddle_ref, out_ref, signal_ref
):
    parts = seg // LANES
    count = devices * parts
    cosine, sine = twiddle_ref[0], twiddle_ref[1]

    def lanes(at):
        return slice(at * LANES, (at + 1) * LANES)

    first, second = send_orders(lax.axis_size("outer"), lax.axis_size("inner"))

    groups = chans
    each = chans // groups
    at = range(groups)
    for group in at:
        for kind in range(2):
            for chan in range(each):
                for device in range(devices):
                    came = ((device * 2 + kind) * chans + group * each + chan) * parts
                    to = first[device] * parts
                    signal_ref[group, to : to + parts, lanes(kind * each + chan)] = data_ref[came : came + parts, :]

    def times(pieces, table_ref):
        size = table_ref.shape[0] // 2
        by_high = dot(jnp.concatenate(pieces, axis=0), table_ref[:size, :])
        total = dot(pieces[0], table_ref[size:, :])
        rows = total.shape[0]
        for piece in reversed(range(len(pieces))):
            total = total + by_high[piece * rows : (piece + 1) * rows]
        return total

    def start(group):
        high, low = split(signal_ref[group])
        return dot(first_ref[...], jnp.concatenate([high, low, high, low], axis=0))

    def spectra(begun):
        turned = []
        for signal in range(2 * each):
            real, imag = begun[:count, lanes(signal)], begun[count:, lanes(signal)]
            turned.append(jnp.concatenate([real * cosine + imag * sine, imag * cosine - real * sine], axis=1))
        return times(split(jnp.concatenate(turned, axis=0), 3), rows_ref)

    def back(spectrum):
        mid = each * count
        sig_real, sig_imag = spectrum[:mid, :LANES], spectrum[:mid, LANES:]
        filt_real, filt_imag = spectrum[mid:, :LANES], spectrum[mid:, LANES:]
        real = sig_real * filt_real - sig_imag * filt_imag
        imag = sig_real * filt_imag + sig_imag * filt_real
        return times(split(jnp.concatenate([real, imag], axis=1)), back_ref)

    def end(backed):
        turned = []
        for chan in range(each):
            real = backed[chan * count : (chan + 1) * count, :LANES]
            imag = backed[chan * count : (chan + 1) * count, LANES:]
            turned.append(jnp.concatenate([real * cosine - imag * sine, imag * cosine + real * sine], axis=0))
        high, low = split(jnp.concatenate(turned, axis=1))
        return dot(last_ref[...], jnp.concatenate([high, low, high], axis=0))

    begun = [start(group) for group in at]
    spectrum = [spectra(begun[group]) for group in at]
    backed = [back(spectrum[group]) for group in at]
    conv = [end(backed[group]) for group in at]
    for group in at:
        for chan in range(each):
            own = group * each + chan
            for device in range(devices):
                to = (device * chans + own) * parts
                came = second[device] * parts
                out_ref[to : to + parts, :] = conv[group][came : came + parts, lanes(chan)]


def gather_kernel(order, product_ref, taps_ref, out_ref):
    rows = product_ref.shape[0] * product_ref.shape[1] // LANES // len(order)
    for kind, ref in enumerate((product_ref, taps_ref)):
        source = ref[...].reshape(len(order) * rows, LANES)
        for at, rank in enumerate(order):
            to = (2 * at + kind) * rows
            out_ref[to : to + rows, :] = source[rank * rows : (rank + 1) * rows]


def gate_kernel(order, gate_ref, skip_ref, conv_ref, out_hbm, out_ref, sems):
    chans, seg = gate_ref.shape
    pieces = sems.shape[0]
    step = chans // pieces
    rows = conv_ref.shape[0] // len(order)
    each = len(order) // pieces
    place = {rank: at * rows for at, rank in enumerate(order)}
    copies = []
    for piece in range(pieces):
        at = slice(piece * step, (piece + 1) * step)
        came = [conv_ref[place[rank] : place[rank] + rows, :] for rank in range(piece * each, (piece + 1) * each)]
        conv = jnp.concatenate(came, axis=0).reshape(step, seg)
        out_ref[at, :] = gate_ref[at, :] * (conv + skip_ref[at, :])
        copies.append(pltpu.make_async_copy(out_ref.at[at, :], out_hbm.at[at, :], sems.at[piece]))
        copies[piece].start()
    for copy in copies:
        copy.wait()


def on_core(kernel, shape, moved, flops=10**6, scratch=(), **more):
    return pl.pallas_call(
        kernel,
        out_shape=jax.ShapeDtypeStruct(shape, jnp.float32),
        scratch_shapes=scratch,
        compiler_params=pltpu.CompilerParams(vmem_limit_bytes=32 * 2**20),
        cost_estimate=pl.CostEstimate(flops=flops, bytes_accessed=moved, transcendentals=0),
        **more,
    )


def by_channels(gate, keys, values, taps, skip_gain):
    devices = lax.axis_size("outer") * lax.axis_size("inner")
    chans, seg = keys.shape
    own = chans // devices
    tiles = seg // LANES
    tables = [jnp.asarray(table) for table in transform_tables(devices, seg)]
    orders = send_orders(lax.axis_size("outer"), lax.axis_size("inner"))

    def regroup(rows, order):
        return lax.all_to_all(rows, AXES, split_axis=0, concat_axis=0, tiled=True, axis_index_groups=[order])

    product = keys * values
    product, skip = lax.optimization_barrier((product, skip_gain[:, None] * product))
    sent = on_core(partial(gather_kernel, orders[0]), (2 * chans * tiles, LANES), 4 * chans * seg * 4)(product, taps)
    groups = own
    conv = on_core(
        partial(convolve_kernel, devices, own, seg),
        (chans * tiles, LANES),
        2 * 10**6,
        10**9,
        [pltpu.VMEM((groups, devices * tiles, 2 * own // groups * LANES), jnp.float32)],
    )(regroup(sent, orders[0]), *tables)
    pieces = 4
    return on_core(
        partial(gate_kernel, orders[1]),
        (chans, seg),
        4 * chans * seg * 4,
        scratch=[pltpu.VMEM((chans, seg), jnp.float32), pltpu.SemaphoreType.DMA((pieces,))],
        out_specs=pl.BlockSpec(memory_space=pl.ANY),
    )(gate, skip, regroup(conv, orders[1]))


def on_device(gate, keys, values, taps, skip_gain):
    devices = lax.axis_size("outer") * lax.axis_size("inner")
    chans, seg = keys.shape
    if chans % devices == 0 and seg % LANES == 0 and devices % 8 == 0:
        return by_channels(gate, keys, values, taps, skip_gain)
    return by_sections(gate, keys, values, taps, skip_gain)


def solution(mesh):
    placed = (
        P(None, ("outer", "inner")),
        P(None, ("outer", "inner")),
        P(None, ("outer", "inner")),
        P(None, ("outer", "inner")),
        P(),
    )
    return jax.shard_map(
        on_device,
        mesh=mesh,
        in_specs=placed,
        out_specs=P(None, ("outer", "inner")),
        check_vma=False,
    )
```

```python
from functools import partial
import math

import jax
import jax.numpy as jnp
import ml_dtypes
import numpy as np
from jax import lax
from jax.experimental import pallas as pl
from jax.experimental.pallas import tpu as pltpu
from jax.sharding import PartitionSpec as P

LANES = 128
AXES = ("outer", "inner")

TWO_PI = 2.0 * math.pi
HIGHEST = lax.Precision.HIGHEST


def table(count_a, count_b, modulus, sign):
    left = lax.broadcasted_iota(jnp.int32, (count_a, count_b), 0)
    right = lax.broadcasted_iota(jnp.int32, (count_a, count_b), 1)
    phase = TWO_PI / modulus * (left * right % modulus).astype(jnp.float32)
    return (jnp.cos(phase), sign * jnp.sin(phase))


def mix(form, cosine, sine, real, imag):
    contract = partial(jnp.einsum, precision=HIGHEST)
    return (
        contract(form, cosine, real) - contract(form, sine, imag),
        contract(form, sine, real) + contract(form, cosine, imag),
    )


def rotate(real, imag, cosine, sine):
    return (real * cosine - imag * sine, real * sine + imag * cosine)


def forward_rows(real, imag):
    split = 16
    lead = real.shape[:-1]
    size = real.shape[-1]
    short = size // split
    real = real.reshape(lead + (split, short))
    imag = imag.reshape(lead + (split, short))
    cosine, sine = table(split, split, split, -1.0)
    real, imag = mix("ka,...as->...ks", cosine, sine, real, imag)
    cosine, sine = table(split, short, size, -1.0)
    real, imag = rotate(real, imag, cosine, sine)
    cosine, sine = table(short, short, short, -1.0)
    real, imag = mix("sb,...ks->...bk", cosine, sine, real, imag)
    return (real.reshape(lead + (size,)), imag.reshape(lead + (size,)))


def inverse_rows(real, imag):
    split = 16
    lead = real.shape[:-1]
    size = real.shape[-1]
    short = size // split
    real = real.reshape(lead + (short, split))
    imag = imag.reshape(lead + (short, split))
    cosine, sine = table(short, short, short, 1.0)
    real, imag = mix("sb,...bk->...sk", cosine, sine, real, imag)
    cosine, sine = table(short, split, size, 1.0)
    real, imag = rotate(real, imag, cosine, sine)
    cosine, sine = table(split, split, split, 1.0)
    real, imag = mix("ak,...sk->...as", cosine, sine, real, imag)
    return (real.reshape(lead + (size,)), imag.reshape(lead + (size,)))


def by_sections(gate, keys, values, taps, skip_gain):
    inner_count = lax.axis_size("inner")
    devices = lax.axis_size("outer") * inner_count
    rank = lax.axis_index("outer") * inner_count + lax.axis_index("inner")
    chans, seg = keys.shape
    both = 2 * chans
    cols = seg // devices
    blocks = 2 * devices
    full = blocks * seg
    contract = partial(jnp.einsum, precision=HIGHEST)
    product = keys * values
    source = jnp.concatenate([product, taps], axis=0)
    sectioned = lax.all_to_all(
        lax.all_to_all(
            source.reshape(both, 1, 1, seg), "outer", split_axis=3, concat_axis=1, tiled=True
        ),
        "inner",
        split_axis=3,
        concat_axis=2,
        tiled=True,
    )
    sectioned = sectioned.reshape(both, devices, cols)
    cosine, sine = table(blocks, devices, blocks, -1.0)
    real = contract("km,cmj->ckj", cosine, sectioned)
    imag = contract("km,cmj->ckj", sine, sectioned)
    offset = rank * cols + lax.broadcasted_iota(jnp.int32, (blocks, cols), 1)
    residue = lax.broadcasted_iota(jnp.int32, (blocks, cols), 0)
    phase = TWO_PI / full * (offset * residue).astype(jnp.float32)
    real, imag = rotate(real, imag, jnp.cos(phase)[None], -jnp.sin(phase)[None])
    outgoing = jnp.stack([real, imag]).reshape(2, both, blocks, 1, 1, cols)
    moved = lax.all_to_all(
        lax.all_to_all(outgoing, "outer", split_axis=2, concat_axis=3, tiled=True),
        "inner",
        split_axis=2,
        concat_axis=4,
        tiled=True,
    )
    moved = moved.reshape(2, both, 2, seg)
    spec_real, spec_imag = forward_rows(moved[0], moved[1])
    sig_real, filt_real = (spec_real[:chans], spec_real[chans:])
    sig_imag, filt_imag = (spec_imag[:chans], spec_imag[chans:])
    real = sig_real * filt_real - sig_imag * filt_imag
    imag = sig_real * filt_imag + sig_imag * filt_real
    real, imag = inverse_rows(real, imag)
    residue = 2 * rank + lax.broadcasted_iota(jnp.int32, (2, seg), 0)
    offset = lax.broadcasted_iota(jnp.int32, (2, seg), 1)
    phase = TWO_PI / full * (offset * residue).astype(jnp.float32)
    real, imag = rotate(real, imag, jnp.cos(phase)[None], jnp.sin(phase)[None])
    returning = jnp.stack([real, imag]).reshape(2, chans, 1, 1, 2, seg)
    gathered = lax.all_to_all(
        lax.all_to_all(returning, "outer", split_axis=5, concat_axis=2, tiled=True),
        "inner",
        split_axis=5,
        concat_axis=3,
        tiled=True,
    )
    gathered = gathered.reshape(2, chans, blocks, cols)
    cosine, sine = table(devices, blocks, blocks, 1.0)
    conv = contract("mk,ckj->cmj", cosine, gathered[0]) - contract("mk,ckj->cmj", sine, gathered[1])
    conv = conv * (1.0 / full)
    conv = lax.all_to_all(
        lax.all_to_all(
            conv.reshape(chans, devices, 1, 1, cols),
            "outer",
            split_axis=1,
            concat_axis=2,
            tiled=True,
        ),
        "inner",
        split_axis=1,
        concat_axis=3,
        tiled=True,
    )
    conv = conv.reshape(chans, seg)
    return gate * (conv + skip_gain[:, None] * product)


def halves(array):
    high = array.astype(ml_dtypes.bfloat16)
    low = (array - high.astype(np.float64)).astype(ml_dtypes.bfloat16)
    return high, low


def transform_tables(devices, seg):
    length = devices * seg
    count = length // LANES
    odd = 2 * np.arange(count) + 1
    angle = 2 * np.pi / (4 * count) * ((odd[:, None] * np.arange(count)[None, :]) % (4 * count))
    first = np.concatenate([np.cos(angle), -np.sin(angle)], axis=0)
    last = np.concatenate([np.cos(angle).T, -np.sin(angle).T], axis=1) / length
    angle = 2 * np.pi / (4 * length) * ((odd[:, None] * np.arange(LANES)[None, :]) % (4 * length))
    twiddle = np.stack([np.cos(angle), np.sin(angle)]).astype(np.float32)
    angle = 2 * np.pi / LANES * ((np.arange(LANES)[:, None] * np.arange(LANES)[None, :]) % LANES)
    cosine, sine = np.cos(angle), np.sin(angle)
    rows = np.block([[cosine, -sine], [sine, cosine]])
    back = np.block([[cosine, sine], [-sine, cosine]])
    first_high, first_low = halves(first)
    rows_high, rows_low = halves(rows)
    back_high, back_low = halves(back)
    last_high, last_low = halves(last)
    return (
        np.concatenate([first_high, first_high, first_low, first_low], axis=1),
        np.concatenate([rows_high, rows_low], axis=0),
        np.concatenate([back_high, back_low], axis=0),
        np.concatenate([last_high, last_high, last_low], axis=1),
        twiddle,
    )


def send_orders(outer, inner):
    half = inner // 2
    turns = [at // 2 + half * (at % 2) for at in range(2 * half)] + list(range(2 * half, inner))
    ring = [at ^ (at >> 1) for at in range(outer)] if outer & (outer - 1) == 0 else list(range(outer))
    first = [at * inner + step for at in ring[:1] + ring[:0:-1] for step in range(inner)]
    second = [at * inner + step for at in range(outer) for step in turns[1:] + turns[:1]]
    return first, second


def split(array, count=2):
    parts = []
    for _ in range(count):
        parts.append(array.astype(jnp.bfloat16))
        array = array - parts[-1].astype(jnp.float32)
    return parts


def dot(left, right):
    return jnp.dot(left, right, preferred_element_type=jnp.float32)


def convolve_kernel(
    devices, chans, seg, data_ref, first_ref, rows_ref, back_ref, last_ref, twiddle_ref, out_ref, signal_ref
):
    parts = seg // LANES
    count = devices * parts
    cosine, sine = twiddle_ref[0], twiddle_ref[1]

    def lanes(at):
        return slice(at * LANES, (at + 1) * LANES)

    first, second = send_orders(lax.axis_size("outer"), lax.axis_size("inner"))

    groups = chans
    each = chans // groups
    at = range(groups)
    for group in at:
        for kind in range(2):
            for chan in range(each):
                for device in range(devices):
                    came = ((device * 2 + kind) * chans + group * each + chan) * parts
                    to = first[device] * parts
                    signal_ref[group, to : to + parts, lanes(kind * each + chan)] = data_ref[came : came + parts, :]

    def times(pieces, table_ref):
        size = table_ref.shape[0] // 2
        by_high = dot(jnp.concatenate(pieces, axis=0), table_ref[:size, :])
        total = dot(pieces[0], table_ref[size:, :])
        rows = total.shape[0]
        for piece in reversed(range(len(pieces))):
            total = total + by_high[piece * rows : (piece + 1) * rows]
        return total

    def start(group, kind):
        high, low = split(signal_ref[group, :, lanes(kind)])
        return dot(first_ref[...], jnp.concatenate([high, low, high, low], axis=0))

    def spectra(begun):
        real, imag = begun[:count], begun[count:]
        turned = jnp.concatenate([real * cosine + imag * sine, imag * cosine - real * sine], axis=1)
        return times(split(turned, 3), rows_ref)

    def back(signal, filt):
        sig_real, sig_imag = signal[:, :LANES], signal[:, LANES:]
        filt_real, filt_imag = filt[:, :LANES], filt[:, LANES:]
        real = sig_real * filt_real - sig_imag * filt_imag
        imag = sig_real * filt_imag + sig_imag * filt_real
        return times(split(jnp.concatenate([real, imag], axis=1)), back_ref)

    def end(backed):
        turned = []
        for chan in range(each):
            real = backed[chan * count : (chan + 1) * count, :LANES]
            imag = backed[chan * count : (chan + 1) * count, LANES:]
            turned.append(jnp.concatenate([real * cosine - imag * sine, imag * cosine + real * sine], axis=0))
        high, low = split(jnp.concatenate(turned, axis=1))
        return dot(last_ref[...], jnp.concatenate([high, low, high], axis=0))

    begun = [[start(group, kind) for kind in range(2)] for group in at]
    spectrum = [[spectra(begun[group][kind]) for kind in range(2)] for group in at]
    backed = [back(*spectrum[group]) for group in at]
    conv = [end(backed[group]) for group in at]
    for group in at:
        for chan in range(each):
            own = group * each + chan
            for device in range(devices):
                to = (device * chans + own) * parts
                came = second[device] * parts
                out_ref[to : to + parts, :] = conv[group][came : came + parts, lanes(chan)]


def gather_kernel(order, product_ref, taps_ref, out_ref):
    rows = product_ref.shape[0] * product_ref.shape[1] // LANES // len(order)
    for kind, ref in enumerate((product_ref, taps_ref)):
        source = ref[...].reshape(len(order) * rows, LANES)
        for at, rank in enumerate(order):
            to = (2 * at + kind) * rows
            out_ref[to : to + rows, :] = source[rank * rows : (rank + 1) * rows]


def gate_kernel(order, gate_ref, skip_ref, conv_ref, out_hbm, out_ref, sems):
    chans, seg = gate_ref.shape
    pieces = sems.shape[0]
    step = chans // pieces
    rows = conv_ref.shape[0] // len(order)
    each = len(order) // pieces
    place = {rank: at * rows for at, rank in enumerate(order)}
    copies = []
    for piece in range(pieces):
        at = slice(piece * step, (piece + 1) * step)
        came = [conv_ref[place[rank] : place[rank] + rows, :] for rank in range(piece * each, (piece + 1) * each)]
        conv = jnp.concatenate(came, axis=0).reshape(step, seg)
        out_ref[at, :] = gate_ref[at, :] * (conv + skip_ref[at, :])
        copies.append(pltpu.make_async_copy(out_ref.at[at, :], out_hbm.at[at, :], sems.at[piece]))
        copies[piece].start()
    for copy in copies:
        copy.wait()


def on_core(kernel, shape, moved, flops=10**6, scratch=(), **more):
    return pl.pallas_call(
        kernel,
        out_shape=jax.ShapeDtypeStruct(shape, jnp.float32),
        scratch_shapes=scratch,
        compiler_params=pltpu.CompilerParams(vmem_limit_bytes=32 * 2**20),
        cost_estimate=pl.CostEstimate(flops=flops, bytes_accessed=moved, transcendentals=0),
        **more,
    )


def by_channels(gate, keys, values, taps, skip_gain):
    devices = lax.axis_size("outer") * lax.axis_size("inner")
    chans, seg = keys.shape
    own = chans // devices
    tiles = seg // LANES
    tables = [jnp.asarray(table) for table in transform_tables(devices, seg)]
    orders = send_orders(lax.axis_size("outer"), lax.axis_size("inner"))

    def regroup(rows, order):
        return lax.all_to_all(rows, AXES, split_axis=0, concat_axis=0, tiled=True, axis_index_groups=[order])

    product = keys * values
    product, skip = lax.optimization_barrier((product, skip_gain[:, None] * product))
    sent = on_core(partial(gather_kernel, orders[0]), (2 * chans * tiles, LANES), 4 * chans * seg * 4)(product, taps)
    groups = own
    conv = on_core(
        partial(convolve_kernel, devices, own, seg),
        (chans * tiles, LANES),
        2 * 10**6,
        10**9,
        [pltpu.VMEM((groups, devices * tiles, 2 * own // groups * LANES), jnp.float32)],
    )(regroup(sent, orders[0]), *tables)
    pieces = 4
    return on_core(
        partial(gate_kernel, orders[1]),
        (chans, seg),
        4 * chans * seg * 4,
        scratch=[pltpu.VMEM((chans, seg), jnp.float32), pltpu.SemaphoreType.DMA((pieces,))],
        out_specs=pl.BlockSpec(memory_space=pl.ANY),
    )(gate, skip, regroup(conv, orders[1]))


def on_device(gate, keys, values, taps, skip_gain):
    devices = lax.axis_size("outer") * lax.axis_size("inner")
    chans, seg = keys.shape
    if chans % devices == 0 and seg % LANES == 0 and devices % 8 == 0:
        return by_channels(gate, keys, values, taps, skip_gain)
    return by_sections(gate, keys, values, taps, skip_gain)


def solution(mesh):
    placed = (
        P(None, ("outer", "inner")),
        P(None, ("outer", "inner")),
        P(None, ("outer", "inner")),
        P(None, ("outer", "inner")),
        P(),
    )
    return jax.shard_map(
        on_device,
        mesh=mesh,
        in_specs=placed,
        out_specs=P(None, ("outer", "inner")),
        check_vma=False,
    )
```

```python
from functools import partial
import math

import jax
import jax.numpy as jnp
import ml_dtypes
import numpy as np
from jax import lax
from jax.experimental import pallas as pl
from jax.experimental.pallas import tpu as pltpu
from jax.sharding import PartitionSpec as P

LANES = 128
AXES = ("outer", "inner")

TWO_PI = 2.0 * math.pi
HIGHEST = lax.Precision.HIGHEST


def table(count_a, count_b, modulus, sign):
    left = lax.broadcasted_iota(jnp.int32, (count_a, count_b), 0)
    right = lax.broadcasted_iota(jnp.int32, (count_a, count_b), 1)
    phase = TWO_PI / modulus * (left * right % modulus).astype(jnp.float32)
    return (jnp.cos(phase), sign * jnp.sin(phase))


def mix(form, cosine, sine, real, imag):
    contract = partial(jnp.einsum, precision=HIGHEST)
    return (
        contract(form, cosine, real) - contract(form, sine, imag),
        contract(form, sine, real) + contract(form, cosine, imag),
    )


def rotate(real, imag, cosine, sine):
    return (real * cosine - imag * sine, real * sine + imag * cosine)


def forward_rows(real, imag):
    split = 16
    lead = real.shape[:-1]
    size = real.shape[-1]
    short = size // split
    real = real.reshape(lead + (split, short))
    imag = imag.reshape(lead + (split, short))
    cosine, sine = table(split, split, split, -1.0)
    real, imag = mix("ka,...as->...ks", cosine, sine, real, imag)
    cosine, sine = table(split, short, size, -1.0)
    real, imag = rotate(real, imag, cosine, sine)
    cosine, sine = table(short, short, short, -1.0)
    real, imag = mix("sb,...ks->...bk", cosine, sine, real, imag)
    return (real.reshape(lead + (size,)), imag.reshape(lead + (size,)))


def inverse_rows(real, imag):
    split = 16
    lead = real.shape[:-1]
    size = real.shape[-1]
    short = size // split
    real = real.reshape(lead + (short, split))
    imag = imag.reshape(lead + (short, split))
    cosine, sine = table(short, short, short, 1.0)
    real, imag = mix("sb,...bk->...sk", cosine, sine, real, imag)
    cosine, sine = table(short, split, size, 1.0)
    real, imag = rotate(real, imag, cosine, sine)
    cosine, sine = table(split, split, split, 1.0)
    real, imag = mix("ak,...sk->...as", cosine, sine, real, imag)
    return (real.reshape(lead + (size,)), imag.reshape(lead + (size,)))


def by_sections(gate, keys, values, taps, skip_gain):
    inner_count = lax.axis_size("inner")
    devices = lax.axis_size("outer") * inner_count
    rank = lax.axis_index("outer") * inner_count + lax.axis_index("inner")
    chans, seg = keys.shape
    both = 2 * chans
    cols = seg // devices
    blocks = 2 * devices
    full = blocks * seg
    contract = partial(jnp.einsum, precision=HIGHEST)
    product = keys * values
    source = jnp.concatenate([product, taps], axis=0)
    sectioned = lax.all_to_all(
        lax.all_to_all(
            source.reshape(both, 1, 1, seg), "outer", split_axis=3, concat_axis=1, tiled=True
        ),
        "inner",
        split_axis=3,
        concat_axis=2,
        tiled=True,
    )
    sectioned = sectioned.reshape(both, devices, cols)
    cosine, sine = table(blocks, devices, blocks, -1.0)
    real = contract("km,cmj->ckj", cosine, sectioned)
    imag = contract("km,cmj->ckj", sine, sectioned)
    offset = rank * cols + lax.broadcasted_iota(jnp.int32, (blocks, cols), 1)
    residue = lax.broadcasted_iota(jnp.int32, (blocks, cols), 0)
    phase = TWO_PI / full * (offset * residue).astype(jnp.float32)
    real, imag = rotate(real, imag, jnp.cos(phase)[None], -jnp.sin(phase)[None])
    outgoing = jnp.stack([real, imag]).reshape(2, both, blocks, 1, 1, cols)
    moved = lax.all_to_all(
        lax.all_to_all(outgoing, "outer", split_axis=2, concat_axis=3, tiled=True),
        "inner",
        split_axis=2,
        concat_axis=4,
        tiled=True,
    )
    moved = moved.reshape(2, both, 2, seg)
    spec_real, spec_imag = forward_rows(moved[0], moved[1])
    sig_real, filt_real = (spec_real[:chans], spec_real[chans:])
    sig_imag, filt_imag = (spec_imag[:chans], spec_imag[chans:])
    real = sig_real * filt_real - sig_imag * filt_imag
    imag = sig_real * filt_imag + sig_imag * filt_real
    real, imag = inverse_rows(real, imag)
    residue = 2 * rank + lax.broadcasted_iota(jnp.int32, (2, seg), 0)
    offset = lax.broadcasted_iota(jnp.int32, (2, seg), 1)
    phase = TWO_PI / full * (offset * residue).astype(jnp.float32)
    real, imag = rotate(real, imag, jnp.cos(phase)[None], jnp.sin(phase)[None])
    returning = jnp.stack([real, imag]).reshape(2, chans, 1, 1, 2, seg)
    gathered = lax.all_to_all(
        lax.all_to_all(returning, "outer", split_axis=5, concat_axis=2, tiled=True),
        "inner",
        split_axis=5,
        concat_axis=3,
        tiled=True,
    )
    gathered = gathered.reshape(2, chans, blocks, cols)
    cosine, sine = table(devices, blocks, blocks, 1.0)
    conv = contract("mk,ckj->cmj", cosine, gathered[0]) - contract("mk,ckj->cmj", sine, gathered[1])
    conv = conv * (1.0 / full)
    conv = lax.all_to_all(
        lax.all_to_all(
            conv.reshape(chans, devices, 1, 1, cols),
            "outer",
            split_axis=1,
            concat_axis=2,
            tiled=True,
        ),
        "inner",
        split_axis=1,
        concat_axis=3,
        tiled=True,
    )
    conv = conv.reshape(chans, seg)
    return gate * (conv + skip_gain[:, None] * product)


def halves(array):
    high = array.astype(ml_dtypes.bfloat16)
    low = (array - high.astype(np.float64)).astype(ml_dtypes.bfloat16)
    return high, low


def transform_tables(devices, seg):
    length = devices * seg
    count = length // LANES
    odd = 2 * np.arange(count) + 1
    angle = 2 * np.pi / (4 * count) * ((odd[:, None] * np.arange(count)[None, :]) % (4 * count))
    first = np.concatenate([np.cos(angle), -np.sin(angle)], axis=0)
    last = np.concatenate([np.cos(angle).T, -np.sin(angle).T], axis=1) / length
    angle = 2 * np.pi / (4 * length) * ((odd[:, None] * np.arange(LANES)[None, :]) % (4 * length))
    twiddle = np.stack([np.cos(angle), np.sin(angle)]).astype(np.float32)
    angle = 2 * np.pi / LANES * ((np.arange(LANES)[:, None] * np.arange(LANES)[None, :]) % LANES)
    cosine, sine = np.cos(angle), np.sin(angle)
    rows = np.block([[cosine, -sine], [sine, cosine]])
    back = np.block([[cosine, sine], [-sine, cosine]])
    first_high, first_low = halves(first)
    rows_high, rows_low = halves(rows)
    back_high, back_low = halves(back)
    last_high, last_low = halves(last)
    return (
        np.concatenate([first_high, first_high, first_low, first_low], axis=1),
        np.concatenate([rows_high, rows_low], axis=0),
        np.concatenate([back_high, back_low], axis=0),
        np.concatenate([last_high, last_high, last_low], axis=1),
        twiddle,
    )


def send_orders(outer, inner):
    half = inner // 2
    turns = [at // 2 + half * (at % 2) for at in range(2 * half)] + list(range(2 * half, inner))
    ring = [at ^ (at >> 1) for at in range(outer)] if outer & (outer - 1) == 0 else list(range(outer))
    first = [at * inner + step for at in ring[:1] + ring[:0:-1] for step in range(inner)]
    second = [at * inner + step for at in range(outer) for step in turns[1:] + turns[:1]]
    return first, second


def split(array, count=2):
    parts = []
    for _ in range(count):
        parts.append(array.astype(jnp.bfloat16))
        array = array - parts[-1].astype(jnp.float32)
    return parts


def dot(left, right):
    return jnp.dot(left, right, preferred_element_type=jnp.float32)


def convolve_kernel(
    devices, chans, seg, data_ref, first_ref, rows_ref, back_ref, last_ref, twiddle_ref, out_ref, signal_ref
):
    parts = seg // LANES
    count = devices * parts
    cosine, sine = twiddle_ref[0], twiddle_ref[1]

    def lanes(at):
        return slice(at * LANES, (at + 1) * LANES)

    first, second = send_orders(lax.axis_size("outer"), lax.axis_size("inner"))

    groups = chans
    each = chans // groups
    at = range(groups)
    for group in at:
        for kind in range(2):
            for chan in range(each):
                for device in range(devices):
                    came = ((device * 2 + kind) * chans + group * each + chan) * parts
                    to = first[device] * parts
                    signal_ref[group, to : to + parts, lanes(kind * each + chan)] = data_ref[came : came + parts, :]

    def times(pieces, table_ref):
        size = table_ref.shape[0] // 2
        by_high = dot(jnp.concatenate(pieces, axis=0), table_ref[:size, :])
        total = dot(pieces[0], table_ref[size:, :])
        rows = total.shape[0]
        for piece in reversed(range(len(pieces))):
            total = total + by_high[piece * rows : (piece + 1) * rows]
        return total

    def start(group):
        high, low = split(signal_ref[group])
        return dot(first_ref[...], jnp.concatenate([high, low, high, low], axis=0))

    def spectra(begun):
        turned = []
        for signal in range(2 * each):
            real, imag = begun[:count, lanes(signal)], begun[count:, lanes(signal)]
            turned.append(jnp.concatenate([real * cosine + imag * sine, imag * cosine - real * sine], axis=1))
        return times(split(jnp.concatenate(turned, axis=0), 3), rows_ref)

    def back(spectrum):
        mid = each * count
        sig_real, sig_imag = spectrum[:mid, :LANES], spectrum[:mid, LANES:]
        filt_real, filt_imag = spectrum[mid:, :LANES], spectrum[mid:, LANES:]
        real = sig_real * filt_real - sig_imag * filt_imag
        imag = sig_real * filt_imag + sig_imag * filt_real
        return times(split(jnp.concatenate([real, imag], axis=1)), back_ref)

    def turn_back(backed):
        real, imag = backed[:, :LANES], backed[:, LANES:]
        return jnp.concatenate([real * cosine - imag * sine, imag * cosine + real * sine], axis=0)

    begun = [start(group) for group in at]
    spectrum = [spectra(begun[group]) for group in at]
    backed = [back(spectrum[group]) for group in at]
    pair = 2 if chans % 2 == 0 else 1
    for own in range(0, chans, pair):
        high, low = split(jnp.concatenate([turn_back(backed[own + step]) for step in range(pair)], axis=1))
        conv = dot(last_ref[...], jnp.concatenate([high, low, high], axis=0))
        for step in range(pair):
            for device in range(devices):
                to = (device * chans + own + step) * parts
                came = second[device] * parts
                out_ref[to : to + parts, :] = conv[came : came + parts, lanes(step)]


def gather_kernel(order, product_ref, taps_ref, out_ref):
    rows = product_ref.shape[0] * product_ref.shape[1] // LANES // len(order)
    for kind, ref in enumerate((product_ref, taps_ref)):
        source = ref[...].reshape(len(order) * rows, LANES)
        for at, rank in enumerate(order):
            to = (2 * at + kind) * rows
            out_ref[to : to + rows, :] = source[rank * rows : (rank + 1) * rows]


def gate_kernel(order, gate_ref, skip_ref, conv_ref, out_hbm, out_ref, sems):
    chans, seg = gate_ref.shape
    pieces = sems.shape[0]
    step = chans // pieces
    rows = conv_ref.shape[0] // len(order)
    each = len(order) // pieces
    place = {rank: at * rows for at, rank in enumerate(order)}
    copies = []
    for piece in range(pieces):
        at = slice(piece * step, (piece + 1) * step)
        came = [conv_ref[place[rank] : place[rank] + rows, :] for rank in range(piece * each, (piece + 1) * each)]
        conv = jnp.concatenate(came, axis=0).reshape(step, seg)
        out_ref[at, :] = gate_ref[at, :] * (conv + skip_ref[at, :])
        copies.append(pltpu.make_async_copy(out_ref.at[at, :], out_hbm.at[at, :], sems.at[piece]))
        copies[piece].start()
    for copy in copies:
        copy.wait()


def on_core(kernel, shape, moved, flops=10**6, scratch=(), **more):
    return pl.pallas_call(
        kernel,
        out_shape=jax.ShapeDtypeStruct(shape, jnp.float32),
        scratch_shapes=scratch,
        compiler_params=pltpu.CompilerParams(vmem_limit_bytes=32 * 2**20),
        cost_estimate=pl.CostEstimate(flops=flops, bytes_accessed=moved, transcendentals=0),
        **more,
    )


def by_channels(gate, keys, values, taps, skip_gain):
    devices = lax.axis_size("outer") * lax.axis_size("inner")
    chans, seg = keys.shape
    own = chans // devices
    tiles = seg // LANES
    tables = [jnp.asarray(table) for table in transform_tables(devices, seg)]
    orders = send_orders(lax.axis_size("outer"), lax.axis_size("inner"))

    def regroup(rows, order):
        return lax.all_to_all(rows, AXES, split_axis=0, concat_axis=0, tiled=True, axis_index_groups=[order])

    product = keys * values
    product, skip = lax.optimization_barrier((product, skip_gain[:, None] * product))
    sent = on_core(partial(gather_kernel, orders[0]), (2 * chans * tiles, LANES), 4 * chans * seg * 4)(product, taps)
    groups = own
    conv = on_core(
        partial(convolve_kernel, devices, own, seg),
        (chans * tiles, LANES),
        2 * 10**6,
        10**9,
        [pltpu.VMEM((groups, devices * tiles, 2 * own // groups * LANES), jnp.float32)],
    )(regroup(sent, orders[0]), *tables)
    pieces = 4
    return on_core(
        partial(gate_kernel, orders[1]),
        (chans, seg),
        4 * chans * seg * 4,
        scratch=[pltpu.VMEM((chans, seg), jnp.float32), pltpu.SemaphoreType.DMA((pieces,))],
        out_specs=pl.BlockSpec(memory_space=pl.ANY),
    )(gate, skip, regroup(conv, orders[1]))


def on_device(gate, keys, values, taps, skip_gain):
    devices = lax.axis_size("outer") * lax.axis_size("inner")
    chans, seg = keys.shape
    if chans % devices == 0 and seg % LANES == 0 and devices % 8 == 0:
        return by_channels(gate, keys, values, taps, skip_gain)
    return by_sections(gate, keys, values, taps, skip_gain)


def solution(mesh):
    placed = (
        P(None, ("outer", "inner")),
        P(None, ("outer", "inner")),
        P(None, ("outer", "inner")),
        P(None, ("outer", "inner")),
        P(),
    )
    return jax.shard_map(
        on_device,
        mesh=mesh,
        in_specs=placed,
        out_specs=P(None, ("outer", "inner")),
        check_vma=False,
    )
```

```python
from functools import partial
import math

import jax
import jax.numpy as jnp
import ml_dtypes
import numpy as np
from jax import lax
from jax.experimental import pallas as pl
from jax.experimental.pallas import tpu as pltpu
from jax.sharding import PartitionSpec as P

LANES = 128
AXES = ("outer", "inner")

TWO_PI = 2.0 * math.pi
HIGHEST = lax.Precision.HIGHEST


def table(count_a, count_b, modulus, sign):
    left = lax.broadcasted_iota(jnp.int32, (count_a, count_b), 0)
    right = lax.broadcasted_iota(jnp.int32, (count_a, count_b), 1)
    phase = TWO_PI / modulus * (left * right % modulus).astype(jnp.float32)
    return (jnp.cos(phase), sign * jnp.sin(phase))


def mix(form, cosine, sine, real, imag):
    contract = partial(jnp.einsum, precision=HIGHEST)
    return (
        contract(form, cosine, real) - contract(form, sine, imag),
        contract(form, sine, real) + contract(form, cosine, imag),
    )


def rotate(real, imag, cosine, sine):
    return (real * cosine - imag * sine, real * sine + imag * cosine)


def forward_rows(real, imag):
    split = 16
    lead = real.shape[:-1]
    size = real.shape[-1]
    short = size // split
    real = real.reshape(lead + (split, short))
    imag = imag.reshape(lead + (split, short))
    cosine, sine = table(split, split, split, -1.0)
    real, imag = mix("ka,...as->...ks", cosine, sine, real, imag)
    cosine, sine = table(split, short, size, -1.0)
    real, imag = rotate(real, imag, cosine, sine)
    cosine, sine = table(short, short, short, -1.0)
    real, imag = mix("sb,...ks->...bk", cosine, sine, real, imag)
    return (real.reshape(lead + (size,)), imag.reshape(lead + (size,)))


def inverse_rows(real, imag):
    split = 16
    lead = real.shape[:-1]
    size = real.shape[-1]
    short = size // split
    real = real.reshape(lead + (short, split))
    imag = imag.reshape(lead + (short, split))
    cosine, sine = table(short, short, short, 1.0)
    real, imag = mix("sb,...bk->...sk", cosine, sine, real, imag)
    cosine, sine = table(short, split, size, 1.0)
    real, imag = rotate(real, imag, cosine, sine)
    cosine, sine = table(split, split, split, 1.0)
    real, imag = mix("ak,...sk->...as", cosine, sine, real, imag)
    return (real.reshape(lead + (size,)), imag.reshape(lead + (size,)))


def by_sections(gate, keys, values, taps, skip_gain):
    inner_count = lax.axis_size("inner")
    devices = lax.axis_size("outer") * inner_count
    rank = lax.axis_index("outer") * inner_count + lax.axis_index("inner")
    chans, seg = keys.shape
    both = 2 * chans
    cols = seg // devices
    blocks = 2 * devices
    full = blocks * seg
    contract = partial(jnp.einsum, precision=HIGHEST)
    product = keys * values
    source = jnp.concatenate([product, taps], axis=0)
    sectioned = lax.all_to_all(
        lax.all_to_all(
            source.reshape(both, 1, 1, seg), "outer", split_axis=3, concat_axis=1, tiled=True
        ),
        "inner",
        split_axis=3,
        concat_axis=2,
        tiled=True,
    )
    sectioned = sectioned.reshape(both, devices, cols)
    cosine, sine = table(blocks, devices, blocks, -1.0)
    real = contract("km,cmj->ckj", cosine, sectioned)
    imag = contract("km,cmj->ckj", sine, sectioned)
    offset = rank * cols + lax.broadcasted_iota(jnp.int32, (blocks, cols), 1)
    residue = lax.broadcasted_iota(jnp.int32, (blocks, cols), 0)
    phase = TWO_PI / full * (offset * residue).astype(jnp.float32)
    real, imag = rotate(real, imag, jnp.cos(phase)[None], -jnp.sin(phase)[None])
    outgoing = jnp.stack([real, imag]).reshape(2, both, blocks, 1, 1, cols)
    moved = lax.all_to_all(
        lax.all_to_all(outgoing, "outer", split_axis=2, concat_axis=3, tiled=True),
        "inner",
        split_axis=2,
        concat_axis=4,
        tiled=True,
    )
    moved = moved.reshape(2, both, 2, seg)
    spec_real, spec_imag = forward_rows(moved[0], moved[1])
    sig_real, filt_real = (spec_real[:chans], spec_real[chans:])
    sig_imag, filt_imag = (spec_imag[:chans], spec_imag[chans:])
    real = sig_real * filt_real - sig_imag * filt_imag
    imag = sig_real * filt_imag + sig_imag * filt_real
    real, imag = inverse_rows(real, imag)
    residue = 2 * rank + lax.broadcasted_iota(jnp.int32, (2, seg), 0)
    offset = lax.broadcasted_iota(jnp.int32, (2, seg), 1)
    phase = TWO_PI / full * (offset * residue).astype(jnp.float32)
    real, imag = rotate(real, imag, jnp.cos(phase)[None], jnp.sin(phase)[None])
    returning = jnp.stack([real, imag]).reshape(2, chans, 1, 1, 2, seg)
    gathered = lax.all_to_all(
        lax.all_to_all(returning, "outer", split_axis=5, concat_axis=2, tiled=True),
        "inner",
        split_axis=5,
        concat_axis=3,
        tiled=True,
    )
    gathered = gathered.reshape(2, chans, blocks, cols)
    cosine, sine = table(devices, blocks, blocks, 1.0)
    conv = contract("mk,ckj->cmj", cosine, gathered[0]) - contract("mk,ckj->cmj", sine, gathered[1])
    conv = conv * (1.0 / full)
    conv = lax.all_to_all(
        lax.all_to_all(
            conv.reshape(chans, devices, 1, 1, cols),
            "outer",
            split_axis=1,
            concat_axis=2,
            tiled=True,
        ),
        "inner",
        split_axis=1,
        concat_axis=3,
        tiled=True,
    )
    conv = conv.reshape(chans, seg)
    return gate * (conv + skip_gain[:, None] * product)


def halves(array):
    high = array.astype(ml_dtypes.bfloat16)
    low = (array - high.astype(np.float64)).astype(ml_dtypes.bfloat16)
    return high, low


def transform_tables(devices, seg):
    length = devices * seg
    count = length // LANES
    odd = 2 * np.arange(count) + 1
    angle = 2 * np.pi / (4 * count) * ((odd[:, None] * np.arange(count)[None, :]) % (4 * count))
    first = np.concatenate([np.cos(angle), -np.sin(angle)], axis=0)
    last = np.concatenate([np.cos(angle).T, -np.sin(angle).T], axis=1) / length
    angle = 2 * np.pi / (4 * length) * ((odd[:, None] * np.arange(LANES)[None, :]) % (4 * length))
    twiddle = np.stack([np.cos(angle), np.sin(angle)]).astype(np.float32)
    angle = 2 * np.pi / LANES * ((np.arange(LANES)[:, None] * np.arange(LANES)[None, :]) % LANES)
    cosine, sine = np.cos(angle), np.sin(angle)
    rows = np.block([[cosine, -sine], [sine, cosine]])
    back = np.block([[cosine, sine], [-sine, cosine]])
    first_high, first_low = halves(first)
    rows_high, rows_low = halves(rows)
    back_high, back_low = halves(back)
    last_high, last_low = halves(last)
    return (
        np.concatenate([first_high, first_high, first_low, first_low], axis=1),
        np.concatenate([rows_high, rows_low], axis=0),
        np.concatenate([back_high, back_low], axis=0),
        np.concatenate([last_high, last_high, last_low], axis=1),
        twiddle,
    )


def send_orders(outer, inner):
    half = inner // 2
    turns = [at // 2 + half * (at % 2) for at in range(2 * half)] + list(range(2 * half, inner))
    ring = [at ^ (at >> 1) for at in range(outer)] if outer & (outer - 1) == 0 else list(range(outer))
    first = [at * inner + step for at in ring[:1] + ring[:0:-1] for step in range(inner)]
    second = [at * inner + step for at in range(outer) for step in turns[:0:-1][:1] + turns[2:-1] + turns[1:2] + turns[:1]]
    return first, second


def split(array, count=2):
    parts = []
    for _ in range(count):
        parts.append(array.astype(jnp.bfloat16))
        array = array - parts[-1].astype(jnp.float32)
    return parts


def dot(left, right):
    return jnp.dot(left, right, preferred_element_type=jnp.float32)


def convolve_kernel(
    devices, chans, seg, data_ref, first_ref, rows_ref, back_ref, last_ref, twiddle_ref, out_ref, signal_ref
):
    parts = seg // LANES
    count = devices * parts
    cosine, sine = twiddle_ref[0], twiddle_ref[1]

    def lanes(at):
        return slice(at * LANES, (at + 1) * LANES)

    first, second = send_orders(lax.axis_size("outer"), lax.axis_size("inner"))

    groups = chans
    each = chans // groups
    at = range(groups)
    for group in at:
        for kind in range(2):
            for chan in range(each):
                for device in range(devices):
                    came = ((device * 2 + kind) * chans + group * each + chan) * parts
                    to = first[device] * parts
                    signal_ref[group, to : to + parts, lanes(kind * each + chan)] = data_ref[came : came + parts, :]

    def times(pieces, table_ref):
        size = table_ref.shape[0] // 2
        by_high = dot(jnp.concatenate(pieces, axis=0), table_ref[:size, :])
        total = dot(pieces[0], table_ref[size:, :])
        rows = total.shape[0]
        for piece in reversed(range(len(pieces))):
            total = total + by_high[piece * rows : (piece + 1) * rows]
        return total

    def start(group):
        high, low = split(signal_ref[group])
        return dot(first_ref[...], jnp.concatenate([high, low, high, low], axis=0))

    def spectra(begun):
        turned = []
        for signal in range(2 * each):
            real, imag = begun[:count, lanes(signal)], begun[count:, lanes(signal)]
            turned.append(jnp.concatenate([real * cosine + imag * sine, imag * cosine - real * sine], axis=1))
        return times(split(jnp.concatenate(turned, axis=0), 3), rows_ref)

    def back(spectrum):
        mid = each * count
        sig_real, sig_imag = spectrum[:mid, :LANES], spectrum[:mid, LANES:]
        filt_real, filt_imag = spectrum[mid:, :LANES], spectrum[mid:, LANES:]
        real = sig_real * filt_real - sig_imag * filt_imag
        imag = sig_real * filt_imag + sig_imag * filt_real
        return times(split(jnp.concatenate([real, imag], axis=1)), back_ref)

    def turn_back(backed):
        real, imag = backed[:, :LANES], backed[:, LANES:]
        return jnp.concatenate([real * cosine - imag * sine, imag * cosine + real * sine], axis=0)

    begun = [start(group) for group in at]
    spectrum = [spectra(begun[group]) for group in at]
    backed = [back(spectrum[group]) for group in at]
    pair = 2 if chans % 2 == 0 else 1
    for own in range(0, chans, pair):
        high, low = split(jnp.concatenate([turn_back(backed[own + step]) for step in range(pair)], axis=1))
        conv = dot(last_ref[...], jnp.concatenate([high, low, high], axis=0))
        for step in range(pair):
            for device in range(devices):
                to = (device * chans + own + step) * parts
                came = second[device] * parts
                out_ref[to : to + parts, :] = conv[came : came + parts, lanes(step)]


def gather_kernel(order, product_ref, taps_ref, out_ref):
    rows = product_ref.shape[0] * product_ref.shape[1] // LANES // len(order)
    for kind, ref in enumerate((product_ref, taps_ref)):
        source = ref[...].reshape(len(order) * rows, LANES)
        for at, rank in enumerate(order):
            to = (2 * at + kind) * rows
            out_ref[to : to + rows, :] = source[rank * rows : (rank + 1) * rows]


def gate_kernel(order, gate_ref, skip_ref, conv_ref, out_hbm, out_ref, sems):
    chans, seg = gate_ref.shape
    pieces = sems.shape[0]
    step = chans // pieces
    rows = conv_ref.shape[0] // len(order)
    each = len(order) // pieces
    place = {rank: at * rows for at, rank in enumerate(order)}
    copies = []
    for piece in range(pieces):
        at = slice(piece * step, (piece + 1) * step)
        came = [conv_ref[place[rank] : place[rank] + rows, :] for rank in range(piece * each, (piece + 1) * each)]
        conv = jnp.concatenate(came, axis=0).reshape(step, seg)
        out_ref[at, :] = gate_ref[at, :] * (conv + skip_ref[at, :])
        copies.append(pltpu.make_async_copy(out_ref.at[at, :], out_hbm.at[at, :], sems.at[piece]))
        copies[piece].start()
    for copy in copies:
        copy.wait()


def on_core(kernel, shape, moved, flops=10**6, scratch=(), **more):
    return pl.pallas_call(
        kernel,
        out_shape=jax.ShapeDtypeStruct(shape, jnp.float32),
        scratch_shapes=scratch,
        compiler_params=pltpu.CompilerParams(vmem_limit_bytes=32 * 2**20),
        cost_estimate=pl.CostEstimate(flops=flops, bytes_accessed=moved, transcendentals=0),
        **more,
    )


def by_channels(gate, keys, values, taps, skip_gain):
    devices = lax.axis_size("outer") * lax.axis_size("inner")
    chans, seg = keys.shape
    own = chans // devices
    tiles = seg // LANES
    tables = [jnp.asarray(table) for table in transform_tables(devices, seg)]
    orders = send_orders(lax.axis_size("outer"), lax.axis_size("inner"))

    def regroup(rows, order):
        return lax.all_to_all(rows, AXES, split_axis=0, concat_axis=0, tiled=True, axis_index_groups=[order])

    product = keys * values
    product, skip = lax.optimization_barrier((product, skip_gain[:, None] * product))
    sent = on_core(partial(gather_kernel, orders[0]), (2 * chans * tiles, LANES), 4 * chans * seg * 4)(product, taps)
    groups = own
    conv = on_core(
        partial(convolve_kernel, devices, own, seg),
        (chans * tiles, LANES),
        2 * 10**6,
        10**9,
        [pltpu.VMEM((groups, devices * tiles, 2 * own // groups * LANES), jnp.float32)],
    )(regroup(sent, orders[0]), *tables)
    pieces = 4
    return on_core(
        partial(gate_kernel, orders[1]),
        (chans, seg),
        4 * chans * seg * 4,
        scratch=[pltpu.VMEM((chans, seg), jnp.float32), pltpu.SemaphoreType.DMA((pieces,))],
        out_specs=pl.BlockSpec(memory_space=pl.ANY),
    )(gate, skip, regroup(conv, orders[1]))


def on_device(gate, keys, values, taps, skip_gain):
    devices = lax.axis_size("outer") * lax.axis_size("inner")
    chans, seg = keys.shape
    if chans % devices == 0 and seg % LANES == 0 and devices % 8 == 0:
        return by_channels(gate, keys, values, taps, skip_gain)
    return by_sections(gate, keys, values, taps, skip_gain)


def solution(mesh):
    placed = (
        P(None, ("outer", "inner")),
        P(None, ("outer", "inner")),
        P(None, ("outer", "inner")),
        P(None, ("outer", "inner")),
        P(),
    )
    return jax.shard_map(
        on_device,
        mesh=mesh,
        in_specs=placed,
        out_specs=P(None, ("outer", "inner")),
        check_vma=False,
    )
```

```python
from functools import partial
import math

import jax
import jax.numpy as jnp
import ml_dtypes
import numpy as np
from jax import lax
from jax.experimental import pallas as pl
from jax.experimental.pallas import tpu as pltpu
from jax.sharding import PartitionSpec as P

LANES = 128
AXES = ("outer", "inner")

TWO_PI = 2.0 * math.pi
HIGHEST = lax.Precision.HIGHEST


def table(count_a, count_b, modulus, sign):
    left = lax.broadcasted_iota(jnp.int32, (count_a, count_b), 0)
    right = lax.broadcasted_iota(jnp.int32, (count_a, count_b), 1)
    phase = TWO_PI / modulus * (left * right % modulus).astype(jnp.float32)
    return (jnp.cos(phase), sign * jnp.sin(phase))


def mix(form, cosine, sine, real, imag):
    contract = partial(jnp.einsum, precision=HIGHEST)
    return (
        contract(form, cosine, real) - contract(form, sine, imag),
        contract(form, sine, real) + contract(form, cosine, imag),
    )


def rotate(real, imag, cosine, sine):
    return (real * cosine - imag * sine, real * sine + imag * cosine)


def forward_rows(real, imag):
    split = 16
    lead = real.shape[:-1]
    size = real.shape[-1]
    short = size // split
    real = real.reshape(lead + (split, short))
    imag = imag.reshape(lead + (split, short))
    cosine, sine = table(split, split, split, -1.0)
    real, imag = mix("ka,...as->...ks", cosine, sine, real, imag)
    cosine, sine = table(split, short, size, -1.0)
    real, imag = rotate(real, imag, cosine, sine)
    cosine, sine = table(short, short, short, -1.0)
    real, imag = mix("sb,...ks->...bk", cosine, sine, real, imag)
    return (real.reshape(lead + (size,)), imag.reshape(lead + (size,)))


def inverse_rows(real, imag):
    split = 16
    lead = real.shape[:-1]
    size = real.shape[-1]
    short = size // split
    real = real.reshape(lead + (short, split))
    imag = imag.reshape(lead + (short, split))
    cosine, sine = table(short, short, short, 1.0)
    real, imag = mix("sb,...bk->...sk", cosine, sine, real, imag)
    cosine, sine = table(short, split, size, 1.0)
    real, imag = rotate(real, imag, cosine, sine)
    cosine, sine = table(split, split, split, 1.0)
    real, imag = mix("ak,...sk->...as", cosine, sine, real, imag)
    return (real.reshape(lead + (size,)), imag.reshape(lead + (size,)))


def by_sections(gate, keys, values, taps, skip_gain):
    inner_count = lax.axis_size("inner")
    devices = lax.axis_size("outer") * inner_count
    rank = lax.axis_index("outer") * inner_count + lax.axis_index("inner")
    chans, seg = keys.shape
    both = 2 * chans
    cols = seg // devices
    blocks = 2 * devices
    full = blocks * seg
    contract = partial(jnp.einsum, precision=HIGHEST)
    product = keys * values
    source = jnp.concatenate([product, taps], axis=0)
    sectioned = lax.all_to_all(
        lax.all_to_all(
            source.reshape(both, 1, 1, seg), "outer", split_axis=3, concat_axis=1, tiled=True
        ),
        "inner",
        split_axis=3,
        concat_axis=2,
        tiled=True,
    )
    sectioned = sectioned.reshape(both, devices, cols)
    cosine, sine = table(blocks, devices, blocks, -1.0)
    real = contract("km,cmj->ckj", cosine, sectioned)
    imag = contract("km,cmj->ckj", sine, sectioned)
    offset = rank * cols + lax.broadcasted_iota(jnp.int32, (blocks, cols), 1)
    residue = lax.broadcasted_iota(jnp.int32, (blocks, cols), 0)
    phase = TWO_PI / full * (offset * residue).astype(jnp.float32)
    real, imag = rotate(real, imag, jnp.cos(phase)[None], -jnp.sin(phase)[None])
    outgoing = jnp.stack([real, imag]).reshape(2, both, blocks, 1, 1, cols)
    moved = lax.all_to_all(
        lax.all_to_all(outgoing, "outer", split_axis=2, concat_axis=3, tiled=True),
        "inner",
        split_axis=2,
        concat_axis=4,
        tiled=True,
    )
    moved = moved.reshape(2, both, 2, seg)
    spec_real, spec_imag = forward_rows(moved[0], moved[1])
    sig_real, filt_real = (spec_real[:chans], spec_real[chans:])
    sig_imag, filt_imag = (spec_imag[:chans], spec_imag[chans:])
    real = sig_real * filt_real - sig_imag * filt_imag
    imag = sig_real * filt_imag + sig_imag * filt_real
    real, imag = inverse_rows(real, imag)
    residue = 2 * rank + lax.broadcasted_iota(jnp.int32, (2, seg), 0)
    offset = lax.broadcasted_iota(jnp.int32, (2, seg), 1)
    phase = TWO_PI / full * (offset * residue).astype(jnp.float32)
    real, imag = rotate(real, imag, jnp.cos(phase)[None], jnp.sin(phase)[None])
    returning = jnp.stack([real, imag]).reshape(2, chans, 1, 1, 2, seg)
    gathered = lax.all_to_all(
        lax.all_to_all(returning, "outer", split_axis=5, concat_axis=2, tiled=True),
        "inner",
        split_axis=5,
        concat_axis=3,
        tiled=True,
    )
    gathered = gathered.reshape(2, chans, blocks, cols)
    cosine, sine = table(devices, blocks, blocks, 1.0)
    conv = contract("mk,ckj->cmj", cosine, gathered[0]) - contract("mk,ckj->cmj", sine, gathered[1])
    conv = conv * (1.0 / full)
    conv = lax.all_to_all(
        lax.all_to_all(
            conv.reshape(chans, devices, 1, 1, cols),
            "outer",
            split_axis=1,
            concat_axis=2,
            tiled=True,
        ),
        "inner",
        split_axis=1,
        concat_axis=3,
        tiled=True,
    )
    conv = conv.reshape(chans, seg)
    return gate * (conv + skip_gain[:, None] * product)


def halves(array):
    high = array.astype(ml_dtypes.bfloat16)
    low = (array - high.astype(np.float64)).astype(ml_dtypes.bfloat16)
    return high, low


def transform_tables(devices, seg):
    length = devices * seg
    count = length // LANES
    odd = 2 * np.arange(count) + 1
    angle = 2 * np.pi / (4 * count) * ((odd[:, None] * np.arange(count)[None, :]) % (4 * count))
    first = np.concatenate([np.cos(angle), -np.sin(angle)], axis=0)
    last = np.concatenate([np.cos(angle).T, -np.sin(angle).T], axis=1) / length
    angle = 2 * np.pi / (4 * length) * ((odd[:, None] * np.arange(LANES)[None, :]) % (4 * length))
    twiddle = np.stack([np.cos(angle), np.sin(angle)]).astype(np.float32)
    angle = 2 * np.pi / LANES * ((np.arange(LANES)[:, None] * np.arange(LANES)[None, :]) % LANES)
    cosine, sine = np.cos(angle), np.sin(angle)
    rows = np.block([[cosine, -sine], [sine, cosine]])
    back = np.block([[cosine, sine], [-sine, cosine]])
    first_high, first_low = halves(first)
    rows_high, rows_low = halves(rows)
    back_high, back_low = halves(back)
    last_high, last_low = halves(last)
    return (
        np.concatenate([first_high, first_high, first_low, first_low], axis=1),
        np.concatenate([rows_high, rows_low], axis=0),
        np.concatenate([back_high, back_low], axis=0),
        np.concatenate([last_high, last_high, last_low], axis=1),
        twiddle,
    )


def send_orders(outer, inner):
    half = inner // 2
    turns = [at // 2 + half * (at % 2) for at in range(2 * half)] + list(range(2 * half, inner))
    ring = [at ^ (at >> 1) for at in range(outer)] if outer & (outer - 1) == 0 else list(range(outer))
    first = [at * inner + step for at in ring[:1] + ring[:0:-1] for step in range(inner)]
    second = [at * inner + step for at in range(outer) for step in (turns[1:] if at % 2 else turns[:0:-1][:1] + turns[2:-1] + turns[1:2]) + turns[:1]]
    return first, second


def split(array, count=2):
    parts = []
    for _ in range(count):
        parts.append(array.astype(jnp.bfloat16))
        array = array - parts[-1].astype(jnp.float32)
    return parts


def dot(left, right):
    return jnp.dot(left, right, preferred_element_type=jnp.float32)


def convolve_kernel(
    devices, chans, seg, data_ref, first_ref, rows_ref, back_ref, last_ref, twiddle_ref, out_ref, signal_ref
):
    parts = seg // LANES
    count = devices * parts
    cosine, sine = twiddle_ref[0], twiddle_ref[1]

    def lanes(at):
        return slice(at * LANES, (at + 1) * LANES)

    first, second = send_orders(lax.axis_size("outer"), lax.axis_size("inner"))

    groups = chans
    each = chans // groups
    at = range(groups)
    for group in at:
        for kind in range(2):
            for chan in range(each):
                for device in range(devices):
                    came = ((device * 2 + kind) * chans + group * each + chan) * parts
                    to = first[device] * parts
                    signal_ref[group, to : to + parts, lanes(kind * each + chan)] = data_ref[came : came + parts, :]

    def times(pieces, table_ref):
        size = table_ref.shape[0] // 2
        by_high = dot(jnp.concatenate(pieces, axis=0), table_ref[:size, :])
        total = dot(pieces[0], table_ref[size:, :])
        rows = total.shape[0]
        for piece in reversed(range(len(pieces))):
            total = total + by_high[piece * rows : (piece + 1) * rows]
        return total

    def start(group):
        high, low = split(signal_ref[group])
        return dot(first_ref[...], jnp.concatenate([high, low, high, low], axis=0))

    def spectra(begun):
        turned = []
        for signal in range(2 * each):
            real, imag = begun[:count, lanes(signal)], begun[count:, lanes(signal)]
            turned.append(jnp.concatenate([real * cosine + imag * sine, imag * cosine - real * sine], axis=1))
        return times(split(jnp.concatenate(turned, axis=0), 3), rows_ref)

    def back(spectrum):
        mid = each * count
        sig_real, sig_imag = spectrum[:mid, :LANES], spectrum[:mid, LANES:]
        filt_real, filt_imag = spectrum[mid:, :LANES], spectrum[mid:, LANES:]
        real = sig_real * filt_real - sig_imag * filt_imag
        imag = sig_real * filt_imag + sig_imag * filt_real
        return times(split(jnp.concatenate([real, imag], axis=1)), back_ref)

    def turn_back(backed):
        real, imag = backed[:, :LANES], backed[:, LANES:]
        return jnp.concatenate([real * cosine - imag * sine, imag * cosine + real * sine], axis=0)

    begun = [start(group) for group in at]
    spectrum = [spectra(begun[group]) for group in at]
    backed = [back(spectrum[group]) for group in at]
    pair = 2 if chans % 2 == 0 else 1
    for own in range(0, chans, pair):
        high, low = split(jnp.concatenate([turn_back(backed[own + step]) for step in range(pair)], axis=1))
        conv = dot(last_ref[...], jnp.concatenate([high, low, high], axis=0))
        for step in range(pair):
            for device in range(devices):
                to = (device * chans + own + step) * parts
                came = second[device] * parts
                out_ref[to : to + parts, :] = conv[came : came + parts, lanes(step)]


def gather_kernel(order, product_ref, taps_ref, out_ref):
    rows = product_ref.shape[0] * product_ref.shape[1] // LANES // len(order)
    for kind, ref in enumerate((product_ref, taps_ref)):
        source = ref[...].reshape(len(order) * rows, LANES)
        for at, rank in enumerate(order):
            to = (2 * at + kind) * rows
            out_ref[to : to + rows, :] = source[rank * rows : (rank + 1) * rows]


def gate_kernel(order, gate_ref, skip_ref, conv_ref, out_hbm, out_ref, sems):
    chans, seg = gate_ref.shape
    pieces = sems.shape[0]
    step = chans // pieces
    rows = conv_ref.shape[0] // len(order)
    each = len(order) // pieces
    place = {rank: at * rows for at, rank in enumerate(order)}
    copies = []
    for piece in range(pieces):
        at = slice(piece * step, (piece + 1) * step)
        came = [conv_ref[place[rank] : place[rank] + rows, :] for rank in range(piece * each, (piece + 1) * each)]
        conv = jnp.concatenate(came, axis=0).reshape(step, seg)
        out_ref[at, :] = gate_ref[at, :] * (conv + skip_ref[at, :])
        copies.append(pltpu.make_async_copy(out_ref.at[at, :], out_hbm.at[at, :], sems.at[piece]))
        copies[piece].start()
    for copy in copies:
        copy.wait()


def on_core(kernel, shape, moved, flops=10**6, scratch=(), **more):
    return pl.pallas_call(
        kernel,
        out_shape=jax.ShapeDtypeStruct(shape, jnp.float32),
        scratch_shapes=scratch,
        compiler_params=pltpu.CompilerParams(vmem_limit_bytes=32 * 2**20),
        cost_estimate=pl.CostEstimate(flops=flops, bytes_accessed=moved, transcendentals=0),
        **more,
    )


def by_channels(gate, keys, values, taps, skip_gain):
    devices = lax.axis_size("outer") * lax.axis_size("inner")
    chans, seg = keys.shape
    own = chans // devices
    tiles = seg // LANES
    tables = [jnp.asarray(table) for table in transform_tables(devices, seg)]
    orders = send_orders(lax.axis_size("outer"), lax.axis_size("inner"))

    def regroup(rows, order):
        return lax.all_to_all(rows, AXES, split_axis=0, concat_axis=0, tiled=True, axis_index_groups=[order])

    product = keys * values
    product, skip = lax.optimization_barrier((product, skip_gain[:, None] * product))
    sent = on_core(partial(gather_kernel, orders[0]), (2 * chans * tiles, LANES), 4 * chans * seg * 4)(product, taps)
    groups = own
    conv = on_core(
        partial(convolve_kernel, devices, own, seg),
        (chans * tiles, LANES),
        2 * 10**6,
        10**9,
        [pltpu.VMEM((groups, devices * tiles, 2 * own // groups * LANES), jnp.float32)],
    )(regroup(sent, orders[0]), *tables)
    pieces = 4
    return on_core(
        partial(gate_kernel, orders[1]),
        (chans, seg),
        4 * chans * seg * 4,
        scratch=[pltpu.VMEM((chans, seg), jnp.float32), pltpu.SemaphoreType.DMA((pieces,))],
        out_specs=pl.BlockSpec(memory_space=pl.ANY),
    )(gate, skip, regroup(conv, orders[1]))


def on_device(gate, keys, values, taps, skip_gain):
    devices = lax.axis_size("outer") * lax.axis_size("inner")
    chans, seg = keys.shape
    if chans % devices == 0 and seg % LANES == 0 and devices % 8 == 0:
        return by_channels(gate, keys, values, taps, skip_gain)
    return by_sections(gate, keys, values, taps, skip_gain)


def solution(mesh):
    placed = (
        P(None, ("outer", "inner")),
        P(None, ("outer", "inner")),
        P(None, ("outer", "inner")),
        P(None, ("outer", "inner")),
        P(),
    )
    return jax.shard_map(
        on_device,
        mesh=mesh,
        in_specs=placed,
        out_specs=P(None, ("outer", "inner")),
        check_vma=False,
    )
```

```python
from functools import partial
import math

import jax
import jax.numpy as jnp
import ml_dtypes
import numpy as np
from jax import lax
from jax.experimental import pallas as pl
from jax.experimental.pallas import tpu as pltpu
from jax.sharding import PartitionSpec as P

LANES = 128
AXES = ("outer", "inner")

TWO_PI = 2.0 * math.pi
HIGHEST = lax.Precision.HIGHEST


def table(count_a, count_b, modulus, sign):
    left = lax.broadcasted_iota(jnp.int32, (count_a, count_b), 0)
    right = lax.broadcasted_iota(jnp.int32, (count_a, count_b), 1)
    phase = TWO_PI / modulus * (left * right % modulus).astype(jnp.float32)
    return (jnp.cos(phase), sign * jnp.sin(phase))


def mix(form, cosine, sine, real, imag):
    contract = partial(jnp.einsum, precision=HIGHEST)
    return (
        contract(form, cosine, real) - contract(form, sine, imag),
        contract(form, sine, real) + contract(form, cosine, imag),
    )


def rotate(real, imag, cosine, sine):
    return (real * cosine - imag * sine, real * sine + imag * cosine)


def forward_rows(real, imag):
    split = 16
    lead = real.shape[:-1]
    size = real.shape[-1]
    short = size // split
    real = real.reshape(lead + (split, short))
    imag = imag.reshape(lead + (split, short))
    cosine, sine = table(split, split, split, -1.0)
    real, imag = mix("ka,...as->...ks", cosine, sine, real, imag)
    cosine, sine = table(split, short, size, -1.0)
    real, imag = rotate(real, imag, cosine, sine)
    cosine, sine = table(short, short, short, -1.0)
    real, imag = mix("sb,...ks->...bk", cosine, sine, real, imag)
    return (real.reshape(lead + (size,)), imag.reshape(lead + (size,)))


def inverse_rows(real, imag):
    split = 16
    lead = real.shape[:-1]
    size = real.shape[-1]
    short = size // split
    real = real.reshape(lead + (short, split))
    imag = imag.reshape(lead + (short, split))
    cosine, sine = table(short, short, short, 1.0)
    real, imag = mix("sb,...bk->...sk", cosine, sine, real, imag)
    cosine, sine = table(short, split, size, 1.0)
    real, imag = rotate(real, imag, cosine, sine)
    cosine, sine = table(split, split, split, 1.0)
    real, imag = mix("ak,...sk->...as", cosine, sine, real, imag)
    return (real.reshape(lead + (size,)), imag.reshape(lead + (size,)))


def by_sections(gate, keys, values, taps, skip_gain):
    inner_count = lax.axis_size("inner")
    devices = lax.axis_size("outer") * inner_count
    rank = lax.axis_index("outer") * inner_count + lax.axis_index("inner")
    chans, seg = keys.shape
    both = 2 * chans
    cols = seg // devices
    blocks = 2 * devices
    full = blocks * seg
    contract = partial(jnp.einsum, precision=HIGHEST)
    product = keys * values
    source = jnp.concatenate([product, taps], axis=0)
    sectioned = lax.all_to_all(
        lax.all_to_all(
            source.reshape(both, 1, 1, seg), "outer", split_axis=3, concat_axis=1, tiled=True
        ),
        "inner",
        split_axis=3,
        concat_axis=2,
        tiled=True,
    )
    sectioned = sectioned.reshape(both, devices, cols)
    cosine, sine = table(blocks, devices, blocks, -1.0)
    real = contract("km,cmj->ckj", cosine, sectioned)
    imag = contract("km,cmj->ckj", sine, sectioned)
    offset = rank * cols + lax.broadcasted_iota(jnp.int32, (blocks, cols), 1)
    residue = lax.broadcasted_iota(jnp.int32, (blocks, cols), 0)
    phase = TWO_PI / full * (offset * residue).astype(jnp.float32)
    real, imag = rotate(real, imag, jnp.cos(phase)[None], -jnp.sin(phase)[None])
    outgoing = jnp.stack([real, imag]).reshape(2, both, blocks, 1, 1, cols)
    moved = lax.all_to_all(
        lax.all_to_all(outgoing, "outer", split_axis=2, concat_axis=3, tiled=True),
        "inner",
        split_axis=2,
        concat_axis=4,
        tiled=True,
    )
    moved = moved.reshape(2, both, 2, seg)
    spec_real, spec_imag = forward_rows(moved[0], moved[1])
    sig_real, filt_real = (spec_real[:chans], spec_real[chans:])
    sig_imag, filt_imag = (spec_imag[:chans], spec_imag[chans:])
    real = sig_real * filt_real - sig_imag * filt_imag
    imag = sig_real * filt_imag + sig_imag * filt_real
    real, imag = inverse_rows(real, imag)
    residue = 2 * rank + lax.broadcasted_iota(jnp.int32, (2, seg), 0)
    offset = lax.broadcasted_iota(jnp.int32, (2, seg), 1)
    phase = TWO_PI / full * (offset * residue).astype(jnp.float32)
    real, imag = rotate(real, imag, jnp.cos(phase)[None], jnp.sin(phase)[None])
    returning = jnp.stack([real, imag]).reshape(2, chans, 1, 1, 2, seg)
    gathered = lax.all_to_all(
        lax.all_to_all(returning, "outer", split_axis=5, concat_axis=2, tiled=True),
        "inner",
        split_axis=5,
        concat_axis=3,
        tiled=True,
    )
    gathered = gathered.reshape(2, chans, blocks, cols)
    cosine, sine = table(devices, blocks, blocks, 1.0)
    conv = contract("mk,ckj->cmj", cosine, gathered[0]) - contract("mk,ckj->cmj", sine, gathered[1])
    conv = conv * (1.0 / full)
    conv = lax.all_to_all(
        lax.all_to_all(
            conv.reshape(chans, devices, 1, 1, cols),
            "outer",
            split_axis=1,
            concat_axis=2,
            tiled=True,
        ),
        "inner",
        split_axis=1,
        concat_axis=3,
        tiled=True,
    )
    conv = conv.reshape(chans, seg)
    return gate * (conv + skip_gain[:, None] * product)


def halves(array):
    high = array.astype(ml_dtypes.bfloat16)
    low = (array - high.astype(np.float64)).astype(ml_dtypes.bfloat16)
    return high, low


def transform_tables(devices, seg):
    length = devices * seg
    count = length // LANES
    odd = 2 * np.arange(count) + 1
    angle = 2 * np.pi / (4 * count) * ((odd[:, None] * np.arange(count)[None, :]) % (4 * count))
    first = np.concatenate([np.cos(angle), -np.sin(angle)], axis=0)
    last = np.concatenate([np.cos(angle).T, -np.sin(angle).T], axis=1) / length
    angle = 2 * np.pi / (4 * length) * ((odd[:, None] * np.arange(LANES)[None, :]) % (4 * length))
    twiddle = np.stack([np.cos(angle), np.sin(angle)]).astype(np.float32)
    angle = 2 * np.pi / LANES * ((np.arange(LANES)[:, None] * np.arange(LANES)[None, :]) % LANES)
    cosine, sine = np.cos(angle), np.sin(angle)
    rows = np.block([[cosine, -sine], [sine, cosine]])
    back = np.block([[cosine, sine], [-sine, cosine]])
    first_high, first_low = halves(first)
    rows_high, rows_low = halves(rows)
    back_high, back_low = halves(back)
    last_high, last_low = halves(last)
    return (
        np.concatenate([first_high, first_high, first_low, first_low], axis=1),
        np.concatenate([rows_high, rows_low], axis=0),
        np.concatenate([back_high, back_low], axis=0),
        np.concatenate([last_high, last_high, last_low], axis=1),
        twiddle,
    )


def send_orders(outer, inner):
    half = inner // 2
    turns = [at // 2 + half * (at % 2) for at in range(2 * half)] + list(range(2 * half, inner))
    first = [at * inner + step for at in range(outer) for step in turns[1:] + turns[:1]]
    second = [at * inner + step for at in range(outer) for step in turns[1:] + turns[:1]]
    return first, second


def split(array, count=2):
    parts = []
    for _ in range(count):
        parts.append(array.astype(jnp.bfloat16))
        array = array - parts[-1].astype(jnp.float32)
    return parts


def dot(left, right):
    return jnp.dot(left, right, preferred_element_type=jnp.float32)


def convolve_kernel(
    devices, chans, seg, data_ref, first_ref, rows_ref, back_ref, last_ref, twiddle_ref, out_ref, signal_ref
):
    parts = seg // LANES
    count = devices * parts
    cosine, sine = twiddle_ref[0], twiddle_ref[1]

    def lanes(at):
        return slice(at * LANES, (at + 1) * LANES)

    first, second = send_orders(lax.axis_size("outer"), lax.axis_size("inner"))

    groups = chans
    each = chans // groups
    at = range(groups)
    for group in at:
        for kind in range(2):
            for chan in range(each):
                for device in range(devices):
                    came = ((device * 2 + kind) * chans + group * each + chan) * parts
                    to = first[device] * parts
                    signal_ref[group, to : to + parts, lanes(kind * each + chan)] = data_ref[came : came + parts, :]

    def times(pieces, table_ref):
        size = table_ref.shape[0] // 2
        by_high = dot(jnp.concatenate(pieces, axis=0), table_ref[:size, :])
        total = dot(pieces[0], table_ref[size:, :])
        rows = total.shape[0]
        for piece in reversed(range(len(pieces))):
            total = total + by_high[piece * rows : (piece + 1) * rows]
        return total

    def start(group):
        high, low = split(signal_ref[group])
        return dot(first_ref[...], jnp.concatenate([high, low, high, low], axis=0))

    def spectra(begun):
        turned = []
        for signal in range(2 * each):
            real, imag = begun[:count, lanes(signal)], begun[count:, lanes(signal)]
            turned.append(jnp.concatenate([real * cosine + imag * sine, imag * cosine - real * sine], axis=1))
        return times(split(jnp.concatenate(turned, axis=0), 3), rows_ref)

    def back(spectrum):
        mid = each * count
        sig_real, sig_imag = spectrum[:mid, :LANES], spectrum[:mid, LANES:]
        filt_real, filt_imag = spectrum[mid:, :LANES], spectrum[mid:, LANES:]
        real = sig_real * filt_real - sig_imag * filt_imag
        imag = sig_real * filt_imag + sig_imag * filt_real
        return times(split(jnp.concatenate([real, imag], axis=1)), back_ref)

    def turn_back(backed):
        real, imag = backed[:, :LANES], backed[:, LANES:]
        return jnp.concatenate([real * cosine - imag * sine, imag * cosine + real * sine], axis=0)

    begun = [start(group) for group in at]
    spectrum = [spectra(begun[group]) for group in at]
    backed = [back(spectrum[group]) for group in at]
    pair = 2 if chans % 2 == 0 else 1
    for own in range(0, chans, pair):
        high, low = split(jnp.concatenate([turn_back(backed[own + step]) for step in range(pair)], axis=1))
        conv = dot(last_ref[...], jnp.concatenate([high, low, high], axis=0))
        for step in range(pair):
            for device in range(devices):
                to = (device * chans + own + step) * parts
                came = second[device] * parts
                out_ref[to : to + parts, :] = conv[came : came + parts, lanes(step)]


def gather_kernel(order, product_ref, taps_ref, out_ref):
    rows = product_ref.shape[0] * product_ref.shape[1] // LANES // len(order)
    for kind, ref in enumerate((product_ref, taps_ref)):
        source = ref[...].reshape(len(order) * rows, LANES)
        for at, rank in enumerate(order):
            to = (2 * at + kind) * rows
            out_ref[to : to + rows, :] = source[rank * rows : (rank + 1) * rows]


def gate_kernel(order, gate_ref, skip_ref, conv_ref, out_hbm, out_ref, sems):
    chans, seg = gate_ref.shape
    pieces = sems.shape[0]
    step = chans // pieces
    rows = conv_ref.shape[0] // len(order)
    each = len(order) // pieces
    place = {rank: at * rows for at, rank in enumerate(order)}
    copies = []
    for piece in range(pieces):
        at = slice(piece * step, (piece + 1) * step)
        came = [conv_ref[place[rank] : place[rank] + rows, :] for rank in range(piece * each, (piece + 1) * each)]
        conv = jnp.concatenate(came, axis=0).reshape(step, seg)
        out_ref[at, :] = gate_ref[at, :] * (conv + skip_ref[at, :])
        copies.append(pltpu.make_async_copy(out_ref.at[at, :], out_hbm.at[at, :], sems.at[piece]))
        copies[piece].start()
    for copy in copies:
        copy.wait()


def on_core(kernel, shape, moved, flops=10**6, scratch=(), **more):
    return pl.pallas_call(
        kernel,
        out_shape=jax.ShapeDtypeStruct(shape, jnp.float32),
        scratch_shapes=scratch,
        compiler_params=pltpu.CompilerParams(vmem_limit_bytes=32 * 2**20),
        cost_estimate=pl.CostEstimate(flops=flops, bytes_accessed=moved, transcendentals=0),
        **more,
    )


def by_channels(gate, keys, values, taps, skip_gain):
    devices = lax.axis_size("outer") * lax.axis_size("inner")
    chans, seg = keys.shape
    own = chans // devices
    tiles = seg // LANES
    tables = [jnp.asarray(table) for table in transform_tables(devices, seg)]
    orders = send_orders(lax.axis_size("outer"), lax.axis_size("inner"))

    def regroup(rows, order):
        return lax.all_to_all(rows, AXES, split_axis=0, concat_axis=0, tiled=True, axis_index_groups=[order])

    product = keys * values
    product, skip = lax.optimization_barrier((product, skip_gain[:, None] * product))
    sent = on_core(partial(gather_kernel, orders[0]), (2 * chans * tiles, LANES), 4 * chans * seg * 4)(product, taps)
    groups = own
    conv = on_core(
        partial(convolve_kernel, devices, own, seg),
        (chans * tiles, LANES),
        2 * 10**6,
        10**9,
        [pltpu.VMEM((groups, devices * tiles, 2 * own // groups * LANES), jnp.float32)],
    )(regroup(sent, orders[0]), *tables)
    pieces = 4
    return on_core(
        partial(gate_kernel, orders[1]),
        (chans, seg),
        4 * chans * seg * 4,
        scratch=[pltpu.VMEM((chans, seg), jnp.float32), pltpu.SemaphoreType.DMA((pieces,))],
        out_specs=pl.BlockSpec(memory_space=pl.ANY),
    )(gate, skip, regroup(conv, orders[1]))


def on_device(gate, keys, values, taps, skip_gain):
    devices = lax.axis_size("outer") * lax.axis_size("inner")
    chans, seg = keys.shape
    if chans % devices == 0 and seg % LANES == 0 and devices % 8 == 0:
        return by_channels(gate, keys, values, taps, skip_gain)
    return by_sections(gate, keys, values, taps, skip_gain)


def solution(mesh):
    placed = (
        P(None, ("outer", "inner")),
        P(None, ("outer", "inner")),
        P(None, ("outer", "inner")),
        P(None, ("outer", "inner")),
        P(),
    )
    return jax.shard_map(
        on_device,
        mesh=mesh,
        in_specs=placed,
        out_specs=P(None, ("outer", "inner")),
        check_vma=False,
    )
```

```python
from functools import partial
import math

import jax
import jax.numpy as jnp
import ml_dtypes
import numpy as np
from jax import lax
from jax.experimental import pallas as pl
from jax.experimental.pallas import tpu as pltpu
from jax.sharding import PartitionSpec as P

LANES = 128
AXES = ("outer", "inner")

TWO_PI = 2.0 * math.pi
HIGHEST = lax.Precision.HIGHEST


def table(count_a, count_b, modulus, sign):
    left = lax.broadcasted_iota(jnp.int32, (count_a, count_b), 0)
    right = lax.broadcasted_iota(jnp.int32, (count_a, count_b), 1)
    phase = TWO_PI / modulus * (left * right % modulus).astype(jnp.float32)
    return (jnp.cos(phase), sign * jnp.sin(phase))


def mix(form, cosine, sine, real, imag):
    contract = partial(jnp.einsum, precision=HIGHEST)
    return (
        contract(form, cosine, real) - contract(form, sine, imag),
        contract(form, sine, real) + contract(form, cosine, imag),
    )


def rotate(real, imag, cosine, sine):
    return (real * cosine - imag * sine, real * sine + imag * cosine)


def forward_rows(real, imag):
    split = 16
    lead = real.shape[:-1]
    size = real.shape[-1]
    short = size // split
    real = real.reshape(lead + (split, short))
    imag = imag.reshape(lead + (split, short))
    cosine, sine = table(split, split, split, -1.0)
    real, imag = mix("ka,...as->...ks", cosine, sine, real, imag)
    cosine, sine = table(split, short, size, -1.0)
    real, imag = rotate(real, imag, cosine, sine)
    cosine, sine = table(short, short, short, -1.0)
    real, imag = mix("sb,...ks->...bk", cosine, sine, real, imag)
    return (real.reshape(lead + (size,)), imag.reshape(lead + (size,)))


def inverse_rows(real, imag):
    split = 16
    lead = real.shape[:-1]
    size = real.shape[-1]
    short = size // split
    real = real.reshape(lead + (short, split))
    imag = imag.reshape(lead + (short, split))
    cosine, sine = table(short, short, short, 1.0)
    real, imag = mix("sb,...bk->...sk", cosine, sine, real, imag)
    cosine, sine = table(short, split, size, 1.0)
    real, imag = rotate(real, imag, cosine, sine)
    cosine, sine = table(split, split, split, 1.0)
    real, imag = mix("ak,...sk->...as", cosine, sine, real, imag)
    return (real.reshape(lead + (size,)), imag.reshape(lead + (size,)))


def by_sections(gate, keys, values, taps, skip_gain):
    inner_count = lax.axis_size("inner")
    devices = lax.axis_size("outer") * inner_count
    rank = lax.axis_index("outer") * inner_count + lax.axis_index("inner")
    chans, seg = keys.shape
    both = 2 * chans
    cols = seg // devices
    blocks = 2 * devices
    full = blocks * seg
    contract = partial(jnp.einsum, precision=HIGHEST)
    product = keys * values
    source = jnp.concatenate([product, taps], axis=0)
    sectioned = lax.all_to_all(
        lax.all_to_all(
            source.reshape(both, 1, 1, seg), "outer", split_axis=3, concat_axis=1, tiled=True
        ),
        "inner",
        split_axis=3,
        concat_axis=2,
        tiled=True,
    )
    sectioned = sectioned.reshape(both, devices, cols)
    cosine, sine = table(blocks, devices, blocks, -1.0)
    real = contract("km,cmj->ckj", cosine, sectioned)
    imag = contract("km,cmj->ckj", sine, sectioned)
    offset = rank * cols + lax.broadcasted_iota(jnp.int32, (blocks, cols), 1)
    residue = lax.broadcasted_iota(jnp.int32, (blocks, cols), 0)
    phase = TWO_PI / full * (offset * residue).astype(jnp.float32)
    real, imag = rotate(real, imag, jnp.cos(phase)[None], -jnp.sin(phase)[None])
    outgoing = jnp.stack([real, imag]).reshape(2, both, blocks, 1, 1, cols)
    moved = lax.all_to_all(
        lax.all_to_all(outgoing, "outer", split_axis=2, concat_axis=3, tiled=True),
        "inner",
        split_axis=2,
        concat_axis=4,
        tiled=True,
    )
    moved = moved.reshape(2, both, 2, seg)
    spec_real, spec_imag = forward_rows(moved[0], moved[1])
    sig_real, filt_real = (spec_real[:chans], spec_real[chans:])
    sig_imag, filt_imag = (spec_imag[:chans], spec_imag[chans:])
    real = sig_real * filt_real - sig_imag * filt_imag
    imag = sig_real * filt_imag + sig_imag * filt_real
    real, imag = inverse_rows(real, imag)
    residue = 2 * rank + lax.broadcasted_iota(jnp.int32, (2, seg), 0)
    offset = lax.broadcasted_iota(jnp.int32, (2, seg), 1)
    phase = TWO_PI / full * (offset * residue).astype(jnp.float32)
    real, imag = rotate(real, imag, jnp.cos(phase)[None], jnp.sin(phase)[None])
    returning = jnp.stack([real, imag]).reshape(2, chans, 1, 1, 2, seg)
    gathered = lax.all_to_all(
        lax.all_to_all(returning, "outer", split_axis=5, concat_axis=2, tiled=True),
        "inner",
        split_axis=5,
        concat_axis=3,
        tiled=True,
    )
    gathered = gathered.reshape(2, chans, blocks, cols)
    cosine, sine = table(devices, blocks, blocks, 1.0)
    conv = contract("mk,ckj->cmj", cosine, gathered[0]) - contract("mk,ckj->cmj", sine, gathered[1])
    conv = conv * (1.0 / full)
    conv = lax.all_to_all(
        lax.all_to_all(
            conv.reshape(chans, devices, 1, 1, cols),
            "outer",
            split_axis=1,
            concat_axis=2,
            tiled=True,
        ),
        "inner",
        split_axis=1,
        concat_axis=3,
        tiled=True,
    )
    conv = conv.reshape(chans, seg)
    return gate * (conv + skip_gain[:, None] * product)


def halves(array):
    high = array.astype(ml_dtypes.bfloat16)
    low = (array - high.astype(np.float64)).astype(ml_dtypes.bfloat16)
    return high, low


def transform_tables(devices, seg):
    length = devices * seg
    count = length // LANES
    odd = 2 * np.arange(count) + 1
    angle = 2 * np.pi / (4 * count) * ((odd[:, None] * np.arange(count)[None, :]) % (4 * count))
    first = np.concatenate([np.cos(angle), -np.sin(angle)], axis=0)
    last = np.concatenate([np.cos(angle).T, -np.sin(angle).T], axis=1) / length
    angle = 2 * np.pi / (4 * length) * ((odd[:, None] * np.arange(LANES)[None, :]) % (4 * length))
    twiddle = np.stack([np.cos(angle), np.sin(angle)]).astype(np.float32)
    angle = 2 * np.pi / LANES * ((np.arange(LANES)[:, None] * np.arange(LANES)[None, :]) % LANES)
    cosine, sine = np.cos(angle), np.sin(angle)
    rows = np.block([[cosine, -sine], [sine, cosine]])
    back = np.block([[cosine, sine], [-sine, cosine]])
    first_high, first_low = halves(first)
    rows_high, rows_low = halves(rows)
    back_high, back_low = halves(back)
    last_high, last_low = halves(last)
    return (
        np.concatenate([first_high, first_high, first_low, first_low], axis=1),
        np.concatenate([rows_high, rows_low], axis=0),
        np.concatenate([back_high, back_low], axis=0),
        np.concatenate([last_high, last_high, last_low], axis=1),
        twiddle,
    )


def send_orders(outer, inner):
    half = inner // 2
    turns = [at // 2 + half * (at % 2) for at in range(2 * half)] + list(range(2 * half, inner))
    ring = [at ^ (at >> 1) for at in range(outer)] if outer & (outer - 1) == 0 else list(range(outer))
    first = [at * inner + step for at in ring[:1] + ring[:0:-1] for step in range(inner)]
    across = [0, 1, 4, 5, 2, 3, 6, 7] if outer == 8 else list(range(outer))
    second = [at * inner + step for at in across for step in turns[1:] + turns[:1]]
    return first, second


def split(array, count=2):
    parts = []
    for _ in range(count):
        parts.append(array.astype(jnp.bfloat16))
        array = array - parts[-1].astype(jnp.float32)
    return parts


def dot(left, right):
    return jnp.dot(left, right, preferred_element_type=jnp.float32)


def convolve_kernel(
    devices, chans, seg, data_ref, first_ref, rows_ref, back_ref, last_ref, twiddle_ref, out_ref, signal_ref
):
    parts = seg // LANES
    count = devices * parts
    cosine, sine = twiddle_ref[0], twiddle_ref[1]

    def lanes(at):
        return slice(at * LANES, (at + 1) * LANES)

    first, second = send_orders(lax.axis_size("outer"), lax.axis_size("inner"))

    groups = chans
    each = chans // groups
    at = range(groups)
    for group in at:
        for kind in range(2):
            for chan in range(each):
                for device in range(devices):
                    came = ((device * 2 + kind) * chans + group * each + chan) * parts
                    to = first[device] * parts
                    signal_ref[group, to : to + parts, lanes(kind * each + chan)] = data_ref[came : came + parts, :]

    def times(pieces, table_ref):
        size = table_ref.shape[0] // 2
        by_high = dot(jnp.concatenate(pieces, axis=0), table_ref[:size, :])
        total = dot(pieces[0], table_ref[size:, :])
        rows = total.shape[0]
        for piece in reversed(range(len(pieces))):
            total = total + by_high[piece * rows : (piece + 1) * rows]
        return total

    def start(group):
        high, low = split(signal_ref[group])
        return dot(first_ref[...], jnp.concatenate([high, low, high, low], axis=0))

    def spectra(begun):
        turned = []
        for signal in range(2 * each):
            real, imag = begun[:count, lanes(signal)], begun[count:, lanes(signal)]
            turned.append(jnp.concatenate([real * cosine + imag * sine, imag * cosine - real * sine], axis=1))
        return times(split(jnp.concatenate(turned, axis=0), 3), rows_ref)

    def back(spectrum):
        mid = each * count
        sig_real, sig_imag = spectrum[:mid, :LANES], spectrum[:mid, LANES:]
        filt_real, filt_imag = spectrum[mid:, :LANES], spectrum[mid:, LANES:]
        real = sig_real * filt_real - sig_imag * filt_imag
        imag = sig_real * filt_imag + sig_imag * filt_real
        return times(split(jnp.concatenate([real, imag], axis=1)), back_ref)

    def turn_back(backed):
        real, imag = backed[:, :LANES], backed[:, LANES:]
        return jnp.concatenate([real * cosine - imag * sine, imag * cosine + real * sine], axis=0)

    begun = [start(group) for group in at]
    spectrum = [spectra(begun[group]) for group in at]
    backed = [back(spectrum[group]) for group in at]
    pair = 2 if chans % 2 == 0 else 1
    for own in range(0, chans, pair):
        high, low = split(jnp.concatenate([turn_back(backed[own + step]) for step in range(pair)], axis=1))
        conv = dot(last_ref[...], jnp.concatenate([high, low, high], axis=0))
        for step in range(pair):
            for device in range(devices):
                to = (device * chans + own + step) * parts
                came = second[device] * parts
                out_ref[to : to + parts, :] = conv[came : came + parts, lanes(step)]


def gather_kernel(order, product_ref, taps_ref, out_ref):
    rows = product_ref.shape[0] * product_ref.shape[1] // LANES // len(order)
    for kind, ref in enumerate((product_ref, taps_ref)):
        source = ref[...].reshape(len(order) * rows, LANES)
        for at, rank in enumerate(order):
            to = (2 * at + kind) * rows
            out_ref[to : to + rows, :] = source[rank * rows : (rank + 1) * rows]


def gate_kernel(order, gate_ref, skip_ref, conv_ref, out_hbm, out_ref, sems):
    chans, seg = gate_ref.shape
    pieces = sems.shape[0]
    step = chans // pieces
    rows = conv_ref.shape[0] // len(order)
    each = len(order) // pieces
    place = {rank: at * rows for at, rank in enumerate(order)}
    copies = []
    for piece in range(pieces):
        at = slice(piece * step, (piece + 1) * step)
        came = [conv_ref[place[rank] : place[rank] + rows, :] for rank in range(piece * each, (piece + 1) * each)]
        conv = jnp.concatenate(came, axis=0).reshape(step, seg)
        out_ref[at, :] = gate_ref[at, :] * (conv + skip_ref[at, :])
        copies.append(pltpu.make_async_copy(out_ref.at[at, :], out_hbm.at[at, :], sems.at[piece]))
        copies[piece].start()
    for copy in copies:
        copy.wait()


def on_core(kernel, shape, moved, flops=10**6, scratch=(), **more):
    return pl.pallas_call(
        kernel,
        out_shape=jax.ShapeDtypeStruct(shape, jnp.float32),
        scratch_shapes=scratch,
        compiler_params=pltpu.CompilerParams(vmem_limit_bytes=32 * 2**20),
        cost_estimate=pl.CostEstimate(flops=flops, bytes_accessed=moved, transcendentals=0),
        **more,
    )


def by_channels(gate, keys, values, taps, skip_gain):
    devices = lax.axis_size("outer") * lax.axis_size("inner")
    chans, seg = keys.shape
    own = chans // devices
    tiles = seg // LANES
    tables = [jnp.asarray(table) for table in transform_tables(devices, seg)]
    orders = send_orders(lax.axis_size("outer"), lax.axis_size("inner"))

    def regroup(rows, order):
        return lax.all_to_all(rows, AXES, split_axis=0, concat_axis=0, tiled=True, axis_index_groups=[order])

    product = keys * values
    product, skip = lax.optimization_barrier((product, skip_gain[:, None] * product))
    sent = on_core(partial(gather_kernel, orders[0]), (2 * chans * tiles, LANES), 4 * chans * seg * 4)(product, taps)
    groups = own
    conv = on_core(
        partial(convolve_kernel, devices, own, seg),
        (chans * tiles, LANES),
        2 * 10**6,
        10**9,
        [pltpu.VMEM((groups, devices * tiles, 2 * own // groups * LANES), jnp.float32)],
    )(regroup(sent, orders[0]), *tables)
    pieces = 4
    return on_core(
        partial(gate_kernel, orders[1]),
        (chans, seg),
        4 * chans * seg * 4,
        scratch=[pltpu.VMEM((chans, seg), jnp.float32), pltpu.SemaphoreType.DMA((pieces,))],
        out_specs=pl.BlockSpec(memory_space=pl.ANY),
    )(gate, skip, regroup(conv, orders[1]))


def on_device(gate, keys, values, taps, skip_gain):
    devices = lax.axis_size("outer") * lax.axis_size("inner")
    chans, seg = keys.shape
    if chans % devices == 0 and seg % LANES == 0 and devices % 8 == 0:
        return by_channels(gate, keys, values, taps, skip_gain)
    return by_sections(gate, keys, values, taps, skip_gain)


def solution(mesh):
    placed = (
        P(None, ("outer", "inner")),
        P(None, ("outer", "inner")),
        P(None, ("outer", "inner")),
        P(None, ("outer", "inner")),
        P(),
    )
    return jax.shard_map(
        on_device,
        mesh=mesh,
        in_specs=placed,
        out_specs=P(None, ("outer", "inner")),
        check_vma=False,
    )
```

```python
from functools import partial
import math

import jax
import jax.numpy as jnp
import ml_dtypes
import numpy as np
from jax import lax
from jax.experimental import pallas as pl
from jax.experimental.pallas import tpu as pltpu
from jax.sharding import PartitionSpec as P

LANES = 128
AXES = ("outer", "inner")

TWO_PI = 2.0 * math.pi
HIGHEST = lax.Precision.HIGHEST


def table(count_a, count_b, modulus, sign):
    left = lax.broadcasted_iota(jnp.int32, (count_a, count_b), 0)
    right = lax.broadcasted_iota(jnp.int32, (count_a, count_b), 1)
    phase = TWO_PI / modulus * (left * right % modulus).astype(jnp.float32)
    return (jnp.cos(phase), sign * jnp.sin(phase))


def mix(form, cosine, sine, real, imag):
    contract = partial(jnp.einsum, precision=HIGHEST)
    return (
        contract(form, cosine, real) - contract(form, sine, imag),
        contract(form, sine, real) + contract(form, cosine, imag),
    )


def rotate(real, imag, cosine, sine):
    return (real * cosine - imag * sine, real * sine + imag * cosine)


def forward_rows(real, imag):
    split = 16
    lead = real.shape[:-1]
    size = real.shape[-1]
    short = size // split
    real = real.reshape(lead + (split, short))
    imag = imag.reshape(lead + (split, short))
    cosine, sine = table(split, split, split, -1.0)
    real, imag = mix("ka,...as->...ks", cosine, sine, real, imag)
    cosine, sine = table(split, short, size, -1.0)
    real, imag = rotate(real, imag, cosine, sine)
    cosine, sine = table(short, short, short, -1.0)
    real, imag = mix("sb,...ks->...bk", cosine, sine, real, imag)
    return (real.reshape(lead + (size,)), imag.reshape(lead + (size,)))


def inverse_rows(real, imag):
    split = 16
    lead = real.shape[:-1]
    size = real.shape[-1]
    short = size // split
    real = real.reshape(lead + (short, split))
    imag = imag.reshape(lead + (short, split))
    cosine, sine = table(short, short, short, 1.0)
    real, imag = mix("sb,...bk->...sk", cosine, sine, real, imag)
    cosine, sine = table(short, split, size, 1.0)
    real, imag = rotate(real, imag, cosine, sine)
    cosine, sine = table(split, split, split, 1.0)
    real, imag = mix("ak,...sk->...as", cosine, sine, real, imag)
    return (real.reshape(lead + (size,)), imag.reshape(lead + (size,)))


def by_sections(gate, keys, values, taps, skip_gain):
    inner_count = lax.axis_size("inner")
    devices = lax.axis_size("outer") * inner_count
    rank = lax.axis_index("outer") * inner_count + lax.axis_index("inner")
    chans, seg = keys.shape
    both = 2 * chans
    cols = seg // devices
    blocks = 2 * devices
    full = blocks * seg
    contract = partial(jnp.einsum, precision=HIGHEST)
    product = keys * values
    source = jnp.concatenate([product, taps], axis=0)
    sectioned = lax.all_to_all(
        lax.all_to_all(
            source.reshape(both, 1, 1, seg), "outer", split_axis=3, concat_axis=1, tiled=True
        ),
        "inner",
        split_axis=3,
        concat_axis=2,
        tiled=True,
    )
    sectioned = sectioned.reshape(both, devices, cols)
    cosine, sine = table(blocks, devices, blocks, -1.0)
    real = contract("km,cmj->ckj", cosine, sectioned)
    imag = contract("km,cmj->ckj", sine, sectioned)
    offset = rank * cols + lax.broadcasted_iota(jnp.int32, (blocks, cols), 1)
    residue = lax.broadcasted_iota(jnp.int32, (blocks, cols), 0)
    phase = TWO_PI / full * (offset * residue).astype(jnp.float32)
    real, imag = rotate(real, imag, jnp.cos(phase)[None], -jnp.sin(phase)[None])
    outgoing = jnp.stack([real, imag]).reshape(2, both, blocks, 1, 1, cols)
    moved = lax.all_to_all(
        lax.all_to_all(outgoing, "outer", split_axis=2, concat_axis=3, tiled=True),
        "inner",
        split_axis=2,
        concat_axis=4,
        tiled=True,
    )
    moved = moved.reshape(2, both, 2, seg)
    spec_real, spec_imag = forward_rows(moved[0], moved[1])
    sig_real, filt_real = (spec_real[:chans], spec_real[chans:])
    sig_imag, filt_imag = (spec_imag[:chans], spec_imag[chans:])
    real = sig_real * filt_real - sig_imag * filt_imag
    imag = sig_real * filt_imag + sig_imag * filt_real
    real, imag = inverse_rows(real, imag)
    residue = 2 * rank + lax.broadcasted_iota(jnp.int32, (2, seg), 0)
    offset = lax.broadcasted_iota(jnp.int32, (2, seg), 1)
    phase = TWO_PI / full * (offset * residue).astype(jnp.float32)
    real, imag = rotate(real, imag, jnp.cos(phase)[None], jnp.sin(phase)[None])
    returning = jnp.stack([real, imag]).reshape(2, chans, 1, 1, 2, seg)
    gathered = lax.all_to_all(
        lax.all_to_all(returning, "outer", split_axis=5, concat_axis=2, tiled=True),
        "inner",
        split_axis=5,
        concat_axis=3,
        tiled=True,
    )
    gathered = gathered.reshape(2, chans, blocks, cols)
    cosine, sine = table(devices, blocks, blocks, 1.0)
    conv = contract("mk,ckj->cmj", cosine, gathered[0]) - contract("mk,ckj->cmj", sine, gathered[1])
    conv = conv * (1.0 / full)
    conv = lax.all_to_all(
        lax.all_to_all(
            conv.reshape(chans, devices, 1, 1, cols),
            "outer",
            split_axis=1,
            concat_axis=2,
            tiled=True,
        ),
        "inner",
        split_axis=1,
        concat_axis=3,
        tiled=True,
    )
    conv = conv.reshape(chans, seg)
    return gate * (conv + skip_gain[:, None] * product)


def halves(array):
    high = array.astype(ml_dtypes.bfloat16)
    low = (array - high.astype(np.float64)).astype(ml_dtypes.bfloat16)
    return high, low


def transform_tables(devices, seg):
    length = devices * seg
    count = length // LANES
    odd = 2 * np.arange(count) + 1
    angle = 2 * np.pi / (4 * count) * ((odd[:, None] * np.arange(count)[None, :]) % (4 * count))
    first = np.concatenate([np.cos(angle), -np.sin(angle)], axis=0)
    last = np.concatenate([np.cos(angle).T, -np.sin(angle).T], axis=1) / length
    angle = 2 * np.pi / (4 * length) * ((odd[:, None] * np.arange(LANES)[None, :]) % (4 * length))
    twiddle = np.stack([np.cos(angle), np.sin(angle)]).astype(np.float32)
    angle = 2 * np.pi / LANES * ((np.arange(LANES)[:, None] * np.arange(LANES)[None, :]) % LANES)
    cosine, sine = np.cos(angle), np.sin(angle)
    rows = np.block([[cosine, -sine], [sine, cosine]])
    back = np.block([[cosine, sine], [-sine, cosine]])
    first_high, first_low = halves(first)
    rows_high, rows_low = halves(rows)
    back_high, back_low = halves(back)
    last_high, last_low = halves(last)
    return (
        np.concatenate([first_high, first_high, first_low, first_low], axis=1),
        np.concatenate([rows_high, rows_low], axis=0),
        np.concatenate([back_high, back_low], axis=0),
        np.concatenate([last_high, last_high, last_low], axis=1),
        twiddle,
    )


def send_orders(outer, inner):
    half = inner // 2
    turns = [at // 2 + half * (at % 2) for at in range(2 * half)] + list(range(2 * half, inner))
    ring = [at ^ (at >> 1) for at in range(outer)] if outer & (outer - 1) == 0 else list(range(outer))
    first = [at * inner + step for at in ring for step in range(inner)]
    second = [at * inner + step for at in range(outer) for step in turns[1:] + turns[:1]]
    return first, second


def split(array, count=2):
    parts = []
    for _ in range(count):
        parts.append(array.astype(jnp.bfloat16))
        array = array - parts[-1].astype(jnp.float32)
    return parts


def dot(left, right):
    return jnp.dot(left, right, preferred_element_type=jnp.float32)


def convolve_kernel(
    devices, chans, seg, data_ref, first_ref, rows_ref, back_ref, last_ref, twiddle_ref, out_ref, signal_ref
):
    parts = seg // LANES
    count = devices * parts
    cosine, sine = twiddle_ref[0], twiddle_ref[1]

    def lanes(at):
        return slice(at * LANES, (at + 1) * LANES)

    first, second = send_orders(lax.axis_size("outer"), lax.axis_size("inner"))

    groups = chans
    each = chans // groups
    at = range(groups)
    for group in at:
        for kind in range(2):
            for chan in range(each):
                for device in range(devices):
                    came = ((device * 2 + kind) * chans + group * each + chan) * parts
                    to = first[device] * parts
                    signal_ref[group, to : to + parts, lanes(kind * each + chan)] = data_ref[came : came + parts, :]

    def times(pieces, table_ref):
        size = table_ref.shape[0] // 2
        by_high = dot(jnp.concatenate(pieces, axis=0), table_ref[:size, :])
        total = dot(pieces[0], table_ref[size:, :])
        rows = total.shape[0]
        for piece in reversed(range(len(pieces))):
            total = total + by_high[piece * rows : (piece + 1) * rows]
        return total

    def start(group):
        high, low = split(signal_ref[group])
        return dot(first_ref[...], jnp.concatenate([high, low, high, low], axis=0))

    def spectra(begun):
        turned = []
        for signal in range(2 * each):
            real, imag = begun[:count, lanes(signal)], begun[count:, lanes(signal)]
            turned.append(jnp.concatenate([real * cosine + imag * sine, imag * cosine - real * sine], axis=1))
        return times(split(jnp.concatenate(turned, axis=0), 3), rows_ref)

    def back(spectrum):
        mid = each * count
        sig_real, sig_imag = spectrum[:mid, :LANES], spectrum[:mid, LANES:]
        filt_real, filt_imag = spectrum[mid:, :LANES], spectrum[mid:, LANES:]
        real = sig_real * filt_real - sig_imag * filt_imag
        imag = sig_real * filt_imag + sig_imag * filt_real
        return times(split(jnp.concatenate([real, imag], axis=1)), back_ref)

    def turn_back(backed):
        real, imag = backed[:, :LANES], backed[:, LANES:]
        return jnp.concatenate([real * cosine - imag * sine, imag * cosine + real * sine], axis=0)

    begun = [start(group) for group in at]
    spectrum = [spectra(begun[group]) for group in at]
    backed = [back(spectrum[group]) for group in at]
    pair = 2 if chans % 2 == 0 else 1
    for own in range(0, chans, pair):
        high, low = split(jnp.concatenate([turn_back(backed[own + step]) for step in range(pair)], axis=1))
        conv = dot(last_ref[...], jnp.concatenate([high, low, high], axis=0))
        for step in range(pair):
            for device in range(devices):
                to = (device * chans + own + step) * parts
                came = second[device] * parts
                out_ref[to : to + parts, :] = conv[came : came + parts, lanes(step)]


def gather_kernel(order, product_ref, taps_ref, out_ref):
    rows = product_ref.shape[0] * product_ref.shape[1] // LANES // len(order)
    for kind, ref in enumerate((product_ref, taps_ref)):
        source = ref[...].reshape(len(order) * rows, LANES)
        for at, rank in enumerate(order):
            to = (2 * at + kind) * rows
            out_ref[to : to + rows, :] = source[rank * rows : (rank + 1) * rows]


def gate_kernel(order, gate_ref, skip_ref, conv_ref, out_hbm, out_ref, sems):
    chans, seg = gate_ref.shape
    pieces = sems.shape[0]
    step = chans // pieces
    rows = conv_ref.shape[0] // len(order)
    each = len(order) // pieces
    place = {rank: at * rows for at, rank in enumerate(order)}
    copies = []
    for piece in range(pieces):
        at = slice(piece * step, (piece + 1) * step)
        came = [conv_ref[place[rank] : place[rank] + rows, :] for rank in range(piece * each, (piece + 1) * each)]
        conv = jnp.concatenate(came, axis=0).reshape(step, seg)
        out_ref[at, :] = gate_ref[at, :] * (conv + skip_ref[at, :])
        copies.append(pltpu.make_async_copy(out_ref.at[at, :], out_hbm.at[at, :], sems.at[piece]))
        copies[piece].start()
    for copy in copies:
        copy.wait()


def on_core(kernel, shape, moved, flops=10**6, scratch=(), **more):
    return pl.pallas_call(
        kernel,
        out_shape=jax.ShapeDtypeStruct(shape, jnp.float32),
        scratch_shapes=scratch,
        compiler_params=pltpu.CompilerParams(vmem_limit_bytes=32 * 2**20),
        cost_estimate=pl.CostEstimate(flops=flops, bytes_accessed=moved, transcendentals=0),
        **more,
    )


def by_channels(gate, keys, values, taps, skip_gain):
    devices = lax.axis_size("outer") * lax.axis_size("inner")
    chans, seg = keys.shape
    own = chans // devices
    tiles = seg // LANES
    tables = [jnp.asarray(table) for table in transform_tables(devices, seg)]
    orders = send_orders(lax.axis_size("outer"), lax.axis_size("inner"))

    def regroup(rows, order):
        return lax.all_to_all(rows, AXES, split_axis=0, concat_axis=0, tiled=True, axis_index_groups=[order])

    product = keys * values
    product, skip = lax.optimization_barrier((product, skip_gain[:, None] * product))
    sent = on_core(partial(gather_kernel, orders[0]), (2 * chans * tiles, LANES), 4 * chans * seg * 4)(product, taps)
    groups = own
    conv = on_core(
        partial(convolve_kernel, devices, own, seg),
        (chans * tiles, LANES),
        2 * 10**6,
        10**9,
        [pltpu.VMEM((groups, devices * tiles, 2 * own // groups * LANES), jnp.float32)],
    )(regroup(sent, orders[0]), *tables)
    pieces = 4
    return on_core(
        partial(gate_kernel, orders[1]),
        (chans, seg),
        4 * chans * seg * 4,
        scratch=[pltpu.VMEM((chans, seg), jnp.float32), pltpu.SemaphoreType.DMA((pieces,))],
        out_specs=pl.BlockSpec(memory_space=pl.ANY),
    )(gate, skip, regroup(conv, orders[1]))


def on_device(gate, keys, values, taps, skip_gain):
    devices = lax.axis_size("outer") * lax.axis_size("inner")
    chans, seg = keys.shape
    if chans % devices == 0 and seg % LANES == 0 and devices % 8 == 0:
        return by_channels(gate, keys, values, taps, skip_gain)
    return by_sections(gate, keys, values, taps, skip_gain)


def solution(mesh):
    placed = (
        P(None, ("outer", "inner")),
        P(None, ("outer", "inner")),
        P(None, ("outer", "inner")),
        P(None, ("outer", "inner")),
        P(),
    )
    return jax.shard_map(
        on_device,
        mesh=mesh,
        in_specs=placed,
        out_specs=P(None, ("outer", "inner")),
        check_vma=False,
    )
```

```python
from functools import partial
import math

import jax
import jax.numpy as jnp
import ml_dtypes
import numpy as np
from jax import lax
from jax.experimental import pallas as pl
from jax.experimental.pallas import tpu as pltpu
from jax.sharding import PartitionSpec as P

LANES = 128
AXES = ("outer", "inner")

TWO_PI = 2.0 * math.pi
HIGHEST = lax.Precision.HIGHEST


def table(count_a, count_b, modulus, sign):
    left = lax.broadcasted_iota(jnp.int32, (count_a, count_b), 0)
    right = lax.broadcasted_iota(jnp.int32, (count_a, count_b), 1)
    phase = TWO_PI / modulus * (left * right % modulus).astype(jnp.float32)
    return (jnp.cos(phase), sign * jnp.sin(phase))


def mix(form, cosine, sine, real, imag):
    contract = partial(jnp.einsum, precision=HIGHEST)
    return (
        contract(form, cosine, real) - contract(form, sine, imag),
        contract(form, sine, real) + contract(form, cosine, imag),
    )


def rotate(real, imag, cosine, sine):
    return (real * cosine - imag * sine, real * sine + imag * cosine)


def forward_rows(real, imag):
    split = 16
    lead = real.shape[:-1]
    size = real.shape[-1]
    short = size // split
    real = real.reshape(lead + (split, short))
    imag = imag.reshape(lead + (split, short))
    cosine, sine = table(split, split, split, -1.0)
    real, imag = mix("ka,...as->...ks", cosine, sine, real, imag)
    cosine, sine = table(split, short, size, -1.0)
    real, imag = rotate(real, imag, cosine, sine)
    cosine, sine = table(short, short, short, -1.0)
    real, imag = mix("sb,...ks->...bk", cosine, sine, real, imag)
    return (real.reshape(lead + (size,)), imag.reshape(lead + (size,)))


def inverse_rows(real, imag):
    split = 16
    lead = real.shape[:-1]
    size = real.shape[-1]
    short = size // split
    real = real.reshape(lead + (short, split))
    imag = imag.reshape(lead + (short, split))
    cosine, sine = table(short, short, short, 1.0)
    real, imag = mix("sb,...bk->...sk", cosine, sine, real, imag)
    cosine, sine = table(short, split, size, 1.0)
    real, imag = rotate(real, imag, cosine, sine)
    cosine, sine = table(split, split, split, 1.0)
    real, imag = mix("ak,...sk->...as", cosine, sine, real, imag)
    return (real.reshape(lead + (size,)), imag.reshape(lead + (size,)))


def by_sections(gate, keys, values, taps, skip_gain):
    inner_count = lax.axis_size("inner")
    devices = lax.axis_size("outer") * inner_count
    rank = lax.axis_index("outer") * inner_count + lax.axis_index("inner")
    chans, seg = keys.shape
    both = 2 * chans
    cols = seg // devices
    blocks = 2 * devices
    full = blocks * seg
    contract = partial(jnp.einsum, precision=HIGHEST)
    product = keys * values
    source = jnp.concatenate([product, taps], axis=0)
    sectioned = lax.all_to_all(
        lax.all_to_all(
            source.reshape(both, 1, 1, seg), "outer", split_axis=3, concat_axis=1, tiled=True
        ),
        "inner",
        split_axis=3,
        concat_axis=2,
        tiled=True,
    )
    sectioned = sectioned.reshape(both, devices, cols)
    cosine, sine = table(blocks, devices, blocks, -1.0)
    real = contract("km,cmj->ckj", cosine, sectioned)
    imag = contract("km,cmj->ckj", sine, sectioned)
    offset = rank * cols + lax.broadcasted_iota(jnp.int32, (blocks, cols), 1)
    residue = lax.broadcasted_iota(jnp.int32, (blocks, cols), 0)
    phase = TWO_PI / full * (offset * residue).astype(jnp.float32)
    real, imag = rotate(real, imag, jnp.cos(phase)[None], -jnp.sin(phase)[None])
    outgoing = jnp.stack([real, imag]).reshape(2, both, blocks, 1, 1, cols)
    moved = lax.all_to_all(
        lax.all_to_all(outgoing, "outer", split_axis=2, concat_axis=3, tiled=True),
        "inner",
        split_axis=2,
        concat_axis=4,
        tiled=True,
    )
    moved = moved.reshape(2, both, 2, seg)
    spec_real, spec_imag = forward_rows(moved[0], moved[1])
    sig_real, filt_real = (spec_real[:chans], spec_real[chans:])
    sig_imag, filt_imag = (spec_imag[:chans], spec_imag[chans:])
    real = sig_real * filt_real - sig_imag * filt_imag
    imag = sig_real * filt_imag + sig_imag * filt_real
    real, imag = inverse_rows(real, imag)
    residue = 2 * rank + lax.broadcasted_iota(jnp.int32, (2, seg), 0)
    offset = lax.broadcasted_iota(jnp.int32, (2, seg), 1)
    phase = TWO_PI / full * (offset * residue).astype(jnp.float32)
    real, imag = rotate(real, imag, jnp.cos(phase)[None], jnp.sin(phase)[None])
    returning = jnp.stack([real, imag]).reshape(2, chans, 1, 1, 2, seg)
    gathered = lax.all_to_all(
        lax.all_to_all(returning, "outer", split_axis=5, concat_axis=2, tiled=True),
        "inner",
        split_axis=5,
        concat_axis=3,
        tiled=True,
    )
    gathered = gathered.reshape(2, chans, blocks, cols)
    cosine, sine = table(devices, blocks, blocks, 1.0)
    conv = contract("mk,ckj->cmj", cosine, gathered[0]) - contract("mk,ckj->cmj", sine, gathered[1])
    conv = conv * (1.0 / full)
    conv = lax.all_to_all(
        lax.all_to_all(
            conv.reshape(chans, devices, 1, 1, cols),
            "outer",
            split_axis=1,
            concat_axis=2,
            tiled=True,
        ),
        "inner",
        split_axis=1,
        concat_axis=3,
        tiled=True,
    )
    conv = conv.reshape(chans, seg)
    return gate * (conv + skip_gain[:, None] * product)


def halves(array):
    high = array.astype(ml_dtypes.bfloat16)
    low = (array - high.astype(np.float64)).astype(ml_dtypes.bfloat16)
    return high, low


def transform_tables(devices, seg):
    length = devices * seg
    count = length // LANES
    odd = 2 * np.arange(count) + 1
    angle = 2 * np.pi / (4 * count) * ((odd[:, None] * np.arange(count)[None, :]) % (4 * count))
    first = np.concatenate([np.cos(angle), -np.sin(angle)], axis=0)
    last = np.concatenate([np.cos(angle).T, -np.sin(angle).T], axis=1) / length
    angle = 2 * np.pi / (4 * length) * ((odd[:, None] * np.arange(LANES)[None, :]) % (4 * length))
    twiddle = np.stack([np.cos(angle), np.sin(angle)]).astype(np.float32)
    angle = 2 * np.pi / LANES * ((np.arange(LANES)[:, None] * np.arange(LANES)[None, :]) % LANES)
    cosine, sine = np.cos(angle), np.sin(angle)
    rows = np.block([[cosine, -sine], [sine, cosine]])
    back = np.block([[cosine, sine], [-sine, cosine]])
    first_high, first_low = halves(first)
    rows_high, rows_low = halves(rows)
    back_high, back_low = halves(back)
    last_high, last_low = halves(last)
    return (
        np.concatenate([first_high, first_high, first_low, first_low], axis=1),
        np.concatenate([rows_high, rows_low], axis=0),
        np.concatenate([back_high, back_low], axis=0),
        np.concatenate([last_high, last_high, last_low], axis=1),
        twiddle,
    )


def send_orders(outer, inner):
    half = inner // 2
    turns = [at // 2 + half * (at % 2) for at in range(2 * half)] + list(range(2 * half, inner))
    ring = [at ^ (at >> 1) for at in range(outer)] if outer & (outer - 1) == 0 else list(range(outer))
    first = [at * inner + step for at in ring[:1] + ring[:0:-1] for step in range(inner)]
    second = [at * inner + step for at in range(outer) for step in turns[1:] + turns[:1]]
    return first, second


def split(array, count=2):
    parts = []
    for _ in range(count):
        parts.append(array.astype(jnp.bfloat16))
        array = array - parts[-1].astype(jnp.float32)
    return parts


def dot(left, right):
    return jnp.dot(left, right, preferred_element_type=jnp.float32)


def convolve_kernel(
    devices, chans, seg, data_ref, first_ref, rows_ref, back_ref, last_ref, twiddle_ref, out_ref, signal_ref
):
    parts = seg // LANES
    count = devices * parts
    cosine, sine = twiddle_ref[0], twiddle_ref[1]

    def lanes(at):
        return slice(at * LANES, (at + 1) * LANES)

    first, second = send_orders(lax.axis_size("outer"), lax.axis_size("inner"))

    groups = chans
    each = chans // groups
    at = range(groups)
    for group in at:
        for kind in range(2):
            for chan in range(each):
                for device in range(devices):
                    came = ((device * 2 + kind) * chans + group * each + chan) * parts
                    to = first[device] * parts
                    signal_ref[group, to : to + parts, lanes(kind * each + chan)] = data_ref[came : came + parts, :]

    def times(pieces, table_ref):
        size = table_ref.shape[0] // 2
        by_high = dot(jnp.concatenate(pieces, axis=0), table_ref[:size, :])
        total = dot(pieces[0], table_ref[size:, :])
        rows = total.shape[0]
        for piece in reversed(range(len(pieces))):
            total = total + by_high[piece * rows : (piece + 1) * rows]
        return total

    def start(group):
        high, low = split(signal_ref[group])
        return dot(first_ref[...], jnp.concatenate([high, low, high, low], axis=0))

    def spectra(begun):
        turned = []
        for signal in range(2 * each):
            real, imag = begun[:count, lanes(signal)], begun[count:, lanes(signal)]
            turned.append(jnp.concatenate([real * cosine + imag * sine, imag * cosine - real * sine], axis=1))
        return times(split(jnp.concatenate(turned, axis=0), 3), rows_ref)

    def back(spectrum):
        mid = each * count
        sig_real, sig_imag = spectrum[:mid, :LANES], spectrum[:mid, LANES:]
        filt_real, filt_imag = spectrum[mid:, :LANES], spectrum[mid:, LANES:]
        real = sig_real * filt_real - sig_imag * filt_imag
        imag = sig_real * filt_imag + sig_imag * filt_real
        return times(split(jnp.concatenate([real, imag], axis=1)), back_ref)

    def turn_back(backed):
        real, imag = backed[:, :LANES], backed[:, LANES:]
        return jnp.concatenate([real * cosine - imag * sine, imag * cosine + real * sine], axis=0)

    begun = [start(group) for group in at]
    spectrum = [spectra(begun[group]) for group in at]
    backed = [back(spectrum[group]) for group in at]
    pair = 2 if chans % 2 == 0 else 1
    for own in range(0, chans, pair):
        high, low = split(jnp.concatenate([turn_back(backed[own + step]) for step in range(pair)], axis=1))
        conv = dot(last_ref[...], jnp.concatenate([high, low, high], axis=0))
        for step in range(pair):
            for device in range(devices):
                to = (device * chans + own + step) * parts
                came = second[device] * parts
                out_ref[to : to + parts, :] = conv[came : came + parts, lanes(step)]


def gather_kernel(order, product_ref, taps_ref, out_ref):
    rows = product_ref.shape[0] * product_ref.shape[1] // LANES // len(order)
    for kind, ref in enumerate((product_ref, taps_ref)):
        source = ref[...].reshape(len(order) * rows, LANES)
        for at, rank in enumerate(order):
            to = (2 * at + kind) * rows
            out_ref[to : to + rows, :] = source[rank * rows : (rank + 1) * rows]


def gate_kernel(order, gate_ref, skip_ref, conv_ref, out_hbm, out_ref, sems):
    chans, seg = gate_ref.shape
    pieces = sems.shape[0]
    step = chans // pieces
    rows = conv_ref.shape[0] // len(order)
    each = len(order) // pieces
    place = {rank: at * rows for at, rank in enumerate(order)}
    copies = []
    for piece in range(pieces):
        at = slice(piece * step, (piece + 1) * step)
        came = [conv_ref[place[rank] : place[rank] + rows, :] for rank in range(piece * each, (piece + 1) * each)]
        conv = jnp.concatenate(came, axis=0).reshape(step, seg)
        out_ref[at, :] = gate_ref[at, :] * (conv + skip_ref[at, :])
        copies.append(pltpu.make_async_copy(out_ref.at[at, :], out_hbm.at[at, :], sems.at[piece]))
        copies[piece].start()
    for copy in copies:
        copy.wait()


def on_core(kernel, shape, moved, flops=10**6, scratch=(), **more):
    return pl.pallas_call(
        kernel,
        out_shape=jax.ShapeDtypeStruct(shape, jnp.float32),
        scratch_shapes=scratch,
        compiler_params=pltpu.CompilerParams(vmem_limit_bytes=32 * 2**20),
        cost_estimate=pl.CostEstimate(flops=flops, bytes_accessed=moved, transcendentals=0),
        **more,
    )


def by_channels(gate, keys, values, taps, skip_gain):
    devices = lax.axis_size("outer") * lax.axis_size("inner")
    chans, seg = keys.shape
    own = chans // devices
    tiles = seg // LANES
    tables = [jnp.asarray(table) for table in transform_tables(devices, seg)]
    orders = send_orders(lax.axis_size("outer"), lax.axis_size("inner"))

    def regroup(rows, order):
        return lax.all_to_all(rows, AXES, split_axis=0, concat_axis=0, tiled=True, axis_index_groups=[order])

    product = keys * values
    product, skip = lax.optimization_barrier((product, skip_gain[:, None] * product))
    sent = on_core(partial(gather_kernel, orders[0]), (2 * chans * tiles, LANES), 4 * chans * seg * 4)(product, taps)
    groups = own
    conv = on_core(
        partial(convolve_kernel, devices, own, seg),
        (chans * tiles, LANES),
        2 * 10**6,
        10**9,
        [pltpu.VMEM((groups, devices * tiles, 2 * own // groups * LANES), jnp.float32)],
    )(regroup(sent, orders[0]), *tables)
    pieces = 8
    return on_core(
        partial(gate_kernel, orders[1]),
        (chans, seg),
        4 * chans * seg * 4,
        scratch=[pltpu.VMEM((chans, seg), jnp.float32), pltpu.SemaphoreType.DMA((pieces,))],
        out_specs=pl.BlockSpec(memory_space=pl.ANY),
    )(gate, skip, regroup(conv, orders[1]))


def on_device(gate, keys, values, taps, skip_gain):
    devices = lax.axis_size("outer") * lax.axis_size("inner")
    chans, seg = keys.shape
    if chans % devices == 0 and seg % LANES == 0 and devices % 8 == 0:
        return by_channels(gate, keys, values, taps, skip_gain)
    return by_sections(gate, keys, values, taps, skip_gain)


def solution(mesh):
    placed = (
        P(None, ("outer", "inner")),
        P(None, ("outer", "inner")),
        P(None, ("outer", "inner")),
        P(None, ("outer", "inner")),
        P(),
    )
    return jax.shard_map(
        on_device,
        mesh=mesh,
        in_specs=placed,
        out_specs=P(None, ("outer", "inner")),
        check_vma=False,
    )
```

```python
from functools import partial
import math

import jax
import jax.numpy as jnp
import ml_dtypes
import numpy as np
from jax import lax
from jax.experimental import pallas as pl
from jax.experimental.pallas import tpu as pltpu
from jax.sharding import PartitionSpec as P

LANES = 128
AXES = ("outer", "inner")

TWO_PI = 2.0 * math.pi
HIGHEST = lax.Precision.HIGHEST


def table(count_a, count_b, modulus, sign):
    left = lax.broadcasted_iota(jnp.int32, (count_a, count_b), 0)
    right = lax.broadcasted_iota(jnp.int32, (count_a, count_b), 1)
    phase = TWO_PI / modulus * (left * right % modulus).astype(jnp.float32)
    return (jnp.cos(phase), sign * jnp.sin(phase))


def mix(form, cosine, sine, real, imag):
    contract = partial(jnp.einsum, precision=HIGHEST)
    return (
        contract(form, cosine, real) - contract(form, sine, imag),
        contract(form, sine, real) + contract(form, cosine, imag),
    )


def rotate(real, imag, cosine, sine):
    return (real * cosine - imag * sine, real * sine + imag * cosine)


def forward_rows(real, imag):
    split = 16
    lead = real.shape[:-1]
    size = real.shape[-1]
    short = size // split
    real = real.reshape(lead + (split, short))
    imag = imag.reshape(lead + (split, short))
    cosine, sine = table(split, split, split, -1.0)
    real, imag = mix("ka,...as->...ks", cosine, sine, real, imag)
    cosine, sine = table(split, short, size, -1.0)
    real, imag = rotate(real, imag, cosine, sine)
    cosine, sine = table(short, short, short, -1.0)
    real, imag = mix("sb,...ks->...bk", cosine, sine, real, imag)
    return (real.reshape(lead + (size,)), imag.reshape(lead + (size,)))


def inverse_rows(real, imag):
    split = 16
    lead = real.shape[:-1]
    size = real.shape[-1]
    short = size // split
    real = real.reshape(lead + (short, split))
    imag = imag.reshape(lead + (short, split))
    cosine, sine = table(short, short, short, 1.0)
    real, imag = mix("sb,...bk->...sk", cosine, sine, real, imag)
    cosine, sine = table(short, split, size, 1.0)
    real, imag = rotate(real, imag, cosine, sine)
    cosine, sine = table(split, split, split, 1.0)
    real, imag = mix("ak,...sk->...as", cosine, sine, real, imag)
    return (real.reshape(lead + (size,)), imag.reshape(lead + (size,)))


def by_sections(gate, keys, values, taps, skip_gain):
    inner_count = lax.axis_size("inner")
    devices = lax.axis_size("outer") * inner_count
    rank = lax.axis_index("outer") * inner_count + lax.axis_index("inner")
    chans, seg = keys.shape
    both = 2 * chans
    cols = seg // devices
    blocks = 2 * devices
    full = blocks * seg
    contract = partial(jnp.einsum, precision=HIGHEST)
    product = keys * values
    source = jnp.concatenate([product, taps], axis=0)
    sectioned = lax.all_to_all(
        lax.all_to_all(
            source.reshape(both, 1, 1, seg), "outer", split_axis=3, concat_axis=1, tiled=True
        ),
        "inner",
        split_axis=3,
        concat_axis=2,
        tiled=True,
    )
    sectioned = sectioned.reshape(both, devices, cols)
    cosine, sine = table(blocks, devices, blocks, -1.0)
    real = contract("km,cmj->ckj", cosine, sectioned)
    imag = contract("km,cmj->ckj", sine, sectioned)
    offset = rank * cols + lax.broadcasted_iota(jnp.int32, (blocks, cols), 1)
    residue = lax.broadcasted_iota(jnp.int32, (blocks, cols), 0)
    phase = TWO_PI / full * (offset * residue).astype(jnp.float32)
    real, imag = rotate(real, imag, jnp.cos(phase)[None], -jnp.sin(phase)[None])
    outgoing = jnp.stack([real, imag]).reshape(2, both, blocks, 1, 1, cols)
    moved = lax.all_to_all(
        lax.all_to_all(outgoing, "outer", split_axis=2, concat_axis=3, tiled=True),
        "inner",
        split_axis=2,
        concat_axis=4,
        tiled=True,
    )
    moved = moved.reshape(2, both, 2, seg)
    spec_real, spec_imag = forward_rows(moved[0], moved[1])
    sig_real, filt_real = (spec_real[:chans], spec_real[chans:])
    sig_imag, filt_imag = (spec_imag[:chans], spec_imag[chans:])
    real = sig_real * filt_real - sig_imag * filt_imag
    imag = sig_real * filt_imag + sig_imag * filt_real
    real, imag = inverse_rows(real, imag)
    residue = 2 * rank + lax.broadcasted_iota(jnp.int32, (2, seg), 0)
    offset = lax.broadcasted_iota(jnp.int32, (2, seg), 1)
    phase = TWO_PI / full * (offset * residue).astype(jnp.float32)
    real, imag = rotate(real, imag, jnp.cos(phase)[None], jnp.sin(phase)[None])
    returning = jnp.stack([real, imag]).reshape(2, chans, 1, 1, 2, seg)
    gathered = lax.all_to_all(
        lax.all_to_all(returning, "outer", split_axis=5, concat_axis=2, tiled=True),
        "inner",
        split_axis=5,
        concat_axis=3,
        tiled=True,
    )
    gathered = gathered.reshape(2, chans, blocks, cols)
    cosine, sine = table(devices, blocks, blocks, 1.0)
    conv = contract("mk,ckj->cmj", cosine, gathered[0]) - contract("mk,ckj->cmj", sine, gathered[1])
    conv = conv * (1.0 / full)
    conv = lax.all_to_all(
        lax.all_to_all(
            conv.reshape(chans, devices, 1, 1, cols),
            "outer",
            split_axis=1,
            concat_axis=2,
            tiled=True,
        ),
        "inner",
        split_axis=1,
        concat_axis=3,
        tiled=True,
    )
    conv = conv.reshape(chans, seg)
    return gate * (conv + skip_gain[:, None] * product)


def halves(array):
    high = array.astype(ml_dtypes.bfloat16)
    low = (array - high.astype(np.float64)).astype(ml_dtypes.bfloat16)
    return high, low


def transform_tables(devices, seg):
    length = devices * seg
    count = length // LANES
    odd = 2 * np.arange(count) + 1
    angle = 2 * np.pi / (4 * count) * ((odd[:, None] * np.arange(count)[None, :]) % (4 * count))
    first = np.concatenate([np.cos(angle), -np.sin(angle)], axis=0)
    last = np.concatenate([np.cos(angle).T, -np.sin(angle).T], axis=1) / length
    angle = 2 * np.pi / (4 * length) * ((odd[:, None] * np.arange(LANES)[None, :]) % (4 * length))
    twiddle = np.stack([np.cos(angle), np.sin(angle)]).astype(np.float32)
    angle = 2 * np.pi / LANES * ((np.arange(LANES)[:, None] * np.arange(LANES)[None, :]) % LANES)
    cosine, sine = np.cos(angle), np.sin(angle)
    rows = np.block([[cosine, -sine], [sine, cosine]])
    back = np.block([[cosine, sine], [-sine, cosine]])
    first_high, first_low = halves(first)
    rows_high, rows_low = halves(rows)
    back_high, back_low = halves(back)
    last_high, last_low = halves(last)
    return (
        np.concatenate([first_high, first_high, first_low, first_low], axis=1),
        np.concatenate([rows_high, rows_high, rows_high, rows_low], axis=0),
        np.concatenate([back_high, back_high, back_low], axis=0),
        np.concatenate([last_high, last_high, last_low], axis=1),
        twiddle,
    )


def send_orders(outer, inner):
    half = inner // 2
    turns = [at // 2 + half * (at % 2) for at in range(2 * half)] + list(range(2 * half, inner))
    ring = [at ^ (at >> 1) for at in range(outer)] if outer & (outer - 1) == 0 else list(range(outer))
    first = [at * inner + step for at in ring[:1] + ring[:0:-1] for step in range(inner)]
    second = [at * inner + step for at in range(outer) for step in turns[1:] + turns[:1]]
    return first, second


def split(array, count=2):
    parts = []
    for _ in range(count):
        parts.append(array.astype(jnp.bfloat16))
        array = array - parts[-1].astype(jnp.float32)
    return parts


def dot(left, right):
    return jnp.dot(left, right, preferred_element_type=jnp.float32)


def convolve_kernel(
    devices, chans, seg, data_ref, first_ref, rows_ref, back_ref, last_ref, twiddle_ref, out_ref, signal_ref
):
    parts = seg // LANES
    count = devices * parts
    cosine, sine = twiddle_ref[0], twiddle_ref[1]

    def lanes(at):
        return slice(at * LANES, (at + 1) * LANES)

    first, second = send_orders(lax.axis_size("outer"), lax.axis_size("inner"))

    groups = chans
    each = chans // groups
    at = range(groups)
    for group in at:
        for kind in range(2):
            for chan in range(each):
                for device in range(devices):
                    came = ((device * 2 + kind) * chans + group * each + chan) * parts
                    to = first[device] * parts
                    signal_ref[group, to : to + parts, lanes(kind * each + chan)] = data_ref[came : came + parts, :]

    def start(group):
        high, low = split(signal_ref[group])
        return dot(first_ref[...], jnp.concatenate([high, low, high, low], axis=0))

    def spectra(begun):
        turned = []
        for signal in range(2 * each):
            real, imag = begun[:count, lanes(signal)], begun[count:, lanes(signal)]
            turned.append(jnp.concatenate([real * cosine + imag * sine, imag * cosine - real * sine], axis=1))
        high, low, rest = split(jnp.concatenate(turned, axis=0), 3)
        return dot(jnp.concatenate([high, low, rest, high], axis=1), rows_ref[...])

    def back(spectrum):
        mid = each * count
        sig_real, sig_imag = spectrum[:mid, :LANES], spectrum[:mid, LANES:]
        filt_real, filt_imag = spectrum[mid:, :LANES], spectrum[mid:, LANES:]
        real = sig_real * filt_real - sig_imag * filt_imag
        imag = sig_real * filt_imag + sig_imag * filt_real
        high, low = split(jnp.concatenate([real, imag], axis=1))
        return dot(jnp.concatenate([high, low, high], axis=1), back_ref[...])

    def turn_back(backed):
        real, imag = backed[:, :LANES], backed[:, LANES:]
        return jnp.concatenate([real * cosine - imag * sine, imag * cosine + real * sine], axis=0)

    begun = [start(group) for group in at]
    spectrum = [spectra(begun[group]) for group in at]
    backed = [back(spectrum[group]) for group in at]
    pair = 2 if chans % 2 == 0 else 1
    for own in range(0, chans, pair):
        high, low = split(jnp.concatenate([turn_back(backed[own + step]) for step in range(pair)], axis=1))
        conv = dot(last_ref[...], jnp.concatenate([high, low, high], axis=0))
        for step in range(pair):
            for device in range(devices):
                to = (device * chans + own + step) * parts
                came = second[device] * parts
                out_ref[to : to + parts, :] = conv[came : came + parts, lanes(step)]


def gather_kernel(order, product_ref, taps_ref, out_ref):
    rows = product_ref.shape[0] * product_ref.shape[1] // LANES // len(order)
    for kind, ref in enumerate((product_ref, taps_ref)):
        source = ref[...].reshape(len(order) * rows, LANES)
        for at, rank in enumerate(order):
            to = (2 * at + kind) * rows
            out_ref[to : to + rows, :] = source[rank * rows : (rank + 1) * rows]


def gate_kernel(order, gate_ref, skip_ref, conv_ref, out_hbm, out_ref, sems):
    chans, seg = gate_ref.shape
    pieces = sems.shape[0]
    step = chans // pieces
    rows = conv_ref.shape[0] // len(order)
    each = len(order) // pieces
    place = {rank: at * rows for at, rank in enumerate(order)}
    copies = []
    for piece in range(pieces):
        at = slice(piece * step, (piece + 1) * step)
        came = [conv_ref[place[rank] : place[rank] + rows, :] for rank in range(piece * each, (piece + 1) * each)]
        conv = jnp.concatenate(came, axis=0).reshape(step, seg)
        out_ref[at, :] = gate_ref[at, :] * (conv + skip_ref[at, :])
        copies.append(pltpu.make_async_copy(out_ref.at[at, :], out_hbm.at[at, :], sems.at[piece]))
        copies[piece].start()
    for copy in copies:
        copy.wait()


def on_core(kernel, shape, moved, flops=10**6, scratch=(), **more):
    return pl.pallas_call(
        kernel,
        out_shape=jax.ShapeDtypeStruct(shape, jnp.float32),
        scratch_shapes=scratch,
        compiler_params=pltpu.CompilerParams(vmem_limit_bytes=32 * 2**20),
        cost_estimate=pl.CostEstimate(flops=flops, bytes_accessed=moved, transcendentals=0),
        **more,
    )


def by_channels(gate, keys, values, taps, skip_gain):
    devices = lax.axis_size("outer") * lax.axis_size("inner")
    chans, seg = keys.shape
    own = chans // devices
    tiles = seg // LANES
    tables = [jnp.asarray(table) for table in transform_tables(devices, seg)]
    orders = send_orders(lax.axis_size("outer"), lax.axis_size("inner"))

    def regroup(rows, order):
        return lax.all_to_all(rows, AXES, split_axis=0, concat_axis=0, tiled=True, axis_index_groups=[order])

    product = keys * values
    product, skip = lax.optimization_barrier((product, skip_gain[:, None] * product))
    sent = on_core(partial(gather_kernel, orders[0]), (2 * chans * tiles, LANES), 4 * chans * seg * 4)(product, taps)
    groups = own
    conv = on_core(
        partial(convolve_kernel, devices, own, seg),
        (chans * tiles, LANES),
        2 * 10**6,
        10**9,
        [pltpu.VMEM((groups, devices * tiles, 2 * own // groups * LANES), jnp.float32)],
    )(regroup(sent, orders[0]), *tables)
    pieces = 4
    return on_core(
        partial(gate_kernel, orders[1]),
        (chans, seg),
        4 * chans * seg * 4,
        scratch=[pltpu.VMEM((chans, seg), jnp.float32), pltpu.SemaphoreType.DMA((pieces,))],
        out_specs=pl.BlockSpec(memory_space=pl.ANY),
    )(gate, skip, regroup(conv, orders[1]))


def on_device(gate, keys, values, taps, skip_gain):
    devices = lax.axis_size("outer") * lax.axis_size("inner")
    chans, seg = keys.shape
    if chans % devices == 0 and seg % LANES == 0 and devices % 8 == 0:
        return by_channels(gate, keys, values, taps, skip_gain)
    return by_sections(gate, keys, values, taps, skip_gain)


def solution(mesh):
    placed = (
        P(None, ("outer", "inner")),
        P(None, ("outer", "inner")),
        P(None, ("outer", "inner")),
        P(None, ("outer", "inner")),
        P(),
    )
    return jax.shard_map(
        on_device,
        mesh=mesh,
        in_specs=placed,
        out_specs=P(None, ("outer", "inner")),
        check_vma=False,
    )
```
